32 devices in a mesh: wide: 8 (over z, x), narrow: 4 (over y, core).
Axes of the slice: x: 2, y: 2, z: 4, core: 2. Of those that a mesh axis runs over, the one named last changes fastest.
Arguments:
- embed_table: bfloat16 [131072, 640], P('wide', 'narrow'), may hold values from -6 to 6
- requests: int32 [8, 8, 768, 40], P('wide', None, None, 'narrow'), may hold values from -1 to 16383, as said below
- slot_index: int32 [49152, 40], P('wide', 'narrow'), may hold values from 0 to 6143, as said below
- event_mask: int32 [49152], P(('wide', 'narrow')), may hold values from 0 to 1, as said below
- labels: int32 [49152], P(('wide', 'narrow')), may hold values from 0 to 1
- dense_feats: float32 [49152, 128], P(('wide', 'narrow')), may hold values from -40 to 40
- proj_weight: bfloat16 [640, 512], P('narrow'), may hold values from -0.25 to 0.25
- dense_weight: bfloat16 [128, 512], replicated, may hold values from -0.5 to 0.5
- proj_bias: bfloat16 [512], replicated, may hold values from -4 to 4
- up_weight: bfloat16 [14, 512, 1024], P(None, None, 'narrow'), may hold values from -0.25 to 0.25
- down_weight: bfloat16 [14, 1024, 512], P(None, 'narrow'), may hold values from -0.1875 to 0.1875
- norm_gain: bfloat16 [14, 512], replicated, may hold values from 0.5 to 1.5
- norm_shift: bfloat16 [14, 512], replicated, may hold values from -4 to 4
- gate_weight: bfloat16 [6, 512, 6], replicated, may hold values from -0.125 to 0.125
- tower_in: bfloat16 [6, 512, 128], replicated, may hold values from -0.25 to 0.25
- tower_bias: bfloat16 [6, 128], replicated, may hold values from -4 to 4
- tower_out: bfloat16 [6, 128], replicated, may hold values from -0.5 to 0.5
- tower_out_bias: bfloat16 [6], replicated, may hold values from -6 to 6
Outputs:
- logits: float32 [49152], P(('wide', 'narrow'))
- row_grads: float32 [8, 8, 768, 640], P('wide', None, None, 'narrow')
- proj_weight_grad: float32 [640, 512], P('narrow')
- dense_weight_grad: float32 [128, 512], replicated
- proj_bias_grad: float32 [512], replicated
- up_weight_grad: float32 [14, 512, 1024], P(None, None, 'narrow')
- down_weight_grad: float32 [14, 1024, 512], P(None, 'narrow')
- norm_gain_grad: float32 [14, 512], replicated
- norm_shift_grad: float32 [14, 512], replicated
- gate_weight_grad: float32 [6, 512, 6], replicated
- tower_in_grad: float32 [6, 512, 128], replicated
- tower_bias_grad: float32 [6, 128], replicated
- tower_out_grad: float32 [6, 128], replicated
- tower_out_bias_grad: float32 [6], replicated
The draws below stay inside these ranges and needn't reach their ends.
Inputs may be any that keep to these rules, and one draw needn't show every extreme that they name: requests[w, o, s, f] is the row, counted within owner o's 16384 rows, looked up by field f of the event of device w whose slot in field f is o * 768 + s; -1 where that event is padding. `slot_index`: for each device of wide and each field, the 6144 events of that device hold distinct slots. `event_mask`: A device's events form 6 blocks of 1024, block d holding domain d; live events come first in a block, a quarter or more of each block is live, and every device has a full block.
All inputs are finite; a program needn't handle non-finite values.
Results may differ from the reference program's by a relative error of at most 0.01.
Values may be sent and summed in bfloat16 or wider, within the bound.
A program may use at most 320 MiB of HBM per device.

```python
import jax
import jax.numpy as jnp
from jax import lax

D = 512
HID = 1024
FIELDS = 40
EMB = 16
DENSE = 128
TW = 128
DOMAINS = 6
SHARED = 2
DOM_EXP = 2
EV_DEV = 6144
R_DEV = 16384
NEXP = 14
GATES = 6
DSLOT = 1024
CAP = 768
EVENTS = 49152
ROWS = 131072
N_WIDE = 8


def event_layout(key):
    count_key = jax.random.fold_in(key, 11)
    order_key = jax.random.fold_in(key, 12)
    row_key = jax.random.fold_in(key, 13)
    counts = jax.random.randint(count_key, (N_WIDE, DOMAINS), DSLOT // 4, DSLOT + 1)
    full_block = jnp.arange(DOMAINS)[None, :] == jnp.arange(N_WIDE)[:, None] % DOMAINS
    counts = jnp.where(full_block, DSLOT, counts)
    live = (jnp.arange(DSLOT)[None, None, :] < counts[:, :, None]).astype(jnp.int32).reshape(N_WIDE, EV_DEV)
    scores = jax.random.randint(order_key, (N_WIDE, FIELDS, EV_DEV), 0, 1 << 20) * EV_DEV + jnp.arange(EV_DEV)
    event_at = jnp.argsort(scores, axis=-1).astype(jnp.int32)
    places = jnp.argsort(event_at, axis=-1).astype(jnp.int32)
    live_wide = jnp.broadcast_to(live[:, None, :], (N_WIDE, FIELDS, EV_DEV))
    live_at = jnp.take_along_axis(live_wide, event_at, axis=-1)
    row_ids = jax.random.randint(row_key, (N_WIDE, FIELDS, EV_DEV), 0, R_DEV)
    wanted = jnp.where(live_at == 1, row_ids, -1).astype(jnp.int32)
    wanted = wanted.reshape(N_WIDE, FIELDS, N_WIDE, CAP).transpose(0, 2, 3, 1)
    slot_table = places.transpose(0, 2, 1).reshape(N_WIDE * EV_DEV, FIELDS)
    return (live.reshape(N_WIDE * EV_DEV), slot_table, wanted)


def draw_requests(key, part):
    return event_layout(key)[2]


def draw_slot_index(key, part):
    return event_layout(key)[1]


def draw_event_mask(key, part):
    return event_layout(key)[0]


def draw_dense_feats(key, part):
    key = jax.random.fold_in(key, 5)
    keys = jax.random.split(key, 3)
    positions = jnp.arange(EVENTS, dtype=jnp.float32)
    rising = 1.0 + 2.0 * positions / EVENTS
    column_scale = jnp.exp(jax.random.uniform(keys[0], (DENSE,), minval=jnp.log(0.3), maxval=jnp.log(3.0)))
    offsets = jax.random.uniform(keys[1], (DENSE,), minval=-1.0, maxval=1.0)
    base = jnp.clip(jax.random.normal(keys[2], (EVENTS, DENSE)), -4.0, 4.0)
    return (column_scale[None, :] * (offsets[None, :] + rising[:, None] * base)).astype(jnp.float32)


def place_ends(entries, key, smallest, high):
    spot = [jax.random.randint(jax.random.fold_in(key, axis), (), 0, length) for axis, length in enumerate(entries.shape)]
    main_axis = entries.shape.index(max(entries.shape))
    next_to = spot[:main_axis] + [(spot[main_axis] + 1) % entries.shape[main_axis]] + spot[main_axis + 1:]
    return entries.at[tuple(spot)].set(smallest).at[tuple(next_to)].set(high)


def level_of(own_key, extent, cuts, smallest, high):
    level = 1.0
    for dim, parts in cuts:
        steps = jax.random.uniform(jax.random.fold_in(jax.random.fold_in(own_key, 6), dim), (parts,), jnp.float32, smallest / len(cuts), high / len(cuts))
        level = level * jnp.repeat(jnp.exp(steps), extent[dim] // parts).reshape((-1,) + (1,) * (len(extent) - 1 - dim))
    return level


def scatter_about(key, dims, scale, most, cuts=(), kind=jnp.bfloat16):
    entries = scale * jax.random.normal(key, dims, jnp.float32)
    if cuts:
        entries = entries * level_of(key, dims, cuts, -0.22, 0.18)
    return jnp.clip(entries, -most, most).astype(kind)


def setup_inputs(seed: int = 0) -> dict:
    key_of = jax.random.split(jax.random.key(seed), 19)
    return {
        "embed_table": scatter_about(key_of[0], (ROWS, FIELDS * EMB), 1.0, 6.0, ((0, 8), (1, 4))),
        "requests": draw_requests(jax.random.fold_in(key_of[18], 71), 0),
        "slot_index": draw_slot_index(jax.random.fold_in(key_of[18], 71), 0),
        "event_mask": draw_event_mask(jax.random.fold_in(key_of[18], 71), 0),
        "labels": place_ends(jax.random.randint(key_of[4], (EVENTS,), 0, 2), jax.random.fold_in(key_of[4], 1), 0, 1).astype(jnp.int32),
        "dense_feats": draw_dense_feats(jax.random.fold_in(key_of[18], 71), 0),
        "proj_weight": scatter_about(key_of[6], (FIELDS * EMB, D), (FIELDS * EMB) ** -0.5, 0.25, ((0, 4),)),
        "dense_weight": scatter_about(key_of[7], (DENSE, D), DENSE ** -0.5, 0.5),
        "proj_bias": scatter_about(key_of[8], (D,), 0.3, 4.0),
        "up_weight": scatter_about(key_of[9], (NEXP, D, HID), D ** -0.5, 0.25, ((2, 4),)),
        "down_weight": scatter_about(key_of[10], (NEXP, HID, D), HID ** -0.5, 0.1875, ((1, 4),)),
        "norm_gain": jnp.clip(1.0 + 0.1 * jax.random.normal(key_of[11], (NEXP, D), jnp.float32), 0.5, 1.5).astype(jnp.bfloat16),
        "norm_shift": scatter_about(key_of[12], (NEXP, D), 0.3, 4.0),
        "gate_weight": scatter_about(key_of[13], (DOMAINS, D, GATES), (4 * D) ** -0.5, 0.125),
        "tower_in": scatter_about(key_of[14], (DOMAINS, D, TW), D ** -0.5, 0.25),
        "tower_bias": scatter_about(key_of[15], (DOMAINS, TW), 0.3, 4.0),
        "tower_out": scatter_about(key_of[16], (DOMAINS, TW), TW ** -0.5, 0.5),
        "tower_out_bias": scatter_about(key_of[17], (DOMAINS,), 0.5, 6.0),
    }


@jax.custom_vjp
def low(v):
    return lax.optimization_barrier(v.astype(jnp.bfloat16)).astype(jnp.float32)

@jax.custom_vjp
def low_back(v):
    return v

def low_keep(v):
    return (low(v), None)

def low_pass(kept, grad):
    return (grad,)

def back_keep(v):
    return (v, None)

def back_low(kept, grad):
    return (low(grad),)
low.defvjp(low_keep, low_pass)
low_back.defvjp(back_keep, back_low)
highest = lax.Precision.HIGHEST

def layer_norm(values, gains, shifts):
    center = lax.optimization_barrier(jnp.mean(values, axis=-1, keepdims=True))
    centered = values - center
    variance = lax.optimization_barrier(jnp.mean(centered * centered, axis=-1, keepdims=True))
    return centered * lax.rsqrt(variance + 1e-05) * gains + shifts

def forward(received, proj_weight, dense_weight, proj_bias, up_weight, down_weight, norm_gain, norm_shift, gate_weight, tower_in, tower_bias, tower_out, tower_out_bias, dense_low, slot_index, live_rows, label_rows):
    rows_four = received.reshape(N_WIDE, EV_DEV, FIELDS, EMB)
    place = slot_index.reshape(N_WIDE, EV_DEV, FIELDS, 1)
    embedded = jnp.take_along_axis(rows_four, place, axis=1).reshape(EVENTS, FIELDS * EMB)
    projected = jnp.dot(embedded, proj_weight, precision=highest)
    projected = projected + jnp.dot(dense_low, dense_weight, precision=highest) + proj_bias
    inputs = low_back(low(projected))
    blocks = inputs.reshape(N_WIDE, DOMAINS, DSLOT, D)
    pre_shared = low_back(jnp.einsum('rm,kmh->krh', inputs, up_weight[:SHARED], precision=highest))
    act_shared = low(jax.nn.gelu(pre_shared))
    out_shared = low_back(jnp.einsum('krh,khm->krm', act_shared, down_weight[:SHARED], precision=highest))
    normed_shared = layer_norm(out_shared, norm_gain[:SHARED][:, None, :], norm_shift[:SHARED][:, None, :])
    up_domain = up_weight[SHARED:].reshape(DOMAINS, DOM_EXP, D, HID)
    down_domain = down_weight[SHARED:].reshape(DOMAINS, DOM_EXP, HID, D)
    pre_domain = low_back(jnp.einsum('wdsm,djmh->jwdsh', blocks, up_domain, precision=highest))
    act_domain = low(jax.nn.gelu(pre_domain))
    out_domain = low_back(jnp.einsum('jwdsh,djhm->jwdsm', act_domain, down_domain, precision=highest))
    gain_domain = norm_gain[SHARED:].reshape(DOMAINS, DOM_EXP, D).transpose(1, 0, 2)[:, None, :, None, :]
    shift_domain = norm_shift[SHARED:].reshape(DOMAINS, DOM_EXP, D).transpose(1, 0, 2)[:, None, :, None, :]
    normed_domain = layer_norm(out_domain, gain_domain, shift_domain).reshape(DOM_EXP, EVENTS, D)
    gate_logits = jnp.einsum('wdsm,dmg->wdsg', blocks, gate_weight, precision=highest).reshape(EVENTS, GATES)
    shared_gates = jax.nn.softmax(gate_logits[:, :SHARED], axis=-1)
    domain_gates = jax.nn.softmax(gate_logits[:, SHARED:SHARED + DOM_EXP], axis=-1)
    top_gates = jax.nn.softmax(gate_logits[:, SHARED + DOM_EXP:], axis=-1)
    mixture = top_gates[:, 0:1] * jnp.einsum('rk,krm->rm', shared_gates, normed_shared, precision=highest)
    mixture = mixture + top_gates[:, 1:2] * jnp.einsum('rj,jrm->rm', domain_gates, normed_domain, precision=highest)
    hidden = low(mixture).reshape(N_WIDE, DOMAINS, DSLOT, D)
    tower_pre = jnp.einsum('wdsm,dmk->wdsk', hidden, tower_in, precision=highest) + tower_bias[None, :, None, :]
    tower_act = jax.nn.gelu(low_back(tower_pre))
    logits = lax.optimization_barrier(jnp.sum(tower_act * tower_out[None, :, None, :], axis=-1)) + tower_out_bias[None, :, None]
    logits = logits.reshape(EVENTS)
    per_event = jax.nn.softplus(logits) - label_rows * logits
    return (jnp.sum(live_rows * per_event), logits)

def reference(embed_table, requests, slot_index, event_mask, labels, dense_feats, proj_weight, dense_weight, proj_bias, up_weight, down_weight, norm_gain, norm_shift, gate_weight, tower_in, tower_bias, tower_out, tower_out_bias):
    table_rows = embed_table.astype(jnp.float32).reshape(ROWS * FIELDS, EMB)
    owners = jnp.arange(N_WIDE, dtype=jnp.int32)[None, :, None, None]
    field_ids = jnp.arange(FIELDS, dtype=jnp.int32)[None, None, None, :]
    flat_index = ((owners * R_DEV + jnp.maximum(requests, 0)) * FIELDS + field_ids).astype(jnp.int32)
    found = jnp.take(table_rows, flat_index, axis=0)
    found = jnp.where((requests >= 0)[..., None], found, jnp.zeros_like(found))
    received = found.reshape(N_WIDE, N_WIDE, CAP, FIELDS * EMB)
    live_rows = event_mask.astype(jnp.float32)
    dense_four = dense_feats.reshape(N_WIDE, DOMAINS, DSLOT, DENSE)
    live_four = live_rows.reshape(N_WIDE, DOMAINS, DSLOT, 1)
    counts = lax.optimization_barrier(jnp.sum(live_four, axis=(0, 2)))
    domain_means = lax.optimization_barrier(jnp.sum(live_four * dense_four, axis=(0, 2))) / counts
    centered = dense_four - domain_means[None, :, None, :]
    spread = lax.optimization_barrier(jnp.sum(live_four * centered * centered, axis=(0, 2))) / counts
    dense_low = low(centered * lax.rsqrt(spread[None, :, None, :] + 1e-05)).reshape(EVENTS, DENSE)
    weights = tuple((weight.astype(jnp.float32) for weight in (proj_weight, dense_weight, proj_bias, up_weight, down_weight, norm_gain, norm_shift, gate_weight, tower_in, tower_bias, tower_out, tower_out_bias)))
    label_rows = labels.astype(jnp.float32)

    def loss_of(received_rows, *params):
        return forward(received_rows, *params, dense_low, slot_index, live_rows, label_rows)
    loss, pullback, logits = jax.vjp(loss_of, received, *weights, has_aux=True)
    grads = pullback(jnp.ones_like(loss))
    row_grads = jnp.transpose(grads[0], (1, 0, 2, 3))
    return (logits, row_grads, grads[1], grads[2], grads[3], grads[4], grads[5], grads[6], grads[7], grads[8], grads[9], grads[10], grads[11], grads[12])
```

```python
import functools

import jax
import jax.numpy as jnp
from jax import lax
from jax.experimental import pallas as pl
from jax.experimental.pallas import tpu as pltpu
from jax.sharding import PartitionSpec as P

D = 512
HID = 1024
EMB = 16
DENSE = 128
DOMAINS = 6
SHARED = 2
DOM_EXP = 2
DSLOT = 1024
HALF = DSLOT // 2
VMEM = 56 * 2**20
BF = jnp.bfloat16
F32 = jnp.float32


def dot(a, b, ca, cb):
    return lax.dot_general(a, b, (((ca,), (cb,)), ((), ())), preferred_element_type=F32)


def lookup_kernel(lo_n, hi_n, fields, idx_ref, tab_ref, out_ref):
    length = idx_ref.shape[-1]
    shift = hi_n.bit_length() - 1
    for f in range(fields):
        idx = idx_ref[0, f : f + 1, :]
        hi = jnp.where(idx >= 0, idx & (hi_n - 1), -1)
        lo = lax.shift_right_logical(jnp.maximum(idx, 0), shift)
        hot = (lax.broadcasted_iota(jnp.int32, (hi_n, length), 0) == hi).astype(BF)
        lhs = tab_ref[:, f * EMB : (f + 1) * EMB, :].reshape(lo_n * EMB, hi_n)
        res = jnp.dot(lhs, hot, preferred_element_type=F32)
        acc = res[0:EMB]
        for step in range(1, lo_n):
            acc = jnp.where(lo == step, res[step * EMB : (step + 1) * EMB], acc)
        out_ref[0, f * EMB : (f + 1) * EMB, :] = acc.astype(BF)


def lookup(idx, tab, name, order=lambda i: i):
    groups, fields, length = idx.shape
    lo_n, cols, hi_n = tab.shape
    return pl.pallas_call(
        functools.partial(lookup_kernel, lo_n, hi_n, fields),
        grid=(groups,),
        in_specs=[
            pl.BlockSpec((1, fields, length), lambda i: (order(i), 0, 0)),
            pl.BlockSpec((lo_n, cols, hi_n), lambda i: (0, 0, 0)),
        ],
        out_specs=pl.BlockSpec((1, cols, length), lambda i: (i, 0, 0)),
        out_shape=jax.ShapeDtypeStruct((groups, cols, length), BF),
        compiler_params=pltpu.CompilerParams(vmem_limit_bytes=VMEM),
        cost_estimate=pl.CostEstimate(
            flops=2 * groups * length * cols * lo_n * hi_n, bytes_accessed=8 * 2**20, transcendentals=0
        ),
        name=name,
    )(idx, tab)


def place_kernel(lo_n, hi_n, steps, idx_ref, grad_ref, out_ref):
    length = idx_ref.shape[-1] // steps
    shift = hi_n.bit_length() - 1
    total = None
    for s in range(steps):
        cols = slice(s * length, (s + 1) * length)
        idx = idx_ref[0, :, cols]
        hi = idx & (hi_n - 1)
        lo = lax.shift_right_logical(idx, shift)
        grad = grad_ref[0, :, cols]
        hot = (lax.broadcasted_iota(jnp.int32, (hi_n, length), 0) == hi).astype(BF)
        lhs = jnp.concatenate(
            [jnp.where(lo == step, grad, jnp.zeros_like(grad)) for step in range(lo_n)], axis=0
        )
        part = dot(lhs, hot, 1, 1)
        total = part if total is None else total + part
    out_ref[...] = total.reshape(lo_n, EMB, hi_n).astype(BF)


def place(idx, grad, lo_n, hi_n):
    fields, _, length = idx.shape
    return pl.pallas_call(
        functools.partial(place_kernel, lo_n, hi_n, 4),
        grid=(fields,),
        in_specs=[
            pl.BlockSpec((1, 1, length), lambda i: (i, 0, 0)),
            pl.BlockSpec((1, EMB, length), lambda i: (i, 0, 0)),
        ],
        out_specs=pl.BlockSpec((lo_n, EMB, hi_n), lambda i: (0, i, 0)),
        out_shape=jax.ShapeDtypeStruct((lo_n, fields * EMB, hi_n), BF),
        compiler_params=pltpu.CompilerParams(vmem_limit_bytes=VMEM),
        cost_estimate=pl.CostEstimate(
            flops=2 * fields * EMB * length * lo_n * hi_n, bytes_accessed=6 * 2**20, transcendentals=0
        ),
        name="place_rows",
    )(idx, grad)


def layer_norm(values, gains, shifts):
    center = jnp.mean(values, axis=-1, keepdims=True)
    centered = values - center
    variance = jnp.mean(centered * centered, axis=-1, keepdims=True)
    return centered * lax.rsqrt(variance + 1e-05) * gains + shifts


def combine(outputs, logits_gate, gains, shifts):
    normed = layer_norm(outputs, gains, shifts)
    shared_gates = jax.nn.softmax(logits_gate[:, :SHARED], axis=-1)
    domain_gates = jax.nn.softmax(logits_gate[:, SHARED : SHARED + DOM_EXP], axis=-1)
    top_gates = jax.nn.softmax(logits_gate[:, SHARED + DOM_EXP :], axis=-1)
    shared = sum(shared_gates[:, k : k + 1] * normed[k] for k in range(SHARED))
    own = sum(domain_gates[:, k : k + 1] * normed[SHARED + k] for k in range(DOM_EXP))
    return top_gates[:, 0:1] * shared + top_gates[:, 1:2] * own


def split_dot(rows, weights, spec):
    return jnp.concatenate(
        [
            jnp.einsum(spec, rows[:DSLOT], weights[0], preferred_element_type=F32),
            jnp.einsum(spec, rows[DSLOT:], weights[1], preferred_element_type=F32),
        ],
        axis=0,
    )


def split_sum(rows):
    return jnp.stack([jnp.sum(rows[:DSLOT], axis=0), jnp.sum(rows[DSLOT:], axis=0)])


def spread_rows(pair, rows):
    full = jnp.broadcast_to(pair[0], (DSLOT,) + pair[0].shape)
    half = jnp.broadcast_to(pair[1], (rows - DSLOT,) + pair[1].shape)
    return jnp.concatenate([full, half], axis=0)


def own_stats(rows, weight):
    count = jnp.sum(weight)
    mean = jnp.sum(rows * weight[:, None], axis=0) / jnp.maximum(count, 1.0)
    off = rows - mean
    return [mean, jnp.sum(off * off * weight[:, None], axis=0), jnp.broadcast_to(count, mean.shape)]


def pool(means, squares, counts):
    total = jnp.sum(counts, axis=0)
    mean = jnp.sum(counts * means, axis=0) / total
    off = means - mean
    return mean, (jnp.sum(squares, axis=0) + jnp.sum(counts * off * off, axis=0)) / total


def shards(
    embed_table,
    requests,
    slot_index,
    event_mask,
    labels,
    dense_feats,
    proj_weight,
    dense_weight,
    proj_bias,
    up_weight,
    down_weight,
    norm_gain,
    norm_shift,
    gate_weight,
    tower_in,
    tower_bias,
    tower_out,
    tower_out_bias,
):
    narrow = lax.axis_size("narrow")
    me = lax.axis_index("narrow")
    chip, core = me // 2, me % 2
    ev_rows, fields = slot_index.shape
    rows = ev_rows // narrow
    owners, cap = requests.shape[1], requests.shape[2]
    hid_here = up_weight.shape[2]
    other_chip = [(i, i ^ 2) for i in range(narrow)]
    other_core = [(i, i ^ 1) for i in range(narrow)]
    full = 3 * chip + 2 * core
    half = 3 * chip + 1

    def swap(x, pairs):
        return lax.ppermute(x, "narrow", pairs)

    asked = lax.all_to_all(requests[0].transpose(0, 2, 1), "wide", 0, 0, tiled=True)

    def chip_experts(w, which):
        return jnp.concatenate(
            [w[:SHARED], lax.dynamic_slice_in_dim(w, SHARED + 6 * which, 6, axis=0)], axis=0
        )

    def core_experts(w, which, axis):
        at = lambda start, size: lax.dynamic_slice_in_dim(w, start, size, axis=axis)
        return jnp.concatenate([at(0, 2), at(2 + 4 * which, 2), at(4, 2)], axis=axis)

    def bring(w):
        near = chip_experts(w, chip)
        far = swap(chip_experts(w, 1 - chip), other_chip)
        both = jnp.stack([near, far])
        mine = core_experts(both, core, 1)
        theirs = swap(core_experts(both, 1 - core, 1), other_core)
        return jnp.concatenate([mine, theirs], axis=0)

    up = bring(up_weight)
    down = bring(down_weight)
    up = up.transpose(1, 2, 0, 3).reshape(6, D, HID)
    down = down.transpose(1, 0, 2, 3).reshape(6, HID, D)
    proj_full = lax.all_gather(proj_weight, "narrow", axis=0, tiled=True)

    def turned(x):
        return jnp.where(core == 1, jnp.roll(x, -HALF, axis=0), x)

    live = turned(event_mask).astype(F32)
    label_rows = turned(labels).astype(F32)
    feats = turned(dense_feats)
    blank = jnp.zeros((2, DENSE), F32)
    stats = jnp.stack(own_stats(feats[:DSLOT], live[:DSLOT]) + own_stats(feats[DSLOT:], live[DSLOT:]))
    stats = jnp.concatenate([stats, blank], axis=0)
    stats = jnp.concatenate([stats, swap(stats, other_core)], axis=0)
    every = lax.all_to_all(
        jnp.broadcast_to(stats, (owners,) + stats.shape), "wide", 0, 0, tiled=True
    )
    full_mean, full_spread = pool(every[:, 0], every[:, 1], every[:, 2])
    both = jnp.concatenate([every[:, 3:6], every[:, 11:14]], axis=0)
    half_mean, half_spread = pool(both[:, 0], both[:, 1], both[:, 2])
    centered = feats - spread_rows(jnp.stack([full_mean, half_mean]), rows)
    scale = lax.rsqrt(jnp.stack([full_spread, half_spread]) + 1e-05)
    dense_low = (centered * spread_rows(scale, rows)).astype(BF)

    table_rows = embed_table.shape[0]
    tab = embed_table.reshape(32, table_rows // 32, fields * EMB).transpose(0, 2, 1)
    if cap % 128 == 0:
        found = lookup(asked, tab, "lookup_rows")
    else:
        flat = asked.transpose(1, 0, 2).reshape(fields, DOMAINS, DSLOT).transpose(1, 0, 2)
        found = lookup(flat, tab, "lookup_rows")
        found = found.transpose(1, 0, 2).reshape(fields * EMB, owners, cap).transpose(1, 0, 2)
    received = lax.all_to_all(found, "wide", 0, 0, tiled=True)

    hi_n = 256
    lo_n = ev_rows // hi_n
    received = received.transpose(1, 0, 2).reshape(fields * EMB, lo_n, hi_n).transpose(1, 0, 2)
    blocks = ev_rows // HALF
    order = [q * 3 + (s + q % 2) % 3 for q in range(narrow) for s in range(3)]
    slots = slot_index.reshape(blocks, HALF, fields)
    slots = jnp.stack([slots[b] for b in order]).transpose(0, 2, 1)
    embedded = lookup(slots, received, "order_rows")
    embedded = embedded.reshape(narrow, 3, fields * EMB, HALF).transpose(0, 2, 1, 3)
    embedded = embedded.reshape(narrow, fields * EMB, rows)
    embedded = lax.all_to_all(embedded, "narrow", 0, 0, tiled=True)
    embedded = embedded.reshape(narrow * fields * EMB, rows)

    projected = dot(embedded, proj_full, 0, 0) + jnp.dot(dense_low, dense_weight, preferred_element_type=F32)
    projected = projected + proj_bias.astype(F32)
    inputs = projected.astype(BF)

    parts = ((slice(0, 2), slice(0, rows)), (slice(2, 4), slice(0, DSLOT)), (slice(4, 6), slice(DSLOT, rows)))
    pres = [jnp.einsum("rm,kmh->krh", inputs[r], up[k], preferred_element_type=F32) for k, r in parts]
    gelus = [jax.vjp(jax.nn.gelu, pre) for pre in pres]
    acts = [g[0].astype(BF) for g in gelus]
    outs = [
        jnp.einsum("krh,khm->krm", a, down[k], preferred_element_type=F32) for a, (k, r) in zip(acts, parts)
    ]
    expert_out = jnp.concatenate([outs[0], jnp.concatenate(outs[1:], axis=1)], axis=0)

    def pick(w):
        return jnp.stack(
            [
                lax.dynamic_index_in_dim(w, full, keepdims=False),
                lax.dynamic_index_in_dim(w, half, keepdims=False),
            ]
        )

    def expert_rows(w):
        w = w.astype(F32)
        own = pick(w[SHARED:].reshape(DOMAINS, DOM_EXP, D))
        return jnp.concatenate(
            [
                jnp.broadcast_to(w[:SHARED, None, :], (SHARED, rows, D)),
                spread_rows(own, rows).transpose(1, 0, 2),
            ],
            axis=0,
        )

    gate_two = pick(gate_weight)
    gate_logits = split_dot(inputs, gate_two, "rm,mg->rg")
    mixture, combine_back = jax.vjp(
        combine, expert_out, gate_logits, expert_rows(norm_gain), expert_rows(norm_shift)
    )
    hidden = mixture.astype(BF)
    tower_two = pick(tower_in)
    tower_pre = split_dot(hidden, tower_two, "rm,mk->rk")
    tower_pre = tower_pre + spread_rows(pick(tower_bias).astype(F32), rows)
    tower_act, tower_back = jax.vjp(jax.nn.gelu, tower_pre)
    out_rows = spread_rows(pick(tower_out).astype(F32), rows)
    logits = jnp.sum(tower_act * out_rows, axis=1)
    logits = logits + spread_rows(pick(tower_out_bias).astype(F32), rows)
    logit_grad = (jax.nn.sigmoid(logits) - label_rows) * live
    out_bias_grad = split_sum(logit_grad)
    out_vector_grad = split_sum(logit_grad[:, None] * tower_act)
    pre_low = tower_back(logit_grad[:, None] * out_rows)[0].astype(BF)
    bias_tower_grad = split_sum(pre_low.astype(F32))

    def split_outer(a, b):
        return jnp.stack(
            [dot(a[:DSLOT], b[:DSLOT], 0, 0), dot(a[DSLOT:], b[DSLOT:], 0, 0)]
        )

    tower_weight_grad = split_outer(hidden, pre_low)
    hidden_grad = split_dot(pre_low, tower_two, "rk,mk->rm")
    out_grad, gate_logit_grad, gain_rows_grad, shift_rows_grad = combine_back(hidden_grad)

    def expert_sums(g):
        own = jnp.stack([jnp.sum(g[SHARED:, :DSLOT], axis=1), jnp.sum(g[SHARED:, DSLOT:], axis=1)])
        return jnp.sum(g[:SHARED], axis=1), own

    gain_shared, gain_own = expert_sums(gain_rows_grad)
    shift_shared, shift_own = expert_sums(shift_rows_grad)
    gate_low = gate_logit_grad
    gate_grad = jnp.stack(
        [
            jnp.dot(inputs[:DSLOT].astype(F32).T, gate_low[:DSLOT], precision=lax.Precision.HIGHEST),
            jnp.dot(inputs[DSLOT:].astype(F32).T, gate_low[DSLOT:], precision=lax.Precision.HIGHEST),
        ]
    )
    inputs_gate_grad = jnp.concatenate(
        [
            jnp.dot(gate_low[:DSLOT], gate_two[0].astype(F32).T, precision=lax.Precision.HIGHEST),
            jnp.dot(gate_low[DSLOT:], gate_two[1].astype(F32).T, precision=lax.Precision.HIGHEST),
        ],
        axis=0,
    )
    out_low = out_grad.astype(BF)
    out_parts = [out_low[:SHARED], out_low[SHARED:, :DSLOT], out_low[SHARED:, DSLOT:]]
    act_grads = [
        jnp.einsum("krm,khm->krh", g, down[k], preferred_element_type=F32) for g, (k, r) in zip(out_parts, parts)
    ]
    pre_grads = [g[1](a)[0].astype(BF) for g, a in zip(gelus, act_grads)]
    down_grads = [
        jnp.einsum("krh,krm->khm", a, g, preferred_element_type=F32).astype(BF) for a, g in zip(acts, out_parts)
    ]
    up_grads = [
        jnp.einsum("rm,krh->kmh", inputs[r], g, preferred_element_type=F32).astype(BF)
        for g, (k, r) in zip(pre_grads, parts)
    ]
    input_parts = [
        jnp.einsum("krh,kmh->rm", g, up[k], preferred_element_type=F32) for g, (k, r) in zip(pre_grads, parts)
    ]
    input_sum = input_parts[0] + jnp.concatenate(input_parts[1:], axis=0) + inputs_gate_grad
    input_low = input_sum.astype(BF)

    embed_grad = dot(proj_full, input_low, 1, 1).astype(BF).reshape(narrow, fields * EMB, rows)
    embed_grad = lax.all_to_all(embed_grad, "narrow", 0, 0, tiled=True)
    embed_grad = embed_grad.transpose(1, 0, 2).reshape(fields, EMB, ev_rows)
    slot_rows = slots.transpose(1, 0, 2).reshape(fields, 1, ev_rows)
    returned = place(slot_rows, embed_grad, lo_n, hi_n)
    returned = returned.transpose(1, 0, 2).reshape(fields * EMB, owners, cap).transpose(1, 0, 2)
    row_grads = lax.all_to_all(returned, "wide", 0, 0, tiled=True)
    row_grads = row_grads.transpose(0, 2, 1).astype(F32)[None]

    up_g = jnp.concatenate(up_grads, axis=0).reshape(6, D, narrow, hid_here).transpose(2, 0, 1, 3)
    down_g = jnp.concatenate(down_grads, axis=0).reshape(6, narrow, hid_here, D).transpose(1, 0, 2, 3)
    down_g = down_g.reshape(narrow, 6, hid_here, 2, D // 2).transpose(0, 1, 3, 2, 4)
    grads = jnp.concatenate([up_g, down_g.reshape(narrow, 6, 2 * hid_here, D // 2)], axis=2)
    mine, theirs = grads[:2], swap(grads[2:], other_core)
    add = lambda a, b: (a.astype(F32) + b.astype(F32)).astype(BF)
    first = jnp.where(core == 0, mine[:, 2:4], theirs[:, 2:4])
    last = jnp.where(core == 0, theirs[:, 2:4], mine[:, 2:4])
    chip_sum = jnp.concatenate(
        [add(mine[:, :2], theirs[:, :2]), first, add(mine[:, 4:], theirs[:, 4:]), last], axis=1
    )
    part = lax.psum_scatter(chip_sum, "wide", scatter_dimension=2, tiled=True)
    far = swap(part[1], other_chip)
    near = part[0]
    low_half = jnp.where(chip == 0, near[2:], far[2:])
    high_half = jnp.where(chip == 0, far[2:], near[2:])
    part = jnp.concatenate([add(near[:2], far[:2]), low_half, high_half], axis=0)
    whole = lax.all_gather(part, "wide", axis=1, tiled=True)
    up_grad = whole[:, :D].astype(F32)
    down_grad = whole[:, D:].reshape(14, 2, hid_here, D // 2).transpose(0, 2, 1, 3)
    down_grad = down_grad.reshape(14, hid_here, D).astype(F32)

    proj_grad = dot(embedded, input_low, 1, 0)
    dense_grad = dot(dense_low, input_low, 0, 0)
    bias_grad = jnp.sum(input_low.astype(F32), axis=0)

    def put(pair):
        zero = jnp.zeros((DOMAINS,) + pair.shape[1:], F32)
        zero = lax.dynamic_update_index_in_dim(zero, pair[0], full, 0)
        return lax.dynamic_update_index_in_dim(zero, pair[1], half, 0)

    def put_experts(shared, own):
        return jnp.concatenate([shared, put(own).reshape(DOMAINS * DOM_EXP, D)], axis=0)

    proj_grad = lax.psum_scatter(proj_grad, "narrow", scatter_dimension=0, tiled=True)
    proj_grad = lax.psum(proj_grad, "wide")
    common = lax.psum(
        (
            dense_grad,
            bias_grad,
            put_experts(gain_shared, gain_own),
            put_experts(shift_shared, shift_own),
            put(gate_grad),
            put(tower_weight_grad),
            put(bias_tower_grad),
            put(out_vector_grad),
            put(out_bias_grad),
        ),
        ("wide", "narrow"),
    )
    logits = jnp.where(core == 1, jnp.roll(logits, HALF, axis=0), logits)
    return (
        logits,
        row_grads,
        proj_grad,
        common[0],
        common[1],
        up_grad,
        down_grad,
        common[2],
        common[3],
        common[4],
        common[5],
        common[6],
        common[7],
        common[8],
    )


def solution(mesh):
    placed = (
        P("wide", "narrow"),
        P("wide", None, None, "narrow"),
        P("wide", "narrow"),
        P(("wide", "narrow")),
        P(("wide", "narrow")),
        P(("wide", "narrow"), None),
        P("narrow", None),
        P(),
        P(),
        P(None, None, "narrow"),
        P(None, "narrow", None),
        P(),
        P(),
        P(),
        P(),
        P(),
        P(),
        P(),
    )
    return jax.shard_map(
        shards,
        mesh=mesh,
        in_specs=placed,
        out_specs=(
            P(("wide", "narrow")),
            P("wide", None, None, "narrow"),
            P("narrow", None),
            P(),
            P(),
            P(None, None, "narrow"),
            P(None, "narrow", None),
            P(),
            P(),
            P(),
            P(),
            P(),
            P(),
            P(),
        ),
        check_vma=False,
    )
```

```python
import functools

import jax
import jax.numpy as jnp
from jax import lax
from jax.experimental import pallas as pl
from jax.experimental.pallas import tpu as pltpu
from jax.sharding import PartitionSpec as P

D = 512
HID = 1024
EMB = 16
DENSE = 128
DOMAINS = 6
SHARED = 2
DOM_EXP = 2
DSLOT = 1024
HALF = DSLOT // 2
VMEM = 56 * 2**20
BF = jnp.bfloat16
F32 = jnp.float32
MESH = pl.DeviceIdType.MESH
UNITS = 9
ROWS_U = 1024
LANES = 256
PROJ_ROWS = 320
REP_ROWS = 704


def dot(a, b, ca, cb):
    return lax.dot_general(a, b, (((ca,), (cb,)), ((), ())), preferred_element_type=F32)


def lookup_kernel(lo_n, hi_n, fields, idx_ref, tab_ref, out_ref):
    length = idx_ref.shape[-1]
    shift = hi_n.bit_length() - 1
    for f in range(fields):
        idx = idx_ref[0, f : f + 1, :]
        hi = jnp.where(idx >= 0, idx & (hi_n - 1), -1)
        lo = lax.shift_right_logical(jnp.maximum(idx, 0), shift)
        hot = (lax.broadcasted_iota(jnp.int32, (hi_n, length), 0) == hi).astype(BF)
        cols = slice(f * EMB, (f + 1) * EMB)
        parts = [
            tab_ref[:, cols, j * hi_n : (j + 1) * hi_n].reshape(-1, hi_n) for j in range(tab_ref.shape[2] // hi_n)
        ]
        res = jnp.dot(jnp.concatenate(parts, axis=0), hot, preferred_element_type=F32)
        acc = res[0:EMB]
        for step in range(1, lo_n):
            acc = jnp.where(lo == step, res[step * EMB : (step + 1) * EMB], acc)
        out_ref[0, cols, :] = acc.astype(BF)


def lookup(idx, tab, hi_n, name, out_groups, order=lambda i: i):
    groups, fields, length = idx.shape
    outer, cols, inner = tab.shape
    lo_n = outer * inner // hi_n
    each = groups // out_groups
    return pl.pallas_call(
        functools.partial(lookup_kernel, lo_n, hi_n, fields),
        grid=(groups,),
        in_specs=[
            pl.BlockSpec((1, fields, length), lambda i: (order(i), 0, 0)),
            pl.BlockSpec(tab.shape, lambda i: (0, 0, 0)),
        ],
        out_specs=pl.BlockSpec((1, cols, length), lambda i: (i // each, 0, i % each)),
        out_shape=jax.ShapeDtypeStruct((out_groups, cols, length * each), BF),
        compiler_params=pltpu.CompilerParams(vmem_limit_bytes=VMEM),
        cost_estimate=pl.CostEstimate(
            flops=2 * groups * length * cols * lo_n * hi_n, bytes_accessed=8 * 2**20, transcendentals=0
        ),
        name=name,
    )(idx, tab)


def place_one(idx_ref, grad_ref, out_ref, field):
    outer, _, inner = out_ref.shape
    length = grad_ref.shape[2]
    hi_n = 256
    lo_n = outer * inner // hi_n
    cols = pl.ds(pl.multiple_of(field * EMB, EMB), EMB)
    total = None
    for s in range(grad_ref.shape[0]):
        idx = idx_ref[field, :, s * length : (s + 1) * length]
        hi = idx & (hi_n - 1)
        lo = lax.shift_right_logical(idx, hi_n.bit_length() - 1)
        grad = grad_ref[s, cols, :]
        hot = (lax.broadcasted_iota(jnp.int32, (hi_n, length), 0) == hi).astype(BF)
        lhs = jnp.concatenate(
            [jnp.where(lo == step, grad, jnp.zeros_like(grad)) for step in range(lo_n)], axis=0
        )
        part = dot(lhs, hot, 1, 1)
        total = part if total is None else total + part
    for j in range(inner // hi_n):
        piece = total[j * outer * EMB : (j + 1) * outer * EMB]
        out_ref[:, cols, j * hi_n : (j + 1) * hi_n] = piece.reshape(outer, EMB, hi_n).astype(BF)


def place_kernel(idx_ref, grad_ref, out_ref):
    place_one(idx_ref, grad_ref, out_ref, 0)


def place(idx, grad, hi_n, out_shape):
    fields, _, length = idx.shape
    parts, cols, each = grad.shape
    outer, _, inner = out_shape
    lo_n = outer * inner // hi_n
    return pl.pallas_call(
        place_kernel,
        grid=(fields,),
        in_specs=[
            pl.BlockSpec((1, 1, length), lambda i: (i, 0, 0)),
            pl.BlockSpec((parts, EMB, each), lambda i: (0, i, 0)),
        ],
        out_specs=pl.BlockSpec((outer, EMB, inner), lambda i: (0, i, 0)),
        out_shape=jax.ShapeDtypeStruct(out_shape, BF),
        compiler_params=pltpu.CompilerParams(vmem_limit_bytes=VMEM),
        cost_estimate=pl.CostEstimate(
            flops=2 * cols * length * lo_n * hi_n, bytes_accessed=6 * 2**20, transcendentals=0
        ),
        name="place_rows",
    )(idx, grad)


def reduce_kernel(bits, with_rows, own_ref, extra_ref, *refs):
    if with_rows:
        slot_ref, grad_ref, out_ref, rep_ref, back_ref = refs[:5]
        grads, placed, near_send, near_recv, far_send, far_recv, keep_sem = refs[-7:]
        refs = refs[5:-7]
    else:
        out_ref, rep_ref = refs[:2]
        refs = refs[2:]
    acc, stage_buf, halves, got, local_sem, send, recv, rep_send, rep_recv, out_sem = refs
    wide=lax.axis_index("wide"); me=lax.axis_index("narrow")
    chip=me//2; core=me%2
    block=ROWS_U>>bits
    mates=[{"narrow": me+1-2*core},{"narrow": me+2-4*chip}]
    pairs=[{"wide": wide+(1<<k)*(1-2*((wide//(1<<k))%2))} for k in range(bits)]
    far={"narrow": 3-me}
    barrier=pltpu.get_barrier_semaphore()
    owners=1<<bits
    others=[{"wide": (wide+d)%owners} for d in range(1,owners)] if with_rows else pairs
    for mate in mates+[far]+others:
        pl.semaphore_signal(barrier, inc=1, device_id=mate, device_id_type=MESH)
    pl.semaphore_wait(barrier, len(others)+3)
    def bit(k): return (wide//(1<<k))%2
    def start_of(k):
        at=0
        for j in range(k):
            at=at+bit(j)*(ROWS_U>>(j+1))
        return pl.multiple_of(at, 16) if k else 0
    stages=2*bits+2
    def copy(src,dst,s,u,mate):
        return pltpu.make_async_remote_copy(src_ref=src,dst_ref=dst,send_sem=send.at[s,u],recv_sem=recv.at[s,u],device_id=mate,device_id_type=MESH)
    def mine(u): return jnp.logical_or(jnp.logical_or(u<3,u>=7), jnp.logical_and(u<5,core==0)|jnp.logical_and(u>=5,core==1))
    def theirs(u): return jnp.logical_or(jnp.logical_or(u<3,u>=7), jnp.logical_and(u<5,core==1)|jnp.logical_and(u>=5,core==0))
    def local_at(u):
        return jnp.where(u<3,u-1,jnp.where(u<5,u-1,u-3))
    def core_copy(u, src):
        return copy(src, acc.at[u], 0, u, mates[0])
    def near_copy(u, src):
        return pltpu.make_async_copy(src, stage_buf.at[u%2], local_sem.at[u%2])
    def begin(u):
        @pl.when(u==0)
        def _():
            core_copy(u, extra_ref.at[pl.ds(2,2)]).start()
            near_copy(u, extra_ref.at[pl.ds(0,2)]).start()
        @pl.when(jnp.logical_and(u>0, mine(u)))
        def _():
            core_copy(u, own_ref.at[local_at(u), pl.ds(2,2)]).start()
            near_copy(u, own_ref.at[local_at(u), pl.ds(0,2)]).start()
    def add_region(u, sl, at, rows, src):
        tile=min(rows,64)
        def body(i,_):
            r=pl.multiple_of(at+i*tile,16); q=pl.multiple_of(i*tile,16)
            for h in sl:
                a=acc[u,h,pl.ds(r,tile),:].astype(F32)+src[h,pl.ds(q,tile),:].astype(F32)
                acc[u,h,pl.ds(r,tile),:]=a.astype(BF)
            return 0
        lax.fori_loop(0,rows//tile,body,0)
    half_at=[0]
    for k in range(bits): half_at.append(half_at[-1]+(ROWS_U>>(k+1)))
    def half_view(u,k):
        return halves.at[u,:,pl.ds(half_at[k],ROWS_U>>(k+1)),:]
    def send_half(u,k):
        size=ROWS_U>>(k+1)
        at=pl.multiple_of(start_of(k)+(1-bit(k))*size,16)
        return copy(acc.at[u,:,pl.ds(at,size),:], half_view(u,k), 1+k, u, pairs[k])
    def combine(u):
        @pl.when(theirs(u))
        def _():
            core_copy(u, acc.at[u]).wait_recv()
        @pl.when(mine(u))
        def _():
            near_copy(u, acc.at[u]).wait()
            sb=stage_buf.at[u%2]
            @pl.when(theirs(u))
            def _():
                add_region(u,(0,1),0,ROWS_U,sb)
            @pl.when(jnp.logical_not(theirs(u)))
            def _():
                def body(i,_):
                    r=pl.multiple_of(i*64,16)
                    for h in (0,1): acc[u,h,pl.ds(r,64),:]=sb[h,pl.ds(r,64),:]
                    return 0
                lax.fori_loop(0,ROWS_U//64,body,0)
        send_half(u,0).start()
    def halve(u,k):
        size=ROWS_U>>k
        copy(acc.at[u,:,pl.ds(0,size),:], half_view(u,k-1), k, u, pairs[k-1]).wait_recv()
        add_region(u,(0,1),start_of(k),size,halves.at[u,:,pl.ds(half_at[k-1],size),:])
        if k<bits:
            send_half(u,k).start()
        else:
            y_copy(u).start()
    def y_copy(u):
        at=start_of(bits)
        return copy(acc.at[u,1,pl.ds(at,block),:], got.at[u,1,pl.ds(at,block),:], bits+1, u, mates[1])
    def grow_copy(u,j,parts):
        size=ROWS_U>>(j+1)
        at=start_of(j+1)
        view=got.at[u,pl.ds(0,parts),pl.ds(at,size),:]
        return copy(view,view,bits+2+(bits-1-j),u,pairs[j])
    def each_kind(u,f):
        @pl.when(u<3)
        def _(): f(1)
        @pl.when(u>=3)
        def _(): f(2)
    def cross(u):
        y_copy(u).wait_recv()
        at=start_of(bits)
        @pl.when(u<3)
        def _():
            a=acc[u,0,pl.ds(at,block),:].astype(F32)+got[u,1,pl.ds(at,block),:].astype(F32)
            got[u,0,pl.ds(at,block),:]=a.astype(BF)
        @pl.when(u>=3)
        def _():
            got[u,0,pl.ds(at,block),:]=acc[u,0,pl.ds(at,block),:]
        each_kind(u,lambda parts: grow_copy(u,bits-1,parts).start())
    def out_copy(u,parts):
        return pltpu.make_async_copy(got.at[u,pl.ds(0,parts)], out_ref.at[u,pl.ds(0,parts)], out_sem.at[u])
    rep_mates=[mates[0],mates[1],far]
    rep_rows=rep_ref.shape[1]
    def rep_copy(i):
        return pltpu.make_async_remote_copy(src_ref=got.at[0,0,pl.ds(ROWS_U-rep_rows,rep_rows),:],dst_ref=rep_ref.at[i],send_sem=rep_send.at[i],recv_sem=rep_recv.at[i],device_id=rep_mates[i],device_id_type=MESH)
    def grow(u,j):
        each_kind(u,lambda parts: grow_copy(u,j,parts).wait_recv())
        if j>0:
            each_kind(u,lambda parts: grow_copy(u,j-1,parts).start())
        else:
            each_kind(u,lambda parts: out_copy(u,parts).start())
            @pl.when(u==0)
            def _():
                for i in range(3): rep_copy(i).start()
    quarters=mates+[far]
    def quarter_at(i):
        return [me+1-2*core, me+2-4*chip, 3-me][i]
    def near_row_copy(i):
        return pltpu.make_async_remote_copy(src_ref=grad_ref.at[quarter_at(i)],dst_ref=grads.at[me],send_sem=near_send.at[i],recv_sem=near_recv.at[i],device_id=quarters[i],device_id_type=MESH)
    def keep_copy():
        return pltpu.make_async_copy(grad_ref.at[me],grads.at[me],keep_sem.at[0])
    def back_copy(d):
        return pltpu.make_async_remote_copy(src_ref=placed.at[(wide+d)%owners],dst_ref=back_ref.at[wide],send_sem=far_send.at[d],recv_sem=far_recv.at[d],device_id=others[d-1],device_id_type=MESH)
    def keep_back():
        return pltpu.make_async_copy(placed.at[wide],back_ref.at[wide],keep_sem.at[1])
    def place_field(f, _):
        place_one(slot_ref, grads, placed, f)
        return 0
    def row_step(t):
        fields=slot_ref.shape[0]
        @pl.when(t==2)
        def _():
            keep_copy().wait()
            for i in range(3): near_row_copy(i).wait_recv()
        @pl.when(jnp.logical_and(t>=2,t<7))
        def _():
            lax.fori_loop((t-2)*(fields//5),(t-1)*(fields//5),place_field,0)
        @pl.when(t==6)
        def _():
            keep_back().start()
            for d in range(1,owners): back_copy(d).start()
    todo=[begin,combine]+[functools.partial(lambda k,u: halve(u,k),k) for k in range(1,bits+1)]+[cross]+[functools.partial(lambda j,u: grow(u,j),j) for j in reversed(range(bits))]
    def tick(t,_):
        for s in reversed(range(len(todo))):
            u=t-s
            @pl.when(jnp.logical_and(u>=0,u<UNITS))
            def _():
                todo[s](u)
        if with_rows:
            row_step(t)
        return 0
    if with_rows:
        keep_copy().start()
        for i in range(3): near_row_copy(i).start()
    lax.fori_loop(0,UNITS+len(todo)-1,tick,0)
    if with_rows:
        keep_back().wait()
        for i in range(3): near_row_copy(i).wait_send()
        for d in range(1,owners): back_copy(d).wait()
    def finish(u,_):
        @pl.when(mine(u))
        def _():
            core_copy(u, acc.at[u]).wait_send()
        for k in range(bits): send_half(u,k).wait_send()
        y_copy(u).wait_send()
        for j in range(bits): each_kind(u,lambda parts: grow_copy(u,j,parts).wait_send())
        each_kind(u,lambda parts: out_copy(u,parts).wait())
        return 0
    lax.fori_loop(0,UNITS,finish,0)
    for i in range(3):
        rep_copy(i).wait()

def reduce_all(own, extra, wide, rep_rows, rows=None):
    bits = wide.bit_length() - 1
    args = [own, extra]
    any_space = pl.BlockSpec(memory_space=pl.ANY)
    in_specs = [any_space] * 2
    out_shape = [
        jax.ShapeDtypeStruct((UNITS, 2, ROWS_U, LANES), BF),
        jax.ShapeDtypeStruct((3, rep_rows, LANES), BF),
    ]
    scratch = [
        pltpu.VMEM((UNITS, 2, ROWS_U, LANES), BF),
        pltpu.VMEM((2, 2, ROWS_U, LANES), BF),
        pltpu.VMEM((UNITS, 2, ROWS_U, LANES), BF),
        pltpu.VMEM((UNITS, 2, ROWS_U, LANES), BF),
        pltpu.SemaphoreType.DMA((2,)),
        pltpu.SemaphoreType.DMA((2 * bits + 2, UNITS)),
        pltpu.SemaphoreType.DMA((2 * bits + 2, UNITS)),
        pltpu.SemaphoreType.DMA((3,)),
        pltpu.SemaphoreType.DMA((3,)),
        pltpu.SemaphoreType.DMA((UNITS,)),
    ]
    if rows is not None:
        slots, grads, cap = rows
        args += [slots, grads]
        in_specs += [pl.BlockSpec(memory_space=pltpu.VMEM), any_space]
        back = (wide, grads.shape[1], cap)
        out_shape.append(jax.ShapeDtypeStruct(back, BF))
        scratch += [
            pltpu.VMEM(grads.shape, BF),
            pltpu.VMEM(back, BF),
            pltpu.SemaphoreType.DMA((3,)),
            pltpu.SemaphoreType.DMA((3,)),
            pltpu.SemaphoreType.DMA((wide,)),
            pltpu.SemaphoreType.DMA((wide,)),
            pltpu.SemaphoreType.DMA((2,)),
        ]
    return pl.pallas_call(
        functools.partial(reduce_kernel, bits, rows is not None),
        in_specs=in_specs,
        out_specs=[any_space] * len(out_shape),
        out_shape=out_shape,
        scratch_shapes=scratch,
        compiler_params=pltpu.CompilerParams(collective_id=0, has_side_effects=True, vmem_limit_bytes=VMEM),
        cost_estimate=pl.CostEstimate(flops=0, bytes_accessed=60 * 2**20, transcendentals=0),
        name="reduce_all",
    )(*args)


C0 = 0.7978845608028654
C1 = 0.044715


def gelu_both(x):
    square = x * x
    t = jnp.tanh(C0 * x * (1.0 + C1 * square))
    up = 0.5 * (1.0 + t)
    slope = up + 0.5 * x * (1.0 - t * t) * (C0 + (3.0 * C0 * C1) * square)
    return x * up, slope


def soft_pair(a, b):
    top = jnp.maximum(a, b)
    ea, eb = jnp.exp(a - top), jnp.exp(b - top)
    total = ea + eb
    return ea / total, eb / total


def soft_pair_back(pa, pb, ga, gb):
    mean = pa * ga + pb * gb
    return pa * (ga - mean), pb * (gb - mean)


def fold(x):
    return sum(x[:, i * 128 : (i + 1) * 128] for i in range(x.shape[1] // 128))


def wide_lanes(x, n):
    return jnp.concatenate([x] * n, axis=1)


def dense_kernel(
    ids_ref, emb_ref, feat_ref, projw_ref, featw_ref, up_a, up_b, up_c, down_a, down_b, down_c, gain_ref, shift_ref, gate_ref, tin_ref,
    tbias_ref, tout_ref, tob_ref, label_ref, live_ref,
    logit_ref, own_ref, emb_grad_ref, proj_grad_ref, feat_grad_ref, gain_acc, shift_acc, gate_acc, tin_acc,
    tbias_acc, tout_acc, tob_acc,
    xt, act, slope, outs, og, ing, hid, hg, stat, coef, inner, emb, emb_sem,
):
    ups = [up_a.at[0], up_b.at[0], up_c.at[0, 0], up_c.at[1, 0]]
    downs = [down_a.at[0], down_b.at[0], down_c.at[0, 0], down_c.at[1, 0]]
    step = pl.program_id(0)
    chunk, slot = step // 4, step % 4
    rows = xt.shape[1]

    @pl.when(step == 0)
    def _():
        fetch = pltpu.make_async_copy(emb_ref, emb, emb_sem)
        fetch.start()
        fetch.wait()
        for c in range(rows // HALF):
            cols = slice(c * HALF, (c + 1) * HALF)
            x = dot(projw_ref[...], emb[:, cols], 0, 0) + dot(featw_ref[...], feat_ref[:, cols], 0, 0)
            xt[:, cols] = x.astype(BF)
        for ref in (gain_acc, shift_acc, gate_acc, tin_acc, tbias_acc, tout_acc, tob_acc):
            ref[...] = jnp.zeros_like(ref)

    @pl.when(step < 12)
    def _():
        lanes = pl.ds(pl.multiple_of(chunk * HALF, HALF), HALF)

        def piece(s, total):
            pre = dot(ups[s][...], xt[:, lanes], 0, 0)
            a, g = gelu_both(pre)
            a = a.astype(BF)
            act[slot, s, :, lanes] = a
            slope[slot, s, :, lanes] = g.astype(BF)
            return dot(downs[s][...], a, 0, 0)

        outs[slot] = piece(0, None)
        for s in range(1, 4):
            outs[slot] += piece(s, None)

    def middle():
        lanes = pl.ds(pl.multiple_of(chunk * HALF, HALF), HALF)
        dom = chunk // 2
        x = xt[:, lanes]
        gates = dot(gate_ref[dom], x, 1, 0)
        s0, s1 = soft_pair(gates[0:1], gates[1:2])
        d0, d1 = soft_pair(gates[2:3], gates[3:4])
        t0, t1 = soft_pair(gates[4:5], gates[5:6])
        for k, row in enumerate((t0 * s0, t0 * s1, t1 * d0, t1 * d1)):
            coef[k : k + 1, :] = row
        expert = [0, 1, 2 + 2 * dom, 3 + 2 * dom]

        def normalize(t, _):
            cols = pl.ds(pl.multiple_of(t * 128, 128), 128)
            for k in range(4):
                v = outs[k, :, cols]
                mean = jnp.sum(v, axis=0, keepdims=True) * (1.0 / D)
                v = v - mean
                var = jnp.sum(v * v, axis=0, keepdims=True) * (1.0 / D)
                stat[k : k + 1, cols] = mean
                stat[4 + k : 5 + k, cols] = lax.rsqrt(var + 1e-05)
            for r in range(4):
                band = slice(r * 128, (r + 1) * 128)
                acc = None
                for k in range(4):
                    n = (outs[k, band, cols] - stat[k : k + 1, cols]) * stat[4 + k : 5 + k, cols]
                    n = (n * gain_ref[expert[k], band, :].astype(F32) + shift_ref[expert[k], band, :].astype(F32)) * coef[k : k + 1, cols]
                    acc = n if acc is None else acc + n
                hid[band, cols] = acc.astype(BF)
            return 0

        lax.fori_loop(0, 4, normalize, 0)
        h = hid[...]
        pre = dot(tin_ref[dom], h, 0, 0) + wide_lanes(tbias_ref[dom], 4)
        tact, tslope = gelu_both(pre)
        tout = wide_lanes(tout_ref[dom], 4)
        logit = jnp.sum(tact * tout, axis=0, keepdims=True) + wide_lanes(tob_ref[dom, 0:1, :], 4)
        logit_ref[:, lanes] = logit
        grad = (jax.nn.sigmoid(logit) - label_ref[:, lanes]) * live_ref[:, lanes]
        tob_acc[dom, 0:1, :] += fold(grad)
        tout_acc[dom] += fold(grad * tact)
        low = (grad * tout * tslope).astype(BF)
        tbias_acc[dom] += fold(low.astype(F32))
        tin_acc[dom] += dot(h, low, 1, 1)
        hg[...] = dot(tin_ref[dom], low, 1, 0)

        def denormalize(t, _):
            cols = pl.ds(pl.multiple_of(t * 128, 128), 128)
            place = pl.ds(pl.multiple_of(chunk * HALF + t * 128, 128), 128)
            for k in range(4):
                mean, rstd = stat[k : k + 1, cols], stat[4 + k : 5 + k, cols]
                c = coef[k : k + 1, cols]
                m1 = m2 = mb = 0.0
                for r in range(4):
                    band = slice(r * 128, (r + 1) * 128)
                    n = (outs[k, band, cols] - mean) * rstd
                    grad = hg[band, cols]
                    scaled = grad * gain_ref[expert[k], band, :].astype(F32)
                    m1 = m1 + jnp.sum(scaled, axis=0, keepdims=True)
                    m2 = m2 + jnp.sum(scaled * n, axis=0, keepdims=True)
                    mb = mb + jnp.sum(grad * shift_ref[expert[k], band, :].astype(F32), axis=0, keepdims=True)
                    part = c * grad
                    gain_acc[expert[k], band, :] += part * n
                    shift_acc[expert[k], band, :] += part
                inner[k : k + 1, cols] = m2 + mb
                m1, m2, cr = m1 * (1.0 / D), m2 * (1.0 / D), c * rstd
                for r in range(4):
                    band = slice(r * 128, (r + 1) * 128)
                    n = (outs[k, band, cols] - mean) * rstd
                    scaled = hg[band, cols] * gain_ref[expert[k], band, :].astype(F32)
                    og[k, band, place] = (cr * (scaled - m1 - n * m2)).astype(BF)
            return 0

        lax.fori_loop(0, 4, denormalize, 0)
        a = [inner[k : k + 1, :] for k in range(4)]
        g0, g1 = soft_pair_back(s0, s1, t0 * a[0], t0 * a[1])
        g2, g3 = soft_pair_back(d0, d1, t1 * a[2], t1 * a[3])
        g4, g5 = soft_pair_back(t0, t1, s0 * a[0] + s1 * a[1], d0 * a[2] + d1 * a[3])
        zero = jnp.zeros_like(g0)
        g = jnp.concatenate([g0, g1, g2, g3, g4, g5, zero, zero], axis=0)
        high = g.astype(BF).astype(F32)
        g = jnp.concatenate([high, g - high], axis=0).astype(BF)
        gate_acc[dom] += dot(g, x, 1, 1)
        ing[:, lanes] = dot(gate_ref[dom], g, 0, 0)

    @pl.when(jnp.logical_and(step < 12, slot == 3))
    def _():
        middle()

    def back(k, at, n):
        lanes = slice(at, at + n)

        for s in range(4):
            p = dot(downs[s][...], og[k, :, lanes], 1, 0) * slope[k, s, :, lanes].astype(F32)
            slope[k, s, :, lanes] = p.astype(BF)

        def piece(s, _):
            grad, p = og[k, :, lanes], slope[k, s, :, lanes]
            own_ref[0, s, 0:D, :] = dot(xt[:, lanes], p, 1, 1).astype(BF)
            d = dot(act[k, s, :, lanes], grad, 1, 1).astype(BF)
            own_ref[0, s, D : D + 256, :] = d[:, 0:256]
            own_ref[0, s, D + 256 : D + 512, :] = d[:, 256:512]
            return 0

        lax.fori_loop(0, 4, piece, 0)

        def grow(t, _):
            cols = pl.ds(pl.multiple_of(at + t * HALF, HALF), HALF)
            total = dot(ups[0][...], slope[k, 0, :, cols], 1, 0)
            for s in range(1, 4):
                total += dot(ups[s][...], slope[k, s, :, cols], 1, 0)
            ing[:, cols] += total
            return 0

        lax.fori_loop(0, n // HALF, grow, 0)

    expert = step - 12

    @pl.when(jnp.logical_and(expert >= 0, expert < 2))
    def _():
        back(expert, 0, rows)

    @pl.when(jnp.logical_and(expert >= 2, expert < 4))
    def _():
        back(expert, 0, DSLOT)

    @pl.when(expert >= 4)
    def _():
        back(expert - 2, DSLOT, rows - DSLOT)

    @pl.when(expert == 5)
    def _():
        low = ing[...].astype(BF)
        proj_grad_ref[...] = dot(emb[...], low, 1, 1).astype(BF)
        feat_grad_ref[...] = dot(feat_ref[...], low, 1, 1)
        for c in range(rows // HALF):
            cols = slice(c * HALF, (c + 1) * HALF)
            emb[:, cols] = dot(projw_ref[...], low[:, cols], 1, 0).astype(BF)
        put = pltpu.make_async_copy(emb, emb_grad_ref, emb_sem)
        put.start()
        put.wait()


def dense(ids, emb, feat, projw, featw, ups, downs, gains, shifts, gate, tin, tbias, tout, tob, label, live):
    rows = emb.shape[1]

    def ahead(i):
        c, j = i // 4, i % 4
        front = jnp.where(j < 2, j, jnp.where(c < 2, j, j + 2))
        return jnp.where(i < 12, front, i - 12)

    def whole(x):
        return pl.BlockSpec(x.shape, lambda i, ids: (0,) * len(x.shape), pipeline_mode=pl.Buffered(1))

    def shape(s, d):
        return jax.ShapeDtypeStruct(s, d)

    outs = [
        shape((1, rows), F32),
        shape((6, 4, 2 * D, 256), BF),
        shape(emb.shape, BF),
        shape(projw.shape, BF),
        shape(featw.shape, F32),
        shape(gains.shape, F32),
        shape(gains.shape, F32),
        shape(gate.shape, F32),
        shape(tin.shape, F32),
        shape(tbias.shape, F32),
        shape(tout.shape, F32),
        shape(tob.shape, F32),
    ]
    args = (emb, feat, projw, featw) + ups + downs + (gains, shifts, gate, tin, tbias, tout, tob, label, live)
    in_specs = [whole(x) for x in args]
    in_specs[0] = pl.BlockSpec(memory_space=pl.ANY)
    for at, group in ((4, ups), (7, downs)):
        block = group[0].shape[1:]
        in_specs[at] = pl.BlockSpec((1,) + block, lambda i, ids: (ids[ahead(i)], 0, 0))
        in_specs[at + 1] = pl.BlockSpec((1,) + block, lambda i, ids: (ids[6 + ahead(i)], 0, 0))
        in_specs[at + 2] = pl.BlockSpec((2, 1) + block, lambda i, ids: (0, ahead(i), 0, 0))
    out_specs = [whole(x) for x in outs]
    out_specs[2] = pl.BlockSpec(memory_space=pl.ANY)
    out_specs[1] = pl.BlockSpec((1, 4, 2 * D, 256), lambda i, ids: (jnp.maximum(i - 12, 0), 0, 0, 0))
    return pl.pallas_call(
        dense_kernel,
        grid_spec=pltpu.PrefetchScalarGridSpec(
            num_scalar_prefetch=1,
            grid=(18,),
            in_specs=in_specs,
            out_specs=out_specs,
            scratch_shapes=[
            pltpu.VMEM((D, rows), BF),
            pltpu.VMEM((4, 4, 256, rows), BF),
            pltpu.VMEM((4, 4, 256, rows), BF),
            pltpu.VMEM((4, D, HALF), F32),
            pltpu.VMEM((4, D, rows), BF),
            pltpu.VMEM((D, rows), F32),
            pltpu.VMEM((D, HALF), BF),
            pltpu.VMEM((D, HALF), F32),
            pltpu.VMEM((8, HALF), F32),
            pltpu.VMEM((8, HALF), F32),
            pltpu.VMEM((8, HALF), F32),
            pltpu.VMEM(emb.shape, BF),
            pltpu.SemaphoreType.DMA,
                    ]),
        out_shape=outs,
        compiler_params=pltpu.CompilerParams(vmem_limit_bytes=62 * 2**20),
        cost_estimate=pl.CostEstimate(flops=39 * 10**9, bytes_accessed=60 * 2**20, transcendentals=0),
        name="dense_all",
    )(ids, *args)


def own_stats(rows, weight):
    count = jnp.sum(weight)
    mean = jnp.sum(rows * weight, axis=1) / jnp.maximum(count, 1.0)
    off = rows - mean[:, None]
    return [mean, jnp.sum(off * off * weight, axis=1), jnp.broadcast_to(count, mean.shape)]


def pool(means, squares, counts):
    total = jnp.sum(counts, axis=0)
    mean = jnp.sum(counts * means, axis=0) / total
    off = means - mean
    return mean, (jnp.sum(squares, axis=0) + jnp.sum(counts * off * off, axis=0)) / total


def shards(
    embed_table,
    requests,
    slot_index,
    event_mask,
    labels,
    dense_feats,
    proj_weight,
    dense_weight,
    proj_bias,
    up_weight,
    down_weight,
    norm_gain,
    norm_shift,
    gate_weight,
    tower_in,
    tower_bias,
    tower_out,
    tower_out_bias,
):
    narrow = lax.axis_size("narrow")
    me = lax.axis_index("narrow")
    chip, core = me // 2, me % 2
    ev_rows, fields = slot_index.shape
    rows = ev_rows // narrow
    owners, cap = requests.shape[1], requests.shape[2]
    hid_here = up_weight.shape[2]
    other_chip = [(i, i ^ 2) for i in range(narrow)]
    other_core = [(i, i ^ 1) for i in range(narrow)]
    full = 3 * chip + 2 * core
    half = 3 * chip + 1

    def swap(x, pairs):
        return lax.ppermute(x, "narrow", pairs)

    asked = lax.all_to_all(requests[0].transpose(0, 2, 1), "wide", 0, 0, tiled=True)

    def chip_experts(w, which):
        return jnp.concatenate(
            [w[:SHARED], lax.dynamic_slice_in_dim(w, SHARED + 6 * which, 6, axis=0)], axis=0
        )

    def bring(w):
        far = swap(chip_experts(w, 1 - chip), other_chip)
        at = lambda x, start, size: lax.dynamic_slice_in_dim(x, start, size, axis=0)
        base = SHARED + 6 * chip
        away = 4 * (1 - core)
        theirs = jnp.stack(
            [
                jnp.concatenate([w[:SHARED], at(w, base + away, 2), at(w, base + 2, 2)], axis=0),
                jnp.concatenate([far[:SHARED], at(far, 2 + away, 2), far[4:6]], axis=0),
            ]
        )
        return w, far, swap(theirs, other_core)

    ups = bring(up_weight)
    downs = bring(down_weight)
    six = jnp.arange(6, dtype=jnp.int32)
    spot = jnp.where(six < 2, six, jnp.where(six < 4, six + 4 * core, six))
    ids = jnp.concatenate([jnp.where(six < 2, six, spot + 6 * chip), spot])

    def by_offset(x):
        x = x.reshape((2, 2) + x.shape[1:])
        x = jnp.where(chip == 1, x[::-1], x)
        x = jnp.where(core == 1, x[:, ::-1], x)
        return x.reshape((narrow,) + x.shape[2:])

    column = jnp.stack([proj_weight, swap(proj_weight, other_chip)])
    column = jnp.stack([column, swap(column, other_core)], axis=1)
    proj_full = by_offset(column.reshape((narrow,) + proj_weight.shape)).reshape(-1, D)

    def turned(x):
        return jnp.where(core == 1, jnp.roll(x, -HALF, axis=0), x)

    live = turned(event_mask).astype(F32)[None]
    label_rows = turned(labels).astype(F32)[None]
    feats = turned(dense_feats).T
    blank = jnp.zeros((2, DENSE), F32)
    stats = jnp.stack(
        own_stats(feats[:, :DSLOT], live[:, :DSLOT]) + own_stats(feats[:, DSLOT:], live[:, DSLOT:])
    )
    stats = jnp.concatenate([stats, blank], axis=0)
    stats = jnp.concatenate([stats, swap(stats, other_core)], axis=0)
    every = lax.all_to_all(
        jnp.broadcast_to(stats, (owners,) + stats.shape), "wide", 0, 0, tiled=True
    )
    full_mean, full_spread = pool(every[:, 0], every[:, 1], every[:, 2])
    both = jnp.concatenate([every[:, 3:6], every[:, 11:14]], axis=0)
    half_mean, half_spread = pool(both[:, 0], both[:, 1], both[:, 2])
    normal = lambda x, mean, spread: (x - mean[:, None]) * lax.rsqrt(spread + 1e-05)[:, None]
    feat = jnp.concatenate(
        [
            jnp.concatenate(
                [normal(feats[:, :DSLOT], full_mean, full_spread), normal(feats[:, DSLOT:], half_mean, half_spread)],
                axis=1,
            ),
            jnp.ones((1, rows), F32),
            jnp.zeros((15, rows), F32),
        ],
        axis=0,
    ).astype(BF)
    feat_weight = jnp.concatenate([dense_weight, proj_bias[None], jnp.zeros((15, D), BF)], axis=0)

    table_rows = embed_table.shape[0]
    cols = fields * EMB
    direct = cap % 256 == 0
    tab = embed_table.reshape(32, table_rows // 32, cols).transpose(0, 2, 1)
    hi_n = table_rows // 32
    if direct:
        found = lookup(asked, tab, hi_n, "lookup_rows", owners)
    else:
        flat = asked.transpose(1, 0, 2).reshape(fields, DOMAINS, DSLOT).transpose(1, 0, 2)
        found = lookup(flat, tab, hi_n, "lookup_rows", DOMAINS)
        found = found.transpose(1, 0, 2).reshape(cols, owners, cap).transpose(1, 0, 2)
    received = lax.all_to_all(found, "wide", 0, 0, tiled=True)

    hi_n = 256
    lo_n = ev_rows // hi_n
    blocks = ev_rows // HALF
    slots = slot_index
    if direct:
        owner, rest = slots // cap, slots % cap
        slots = ((rest // hi_n) * owners + owner) * hi_n + rest % hi_n
    else:
        received = received.transpose(1, 0, 2).reshape(cols, lo_n, hi_n).transpose(1, 0, 2)
    slots = slots.reshape(blocks, HALF, fields).transpose(0, 2, 1)
    turn = lambda i: (i // 3) * 3 + (i % 3 + (i // 3) % 2) % 3
    embedded = lookup(slots, received, hi_n, "order_rows", narrow, turn)
    embedded = lax.all_to_all(embedded, "narrow", 0, 0, tiled=True)
    embedded = embedded.reshape(narrow * cols, rows)

    def pick(w):
        return jnp.stack(
            [
                lax.dynamic_index_in_dim(w, full, keepdims=False),
                lax.dynamic_index_in_dim(w, half, keepdims=False),
            ]
        )

    def over_lanes(x):
        return jnp.broadcast_to(x.astype(F32)[..., None], x.shape + (128,))

    def expert_rows(w):
        own = pick(w[SHARED:].reshape(DOMAINS, DOM_EXP, D)).reshape(4, D)
        w = jnp.concatenate([w[:SHARED], own], axis=0)
        return jnp.broadcast_to(w[..., None], w.shape + (128,))

    gate = jnp.pad(pick(gate_weight).transpose(0, 2, 1), ((0, 0), (0, 2), (0, 0)))
    gate = jnp.concatenate([gate, gate], axis=1)
    (
        logits, own, embed_grad, proj_grad, feat_grad, gain_sum, shift_sum, gate_grad, tower_grad,
        tower_bias_sum, tower_out_sum, out_bias_sum,
    ) = dense(
        ids, embedded, feat, proj_full, feat_weight, ups, downs, expert_rows(norm_gain), expert_rows(norm_shift),
        gate, pick(tower_in), over_lanes(pick(tower_bias)), over_lanes(pick(tower_out)),
        jnp.broadcast_to(pick(tower_out_bias).astype(F32)[:, None, None], (2, 8, 128)), label_rows, live,
    )
    logits = logits[0]

    embed_grad = embed_grad.reshape(narrow, cols, rows)
    slot_rows = jnp.stack([slots[turn(i)] for i in range(blocks)]).transpose(1, 0, 2)
    slot_rows = slot_rows.reshape(fields, 1, ev_rows)
    if not direct:
        embed_grad = lax.all_to_all(embed_grad, "narrow", 0, 0, tiled=True)
        returned = place(slot_rows, embed_grad, hi_n, (lo_n, cols, hi_n))
        returned = returned.transpose(1, 0, 2).reshape(cols, owners, cap).transpose(1, 0, 2)
        row_grads = lax.all_to_all(returned, "wide", 0, 0, tiled=True)

    def put(pair):
        zero = jnp.zeros((DOMAINS,) + pair.shape[1:], F32)
        zero = lax.dynamic_update_index_in_dim(zero, pair[0], full, 0)
        return lax.dynamic_update_index_in_dim(zero, pair[1], half, 0)

    def put_experts(sums):
        sums = jnp.sum(sums, axis=-1)
        own = put(sums[SHARED:].reshape(2, DOM_EXP, D)).reshape(DOMAINS * DOM_EXP, D)
        return jnp.concatenate([sums[:SHARED], own], axis=0)

    def pack(x):
        return jnp.concatenate([x[:, :LANES], x[:, LANES:]], axis=0)

    def unpack(x):
        return jnp.concatenate([x[: x.shape[0] // 2], x[x.shape[0] // 2 :]], axis=1)

    tower_grad = put(tower_grad).reshape(DOMAINS * D, 128)
    small = [
        jnp.concatenate([tower_grad[: DOMAINS * D // 2], tower_grad[DOMAINS * D // 2 :]], axis=1),
        pack(feat_grad[:DENSE]),
        pack(put(gate_grad[:, :6] + gate_grad[:, 8:14]).reshape(DOMAINS * 6, D)),
        pack(put_experts(gain_sum)),
        pack(put_experts(shift_sum)),
        feat_grad[DENSE].reshape(2, LANES),
        put(jnp.sum(tower_bias_sum, axis=-1)).reshape(3, LANES),
        put(jnp.sum(tower_out_sum, axis=-1)).reshape(3, LANES),
        jnp.pad(put(jnp.sum(out_bias_sum[:, 0], axis=-1)), (0, LANES - DOMAINS))[None],
    ]
    sizes = [x.shape[0] for x in small]
    small = jnp.concatenate(small, axis=0).astype(BF)
    small = jnp.pad(small, ((0, narrow * REP_ROWS - small.shape[0]), (0, 0)))

    proj_rows = proj_grad.reshape(narrow, cols, 2, LANES).transpose(0, 2, 1, 3)
    extra = jnp.concatenate(
        [proj_rows.reshape(narrow, PROJ_ROWS, LANES), small.reshape(narrow, REP_ROWS, LANES)], axis=1
    )
    extra = by_offset(extra)
    extra = jnp.stack([extra[0], extra[2], extra[1], extra[3]])
    if direct:
        sums, others, row_grads = reduce_all(own, extra, owners, REP_ROWS, (slot_rows, embed_grad, cap))
    else:
        sums, others = reduce_all(own, extra, owners, REP_ROWS)
    row_grads = row_grads.transpose(0, 2, 1).astype(F32)[None]

    own_chip, far_chip = [
        jnp.concatenate([sums[3:5, p], sums[7:9, p], sums[5:7, p]], axis=0) for p in (0, 1)
    ]
    low_half = jnp.where(chip == 0, own_chip, far_chip)
    high_half = jnp.where(chip == 0, far_chip, own_chip)
    whole = jnp.concatenate([sums[1:3, 0], low_half, high_half], axis=0)
    up_grad = whole[:, :D].astype(F32)
    down_grad = whole[:, D:].reshape(14, 2, hid_here, D // 2).transpose(0, 2, 1, 3)
    down_grad = down_grad.reshape(14, hid_here, D).astype(F32)
    proj_grad = unpack(sums[0, 0, :PROJ_ROWS]).astype(F32)
    rep = jnp.concatenate([sums[0, 0, None, PROJ_ROWS:], others], axis=0)
    rep = by_offset(rep).reshape(narrow * REP_ROWS, LANES).astype(F32)
    rest, at = [], 0
    for size in sizes:
        rest.append(rep[at : at + size])
        at += size
    tower_grad = jnp.concatenate([rest[0][:, :128], rest[0][:, 128:]], axis=0)
    common = (
        unpack(rest[1]),
        rest[5].reshape(D),
        unpack(rest[3]),
        unpack(rest[4]),
        unpack(rest[2]).reshape(DOMAINS, 6, D).transpose(0, 2, 1),
        tower_grad.reshape(DOMAINS, D, 128),
        rest[6].reshape(DOMAINS, 128),
        rest[7].reshape(DOMAINS, 128),
        rest[8][0, :DOMAINS],
    )
    logits = jnp.where(core == 1, jnp.roll(logits, HALF, axis=0), logits)
    return (
        logits,
        row_grads,
        proj_grad,
        common[0],
        common[1],
        up_grad,
        down_grad,
        common[2],
        common[3],
        common[4],
        common[5],
        common[6],
        common[7],
        common[8],
    )


def solution(mesh):
    placed = (
        P("wide", "narrow"),
        P("wide", None, None, "narrow"),
        P("wide", "narrow"),
        P(("wide", "narrow")),
        P(("wide", "narrow")),
        P(("wide", "narrow"), None),
        P("narrow", None),
        P(),
        P(),
        P(None, None, "narrow"),
        P(None, "narrow", None),
        P(),
        P(),
        P(),
        P(),
        P(),
        P(),
        P(),
    )
    return jax.shard_map(
        shards,
        mesh=mesh,
        in_specs=placed,
        out_specs=(
            P(("wide", "narrow")),
            P("wide", None, None, "narrow"),
            P("narrow", None),
            P(),
            P(),
            P(None, None, "narrow"),
            P(None, "narrow", None),
            P(),
            P(),
            P(),
            P(),
            P(),
            P(),
            P(),
        ),
        check_vma=False,
    )
```

```python
import functools

import jax
import jax.numpy as jnp
from jax import lax
from jax.experimental import pallas as pl
from jax.experimental.pallas import tpu as pltpu
from jax.sharding import PartitionSpec as P

D = 512
HID = 1024
EMB = 16
DENSE = 128
DOMAINS = 6
SHARED = 2
DOM_EXP = 2
DSLOT = 1024
HALF = DSLOT // 2
VMEM = 56 * 2**20
BF = jnp.bfloat16
F32 = jnp.float32
MESH = pl.DeviceIdType.MESH
UNITS = 9
ROWS_U = 1024
LANES = 256
PROJ_ROWS = 320
REP_ROWS = 704


def dot(a, b, ca, cb):
    return lax.dot_general(a, b, (((ca,), (cb,)), ((), ())), preferred_element_type=F32)


def lookup_kernel(lo_n, hi_n, fields, idx_ref, tab_ref, out_ref):
    length = idx_ref.shape[-1]
    shift = hi_n.bit_length() - 1
    for f in range(fields):
        idx = idx_ref[0, f : f + 1, :]
        hi = jnp.where(idx >= 0, idx & (hi_n - 1), -1)
        lo = lax.shift_right_logical(jnp.maximum(idx, 0), shift)
        hot = (lax.broadcasted_iota(jnp.int32, (hi_n, length), 0) == hi).astype(BF)
        cols = slice(f * EMB, (f + 1) * EMB)
        parts = [
            tab_ref[:, cols, j * hi_n : (j + 1) * hi_n].reshape(-1, hi_n) for j in range(tab_ref.shape[2] // hi_n)
        ]
        res = jnp.dot(jnp.concatenate(parts, axis=0), hot, preferred_element_type=F32)
        acc = res[0:EMB]
        for step in range(1, lo_n):
            acc = jnp.where(lo == step, res[step * EMB : (step + 1) * EMB], acc)
        out_ref[0, cols, :] = acc.astype(BF)


def lookup(idx, tab, hi_n, name, out_groups, order=lambda i: i):
    groups, fields, length = idx.shape
    outer, cols, inner = tab.shape
    lo_n = outer * inner // hi_n
    each = groups // out_groups
    return pl.pallas_call(
        functools.partial(lookup_kernel, lo_n, hi_n, fields),
        grid=(groups,),
        in_specs=[
            pl.BlockSpec((1, fields, length), lambda i: (order(i), 0, 0)),
            pl.BlockSpec(tab.shape, lambda i: (0, 0, 0)),
        ],
        out_specs=pl.BlockSpec((1, cols, length), lambda i: (i // each, 0, i % each)),
        out_shape=jax.ShapeDtypeStruct((out_groups, cols, length * each), BF),
        compiler_params=pltpu.CompilerParams(vmem_limit_bytes=VMEM),
        cost_estimate=pl.CostEstimate(
            flops=2 * groups * length * cols * lo_n * hi_n, bytes_accessed=8 * 2**20, transcendentals=0
        ),
        name=name,
    )(idx, tab)


def place_one(idx_ref, grad_ref, out_ref, field):
    outer, _, inner = out_ref.shape
    length = grad_ref.shape[2]
    hi_n = 256
    lo_n = outer * inner // hi_n
    cols = pl.ds(pl.multiple_of(field * EMB, EMB), EMB)
    total = None
    for s in range(grad_ref.shape[0]):
        idx = idx_ref[s, pl.ds(field, 1), :]
        hi = idx & (hi_n - 1)
        lo = lax.shift_right_logical(idx, hi_n.bit_length() - 1)
        grad = grad_ref[s, cols, :]
        hot = (lax.broadcasted_iota(jnp.int32, (hi_n, length), 0) == hi).astype(BF)
        lhs = jnp.concatenate(
            [jnp.where(lo == step, grad, jnp.zeros_like(grad)) for step in range(lo_n)], axis=0
        )
        part = dot(lhs, hot, 1, 1)
        total = part if total is None else total + part
    for j in range(inner // hi_n):
        piece = total[j * outer * EMB : (j + 1) * outer * EMB]
        out_ref[:, cols, j * hi_n : (j + 1) * hi_n] = piece.reshape(outer, EMB, hi_n).astype(BF)


def place_kernel(idx_ref, grad_ref, out_ref):
    def one(field, _):
        place_one(idx_ref, grad_ref, out_ref, field)
        return 0

    lax.fori_loop(0, idx_ref.shape[1], one, 0)


def place(idx, grad, out_shape):
    return pl.pallas_call(
        place_kernel,
        out_shape=jax.ShapeDtypeStruct(out_shape, BF),
        compiler_params=pltpu.CompilerParams(vmem_limit_bytes=VMEM),
        name="place_rows",
    )(idx, grad)


def front_kernel(
    groups, req_ref, tab_ref, slot_ref, stat_ref, up_ref, down_ref, proj_ref,
    emb_ref, far_up, far_down, their_up, their_down, proj_out, every_ref,
    asked, found, received, ordered, both,
    req_send, req_recv, row_send, row_recv, near_send, near_recv, keep_sem,
    far_send, far_recv, side_send, own_send, own_recv, their_send, their_recv, proj_send, proj_recv,
    stat_send, stat_recv,
):
    wide, me = lax.axis_index("wide"), lax.axis_index("narrow")
    chip, core = me // 2, me % 2
    owners, fields, cap = req_ref.shape
    share = fields // groups
    parity = wide % 2
    near = [{"narrow": me + 1 - 2 * core}, {"narrow": me + 2 - 4 * chip}, {"narrow": 3 - me}]
    near_at = [me + 1 - 2 * core, me + 2 - 4 * chip, 3 - me]
    peers = [None] + [{"wide": (wide + d) % owners} for d in range(1, owners)]
    side = {"wide": wide + 1 - 2 * parity}
    barrier = pltpu.get_barrier_semaphore()
    for mate in near + peers[1:]:
        pl.semaphore_signal(barrier, inc=1, device_id=mate, device_id_type=MESH)
    pl.semaphore_wait(barrier, len(near) + len(peers) - 1)

    def remote(src, dst, send, recv, mate):
        return pltpu.make_async_remote_copy(
            src_ref=src, dst_ref=dst, send_sem=send, recv_sem=recv, device_id=mate, device_id_type=MESH
        )

    def req_copy(d):
        return remote(req_ref.at[(wide + d) % owners], asked.at[wide], req_send.at[d], req_recv.at[d], peers[d])

    for d in range(1, owners):
        req_copy(d).start()
    mine = pltpu.make_async_copy(req_ref.at[wide], asked.at[wide], keep_sem.at[0])
    mine.start()

    def stat_core():
        return remote(stat_ref, both.at[pl.ds(8, 8)], stat_send.at[0], stat_recv.at[0], near[0])

    def stat_copy(d):
        return remote(both, every_ref.at[wide], stat_send.at[d], stat_recv.at[d], peers[d])

    stat_core().start()
    both[0:8, :] = stat_ref[...]

    weights = ((up_ref, far_up, their_up), (down_ref, far_down, their_down))

    def far_copy(j, a):
        p = 2 * j + parity
        expert = jnp.where(j == 0, parity, 6 * (1 - chip) + p)
        return remote(weights[a][0].at[expert], weights[a][1].at[p], far_send.at[a, j], far_recv.at[a, p], near[1])

    def side_copy(p, a):
        view = weights[a][1].at[p]
        return remote(view, view, side_send.at[a, p // 2], far_recv.at[a, p], side)

    def own_copy(i, a):
        expert = jnp.where(i < 2, i, 6 * chip + jnp.where(i < 4, i + 4 * (1 - core), i))
        return remote(weights[a][0].at[expert], weights[a][2].at[0, i], own_send.at[a, i], own_recv.at[a, i], near[0])

    def their_copy(p, a):
        i = jnp.where(p < 6, p, p - 4)
        return remote(weights[a][1].at[p], weights[a][2].at[1, i], their_send.at[a, i], their_recv.at[a, i], near[0])

    def wanted(p):
        ends = jnp.logical_or(jnp.logical_and(p < 4, core == 1), jnp.logical_and(p >= 6, core == 0))
        return jnp.logical_or(jnp.logical_or(p < 2, jnp.logical_and(p >= 4, p < 6)), ends)

    def for_all(n, f):
        def body(i, _):
            for a in range(2):
                f(i, a)
            return 0

        lax.fori_loop(0, n, body, 0)

    for_all(4, lambda j, a: far_copy(j, a).start())

    def proj_copy(i):
        return remote(proj_ref, proj_out.at[me], proj_send.at[i], proj_recv.at[i], near[i])

    keep_proj = pltpu.make_async_copy(proj_ref, proj_out.at[me], keep_sem.at[1])
    keep_proj.start()
    for i in range(3):
        proj_copy(i).start()
    for_all(6, lambda i, a: own_copy(i, a).start())
    stat_core().wait_recv()
    for d in range(1, owners):
        stat_copy(d).start()
    keep_stat = pltpu.make_async_copy(both, every_ref.at[wide], keep_sem.at[2])
    keep_stat.start()

    def far_step(j):
        p = 2 * j + parity
        for a in range(2):
            far_copy(j, a).wait_recv()
            side_copy(p, a).start()
        pass_on(p)

    def pass_on(p):
        @pl.when(wanted(p))
        def _():
            for a in range(2):
                their_copy(p, a).start()

    def side_step(j):
        p = 2 * j + 1 - parity
        for a in range(2):
            side_copy(p, a).wait_recv()
        pass_on(p)

    lo_n, _, hi_n = tab_ref.shape

    def find(f, owner_idx):
        idx = asked[owner_idx, pl.ds(f, 1), :]
        hi = jnp.where(idx >= 0, idx & (hi_n - 1), -1)
        lo = lax.shift_right_logical(jnp.maximum(idx, 0), hi_n.bit_length() - 1)
        hot = (lax.broadcasted_iota(jnp.int32, (hi_n, cap), 0) == hi).astype(BF)
        cols = pl.ds(pl.multiple_of(f * EMB, EMB), EMB)
        res = jnp.dot(tab_ref[:, cols, :].reshape(lo_n * EMB, hi_n), hot, preferred_element_type=F32)
        acc = res[0:EMB]
        for step in range(1, lo_n):
            acc = jnp.where(lo == step, res[step * EMB : (step + 1) * EMB], acc)
        return cols, acc.astype(BF)

    def group_rows(g):
        return pl.ds(pl.multiple_of(g * share * EMB, share * EMB), share * EMB)

    def row_copy(g, d, mate):
        rows = group_rows(g)
        return remote(
            found.at[(wide + d) % owners, rows], received.at[wide, rows], row_send.at[g, d], row_recv.at[g, d], mate
        )

    def look(g):
        def one(d, _):
            sender = (wide + d) % owners

            @pl.when(jnp.logical_and(g == 0, d > 0))
            def _():
                remote(req_ref.at[0], asked.at[sender], req_send.at[d], req_recv.at[owners - d], peers[1]).wait_recv()

            for k in range(share):
                cols, block = find(g * share + k, sender)

                @pl.when(d == 0)
                def _():
                    received[wide, cols, :] = block

                @pl.when(d > 0)
                def _():
                    found[sender, cols, :] = block

            @pl.when(d > 0)
            def _():
                row_copy(g, d, {"wide": sender}).start()

            return 0

        lax.fori_loop(0, owners, one, 0)

    hi_e = 256
    outer = owners * cap // hi_e

    def near_copy(g, i):
        rows = group_rows(g)
        return remote(
            ordered.at[near_at[i], rows], emb_ref.at[me, rows], near_send.at[g, i], near_recv.at[g, i], near[i]
        )

    def keep_copy(g):
        rows = group_rows(g)
        return pltpu.make_async_copy(ordered.at[me, rows], emb_ref.at[me, rows], keep_sem.at[3 + g])

    def order(g):
        def arrive(d, _):
            row_copy(g, d, {"wide": (wide + d) % owners}).wait_recv()
            return 0

        lax.fori_loop(1, owners, arrive, 0)
        tables = []
        for k in range(share):
            cols = pl.ds(pl.multiple_of((g * share + k) * EMB, EMB), EMB)
            parts = [
                received[:, cols, j * hi_e : (j + 1) * hi_e].reshape(owners * EMB, hi_e) for j in range(cap // hi_e)
            ]
            tables.append((cols, jnp.concatenate(parts, axis=0)))

        def quarter(q):
            for k, (cols, table) in enumerate(tables):
                idx = slot_ref[q, pl.ds(g * share + k, 1), :]
                hi = idx & (hi_e - 1)
                lo = lax.shift_right_logical(idx, hi_e.bit_length() - 1)
                hot = (lax.broadcasted_iota(jnp.int32, (hi_e, idx.shape[1]), 0) == hi).astype(BF)
                res = jnp.dot(table, hot, preferred_element_type=F32)
                acc = res[0:EMB]
                for step in range(1, outer):
                    acc = jnp.where(lo == step, res[step * EMB : (step + 1) * EMB], acc)
                ordered[q, cols, :] = acc.astype(BF)

        for i in (2, 1, 0):
            quarter(near_at[i])
            near_copy(g, i).start()
        quarter(me)
        keep_copy(g).start()

    mine.wait()

    def tick(t, _):
        @pl.when(t < groups)
        def _():
            look(t)

        @pl.when(jnp.logical_and(t >= 1, t < 5))
        def _():
            far_step(t - 1)

        @pl.when(t >= 2)
        def _():
            order(t - 2)

        @pl.when(t >= 3)
        def _():
            side_step(t - 3)

        return 0

    lax.fori_loop(0, groups + 2, tick, 0)

    for d in range(1, owners):
        req_copy(d).wait_send()
        stat_copy(d).wait()
    stat_core().wait_send()
    keep_stat.wait()
    keep_proj.wait()
    for i in range(3):
        proj_copy(i).wait()

    def rows_left(g, _):
        def one(d, _):
            row_copy(g, d, {"wide": (wide + d) % owners}).wait_send()
            return 0

        lax.fori_loop(1, owners, one, 0)
        for i in range(3):
            near_copy(g, i).wait()
        keep_copy(g).wait()
        return 0

    lax.fori_loop(0, groups, rows_left, 0)

    def weights_left(j, a):
        far_copy(j, a).wait_send()
        side_copy(2 * j + parity, a).wait_send()

    for_all(4, weights_left)
    for_all(6, lambda i, a: own_copy(i, a).wait())

    def passed(p, a):
        @pl.when(wanted(p))
        def _():
            their_copy(p, a).wait_send()

    for_all(8, passed)
    for_all(6, lambda i, a: their_copy(i, a).wait_recv())


def front(req, tab, slots, stats, up, down, proj, groups=5):
    owners, fields, cap = req.shape
    cols = fields * EMB
    quarters, _, rows = slots.shape
    any_space, vmem = pl.BlockSpec(memory_space=pl.ANY), pl.BlockSpec(memory_space=pltpu.VMEM)
    dma = pltpu.SemaphoreType.DMA
    return pl.pallas_call(
        functools.partial(front_kernel, groups),
        in_specs=[vmem] * 4 + [any_space] * 3,
        out_specs=[any_space] * 7,
        out_shape=[
            jax.ShapeDtypeStruct((quarters, cols, rows), BF),
            jax.ShapeDtypeStruct((8,) + up.shape[1:], BF),
            jax.ShapeDtypeStruct((8,) + down.shape[1:], BF),
            jax.ShapeDtypeStruct((2, 6) + up.shape[1:], BF),
            jax.ShapeDtypeStruct((2, 6) + down.shape[1:], BF),
            jax.ShapeDtypeStruct((quarters,) + proj.shape, BF),
            jax.ShapeDtypeStruct((owners, 16, DENSE), F32),
        ],
        scratch_shapes=[
            pltpu.VMEM((owners, fields, cap), jnp.int32),
            pltpu.VMEM((owners, cols, cap), BF),
            pltpu.VMEM((owners, cols, cap), BF),
            pltpu.VMEM((quarters, cols, rows), BF),
            pltpu.VMEM((16, DENSE), F32),
            dma((owners,)),
            dma((owners,)),
            dma((groups, owners)),
            dma((groups, owners)),
            dma((groups, 3)),
            dma((groups, 3)),
            dma((3 + groups,)),
            dma((2, 4)),
            dma((2, 8)),
            dma((2, 4)),
            dma((2, 6)),
            dma((2, 6)),
            dma((2, 6)),
            dma((2, 6)),
            dma((3,)),
            dma((3,)),
            dma((owners,)),
            dma((owners,)),
        ],
        compiler_params=pltpu.CompilerParams(collective_id=1, has_side_effects=True, vmem_limit_bytes=VMEM),
        cost_estimate=pl.CostEstimate(flops=45 * 10**9, bytes_accessed=40 * 2**20, transcendentals=0),
        name="front",
    )(req, tab, slots, stats, up, down, proj)


def reduce_kernel(bits, with_rows, own_ref, extra_ref, *refs):
    if with_rows:
        slot_ref, grad_ref, out_ref, rep_ref, back_ref = refs[:5]
        grads, placed, near_send, near_recv, far_send, far_recv, keep_sem = refs[-7:]
        refs = refs[5:-7]
    else:
        out_ref, rep_ref = refs[:2]
        refs = refs[2:]
    acc, stage_buf, halves, got, local_sem, send, recv, rep_send, rep_recv, out_sem = refs
    wide=lax.axis_index("wide"); me=lax.axis_index("narrow")
    chip=me//2; core=me%2
    block=ROWS_U>>bits
    mates=[{"narrow": me+1-2*core},{"narrow": me+2-4*chip}]
    pairs=[{"wide": wide+(1<<k)*(1-2*((wide//(1<<k))%2))} for k in range(bits)]
    far={"narrow": 3-me}
    barrier=pltpu.get_barrier_semaphore()
    owners=1<<bits
    others=[{"wide": (wide+d)%owners} for d in range(1,owners)] if with_rows else pairs
    for mate in mates+[far]+others:
        pl.semaphore_signal(barrier, inc=1, device_id=mate, device_id_type=MESH)
    pl.semaphore_wait(barrier, len(others)+3)
    def bit(k): return (wide//(1<<k))%2
    def start_of(k):
        at=0
        for j in range(k):
            at=at+bit(j)*(ROWS_U>>(j+1))
        return pl.multiple_of(at, 16) if k else 0
    stages=2*bits+2
    def copy(src,dst,s,u,mate):
        return pltpu.make_async_remote_copy(src_ref=src,dst_ref=dst,send_sem=send.at[s,u],recv_sem=recv.at[s,u],device_id=mate,device_id_type=MESH)
    def mine(u): return jnp.logical_or(jnp.logical_or(u<3,u>=7), jnp.logical_and(u<5,core==0)|jnp.logical_and(u>=5,core==1))
    def theirs(u): return jnp.logical_or(jnp.logical_or(u<3,u>=7), jnp.logical_and(u<5,core==1)|jnp.logical_and(u>=5,core==0))
    def local_at(u):
        return jnp.where(u<3,u-1,jnp.where(u<5,u-1,u-3))
    def core_copy(u, src):
        return copy(src, acc.at[u], 0, u, mates[0])
    def near_copy(u, src):
        return pltpu.make_async_copy(src, stage_buf.at[u%2], local_sem.at[u%2])
    def begin(u):
        @pl.when(u==0)
        def _():
            core_copy(u, extra_ref.at[pl.ds(2,2)]).start()
            near_copy(u, extra_ref.at[pl.ds(0,2)]).start()
        @pl.when(jnp.logical_and(u>0, mine(u)))
        def _():
            core_copy(u, own_ref.at[local_at(u), pl.ds(2,2)]).start()
            near_copy(u, own_ref.at[local_at(u), pl.ds(0,2)]).start()
    def add_region(u, sl, at, rows, src):
        tile=min(rows,64)
        def body(i,_):
            r=pl.multiple_of(at+i*tile,16); q=pl.multiple_of(i*tile,16)
            for h in sl:
                a=acc[u,h,pl.ds(r,tile),:].astype(F32)+src[h,pl.ds(q,tile),:].astype(F32)
                acc[u,h,pl.ds(r,tile),:]=a.astype(BF)
            return 0
        lax.fori_loop(0,rows//tile,body,0)
    half_at=[0]
    for k in range(bits): half_at.append(half_at[-1]+(ROWS_U>>(k+1)))
    def half_view(u,k):
        return halves.at[u,:,pl.ds(half_at[k],ROWS_U>>(k+1)),:]
    def send_half(u,k):
        size=ROWS_U>>(k+1)
        at=pl.multiple_of(start_of(k)+(1-bit(k))*size,16)
        return copy(acc.at[u,:,pl.ds(at,size),:], half_view(u,k), 1+k, u, pairs[k])
    def combine(u):
        @pl.when(theirs(u))
        def _():
            core_copy(u, acc.at[u]).wait_recv()
        @pl.when(mine(u))
        def _():
            near_copy(u, acc.at[u]).wait()
            sb=stage_buf.at[u%2]
            @pl.when(theirs(u))
            def _():
                add_region(u,(0,1),0,ROWS_U,sb)
            @pl.when(jnp.logical_not(theirs(u)))
            def _():
                def body(i,_):
                    r=pl.multiple_of(i*64,16)
                    for h in (0,1): acc[u,h,pl.ds(r,64),:]=sb[h,pl.ds(r,64),:]
                    return 0
                lax.fori_loop(0,ROWS_U//64,body,0)
        send_half(u,0).start()
    def halve(u,k):
        size=ROWS_U>>k
        copy(acc.at[u,:,pl.ds(0,size),:], half_view(u,k-1), k, u, pairs[k-1]).wait_recv()
        add_region(u,(0,1),start_of(k),size,halves.at[u,:,pl.ds(half_at[k-1],size),:])
        if k<bits:
            send_half(u,k).start()
        else:
            y_copy(u).start()
    def y_copy(u):
        at=start_of(bits)
        return copy(acc.at[u,1,pl.ds(at,block),:], got.at[u,1,pl.ds(at,block),:], bits+1, u, mates[1])
    def grow_copy(u,j,parts):
        size=ROWS_U>>(j+1)
        at=start_of(j+1)
        view=got.at[u,pl.ds(0,parts),pl.ds(at,size),:]
        return copy(view,view,bits+2+(bits-1-j),u,pairs[j])
    def each_kind(u,f):
        @pl.when(u<3)
        def _(): f(1)
        @pl.when(u>=3)
        def _(): f(2)
    def cross(u):
        y_copy(u).wait_recv()
        at=start_of(bits)
        @pl.when(u<3)
        def _():
            a=acc[u,0,pl.ds(at,block),:].astype(F32)+got[u,1,pl.ds(at,block),:].astype(F32)
            got[u,0,pl.ds(at,block),:]=a.astype(BF)
        @pl.when(u>=3)
        def _():
            got[u,0,pl.ds(at,block),:]=acc[u,0,pl.ds(at,block),:]
        each_kind(u,lambda parts: grow_copy(u,bits-1,parts).start())
    def out_copy(u,parts):
        return pltpu.make_async_copy(got.at[u,pl.ds(0,parts)], out_ref.at[u,pl.ds(0,parts)], out_sem.at[u])
    rep_mates=[mates[0],mates[1],far]
    rep_rows=rep_ref.shape[1]
    def rep_copy(i):
        return pltpu.make_async_remote_copy(src_ref=got.at[0,0,pl.ds(ROWS_U-rep_rows,rep_rows),:],dst_ref=rep_ref.at[i],send_sem=rep_send.at[i],recv_sem=rep_recv.at[i],device_id=rep_mates[i],device_id_type=MESH)
    def grow(u,j):
        each_kind(u,lambda parts: grow_copy(u,j,parts).wait_recv())
        if j>0:
            each_kind(u,lambda parts: grow_copy(u,j-1,parts).start())
        else:
            each_kind(u,lambda parts: out_copy(u,parts).start())
            @pl.when(u==0)
            def _():
                for i in range(3): rep_copy(i).start()
    quarters=mates+[far]
    def quarter_at(i):
        return [me+1-2*core, me+2-4*chip, 3-me][i]
    def near_row_copy(i):
        return pltpu.make_async_remote_copy(src_ref=grad_ref.at[quarter_at(i)],dst_ref=grads.at[me],send_sem=near_send.at[i],recv_sem=near_recv.at[i],device_id=quarters[i],device_id_type=MESH)
    def keep_copy():
        return pltpu.make_async_copy(grad_ref.at[me],grads.at[me],keep_sem.at[0])
    def back_copy(d):
        return pltpu.make_async_remote_copy(src_ref=placed.at[(wide+d)%owners],dst_ref=back_ref.at[wide],send_sem=far_send.at[d],recv_sem=far_recv.at[d],device_id=others[d-1],device_id_type=MESH)
    def keep_back():
        return pltpu.make_async_copy(placed.at[wide],back_ref.at[wide],keep_sem.at[1])
    def place_field(f, _):
        place_one(slot_ref, grads, placed, f)
        return 0
    def row_step(t):
        fields=slot_ref.shape[1]
        @pl.when(t==2)
        def _():
            keep_copy().wait()
            for i in range(3): near_row_copy(i).wait_recv()
        @pl.when(jnp.logical_and(t>=2,t<7))
        def _():
            lax.fori_loop((t-2)*(fields//5),(t-1)*(fields//5),place_field,0)
        @pl.when(t==6)
        def _():
            keep_back().start()
            for d in range(1,owners): back_copy(d).start()
    todo=[begin,combine]+[functools.partial(lambda k,u: halve(u,k),k) for k in range(1,bits+1)]+[cross]+[functools.partial(lambda j,u: grow(u,j),j) for j in reversed(range(bits))]
    def tick(t,_):
        for s in reversed(range(len(todo))):
            u=t-s
            @pl.when(jnp.logical_and(u>=0,u<UNITS))
            def _():
                todo[s](u)
        if with_rows:
            row_step(t)
        return 0
    if with_rows:
        keep_copy().start()
        for i in range(3): near_row_copy(i).start()
    lax.fori_loop(0,UNITS+len(todo)-1,tick,0)
    if with_rows:
        keep_back().wait()
        for i in range(3): near_row_copy(i).wait_send()
        for d in range(1,owners): back_copy(d).wait()
    def finish(u,_):
        @pl.when(mine(u))
        def _():
            core_copy(u, acc.at[u]).wait_send()
        for k in range(bits): send_half(u,k).wait_send()
        y_copy(u).wait_send()
        for j in range(bits): each_kind(u,lambda parts: grow_copy(u,j,parts).wait_send())
        each_kind(u,lambda parts: out_copy(u,parts).wait())
        return 0
    lax.fori_loop(0,UNITS,finish,0)
    for i in range(3):
        rep_copy(i).wait()

def reduce_all(own, extra, wide, rep_rows, rows=None):
    bits = wide.bit_length() - 1
    args = [own, extra]
    any_space = pl.BlockSpec(memory_space=pl.ANY)
    in_specs = [any_space] * 2
    out_shape = [
        jax.ShapeDtypeStruct((UNITS, 2, ROWS_U, LANES), BF),
        jax.ShapeDtypeStruct((3, rep_rows, LANES), BF),
    ]
    scratch = [
        pltpu.VMEM((UNITS, 2, ROWS_U, LANES), BF),
        pltpu.VMEM((2, 2, ROWS_U, LANES), BF),
        pltpu.VMEM((UNITS, 2, ROWS_U, LANES), BF),
        pltpu.VMEM((UNITS, 2, ROWS_U, LANES), BF),
        pltpu.SemaphoreType.DMA((2,)),
        pltpu.SemaphoreType.DMA((2 * bits + 2, UNITS)),
        pltpu.SemaphoreType.DMA((2 * bits + 2, UNITS)),
        pltpu.SemaphoreType.DMA((3,)),
        pltpu.SemaphoreType.DMA((3,)),
        pltpu.SemaphoreType.DMA((UNITS,)),
    ]
    if rows is not None:
        slots, grads, cap = rows
        args += [slots, grads]
        in_specs += [pl.BlockSpec(memory_space=pltpu.VMEM), any_space]
        back = (wide, grads.shape[1], cap)
        out_shape.append(jax.ShapeDtypeStruct(back, BF))
        scratch += [
            pltpu.VMEM(grads.shape, BF),
            pltpu.VMEM(back, BF),
            pltpu.SemaphoreType.DMA((3,)),
            pltpu.SemaphoreType.DMA((3,)),
            pltpu.SemaphoreType.DMA((wide,)),
            pltpu.SemaphoreType.DMA((wide,)),
            pltpu.SemaphoreType.DMA((2,)),
        ]
    return pl.pallas_call(
        functools.partial(reduce_kernel, bits, rows is not None),
        in_specs=in_specs,
        out_specs=[any_space] * len(out_shape),
        out_shape=out_shape,
        scratch_shapes=scratch,
        compiler_params=pltpu.CompilerParams(collective_id=0, has_side_effects=True, vmem_limit_bytes=VMEM),
        cost_estimate=pl.CostEstimate(flops=0, bytes_accessed=60 * 2**20, transcendentals=0),
        name="reduce_all",
    )(*args)


C0 = 0.7978845608028654
C1 = 0.044715


def gelu_both(x):
    square = x * x
    t = jnp.tanh(C0 * x * (1.0 + C1 * square))
    up = 0.5 * (1.0 + t)
    slope = up + 0.5 * x * (1.0 - t * t) * (C0 + (3.0 * C0 * C1) * square)
    return x * up, slope


def soft_pair(a, b):
    top = jnp.maximum(a, b)
    ea, eb = jnp.exp(a - top), jnp.exp(b - top)
    total = ea + eb
    return ea / total, eb / total


def soft_pair_back(pa, pb, ga, gb):
    mean = pa * ga + pb * gb
    return pa * (ga - mean), pb * (gb - mean)


def fold(x):
    return sum(x[:, i * 128 : (i + 1) * 128] for i in range(x.shape[1] // 128))


def wide_lanes(x, n):
    return jnp.concatenate([x] * n, axis=1)


def dense_kernel(
    ids_ref, emb_ref, feat_ref, projw_ref, featw_ref, up_a, up_b, up_c, down_a, down_b, down_c, gain_ref, shift_ref, gate_ref, tin_ref,
    tbias_ref, tout_ref, tob_ref, label_ref, live_ref,
    logit_ref, own_ref, emb_grad_ref, proj_grad_ref, feat_grad_ref, gain_acc, shift_acc, gate_acc, tin_acc,
    tbias_acc, tout_acc, tob_acc,
    xt, act, slope, outs, og, ing, hid, hg, stat, coef, inner, emb, emb_sem,
):
    ups = [up_a.at[0], up_b.at[0], up_c.at[0, 0], up_c.at[1, 0]]
    downs = [down_a.at[0], down_b.at[0], down_c.at[0, 0], down_c.at[1, 0]]
    step = pl.program_id(0)
    chunk, slot = step // 4, step % 4
    rows = xt.shape[1]

    @pl.when(step == 0)
    def _():
        fetch = pltpu.make_async_copy(emb_ref, emb, emb_sem)
        fetch.start()
        fetch.wait()
        for c in range(rows // HALF):
            cols = slice(c * HALF, (c + 1) * HALF)
            x = dot(projw_ref[...], emb[:, cols], 0, 0) + dot(featw_ref[...], feat_ref[:, cols], 0, 0)
            xt[:, cols] = x.astype(BF)
        for ref in (gain_acc, shift_acc, gate_acc, tin_acc, tbias_acc, tout_acc, tob_acc):
            ref[...] = jnp.zeros_like(ref)

    @pl.when(step < 12)
    def _():
        lanes = pl.ds(pl.multiple_of(chunk * HALF, HALF), HALF)

        def piece(s, total):
            pre = dot(ups[s][...], xt[:, lanes], 0, 0)
            a, g = gelu_both(pre)
            a = a.astype(BF)
            act[slot, s, :, lanes] = a
            slope[slot, s, :, lanes] = g.astype(BF)
            return dot(downs[s][...], a, 0, 0)

        outs[slot] = piece(0, None)
        for s in range(1, 4):
            outs[slot] += piece(s, None)

    def middle():
        lanes = pl.ds(pl.multiple_of(chunk * HALF, HALF), HALF)
        dom = chunk // 2
        x = xt[:, lanes]
        gates = dot(gate_ref[dom], x, 1, 0)
        s0, s1 = soft_pair(gates[0:1], gates[1:2])
        d0, d1 = soft_pair(gates[2:3], gates[3:4])
        t0, t1 = soft_pair(gates[4:5], gates[5:6])
        for k, row in enumerate((t0 * s0, t0 * s1, t1 * d0, t1 * d1)):
            coef[k : k + 1, :] = row
        expert = [0, 1, 2 + 2 * dom, 3 + 2 * dom]

        def normalize(t, _):
            cols = pl.ds(pl.multiple_of(t * 128, 128), 128)
            for k in range(4):
                v = outs[k, :, cols]
                mean = jnp.sum(v, axis=0, keepdims=True) * (1.0 / D)
                v = v - mean
                var = jnp.sum(v * v, axis=0, keepdims=True) * (1.0 / D)
                stat[k : k + 1, cols] = mean
                stat[4 + k : 5 + k, cols] = lax.rsqrt(var + 1e-05)
            for r in range(4):
                band = slice(r * 128, (r + 1) * 128)
                acc = None
                for k in range(4):
                    n = (outs[k, band, cols] - stat[k : k + 1, cols]) * stat[4 + k : 5 + k, cols]
                    n = (n * gain_ref[expert[k], band, :].astype(F32) + shift_ref[expert[k], band, :].astype(F32)) * coef[k : k + 1, cols]
                    acc = n if acc is None else acc + n
                hid[band, cols] = acc.astype(BF)
            return 0

        lax.fori_loop(0, 4, normalize, 0)
        h = hid[...]
        pre = dot(tin_ref[dom], h, 0, 0) + wide_lanes(tbias_ref[dom], 4)
        tact, tslope = gelu_both(pre)
        tout = wide_lanes(tout_ref[dom], 4)
        logit = jnp.sum(tact * tout, axis=0, keepdims=True) + wide_lanes(tob_ref[dom, 0:1, :], 4)
        logit_ref[:, lanes] = logit
        grad = (jax.nn.sigmoid(logit) - label_ref[:, lanes]) * live_ref[:, lanes]
        tob_acc[dom, 0:1, :] += fold(grad)
        tout_acc[dom] += fold(grad * tact)
        low = (grad * tout * tslope).astype(BF)
        tbias_acc[dom] += fold(low.astype(F32))
        tin_acc[dom] += dot(h, low, 1, 1)
        hg[...] = dot(tin_ref[dom], low, 1, 0)

        def denormalize(t, _):
            cols = pl.ds(pl.multiple_of(t * 128, 128), 128)
            place = pl.ds(pl.multiple_of(chunk * HALF + t * 128, 128), 128)
            for k in range(4):
                mean, rstd = stat[k : k + 1, cols], stat[4 + k : 5 + k, cols]
                c = coef[k : k + 1, cols]
                m1 = m2 = mb = 0.0
                for r in range(4):
                    band = slice(r * 128, (r + 1) * 128)
                    n = (outs[k, band, cols] - mean) * rstd
                    grad = hg[band, cols]
                    scaled = grad * gain_ref[expert[k], band, :].astype(F32)
                    m1 = m1 + jnp.sum(scaled, axis=0, keepdims=True)
                    m2 = m2 + jnp.sum(scaled * n, axis=0, keepdims=True)
                    mb = mb + jnp.sum(grad * shift_ref[expert[k], band, :].astype(F32), axis=0, keepdims=True)
                    part = c * grad
                    gain_acc[expert[k], band, :] += part * n
                    shift_acc[expert[k], band, :] += part
                inner[k : k + 1, cols] = m2 + mb
                m1, m2, cr = m1 * (1.0 / D), m2 * (1.0 / D), c * rstd
                for r in range(4):
                    band = slice(r * 128, (r + 1) * 128)
                    n = (outs[k, band, cols] - mean) * rstd
                    scaled = hg[band, cols] * gain_ref[expert[k], band, :].astype(F32)
                    og[k, band, place] = (cr * (scaled - m1 - n * m2)).astype(BF)
            return 0

        lax.fori_loop(0, 4, denormalize, 0)
        a = [inner[k : k + 1, :] for k in range(4)]
        g0, g1 = soft_pair_back(s0, s1, t0 * a[0], t0 * a[1])
        g2, g3 = soft_pair_back(d0, d1, t1 * a[2], t1 * a[3])
        g4, g5 = soft_pair_back(t0, t1, s0 * a[0] + s1 * a[1], d0 * a[2] + d1 * a[3])
        zero = jnp.zeros_like(g0)
        g = jnp.concatenate([g0, g1, g2, g3, g4, g5, zero, zero], axis=0)
        high = g.astype(BF).astype(F32)
        g = jnp.concatenate([high, g - high], axis=0).astype(BF)
        gate_acc[dom] += dot(g, x, 1, 1)
        ing[:, lanes] = dot(gate_ref[dom], g, 0, 0)

    @pl.when(jnp.logical_and(step < 12, slot == 3))
    def _():
        middle()

    def back(k, at, n):
        lanes = slice(at, at + n)

        for s in range(4):
            p = dot(downs[s][...], og[k, :, lanes], 1, 0) * slope[k, s, :, lanes].astype(F32)
            slope[k, s, :, lanes] = p.astype(BF)

        def piece(s, _):
            grad, p = og[k, :, lanes], slope[k, s, :, lanes]
            own_ref[0, s, 0:D, :] = dot(xt[:, lanes], p, 1, 1).astype(BF)
            d = dot(act[k, s, :, lanes], grad, 1, 1).astype(BF)
            own_ref[0, s, D : D + 256, :] = d[:, 0:256]
            own_ref[0, s, D + 256 : D + 512, :] = d[:, 256:512]
            return 0

        lax.fori_loop(0, 4, piece, 0)

        def grow(t, _):
            cols = pl.ds(pl.multiple_of(at + t * HALF, HALF), HALF)
            total = dot(ups[0][...], slope[k, 0, :, cols], 1, 0)
            for s in range(1, 4):
                total += dot(ups[s][...], slope[k, s, :, cols], 1, 0)
            ing[:, cols] += total
            return 0

        lax.fori_loop(0, n // HALF, grow, 0)

    expert = step - 12

    @pl.when(jnp.logical_and(expert >= 0, expert < 2))
    def _():
        back(expert, 0, rows)

    @pl.when(jnp.logical_and(expert >= 2, expert < 4))
    def _():
        back(expert, 0, DSLOT)

    @pl.when(expert >= 4)
    def _():
        back(expert - 2, DSLOT, rows - DSLOT)

    @pl.when(expert == 5)
    def _():
        low = ing[...].astype(BF)
        proj_grad_ref[...] = dot(emb[...], low, 1, 1).astype(BF)
        feat_grad_ref[...] = dot(feat_ref[...], low, 1, 1)
        for c in range(rows // HALF):
            cols = slice(c * HALF, (c + 1) * HALF)
            emb[:, cols] = dot(projw_ref[...], low[:, cols], 1, 0).astype(BF)
        put = pltpu.make_async_copy(emb, emb_grad_ref, emb_sem)
        put.start()
        put.wait()


def dense(ids, emb, feat, projw, featw, ups, downs, gains, shifts, gate, tin, tbias, tout, tob, label, live):
    rows = emb.shape[1]

    def ahead(i):
        c, j = i // 4, i % 4
        front = jnp.where(j < 2, j, jnp.where(c < 2, j, j + 2))
        return jnp.where(i < 12, front, i - 12)

    def whole(x):
        return pl.BlockSpec(x.shape, lambda i, ids: (0,) * len(x.shape), pipeline_mode=pl.Buffered(1))

    def shape(s, d):
        return jax.ShapeDtypeStruct(s, d)

    outs = [
        shape((1, rows), F32),
        shape((6, 4, 2 * D, 256), BF),
        shape(emb.shape, BF),
        shape(projw.shape, BF),
        shape(featw.shape, F32),
        shape(gains.shape, F32),
        shape(gains.shape, F32),
        shape(gate.shape, F32),
        shape(tin.shape, F32),
        shape(tbias.shape, F32),
        shape(tout.shape, F32),
        shape(tob.shape, F32),
    ]
    args = (emb, feat, projw, featw) + ups + downs + (gains, shifts, gate, tin, tbias, tout, tob, label, live)
    in_specs = [whole(x) for x in args]
    in_specs[0] = pl.BlockSpec(memory_space=pl.ANY)
    for at, group in ((4, ups), (7, downs)):
        block = group[0].shape[1:]
        in_specs[at] = pl.BlockSpec((1,) + block, lambda i, ids: (ids[ahead(i)], 0, 0))
        in_specs[at + 1] = pl.BlockSpec((1,) + block, lambda i, ids: (ids[6 + ahead(i)], 0, 0))
        in_specs[at + 2] = pl.BlockSpec((2, 1) + block, lambda i, ids: (0, ahead(i), 0, 0))
    out_specs = [whole(x) for x in outs]
    out_specs[2] = pl.BlockSpec(memory_space=pl.ANY)
    out_specs[1] = pl.BlockSpec((1, 4, 2 * D, 256), lambda i, ids: (jnp.maximum(i - 12, 0), 0, 0, 0))
    return pl.pallas_call(
        dense_kernel,
        grid_spec=pltpu.PrefetchScalarGridSpec(
            num_scalar_prefetch=1,
            grid=(18,),
            in_specs=in_specs,
            out_specs=out_specs,
            scratch_shapes=[
            pltpu.VMEM((D, rows), BF),
            pltpu.VMEM((4, 4, 256, rows), BF),
            pltpu.VMEM((4, 4, 256, rows), BF),
            pltpu.VMEM((4, D, HALF), F32),
            pltpu.VMEM((4, D, rows), BF),
            pltpu.VMEM((D, rows), F32),
            pltpu.VMEM((D, HALF), BF),
            pltpu.VMEM((D, HALF), F32),
            pltpu.VMEM((8, HALF), F32),
            pltpu.VMEM((8, HALF), F32),
            pltpu.VMEM((8, HALF), F32),
            pltpu.VMEM(emb.shape, BF),
            pltpu.SemaphoreType.DMA,
                    ]),
        out_shape=outs,
        compiler_params=pltpu.CompilerParams(vmem_limit_bytes=62 * 2**20),
        cost_estimate=pl.CostEstimate(flops=39 * 10**9, bytes_accessed=60 * 2**20, transcendentals=0),
        name="dense_all",
    )(ids, *args)


def own_stats(rows, weight):
    count = jnp.sum(weight)
    mean = jnp.sum(rows * weight, axis=1) / jnp.maximum(count, 1.0)
    off = rows - mean[:, None]
    return [mean, jnp.sum(off * off * weight, axis=1), jnp.broadcast_to(count, mean.shape)]


def pool(means, squares, counts):
    total = jnp.sum(counts, axis=0)
    mean = jnp.sum(counts * means, axis=0) / total
    off = means - mean
    return mean, (jnp.sum(squares, axis=0) + jnp.sum(counts * off * off, axis=0)) / total


def shards(
    embed_table,
    requests,
    slot_index,
    event_mask,
    labels,
    dense_feats,
    proj_weight,
    dense_weight,
    proj_bias,
    up_weight,
    down_weight,
    norm_gain,
    norm_shift,
    gate_weight,
    tower_in,
    tower_bias,
    tower_out,
    tower_out_bias,
):
    narrow = lax.axis_size("narrow")
    me = lax.axis_index("narrow")
    chip, core = me // 2, me % 2
    ev_rows, fields = slot_index.shape
    rows = ev_rows // narrow
    owners, cap = requests.shape[1], requests.shape[2]
    hid_here = up_weight.shape[2]
    other_chip = [(i, i ^ 2) for i in range(narrow)]
    other_core = [(i, i ^ 1) for i in range(narrow)]
    full = 3 * chip + 2 * core
    half = 3 * chip + 1

    def swap(x, pairs):
        return lax.ppermute(x, "narrow", pairs)

    def chip_experts(w, which):
        return jnp.concatenate(
            [w[:SHARED], lax.dynamic_slice_in_dim(w, SHARED + 6 * which, 6, axis=0)], axis=0
        )

    def bring(w):
        far = swap(chip_experts(w, 1 - chip), other_chip)
        at = lambda x, start, size: lax.dynamic_slice_in_dim(x, start, size, axis=0)
        base = SHARED + 6 * chip
        away = 4 * (1 - core)
        theirs = jnp.stack(
            [
                jnp.concatenate([w[:SHARED], at(w, base + away, 2), at(w, base + 2, 2)], axis=0),
                jnp.concatenate([far[:SHARED], at(far, 2 + away, 2), far[4:6]], axis=0),
            ]
        )
        return w, far, swap(theirs, other_core)

    six = jnp.arange(6, dtype=jnp.int32)
    spot = jnp.where(six < 2, six, jnp.where(six < 4, six + 4 * core, six))
    ids = jnp.concatenate([jnp.where(six < 2, six, spot + 6 * chip), spot])

    def by_offset(x):
        x = x.reshape((2, 2) + x.shape[1:])
        x = jnp.where(chip == 1, x[::-1], x)
        x = jnp.where(core == 1, x[:, ::-1], x)
        return x.reshape((narrow,) + x.shape[2:])

    def turned(x):
        return jnp.where(core == 1, jnp.roll(x, -HALF, axis=0), x)

    live = turned(event_mask).astype(F32)[None]
    label_rows = turned(labels).astype(F32)[None]
    feats = turned(dense_feats).T
    blank = jnp.zeros((2, DENSE), F32)
    stats = jnp.stack(
        own_stats(feats[:, :DSLOT], live[:, :DSLOT]) + own_stats(feats[:, DSLOT:], live[:, DSLOT:])
    )
    stats = jnp.concatenate([stats, blank], axis=0)

    turn = lambda i: (i // 3) * 3 + (i % 3 + (i // 3) % 2) % 3
    table_rows = embed_table.shape[0]
    cols = fields * EMB
    blocks = ev_rows // HALF
    hi_n = 256
    lo_n = ev_rows // hi_n
    direct = cap % hi_n == 0
    tab = embed_table.reshape(32, table_rows // 32, cols).transpose(0, 2, 1)
    slots = slot_index
    if direct:
        owner, rest = slots // cap, slots % cap
        slots = ((rest // hi_n) * owners + owner) * hi_n + rest % hi_n
    slots = slots.reshape(blocks, HALF, fields).transpose(0, 2, 1)
    slot_rows = jnp.stack([slots[turn(i)] for i in range(blocks)]).reshape(narrow, 3, fields, HALF)
    slot_rows = slot_rows.transpose(0, 2, 1, 3).reshape(narrow, fields, rows)
    asked = requests[0].transpose(0, 2, 1)
    if direct:
        embedded, far_up, far_down, their_up, their_down, proj_full, every = front(
            asked, tab, slot_rows, stats, up_weight, down_weight, proj_weight
        )
        ups, downs = (up_weight, far_up, their_up), (down_weight, far_down, their_down)
    else:
        asked = lax.all_to_all(asked, "wide", 0, 0, tiled=True)
        ups, downs = bring(up_weight), bring(down_weight)
        proj_full = lax.all_gather(proj_weight, "narrow", axis=0)
        stats = jnp.concatenate([stats, swap(stats, other_core)], axis=0)
        every = lax.all_to_all(
            jnp.broadcast_to(stats, (owners,) + stats.shape), "wide", 0, 0, tiled=True
        )
        flat = asked.transpose(1, 0, 2).reshape(fields, DOMAINS, DSLOT).transpose(1, 0, 2)
        found = lookup(flat, tab, table_rows // 32, "lookup_rows", DOMAINS)
        found = found.transpose(1, 0, 2).reshape(cols, owners, cap).transpose(1, 0, 2)
        received = lax.all_to_all(found, "wide", 0, 0, tiled=True)
        received = received.transpose(1, 0, 2).reshape(cols, lo_n, hi_n).transpose(1, 0, 2)
        embedded = lookup(slots, received, hi_n, "order_rows", narrow, turn)
        embedded = lax.all_to_all(embedded, "narrow", 0, 0, tiled=True)
    embedded = embedded.reshape(narrow * cols, rows)
    proj_full = proj_full.reshape(narrow * cols, D)
    full_mean, full_spread = pool(every[:, 0], every[:, 1], every[:, 2])
    both = jnp.concatenate([every[:, 3:6], every[:, 11:14]], axis=0)
    half_mean, half_spread = pool(both[:, 0], both[:, 1], both[:, 2])
    normal = lambda x, mean, spread: (x - mean[:, None]) * lax.rsqrt(spread + 1e-05)[:, None]
    feat = jnp.concatenate(
        [
            jnp.concatenate(
                [normal(feats[:, :DSLOT], full_mean, full_spread), normal(feats[:, DSLOT:], half_mean, half_spread)],
                axis=1,
            ),
            jnp.ones((1, rows), F32),
            jnp.zeros((15, rows), F32),
        ],
        axis=0,
    ).astype(BF)
    feat_weight = jnp.concatenate([dense_weight, proj_bias[None], jnp.zeros((15, D), BF)], axis=0)

    def pick(w):
        return jnp.stack(
            [
                lax.dynamic_index_in_dim(w, full, keepdims=False),
                lax.dynamic_index_in_dim(w, half, keepdims=False),
            ]
        )

    def over_lanes(x):
        return jnp.broadcast_to(x.astype(F32)[..., None], x.shape + (128,))

    def expert_rows(w):
        own = pick(w[SHARED:].reshape(DOMAINS, DOM_EXP, D)).reshape(4, D)
        w = jnp.concatenate([w[:SHARED], own], axis=0)
        return jnp.broadcast_to(w[..., None], w.shape + (128,))

    gate = jnp.pad(pick(gate_weight).transpose(0, 2, 1), ((0, 0), (0, 2), (0, 0)))
    gate = jnp.concatenate([gate, gate], axis=1)
    (
        logits, own, embed_grad, proj_grad, feat_grad, gain_sum, shift_sum, gate_grad, tower_grad,
        tower_bias_sum, tower_out_sum, out_bias_sum,
    ) = dense(
        ids, embedded, feat, proj_full, feat_weight, ups, downs, expert_rows(norm_gain), expert_rows(norm_shift),
        gate, pick(tower_in), over_lanes(pick(tower_bias)), over_lanes(pick(tower_out)),
        jnp.broadcast_to(pick(tower_out_bias).astype(F32)[:, None, None], (2, 8, 128)), label_rows, live,
    )
    logits = logits[0]

    embed_grad = embed_grad.reshape(narrow, cols, rows)
    if not direct:
        embed_grad = lax.all_to_all(embed_grad, "narrow", 0, 0, tiled=True)
        returned = place(slot_rows, embed_grad, (lo_n, cols, hi_n))
        returned = returned.transpose(1, 0, 2).reshape(cols, owners, cap).transpose(1, 0, 2)
        row_grads = lax.all_to_all(returned, "wide", 0, 0, tiled=True)

    def put(pair):
        zero = jnp.zeros((DOMAINS,) + pair.shape[1:], F32)
        zero = lax.dynamic_update_index_in_dim(zero, pair[0], full, 0)
        return lax.dynamic_update_index_in_dim(zero, pair[1], half, 0)

    def put_experts(sums):
        sums = jnp.sum(sums, axis=-1)
        own = put(sums[SHARED:].reshape(2, DOM_EXP, D)).reshape(DOMAINS * DOM_EXP, D)
        return jnp.concatenate([sums[:SHARED], own], axis=0)

    def pack(x):
        return jnp.concatenate([x[:, :LANES], x[:, LANES:]], axis=0)

    def unpack(x):
        return jnp.concatenate([x[: x.shape[0] // 2], x[x.shape[0] // 2 :]], axis=1)

    tower_grad = put(tower_grad).reshape(DOMAINS * D, 128)
    small = [
        jnp.concatenate([tower_grad[: DOMAINS * D // 2], tower_grad[DOMAINS * D // 2 :]], axis=1),
        pack(feat_grad[:DENSE]),
        pack(put(gate_grad[:, :6] + gate_grad[:, 8:14]).reshape(DOMAINS * 6, D)),
        pack(put_experts(gain_sum)),
        pack(put_experts(shift_sum)),
        feat_grad[DENSE].reshape(2, LANES),
        put(jnp.sum(tower_bias_sum, axis=-1)).reshape(3, LANES),
        put(jnp.sum(tower_out_sum, axis=-1)).reshape(3, LANES),
        jnp.pad(put(jnp.sum(out_bias_sum[:, 0], axis=-1)), (0, LANES - DOMAINS))[None],
    ]
    sizes = [x.shape[0] for x in small]
    small = jnp.concatenate(small, axis=0).astype(BF)
    small = jnp.pad(small, ((0, narrow * REP_ROWS - small.shape[0]), (0, 0)))

    proj_rows = proj_grad.reshape(narrow, cols, 2, LANES).transpose(0, 2, 1, 3)
    extra = jnp.concatenate(
        [proj_rows.reshape(narrow, PROJ_ROWS, LANES), small.reshape(narrow, REP_ROWS, LANES)], axis=1
    )
    extra = by_offset(extra)
    extra = jnp.stack([extra[0], extra[2], extra[1], extra[3]])
    if direct:
        sums, others, row_grads = reduce_all(own, extra, owners, REP_ROWS, (slot_rows, embed_grad, cap))
    else:
        sums, others = reduce_all(own, extra, owners, REP_ROWS)
    row_grads = row_grads.transpose(0, 2, 1).astype(F32)[None]

    own_chip, far_chip = [
        jnp.concatenate([sums[3:5, p], sums[7:9, p], sums[5:7, p]], axis=0) for p in (0, 1)
    ]
    low_half = jnp.where(chip == 0, own_chip, far_chip)
    high_half = jnp.where(chip == 0, far_chip, own_chip)
    whole = jnp.concatenate([sums[1:3, 0], low_half, high_half], axis=0)
    up_grad = whole[:, :D].astype(F32)
    down_grad = whole[:, D:].reshape(14, 2, hid_here, D // 2).transpose(0, 2, 1, 3)
    down_grad = down_grad.reshape(14, hid_here, D).astype(F32)
    proj_grad = unpack(sums[0, 0, :PROJ_ROWS]).astype(F32)
    rep = jnp.concatenate([sums[0, 0, None, PROJ_ROWS:], others], axis=0)
    rep = by_offset(rep).reshape(narrow * REP_ROWS, LANES).astype(F32)
    rest, at = [], 0
    for size in sizes:
        rest.append(rep[at : at + size])
        at += size
    tower_grad = jnp.concatenate([rest[0][:, :128], rest[0][:, 128:]], axis=0)
    common = (
        unpack(rest[1]),
        rest[5].reshape(D),
        unpack(rest[3]),
        unpack(rest[4]),
        unpack(rest[2]).reshape(DOMAINS, 6, D).transpose(0, 2, 1),
        tower_grad.reshape(DOMAINS, D, 128),
        rest[6].reshape(DOMAINS, 128),
        rest[7].reshape(DOMAINS, 128),
        rest[8][0, :DOMAINS],
    )
    logits = jnp.where(core == 1, jnp.roll(logits, HALF, axis=0), logits)
    return (
        logits,
        row_grads,
        proj_grad,
        common[0],
        common[1],
        up_grad,
        down_grad,
        common[2],
        common[3],
        common[4],
        common[5],
        common[6],
        common[7],
        common[8],
    )


def solution(mesh):
    placed = (
        P("wide", "narrow"),
        P("wide", None, None, "narrow"),
        P("wide", "narrow"),
        P(("wide", "narrow")),
        P(("wide", "narrow")),
        P(("wide", "narrow"), None),
        P("narrow", None),
        P(),
        P(),
        P(None, None, "narrow"),
        P(None, "narrow", None),
        P(),
        P(),
        P(),
        P(),
        P(),
        P(),
        P(),
    )
    return jax.shard_map(
        shards,
        mesh=mesh,
        in_specs=placed,
        out_specs=(
            P(("wide", "narrow")),
            P("wide", None, None, "narrow"),
            P("narrow", None),
            P(),
            P(),
            P(None, None, "narrow"),
            P(None, "narrow", None),
            P(),
            P(),
            P(),
            P(),
            P(),
            P(),
            P(),
        ),
        check_vma=False,
    )
```

```python
import functools

import jax
import jax.numpy as jnp
from jax import lax
from jax.experimental import pallas as pl
from jax.experimental.pallas import tpu as pltpu
from jax.sharding import PartitionSpec as P

D = 512
HID = 1024
EMB = 16
DENSE = 128
DOMAINS = 6
SHARED = 2
DOM_EXP = 2
DSLOT = 1024
HALF = DSLOT // 2
VMEM = 56 * 2**20
BF = jnp.bfloat16
F32 = jnp.float32
MESH = pl.DeviceIdType.MESH
UNITS = 9
TURNED = 0
ROW_AT = 5
ROW_STEP = 1
ROWS_U = 1024
LANES = 256


def dot(a, b, ca, cb):
    return lax.dot_general(a, b, (((ca,), (cb,)), ((), ())), preferred_element_type=F32)


def lookup_kernel(lo_n, hi_n, fields, idx_ref, tab_ref, out_ref):
    length = idx_ref.shape[-1]
    shift = hi_n.bit_length() - 1
    for f in range(fields):
        idx = idx_ref[0, f : f + 1, :]
        hi = jnp.where(idx >= 0, idx & (hi_n - 1), -1)
        lo = lax.shift_right_logical(jnp.maximum(idx, 0), shift)
        hot = (lax.broadcasted_iota(jnp.int32, (hi_n, length), 0) == hi).astype(BF)
        cols = slice(f * EMB, (f + 1) * EMB)
        parts = [
            tab_ref[:, cols, j * hi_n : (j + 1) * hi_n].reshape(-1, hi_n) for j in range(tab_ref.shape[2] // hi_n)
        ]
        res = jnp.dot(jnp.concatenate(parts, axis=0), hot, preferred_element_type=F32)
        acc = res[0:EMB]
        for step in range(1, lo_n):
            acc = jnp.where(lo == step, res[step * EMB : (step + 1) * EMB], acc)
        out_ref[0, cols, :] = acc.astype(BF)


def lookup(idx, tab, hi_n, name, out_groups, order=lambda i: i):
    groups, fields, length = idx.shape
    outer, cols, inner = tab.shape
    lo_n = outer * inner // hi_n
    each = groups // out_groups
    return pl.pallas_call(
        functools.partial(lookup_kernel, lo_n, hi_n, fields),
        grid=(groups,),
        in_specs=[
            pl.BlockSpec((1, fields, length), lambda i: (order(i), 0, 0)),
            pl.BlockSpec(tab.shape, lambda i: (0, 0, 0)),
        ],
        out_specs=pl.BlockSpec((1, cols, length), lambda i: (i // each, 0, i % each)),
        out_shape=jax.ShapeDtypeStruct((out_groups, cols, length * each), BF),
        compiler_params=pltpu.CompilerParams(vmem_limit_bytes=VMEM),
        cost_estimate=pl.CostEstimate(
            flops=2 * groups * length * cols * lo_n * hi_n, bytes_accessed=8 * 2**20, transcendentals=0
        ),
        name=name,
    )(idx, tab)


def quarter_slots(slot_ref, q, field):
    half = slot_ref.shape[1] // 12
    parts = []
    for c in range(3):
        at = q * 3 * half + ((c + q % 2) % 3) * half
        at = at if isinstance(at, int) else pl.multiple_of(at, half)
        parts.append(slot_ref[pl.ds(field, 1), pl.ds(at, half)])
    return jnp.concatenate(parts, axis=1)


def place_one(idx_ref, grad_ref, out_ref, field):
    outer, _, inner = out_ref.shape
    length = grad_ref.shape[2]
    hi_n = 256
    lo_n = outer * inner // hi_n
    cols = pl.ds(pl.multiple_of(field * EMB, EMB), EMB)
    total = None
    for s in range(grad_ref.shape[0]):
        idx = quarter_slots(idx_ref, s, field)
        hi = idx & (hi_n - 1)
        lo = lax.shift_right_logical(idx, hi_n.bit_length() - 1)
        grad = grad_ref[s, cols, :]
        hot = (lax.broadcasted_iota(jnp.int32, (hi_n, length), 0) == hi).astype(BF)
        lhs = jnp.concatenate(
            [jnp.where(lo == step, grad, jnp.zeros_like(grad)) for step in range(lo_n)], axis=0
        )
        part = dot(lhs, hot, 1, 1)
        total = part if total is None else total + part
    total = total.astype(BF)
    each = inner // hi_n
    for i in range(outer * each):
        out_ref[i // each, cols, (i % each) * hi_n : (i % each + 1) * hi_n] = total[i * EMB : (i + 1) * EMB]


def place_kernel(idx_ref, grad_ref, out_ref):
    def one(field, _):
        place_one(idx_ref, grad_ref, out_ref, field)
        return 0

    lax.fori_loop(0, idx_ref.shape[0], one, 0)


def place(idx, grad, out_shape):
    return pl.pallas_call(
        place_kernel,
        out_shape=jax.ShapeDtypeStruct(out_shape, BF),
        compiler_params=pltpu.CompilerParams(vmem_limit_bytes=VMEM),
        name="place_rows",
    )(idx, grad)


def own_stats(feats_ref, mask_ref, out_ref, core):
    highest = lax.Precision.HIGHEST

    def block(c):
        at = pl.ds(pl.multiple_of(((c + core) % 3) * HALF, HALF), HALF)
        weight = jnp.broadcast_to(mask_ref[:, at].astype(F32), (8, HALF))
        return feats_ref[at, :], weight

    def total(weight, x):
        return jnp.dot(weight, x, preferred_element_type=F32, precision=highest)[0:1]

    for row, chunks in ((0, (0, 1)), (3, (2,))):
        count = sum(jnp.sum(block(c)[1][0:1], axis=1, keepdims=True) for c in chunks)
        mean = sum(total(block(c)[1], block(c)[0]) for c in chunks) / jnp.maximum(count, 1.0)
        off = lambda c: block(c)[0] - mean
        out_ref[row : row + 1, :] = mean
        out_ref[row + 1 : row + 2, :] = sum(total(block(c)[1], off(c) * off(c)) for c in chunks)
        out_ref[row + 2 : row + 3, :] = jnp.broadcast_to(count, mean.shape)


def stats_kernel(core_ref, feats_ref, mask_ref, out_ref):
    out_ref[...] = jnp.zeros_like(out_ref)
    own_stats(feats_ref, mask_ref, out_ref, core_ref[0])


def local_stats(core, feats, mask):
    return pl.pallas_call(
        stats_kernel,
        in_specs=[pl.BlockSpec(memory_space=pltpu.SMEM)] + [pl.BlockSpec(memory_space=pltpu.VMEM)] * 2,
        out_shape=jax.ShapeDtypeStruct((8, DENSE), F32),
        compiler_params=pltpu.CompilerParams(vmem_limit_bytes=VMEM),
        name="local_stats",
    )(core, feats, mask)


def front_kernel(
    groups, req_ref, table_ref, slot_ref, feats_ref, mask_ref, up_ref, down_ref, proj_ref,
    emb_ref, far_up, far_down, their_up, their_down, proj_out, every_ref,
    asked, found, received, ordered, both,
    req_send, req_recv, row_send, row_recv, near_send, near_recv, keep_sem,
    far_send, far_recv, side_send, own_send, own_recv, their_send, their_recv, proj_send, proj_recv,
    stat_send, stat_recv,
):
    wide, me = lax.axis_index("wide"), lax.axis_index("narrow")
    chip, core = me // 2, me % 2
    owners, fields, cap = req_ref.shape
    share = fields // groups
    parity = wide % 2
    near = [{"narrow": me + 1 - 2 * core}, {"narrow": me + 2 - 4 * chip}, {"narrow": 3 - me}]
    near_at = [me + 1 - 2 * core, me + 2 - 4 * chip, 3 - me]
    peers = [None] + [{"wide": (wide + d) % owners} for d in range(1, owners)]
    side = {"wide": wide + 1 - 2 * parity}
    barrier = pltpu.get_barrier_semaphore()
    for mate in near + peers[1:]:
        pl.semaphore_signal(barrier, inc=1, device_id=mate, device_id_type=MESH)
    pl.semaphore_wait(barrier, len(near) + len(peers) - 1)

    def remote(src, dst, send, recv, mate):
        return pltpu.make_async_remote_copy(
            src_ref=src, dst_ref=dst, send_sem=send, recv_sem=recv, device_id=mate, device_id_type=MESH
        )

    def req_copy(d):
        return remote(req_ref.at[(wide + d) % owners], asked.at[wide], req_send.at[d], req_recv.at[d], peers[d])

    for d in range(1, owners):
        req_copy(d).start()
    mine = pltpu.make_async_copy(req_ref.at[wide], asked.at[wide], keep_sem.at[0])
    mine.start()

    weights = ((up_ref, far_up, their_up), (down_ref, far_down, their_down))

    def far_copy(j, a):
        p = 2 * j + parity
        expert = jnp.where(j == 0, parity, 6 * (1 - chip) + p)
        return remote(weights[a][0].at[expert], weights[a][1].at[p], far_send.at[a, j], far_recv.at[a, p], near[1])

    def side_copy(p, a):
        view = weights[a][1].at[p]
        return remote(view, view, side_send.at[a, p // 2], far_recv.at[a, p], side)

    def own_copy(i, a):
        expert = jnp.where(i < 2, i, 6 * chip + jnp.where(i < 4, i + 4 * (1 - core), i))
        return remote(weights[a][0].at[expert], weights[a][2].at[0, i], own_send.at[a, i], own_recv.at[a, i], near[0])

    def their_copy(p, a):
        i = jnp.where(p < 6, p, p - 4)
        return remote(weights[a][1].at[p], weights[a][2].at[1, i], their_send.at[a, i], their_recv.at[a, i], near[0])

    def wanted(p):
        ends = jnp.logical_or(jnp.logical_and(p < 4, core == 1), jnp.logical_and(p >= 6, core == 0))
        return jnp.logical_or(jnp.logical_or(p < 2, jnp.logical_and(p >= 4, p < 6)), ends)

    def for_all(n, f):
        def body(i, _):
            for a in range(2):
                f(i, a)
            return 0

        lax.fori_loop(0, n, body, 0)


    for_all(4, lambda j, a: far_copy(j, a).start())

    def stat_core():
        return remote(both.at[pl.ds(0, 8)], both.at[pl.ds(8, 8)], stat_send.at[0], stat_recv.at[0], near[0])

    def stat_copy(d):
        return remote(both, every_ref.at[wide], stat_send.at[d], stat_recv.at[d], peers[d])

    both[0:8, :] = jnp.zeros((8, DENSE), F32)
    own_stats(feats_ref, mask_ref, both, core)
    stat_core().start()

    def proj_copy(i):
        return remote(proj_ref, proj_out.at[me], proj_send.at[i], proj_recv.at[i], near[i])

    keep_proj = pltpu.make_async_copy(proj_ref, proj_out.at[me], keep_sem.at[1])
    keep_proj.start()
    for i in range(3):
        proj_copy(i).start()
    for_all(6, lambda i, a: own_copy(i, a).start())
    stat_core().wait_recv()
    for d in range(1, owners):
        stat_copy(d).start()
    keep_stat = pltpu.make_async_copy(both, every_ref.at[wide], keep_sem.at[2])
    keep_stat.start()

    def far_step(j):
        p = 2 * j + parity
        for a in range(2):
            far_copy(j, a).wait_recv()
            side_copy(p, a).start()
        pass_on(p)

    def pass_on(p):
        @pl.when(wanted(p))
        def _():
            for a in range(2):
                their_copy(p, a).start()

    def side_step(j):
        p = 2 * j + 1 - parity
        for a in range(2):
            side_copy(p, a).wait_recv()
        pass_on(p)

    hi_n = 512
    lo_n = table_ref.shape[1] // hi_n

    def find(f, owner_idx):
        idx = asked[owner_idx, pl.ds(f, 1), :]
        hi = jnp.where(idx >= 0, idx & (hi_n - 1), -1)
        lo = lax.shift_right_logical(jnp.maximum(idx, 0), hi_n.bit_length() - 1)
        hot = (lax.broadcasted_iota(jnp.int32, (hi_n, cap), 0) == hi).astype(BF)
        cols = pl.ds(pl.multiple_of(f * EMB, EMB), EMB)
        part = jnp.concatenate([table_ref[cols, l * hi_n : (l + 1) * hi_n] for l in range(lo_n)], axis=0)
        res = jnp.dot(part, hot, preferred_element_type=F32)
        acc = res[0:EMB]
        for step in range(1, lo_n):
            acc = jnp.where(lo == step, res[step * EMB : (step + 1) * EMB], acc)
        return cols, acc.astype(BF)

    def group_rows(g):
        return pl.ds(pl.multiple_of(g * share * EMB, share * EMB), share * EMB)

    def row_copy(g, d, mate):
        rows = group_rows(g)
        return remote(
            found.at[(wide + d) % owners, rows], received.at[wide, rows], row_send.at[g, d], row_recv.at[g, d], mate
        )

    def look(g):
        def one(d, _):
            sender = (wide + d) % owners

            @pl.when(jnp.logical_and(g == 0, d > 0))
            def _():
                remote(req_ref.at[0], asked.at[sender], req_send.at[d], req_recv.at[owners - d], peers[1]).wait_recv()

            for k in range(share):
                cols, block = find(g * share + k, sender)

                @pl.when(d == 0)
                def _():
                    received[wide, cols, :] = block

                @pl.when(d > 0)
                def _():
                    found[sender, cols, :] = block

            @pl.when(d > 0)
            def _():
                row_copy(g, d, {"wide": sender}).start()

            return 0

        lax.fori_loop(0, owners, one, 0)

    hi_e = 256
    outer = owners * cap // hi_e

    def near_copy(g, i):
        rows = group_rows(g)
        return remote(
            ordered.at[near_at[i], rows], emb_ref.at[me, rows], near_send.at[g, i], near_recv.at[g, i], near[i]
        )

    def keep_copy(g):
        rows = group_rows(g)
        return pltpu.make_async_copy(ordered.at[me, rows], emb_ref.at[me, rows], keep_sem.at[3 + g])

    def order(g):
        def arrive(d, _):
            row_copy(g, d, {"wide": (wide + d) % owners}).wait_recv()
            return 0

        lax.fori_loop(1, owners, arrive, 0)
        tables = []
        for k in range(share):
            cols = pl.ds(pl.multiple_of((g * share + k) * EMB, EMB), EMB)
            parts = [
                received[o, cols, j * hi_e : (j + 1) * hi_e] for o in range(owners) for j in range(cap // hi_e)
            ]
            tables.append((cols, jnp.concatenate(parts, axis=0)))

        def quarter(q):
            for k, (cols, table) in enumerate(tables):
                idx = quarter_slots(slot_ref, q, g * share + k)
                hi = idx & (hi_e - 1)
                lo = lax.shift_right_logical(idx, hi_e.bit_length() - 1)
                hot = (lax.broadcasted_iota(jnp.int32, (hi_e, idx.shape[1]), 0) == hi).astype(BF)
                res = jnp.dot(table, hot, preferred_element_type=F32)
                acc = res[0:EMB]
                for step in range(1, outer):
                    acc = jnp.where(lo == step, res[step * EMB : (step + 1) * EMB], acc)
                ordered[q, cols, :] = acc.astype(BF)

        for i in (2, 1, 0):
            quarter(near_at[i])
            near_copy(g, i).start()
        quarter(me)
        keep_copy(g).start()

    mine.wait()

    def tick(t, _):
        @pl.when(t < groups)
        def _():
            look(t)

        @pl.when(jnp.logical_and(t >= 1, t < 5))
        def _():
            far_step(t - 1)

        @pl.when(t >= 2)
        def _():
            order(t - 2)

        @pl.when(t >= 3)
        def _():
            side_step(t - 3)

        return 0

    lax.fori_loop(0, groups + 2, tick, 0)

    for d in range(1, owners):
        req_copy(d).wait_send()
        stat_copy(d).wait()
    stat_core().wait_send()
    keep_stat.wait()
    keep_proj.wait()
    for i in range(3):
        proj_copy(i).wait()

    def rows_left(g, _):
        def one(d, _):
            row_copy(g, d, {"wide": (wide + d) % owners}).wait_send()
            return 0

        lax.fori_loop(1, owners, one, 0)
        for i in range(3):
            near_copy(g, i).wait()
        keep_copy(g).wait()
        return 0

    lax.fori_loop(0, groups, rows_left, 0)

    def weights_left(j, a):
        far_copy(j, a).wait_send()
        side_copy(2 * j + parity, a).wait_send()

    for_all(4, weights_left)
    for_all(6, lambda i, a: own_copy(i, a).wait())

    def passed(p, a):
        @pl.when(wanted(p))
        def _():
            their_copy(p, a).wait_send()

    for_all(8, passed)
    for_all(6, lambda i, a: their_copy(i, a).wait_recv())


def front(req, table, slots, feats, mask, up, down, proj, groups=5):
    owners, fields, cap = req.shape
    cols = fields * EMB
    quarters = 4
    rows = slots.shape[1] // quarters
    any_space, vmem = pl.BlockSpec(memory_space=pl.ANY), pl.BlockSpec(memory_space=pltpu.VMEM)
    dma = pltpu.SemaphoreType.DMA
    return pl.pallas_call(
        functools.partial(front_kernel, groups),
        in_specs=[vmem] * 5 + [any_space] * 3,
        out_specs=[any_space] * 7,
        out_shape=[
            jax.ShapeDtypeStruct((quarters, cols, rows), BF),
            jax.ShapeDtypeStruct((8,) + up.shape[1:], BF),
            jax.ShapeDtypeStruct((8,) + down.shape[1:], BF),
            jax.ShapeDtypeStruct((2, 6) + up.shape[1:], BF),
            jax.ShapeDtypeStruct((2, 6) + down.shape[1:], BF),
            jax.ShapeDtypeStruct((quarters,) + proj.shape, BF),
            jax.ShapeDtypeStruct((owners, 16, DENSE), F32),
        ],
        scratch_shapes=[
            pltpu.VMEM((owners, fields, cap), jnp.int32),
            pltpu.VMEM((owners, cols, cap), BF),
            pltpu.VMEM((owners, cols, cap), BF),
            pltpu.VMEM((quarters, cols, rows), BF),
            pltpu.VMEM((16, DENSE), F32),
            dma((owners,)),
            dma((owners,)),
            dma((groups, owners)),
            dma((groups, owners)),
            dma((groups, 3)),
            dma((groups, 3)),
            dma((3 + groups,)),
            dma((2, 4)),
            dma((2, 8)),
            dma((2, 4)),
            dma((2, 6)),
            dma((2, 6)),
            dma((2, 6)),
            dma((2, 6)),
            dma((3,)),
            dma((3,)),
            dma((owners,)),
            dma((owners,)),
        ],
        compiler_params=pltpu.CompilerParams(collective_id=1, has_side_effects=True, vmem_limit_bytes=VMEM),
        cost_estimate=pl.CostEstimate(flops=45 * 10**9, bytes_accessed=40 * 2**20, transcendentals=0),
        name="front",
    )(req, table, slots, feats, mask, up, down, proj)


def reduce_kernel(bits, with_rows, own_ref, extra_ref, *refs):
    if with_rows:
        slot_ref, grad_ref, out_ref, rep_ref, back_ref = refs[:5]
        grads, placed, near_send, near_recv, far_send, far_recv, keep_sem = refs[-7:]
        refs = refs[5:-7]
    else:
        out_ref, rep_ref = refs[:2]
        refs = refs[2:]
    acc, stage_buf, halves, got, local_sem, send, recv, rep_send, rep_recv, out_sem = refs
    wide=lax.axis_index("wide"); me=lax.axis_index("narrow")
    chip=me//2; core=me%2
    block=ROWS_U>>bits
    mates=[{"narrow": me+1-2*core},{"narrow": me+2-4*chip}]
    pairs=[{"wide": wide+(1<<k)*(1-2*((wide//(1<<k))%2))} for k in range(bits)]
    far={"narrow": 3-me}
    barrier=pltpu.get_barrier_semaphore()
    owners=1<<bits
    others=[{"wide": (wide+d)%owners} for d in range(1,owners)] if with_rows else pairs
    for mate in mates+[far]+others:
        pl.semaphore_signal(barrier, inc=1, device_id=mate, device_id_type=MESH)
    pl.semaphore_wait(barrier, len(others)+3)
    def power(k):
        return 1 << k, 1 << ((k + 1) % bits)

    def bit(u, k):
        here, there = power(k)
        return jnp.where(u == TURNED, (wide // there) % 2, (wide // here) % 2)

    def pair(u, k):
        here, there = power(k)
        step = jnp.where(u == TURNED, there, here)
        return {"wide": wide + step * (1 - 2 * bit(u, k))}

    def start_of(u, k):
        at = 0
        for j in range(k):
            at = at + bit(u, j) * (ROWS_U >> (j + 1))
        return pl.multiple_of(at, 16) if k else 0

    def copy(src, dst, s, u, mate):
        return pltpu.make_async_remote_copy(
            src_ref=src, dst_ref=dst, send_sem=send.at[s, u], recv_sem=recv.at[s, u], device_id=mate, device_id_type=MESH
        )

    def mine(u):
        return jnp.logical_or(u >= 4, jnp.where(u < 2, core == 0, core == 1))

    def theirs(u):
        return jnp.logical_or(u >= 4, jnp.where(u < 2, core == 1, core == 0))

    def domain_unit(u):
        return u < 6

    def local_at(u):
        return jnp.where(u < 2, u + 2, jnp.where(u < 6, u, u - 7))

    def core_copy(u, src):
        return copy(src, acc.at[u], 0, u, mates[0])

    def near_copy(u, src):
        return pltpu.make_async_copy(src, stage_buf.at[u % 2], local_sem.at[u % 2])

    def begin(u):
        @pl.when(u == 6)
        def _():
            core_copy(u, extra_ref.at[pl.ds(2, 2)]).start()
            near_copy(u, extra_ref.at[pl.ds(0, 2)]).start()

        @pl.when(jnp.logical_and(u != 6, mine(u)))
        def _():
            core_copy(u, own_ref.at[local_at(u), pl.ds(2, 2)]).start()
            near_copy(u, own_ref.at[local_at(u), pl.ds(0, 2)]).start()

    def add_region(u, sl, at, rows, src):
        tile = min(rows, 64)

        def body(i, _):
            r = pl.multiple_of(at + i * tile, 16)
            q = pl.multiple_of(i * tile, 16)
            for h in range(sl):
                a = acc[u, h, pl.ds(r, tile), :].astype(F32) + src[h, pl.ds(q, tile), :].astype(F32)
                acc[u, h, pl.ds(r, tile), :] = a.astype(BF)
            return 0

        lax.fori_loop(0, rows // tile, body, 0)

    half_at = [0]
    for k in range(bits):
        half_at.append(half_at[-1] + (ROWS_U >> (k + 1)))

    def half_view(u, k, parts):
        return halves.at[u, pl.ds(0, parts), pl.ds(half_at[k], ROWS_U >> (k + 1)), :]

    def send_half(u, k, parts):
        size = ROWS_U >> (k + 1)
        at = pl.multiple_of(start_of(u, k) + (1 - bit(u, k)) * size, 16)
        return copy(acc.at[u, pl.ds(0, parts), pl.ds(at, size), :], half_view(u, k, parts), 1 + k, u, pair(u, k))

    def take_half(u, k, parts):
        size = ROWS_U >> k
        copy(acc.at[u, pl.ds(0, parts), pl.ds(0, size), :], half_view(u, k - 1, parts), k, u, pair(u, k - 1)).wait_recv()
        add_region(u, parts, start_of(u, k), size, halves.at[u, :, pl.ds(half_at[k - 1], size), :])

    def y_whole(u):
        return copy(acc.at[u, 1], got.at[u, 1], bits + 1, u, mates[1])

    def y_block(u):
        at = start_of(u, bits)
        return copy(
            acc.at[u, 1, pl.ds(at, block), :], got.at[u, 1, pl.ds(at, block), :], bits + 1, u, mates[1]
        )

    def combine(u):
        @pl.when(theirs(u))
        def _():
            core_copy(u, acc.at[u]).wait_recv()

        @pl.when(mine(u))
        def _():
            near_copy(u, acc.at[u]).wait()
            sb = stage_buf.at[u % 2]

            @pl.when(theirs(u))
            def _():
                add_region(u, 2, 0, ROWS_U, sb)

            @pl.when(jnp.logical_not(theirs(u)))
            def _():
                def body(i, _):
                    r = pl.multiple_of(i * 64, 16)
                    for h in (0, 1):
                        acc[u, h, pl.ds(r, 64), :] = sb[h, pl.ds(r, 64), :]
                    return 0

                lax.fori_loop(0, ROWS_U // 64, body, 0)

    def grow_copy(u, j, parts):
        size = ROWS_U >> (j + 1)
        view = got.at[u, pl.ds(0, parts), pl.ds(start_of(u, j + 1), size), :]
        return copy(view, view, bits + 2 + (bits - 1 - j), u, pair(u, j))

    def out_copy(u, parts):
        return pltpu.make_async_copy(got.at[u, pl.ds(0, parts)], out_ref.at[u, pl.ds(0, parts)], out_sem.at[u])

    rep_mates = [mates[0], mates[1], far]
    rep_rows = rep_ref.shape[1]

    def rep_copy(i):
        return pltpu.make_async_remote_copy(
            src_ref=got.at[6, 0, pl.ds(0, rep_rows), :], dst_ref=rep_ref.at[i], send_sem=rep_send.at[i],
            recv_sem=rep_recv.at[i], device_id=rep_mates[i], device_id_type=MESH,
        )

    def by_kind(u, domain, shared):
        pl.when(domain_unit(u))(domain)
        pl.when(jnp.logical_not(domain_unit(u)))(shared)

    def start_grow(u):
        by_kind(u, lambda: grow_copy(u, bits - 1, 2).start(), lambda: grow_copy(u, bits - 1, 1).start())

    def stage_one(u):
        combine(u)
        by_kind(u, lambda: send_half(u, 0, 2).start(), lambda: y_whole(u).start())

    def halving(k, u):
        def domain():
            take_half(u, k, 2)
            if k < bits:
                send_half(u, k, 2).start()
            else:
                y_block(u).start()

        def shared():
            if k == 1:
                y_whole(u).wait_recv()
                add_region(u, 1, 0, ROWS_U, got.at[u, pl.ds(1, 1)])
            else:
                take_half(u, k - 1, 1)
            send_half(u, k - 1, 1).start()

        by_kind(u, domain, shared)

    def cross(u):
        at = start_of(u, bits)

        def domain():
            y_block(u).wait_recv()

        def shared():
            take_half(u, bits, 1)

        by_kind(u, domain, shared)
        got[u, 0, pl.ds(at, block), :] = acc[u, 0, pl.ds(at, block), :]
        start_grow(u)

    def grow(u, j):
        by_kind(u, lambda: grow_copy(u, j, 2).wait_recv(), lambda: grow_copy(u, j, 1).wait_recv())
        if j > 0:
            by_kind(u, lambda: grow_copy(u, j - 1, 2).start(), lambda: grow_copy(u, j - 1, 1).start())
        else:
            by_kind(u, lambda: out_copy(u, 2).start(), lambda: out_copy(u, 1).start())

            @pl.when(u == 6)
            def _():
                for i in range(3):
                    rep_copy(i).start()

    quarters=mates+[far]
    def quarter_at(i):
        return [me+1-2*core, me+2-4*chip, 3-me][i]
    def near_row_copy(i):
        return pltpu.make_async_remote_copy(src_ref=grad_ref.at[quarter_at(i)],dst_ref=grads.at[me],send_sem=near_send.at[i],recv_sem=near_recv.at[i],device_id=quarters[i],device_id_type=MESH)
    def keep_copy():
        return pltpu.make_async_copy(grad_ref.at[me],grads.at[me],keep_sem.at[0])
    def back_copy(d):
        return pltpu.make_async_remote_copy(src_ref=placed.at[(wide+d)%owners],dst_ref=back_ref.at[wide],send_sem=far_send.at[d],recv_sem=far_recv.at[d],device_id=others[d-1],device_id_type=MESH)
    def keep_back():
        return pltpu.make_async_copy(placed.at[wide],back_ref.at[wide],keep_sem.at[1])
    def place_field(f, _):
        place_one(slot_ref, grads, placed, f)
        return 0
    def row_step(t):
        fields=slot_ref.shape[0]
        @pl.when(t==ROW_AT)
        def _():
            keep_copy().wait()
            for i in range(3): near_row_copy(i).wait_recv()
        @pl.when(jnp.logical_and(t>=ROW_AT,t<ROW_AT+5))
        def _():
            lax.fori_loop((t-ROW_AT)*(fields//5),(t-ROW_AT+1)*(fields//5),place_field,0)
        for d in range(owners):
            @pl.when(t==ROW_AT+4+int(d*ROW_STEP))
            def _():
                if d==0: keep_back().start()
                else: back_copy(d).start()
    todo = [begin, stage_one]
    todo += [functools.partial(halving, k) for k in range(1, bits + 1)] + [cross]
    todo += [functools.partial(lambda j, u: grow(u, j), j) for j in reversed(range(bits))]
    plain_gaps = [0, 1, 2] + [1] * (len(todo) - 4) + [2]
    turned_gaps = [0, 1, 3, 4] + [1] * (len(todo) - 6) + [3, 3]
    plain_lag = [sum(plain_gaps[: i + 1]) for i in range(len(todo))]
    turned_lag = [sum(turned_gaps[: i + 1]) for i in range(len(todo))]

    def tick(t,_):
        for s in reversed(range(len(todo))):
            def stage(c, _):
                plain = t - plain_lag[s]
                u = jnp.where(c == 0, plain, TURNED)
                fits = jnp.logical_and(jnp.logical_and(plain >= 0, plain < UNITS), plain != TURNED)
                due = jnp.where(c == 0, fits, t == TURNED + turned_lag[s])

                @pl.when(due)
                def _():
                    todo[s](u)

                return 0

            lax.fori_loop(0, 2, stage, 0)
        if with_rows:
            row_step(t)
        return 0
    if with_rows:
        keep_copy().start()
        for i in range(3): near_row_copy(i).start()
    lax.fori_loop(0, max(UNITS + plain_lag[-1], TURNED + turned_lag[-1] + 1), tick, 0)
    if with_rows:
        keep_back().wait()
        for i in range(3): near_row_copy(i).wait_send()
        for d in range(1,owners): back_copy(d).wait()
    def finish(u,_):
        @pl.when(mine(u))
        def _():
            core_copy(u, acc.at[u]).wait_send()

        def left(parts):
            for k in range(bits):
                send_half(u, k, parts).wait_send()
            (y_block if parts == 2 else y_whole)(u).wait_send()
            for j in range(bits):
                grow_copy(u, j, parts).wait_send()
            out_copy(u, parts).wait()

        by_kind(u, lambda: left(2), lambda: left(1))
        return 0
    lax.fori_loop(0,UNITS,finish,0)
    for i in range(3):
        rep_copy(i).wait()

def reduce_all(own, extra, wide, rep_rows, rows=None):
    bits = wide.bit_length() - 1
    args = [own, extra]
    any_space = pl.BlockSpec(memory_space=pl.ANY)
    in_specs = [any_space] * 2
    out_shape = [
        jax.ShapeDtypeStruct((UNITS, 2, ROWS_U, LANES), BF),
        jax.ShapeDtypeStruct((3, rep_rows, LANES), BF),
    ]
    scratch = [
        pltpu.VMEM((UNITS, 2, ROWS_U, LANES), BF),
        pltpu.VMEM((2, 2, ROWS_U, LANES), BF),
        pltpu.VMEM((UNITS, 2, ROWS_U, LANES), BF),
        pltpu.VMEM((UNITS, 2, ROWS_U, LANES), BF),
        pltpu.SemaphoreType.DMA((2,)),
        pltpu.SemaphoreType.DMA((2 * bits + 2, UNITS)),
        pltpu.SemaphoreType.DMA((2 * bits + 2, UNITS)),
        pltpu.SemaphoreType.DMA((3,)),
        pltpu.SemaphoreType.DMA((3,)),
        pltpu.SemaphoreType.DMA((UNITS,)),
    ]
    if rows is not None:
        slots, grads, cap = rows
        args += [slots, grads]
        in_specs += [pl.BlockSpec(memory_space=pltpu.VMEM), any_space]
        back = (wide, grads.shape[1], cap)
        out_shape.append(jax.ShapeDtypeStruct(back, BF))
        scratch += [
            pltpu.VMEM(grads.shape, BF),
            pltpu.VMEM(back, BF),
            pltpu.SemaphoreType.DMA((3,)),
            pltpu.SemaphoreType.DMA((3,)),
            pltpu.SemaphoreType.DMA((wide,)),
            pltpu.SemaphoreType.DMA((wide,)),
            pltpu.SemaphoreType.DMA((2,)),
        ]
    return pl.pallas_call(
        functools.partial(reduce_kernel, bits, rows is not None),
        in_specs=in_specs,
        out_specs=[any_space] * len(out_shape),
        out_shape=out_shape,
        scratch_shapes=scratch,
        compiler_params=pltpu.CompilerParams(collective_id=0, has_side_effects=True, vmem_limit_bytes=VMEM),
        cost_estimate=pl.CostEstimate(flops=0, bytes_accessed=60 * 2**20, transcendentals=0),
        name="reduce_all",
    )(*args)


C0 = 0.7978845608028654
C1 = 0.044715
REP_ROWS = 512
GATE_AT = 256
GAIN_AT = 352
SHIFT_AT = 384
MISC_AT = 416


def gelu_both(x):
    square = x * x
    up = 0.5 * jnp.tanh(x * (square * (C0 * C1) + C0)) + 0.5
    act = x * up
    return act, up + (act - act * up) * (square * (6.0 * C0 * C1) + 2.0 * C0)


def soft_pair(a, b):
    top = jnp.maximum(a, b)
    ea, eb = jnp.exp(a - top), jnp.exp(b - top)
    total = ea + eb
    return ea / total, eb / total


def soft_pair_back(pa, pb, ga, gb):
    mean = pa * ga + pb * gb
    return pa * (ga - mean), pb * (gb - mean)


def fold(x):
    return sum(x[:, i * 128 : (i + 1) * 128] for i in range(x.shape[1] // 128))


def wide_lanes(x, n):
    return jnp.concatenate([x] * n, axis=1)


def split_low(x):
    high = x.astype(BF)
    return high, (x - high.astype(F32)).astype(BF)


def iota(shape, axis):
    return lax.broadcasted_iota(jnp.int32, shape, axis)


def row_of(rows, at):
    return (iota((rows, 128), 0) == at).astype(BF)


def dense_kernel(
    ids_ref, emb_ref, feats_ref, every_ref, mask_ref, label_ref, projw_ref, featw_ref, bias_ref,
    up_a, up_b, up_c, down_a, down_b, down_c, gain_ref, shift_ref, gate_f, gate_h, tin_f, tin_h,
    tower_ref,
    logit_ref, own_ref, emb_grad_ref, extra_ref,
    xt, act, slope, outs, og, ing, hid, hg, stat, inner, emb, feat, featw, gains, mixed, shifts, gates, tin,
    tbias, tout, tob, gain_acc, shift_acc, gate_acc, tin_acc, tbias_acc, tout_acc, tob_acc, emb_sem, extra_sem,
):
    ups = [up_a.at[0], up_b.at[0], up_c.at[0, 0], up_c.at[1, 0]]
    downs = [down_a.at[0], down_b.at[0], down_c.at[0, 0], down_c.at[1, 0]]
    step = pl.program_id(0)
    chunk, slot = step // 4, step % 4
    rows = xt.shape[1]
    core = ids_ref[14]
    owners = every_ref.shape[0]

    def expert_of(dom, k):
        return k if k < 2 else ids_ref[2 * dom + k]

    def raw_lanes(c):
        return pl.ds(pl.multiple_of(((c + core) % 3) * HALF, HALF), HALF)

    def pooled(sets):
        def sums(w, carry):
            total, mean = carry
            for at in sets:
                count = every_ref[w, at + 2 : at + 3, :]
                total, mean = total + count, mean + count * every_ref[w, at : at + 1, :]
            return total, mean

        zero = jnp.zeros((1, 128), F32)
        total, mean = lax.fori_loop(0, owners, sums, (zero, zero))
        mean = mean / total

        def squares(w, acc):
            for at in sets:
                off = every_ref[w, at : at + 1, :] - mean
                acc = acc + every_ref[w, at + 1 : at + 2, :] + every_ref[w, at + 2 : at + 3, :] * off * off
            return acc

        return mean, lax.rsqrt(lax.fori_loop(0, owners, squares, zero) / total + 1e-05)

    @pl.when(step == 0)
    def _():
        fetch = pltpu.make_async_copy(emb_ref, emb, emb_sem)
        fetch.start()
        for e in range(6):
            gains[e] = dot(gain_ref[...], row_of(14, ids_ref[e]), 0, 0).astype(BF)
        for dom, (gate, tower) in enumerate(((gate_f, tin_f), (gate_h, tin_h))):
            tin[dom] = tower[0]
            pick = (iota((16, 6), 0) % 8 == iota((16, 6), 1)).astype(BF)
            gates[dom] = dot(pick, gate[0], 1, 0).astype(BF)
            place = iota((16, 14), 0)
            ident = place % 4
            for k in range(4):
                ident = jnp.where(place % 4 == k, expert_of(dom, k), ident)
            same = ident == iota((16, 14), 1)
            first, second = jnp.logical_and(same, place < 4), jnp.logical_and(same, place < 8)
            third = jnp.logical_and(second, place >= 4)
            mixed[dom] = (
                dot(first.astype(BF), gain_ref[...], 1, 0) + dot(third.astype(BF), shift_ref[...], 1, 0)
            ).astype(BF)
            shifts[dom] = dot(second.astype(BF), shift_ref[...], 1, 0).astype(BF)
            d = ids_ref[12 + dom]
            tbias[dom] = dot(tower_ref[...], row_of(16, d), 0, 0)
            tout[dom] = dot(tower_ref[...], row_of(16, 6 + d), 0, 0)
            tob[dom] = dot(tower_ref[...], row_of(128, d), 1, 0)
        featw[0:128, :] = featw_ref[...]
        featw[128:144, :] = jnp.where(iota((16, D), 0) == 0, bias_ref[...].astype(F32), 0.0).astype(BF)
        feat[128:144, :] = (iota((16, rows), 0) == 0).astype(BF)
        moments = [pooled((0,)), pooled((3, 11))]
        for c in range(rows // HALF):
            mean, scale = moments[c // 2]
            x = (feats_ref[raw_lanes(c), :] - mean) * scale
            feat[0:128, c * HALF : (c + 1) * HALF] = x.T.astype(BF)
        for ref in (gain_acc, shift_acc, gate_acc, tin_acc, tbias_acc, tout_acc, tob_acc):
            ref[...] = jnp.zeros_like(ref)
        fetch.wait()
        for c in range(rows // HALF):
            cols = slice(c * HALF, (c + 1) * HALF)
            x = dot(projw_ref[...], emb[:, cols], 0, 0) + dot(featw[...], feat[:, cols], 0, 0)
            xt[:, cols] = x.astype(BF)

    @pl.when(step < 12)
    def _():
        lanes = pl.ds(pl.multiple_of(chunk * HALF, HALF), HALF)

        def piece(s):
            pre = dot(ups[s][...], xt[:, lanes], 0, 0)
            a, g = gelu_both(pre)
            a = a.astype(BF)
            act[slot, s, :, lanes] = a
            slope[slot, s, :, lanes] = g.astype(BF)
            return dot(downs[s][...], a, 0, 0)

        outs[slot] = piece(0)
        for s in range(1, 4):
            outs[slot] += piece(s)

    def middle():
        lanes = pl.ds(pl.multiple_of(chunk * HALF, HALF), HALF)
        dom = chunk // 2
        x = xt[:, lanes]
        logit_gates = dot(gates[dom], x, 1, 0)
        s0, s1 = soft_pair(logit_gates[0:1], logit_gates[1:2])
        d0, d1 = soft_pair(logit_gates[2:3], logit_gates[3:4])
        t0, t1 = soft_pair(logit_gates[4:5], logit_gates[5:6])
        coef = jnp.concatenate([t0 * s0, t0 * s1, t1 * d0, t1 * d1], axis=0)
        high = coef.astype(BF).astype(F32)
        spare = jnp.zeros((8, HALF), F32)
        coef_low = jnp.concatenate([high, coef - high, spare], axis=0).astype(BF)
        hg[...] = dot(shifts[dom], coef_low, 0, 0)
        stat[8:12, :] = coef
        expert = [0, 1, 2 + 2 * dom, 3 + 2 * dom]

        def normalize(t, _):
            cols = pl.ds(pl.multiple_of(t * 128, 128), 128)
            for k in range(4):
                v = outs[k, :, cols]
                mean = jnp.sum(v, axis=0, keepdims=True) * (1.0 / D)
                v = v - mean
                var = jnp.sum(v * v, axis=0, keepdims=True) * (1.0 / D)
                stat[k : k + 1, cols] = mean
                stat[4 + k : 5 + k, cols] = lax.rsqrt(var + 1e-05)
            scale = [stat[4 + k : 5 + k, cols] * stat[8 + k : 9 + k, cols] for k in range(4)]
            for r in range(4):
                band = slice(r * 128, (r + 1) * 128)
                acc = hg[band, cols]
                for k in range(4):
                    n = (outs[k, band, cols] - stat[k : k + 1, cols]) * scale[k]
                    acc = acc + n * gains[expert[k], band, :].astype(F32)
                hid[band, cols] = acc.astype(BF)
            return 0

        lax.fori_loop(0, 4, normalize, 0)
        h = hid[...]
        pre = dot(tin[dom], h, 0, 0) + wide_lanes(tbias[dom], 4)
        tact, tslope = gelu_both(pre)
        weight = wide_lanes(tout[dom], 4)
        logit = jnp.sum(tact * weight, axis=0, keepdims=True) + wide_lanes(tob[dom, 12:13, :], 4)
        logit_ref[:, raw_lanes(chunk)] = logit
        live, label = mask_ref[:, raw_lanes(chunk)].astype(F32), label_ref[:, raw_lanes(chunk)].astype(F32)
        grad = (jax.nn.sigmoid(logit) - label) * live
        tob_acc[dom, 0:1, :] += fold(grad)
        tout_acc[dom] += fold(grad * tact)
        low = (grad * weight * tslope).astype(BF)
        tbias_acc[dom] += fold(low.astype(F32))
        tin_acc[dom] += dot(h, low, 1, 1)
        back = dot(tin[dom], low, 1, 0)
        hg[...] = back
        back_high, back_low = split_low(back)
        shift_acc[dom] += dot(back_high, coef_low, 1, 1) + dot(back_low, coef_low, 1, 1)
        inner[...] = dot(mixed[dom], back_high, 1, 0) + dot(mixed[dom], back_low, 1, 0)

        def denormalize(t, _):
            cols = pl.ds(pl.multiple_of(t * 128, 128), 128)
            place = pl.ds(pl.multiple_of(chunk * HALF + t * 128, 128), 128)
            for k in range(4):
                mean, rstd = stat[k : k + 1, cols], stat[4 + k : 5 + k, cols]
                c = stat[8 + k : 9 + k, cols]
                m2 = 0.0
                for r in range(4):
                    band = slice(r * 128, (r + 1) * 128)
                    w = (outs[k, band, cols] - mean) * rstd * hg[band, cols]
                    m2 = m2 + jnp.sum(w * gains[expert[k], band, :].astype(F32), axis=0, keepdims=True)
                    gain_acc[expert[k], band, :] += w * c
                m1 = inner[k : k + 1, cols]
                inner[4 + k : 5 + k, cols] += m2
                cr = c * rstd
                slant = cr * rstd * m2 * (1.0 / D)
                level = mean * slant - cr * m1 * (1.0 / D)
                for r in range(4):
                    band = slice(r * 128, (r + 1) * 128)
                    scaled = hg[band, cols] * gains[expert[k], band, :].astype(F32)
                    og[k, band, place] = (scaled * cr - outs[k, band, cols] * slant + level).astype(BF)
            return 0

        lax.fori_loop(0, 4, denormalize, 0)
        a = [inner[4 + k : 5 + k, :] for k in range(4)]
        g0, g1 = soft_pair_back(s0, s1, t0 * a[0], t0 * a[1])
        g2, g3 = soft_pair_back(d0, d1, t1 * a[2], t1 * a[3])
        g4, g5 = soft_pair_back(t0, t1, s0 * a[0] + s1 * a[1], d0 * a[2] + d1 * a[3])
        zero = jnp.zeros_like(g0)
        g = jnp.concatenate([g0, g1, g2, g3, g4, g5, zero, zero], axis=0)
        high = g.astype(BF).astype(F32)
        g = jnp.concatenate([high, g - high], axis=0).astype(BF)
        gate_acc[dom] += dot(g, x, 1, 1)
        ing[:, lanes] = dot(gates[dom], g, 0, 0)

    @pl.when(jnp.logical_and(step < 12, slot == 3))
    def _():
        middle()

    def back(k, at, n):
        lanes = slice(at, at + n)
        for s in range(4):
            p = dot(downs[s][...], og[k, :, lanes], 1, 0) * slope[k, s, :, lanes].astype(F32)
            slope[k, s, :, lanes] = p.astype(BF)

        def piece(s, _):
            grad, p = og[k, :, lanes], slope[k, s, :, lanes]
            own_ref[0, s, 0:D, :] = dot(xt[:, lanes], p, 1, 1).astype(BF)
            d = dot(act[k, s, :, lanes], grad, 1, 1).astype(BF)
            own_ref[0, s, D : D + 256, :] = d[:, 0:256]
            own_ref[0, s, D + 256 : D + 512, :] = d[:, 256:512]
            return 0

        lax.fori_loop(0, 4, piece, 0)

        def grow(t, _):
            cols = pl.ds(pl.multiple_of(at + t * HALF, HALF), HALF)
            total = dot(ups[0][...], slope[k, 0, :, cols], 1, 0)
            for s in range(1, 4):
                total += dot(ups[s][...], slope[k, s, :, cols], 1, 0)
            ing[:, cols] += total
            return 0

        lax.fori_loop(0, n // HALF, grow, 0)

    expert = step - 12

    @pl.when(jnp.logical_and(expert >= 0, expert < 2))
    def _():
        back(expert, 0, rows)

    @pl.when(jnp.logical_and(expert >= 2, expert < 4))
    def _():
        back(expert, 0, DSLOT)

    @pl.when(expert >= 4)
    def _():
        back(expert - 2, DSLOT, rows - DSLOT)

    def exact(select, x):
        high, low = split_low(x)
        return dot(select, high, 1, 1) + dot(select, low, 1, 1)

    @pl.when(expert == 5)
    def _():
        low = ing[...].astype(BF)
        proj = dot(emb[...], low, 1, 1).astype(BF)
        feat_grad = dot(feat[...], low, 1, 1)
        for c in range(rows // HALF):
            cols = slice(c * HALF, (c + 1) * HALF)
            emb[:, cols] = dot(projw_ref[...], low[:, cols], 1, 0).astype(BF)
        put = pltpu.make_async_copy(emb, emb_grad_ref, emb_sem)
        put.start()
        unit = act.at[:, :, :, 0:256]
        act[:, :, :, 0:256] = jnp.zeros((4, 4, 256, 256), BF)
        spots = [ids_ref[15 + q] for q in range(4)]
        for q in range(4):
            part = proj[q * 160 : (q + 1) * 160]
            act[spots[q], 2, 0:160, 0:256] = part[:, 0:256]
            act[spots[q], 2, 160:256, 0:256] = part[0:96, 256:512]
            act[spots[q], 3, 0:64, 0:256] = part[96:160, 256:512]
        for dom in range(2):
            d = ids_ref[12 + dom]
            tower = tin_acc[dom].astype(BF)
            act[ids_ref[15 + d // 2], d % 2, :, 0:128] = tower[0:256]
            act[ids_ref[15 + d // 2], d % 2, :, 128:256] = tower[256:512]
            g = gate_acc[dom]
            g = g[0:8] + g[8:16]
            place = pl.ds(pl.multiple_of(d * 16, 16), 16)
            act[spots[3], 1, place, 0:256] = jnp.concatenate([g[:, 0:256], g[:, 256:512]], axis=0).astype(BF)
        act[spots[3], 0, 0:128, 0:256] = feat_grad[0:128, 0:256].astype(BF)
        act[spots[3], 0, 128:256, 0:256] = feat_grad[0:128, 256:512].astype(BF)
        total = 0.0
        for e in range(6):
            total = total + exact(row_of(16, ids_ref[e]), gain_acc[e])
        offset = 0.0
        misc_a = misc_b = 0.0
        line = iota((16, 128), 0)
        lane = iota((16, 128), 1)
        for dom in range(2):
            col = iota((16, 16), 1)
            ident = col % 4
            for k in range(4):
                ident = jnp.where(col % 4 == k, expert_of(dom, k), ident)
            choose = jnp.logical_and(ident == iota((16, 16), 0), col < 8).astype(BF)
            offset = offset + exact(choose, shift_acc[dom])
            d = ids_ref[12 + dom]
            misc_a = misc_a + exact(row_of(16, d), tbias_acc[dom])
            misc_b = misc_b + exact(row_of(16, d), tout_acc[dom])
            bias = jnp.sum(tob_acc[dom, 0:1, :], axis=1, keepdims=True)
            misc_a = misc_a + jnp.where(jnp.logical_and(line == 8, lane == d), bias, 0.0)
        misc = jnp.concatenate([misc_a, misc_b], axis=1)
        line = iota((16, 256), 0)
        misc = misc + jnp.where(line == 6, feat_grad[128:129, 0:256], 0.0)
        misc = misc + jnp.where(line == 7, feat_grad[128:129, 256:512], 0.0)
        for at, x in ((GAIN_AT, total), (SHIFT_AT, offset)):
            act[spots[3], 1, at - 256 : at - 240, 0:256] = x[:, 0:256].astype(BF)
            act[spots[3], 1, at - 240 : at - 224, 0:256] = x[:, 256:512].astype(BF)
        act[spots[3], 1, MISC_AT - 256 : MISC_AT - 240, 0:256] = misc.astype(BF)
        out = pltpu.make_async_copy(unit, extra_ref, extra_sem)
        out.start()
        out.wait()
        put.wait()


def dense(ids, emb, feats, every, mask, label, projw, featw, bias, ups, downs, gains, shifts, gate, tin, tower):
    rows = emb.shape[1]

    def ahead(i):
        c, j = i // 4, i % 4
        front = jnp.where(j < 2, j, jnp.where(c < 2, j, j + 2))
        return jnp.where(i < 12, front, i - 12)

    def whole(x):
        return pl.BlockSpec(x.shape, lambda i, ids: (0,) * len(x.shape), pipeline_mode=pl.Buffered(1))

    any_space = pl.BlockSpec(memory_space=pl.ANY)
    in_specs = [any_space] + [whole(x) for x in (feats, every, mask, label, projw, featw, bias)]
    for group in (ups, downs):
        block = group[0].shape[1:]
        in_specs += [
            pl.BlockSpec((1,) + block, lambda i, ids: (ids[ahead(i)], 0, 0)),
            pl.BlockSpec((1,) + block, lambda i, ids: (ids[6 + ahead(i)], 0, 0)),
            pl.BlockSpec((2, 1) + block, lambda i, ids: (0, ahead(i), 0, 0)),
        ]
    in_specs += [whole(gains), whole(shifts)]
    for x in (gate, tin):
        for dom in range(2):
            in_specs.append(
                pl.BlockSpec(
                    (1,) + x.shape[1:], lambda i, ids, at=12 + dom: (ids[at], 0, 0), pipeline_mode=pl.Buffered(1)
                )
            )
    in_specs.append(whole(tower))
    return pl.pallas_call(
        dense_kernel,
        grid_spec=pltpu.PrefetchScalarGridSpec(
            num_scalar_prefetch=1,
            grid=(18,),
            in_specs=in_specs,
            out_specs=[
                pl.BlockSpec((1, rows), lambda i, ids: (0, 0)),
                pl.BlockSpec((1, 4, 2 * D, 256), lambda i, ids: (jnp.maximum(i - 12, 0), 0, 0, 0)),
                any_space,
                any_space,
            ],
            scratch_shapes=[
                pltpu.VMEM((D, rows), BF),
                pltpu.VMEM((4, 4, 256, rows), BF),
                pltpu.VMEM((4, 4, 256, rows), BF),
                pltpu.VMEM((4, D, HALF), F32),
                pltpu.VMEM((4, D, rows), BF),
                pltpu.VMEM((D, rows), F32),
                pltpu.VMEM((D, HALF), BF),
                pltpu.VMEM((D, HALF), F32),
                pltpu.VMEM((16, HALF), F32),
                pltpu.VMEM((16, HALF), F32),
                pltpu.VMEM(emb.shape, BF),
                pltpu.VMEM((144, rows), BF),
                pltpu.VMEM((144, D), BF),
                pltpu.VMEM((6, D, 128), BF),
                pltpu.VMEM((2, 16, D), BF),
                pltpu.VMEM((2, 16, D), BF),
                pltpu.VMEM((2, 16, D), BF),
                pltpu.VMEM((2, D, 128), BF),
                pltpu.VMEM((2, 128, 128), F32),
                pltpu.VMEM((2, 128, 128), F32),
                pltpu.VMEM((2, 16, 128), F32),
                pltpu.VMEM((6, D, 128), F32),
                pltpu.VMEM((2, D, 16), F32),
                pltpu.VMEM((2, 16, D), F32),
                pltpu.VMEM((2, D, 128), F32),
                pltpu.VMEM((2, 128, 128), F32),
                pltpu.VMEM((2, 128, 128), F32),
                pltpu.VMEM((2, 8, 128), F32),
                pltpu.SemaphoreType.DMA,
                pltpu.SemaphoreType.DMA,
            ],
        ),
        out_shape=[
            jax.ShapeDtypeStruct((1, rows), F32),
            jax.ShapeDtypeStruct((6, 4, 2 * D, 256), BF),
            jax.ShapeDtypeStruct(emb.shape, BF),
            jax.ShapeDtypeStruct((4, 4, 256, 256), BF),
        ],
        compiler_params=pltpu.CompilerParams(vmem_limit_bytes=62 * 2**20),
        cost_estimate=pl.CostEstimate(flops=39 * 10**9, bytes_accessed=60 * 2**20, transcendentals=0),
        name="dense_all",
    )(ids, emb, feats, every, mask, label, projw, featw, bias, *ups, *downs, gains, shifts, gate, gate, tin, tin, tower)


def finish_kernel(with_rows, ids_ref, sums_ref, unit_ref, others_ref, *refs):
    if with_rows:
        back_ref, row_ref = refs[0], refs[1]
        refs = refs[2:]
    (up_ref, down_ref, proj_ref, feat_ref, bias_ref, gain_ref, shift_ref, gate_ref, tin_ref, tbias_ref,
     tout_ref, tob_ref, quarters) = refs
    step = pl.program_id(0)
    up_ref[0] = sums_ref[0, 0, 0:D, :].astype(F32)
    down_ref[0, :, 0:256] = sums_ref[0, 0, D : D + 256, :].astype(F32)
    down_ref[0, :, 256:512] = sums_ref[0, 0, D + 256 : D + 512, :].astype(F32)
    if with_rows:
        @pl.when(step < with_rows)
        def _():
            row_ref[0, 0] = back_ref[0].astype(F32)

    @pl.when(step == 0)
    def _():
        me = ids_ref[14]
        quarters[me] = unit_ref[0, 0, 0:REP_ROWS, :].astype(F32)
        for i in range(3):
            quarters[ids_ref[15 + i]] = others_ref[i].astype(F32)
        cols = proj_ref.shape[0]
        proj_ref[:, 0:256] = unit_ref[0, 0, REP_ROWS : REP_ROWS + cols, :].astype(F32)
        proj_ref[:, 256:512] = unit_ref[0, 0, REP_ROWS + cols : REP_ROWS + 2 * cols, :].astype(F32)
        for d in range(DOMAINS):
            band = slice((d % 2) * 256, (d % 2) * 256 + 256)
            tin_ref[d, 0:256, :] = quarters[d // 2, band, 0:128]
            tin_ref[d, 256:512, :] = quarters[d // 2, band, 128:256]
            g = quarters[3, GATE_AT + 16 * d : GATE_AT + 16 * d + 16, :]
            g = jnp.concatenate([g[0:8], g[8:16]], axis=1)
            gate_ref[d] = g[0:6]
        feat_ref[:, 0:256] = quarters[3, 0:128, :]
        feat_ref[:, 256:512] = quarters[3, 128:256, :]
        for at, ref in ((GAIN_AT, gain_ref), (SHIFT_AT, shift_ref)):
            ref[:, 0:256] = quarters[3, at : at + 14, :]
            ref[:, 256:512] = quarters[3, at + 16 : at + 30, :]
        tbias_ref[...] = quarters[3, MISC_AT : MISC_AT + 6, 0:128]
        tout_ref[...] = quarters[3, MISC_AT : MISC_AT + 6, 128:256]
        bias_ref[:, 0:256] = quarters[3, MISC_AT + 6 : MISC_AT + 7, :]
        bias_ref[:, 256:512] = quarters[3, MISC_AT + 7 : MISC_AT + 8, :]
        tob_ref[...] = quarters[3, MISC_AT + 8 : MISC_AT + 9, 0:128]


def finish(ids, sums, others, proj_cols, back=None):
    def whole(s):
        return pl.BlockSpec(s, lambda i, ids: (0,) * len(s))

    def unit(i, ids):
        return (ids[i] % 16, ids[i] // 16, 0, 0)

    in_specs = [
        pl.BlockSpec((1, 1, ROWS_U, LANES), unit),
        pl.BlockSpec((1, 1, ROWS_U, LANES), lambda i, ids: (6, 0, 0, 0)),
        whole(others.shape),
    ]
    args = [sums, sums, others]
    shapes = [
        (14, D, 256), (14, 256, D), (proj_cols, D), (DENSE, D), (1, D), (14, D), (14, D), (DOMAINS, 6, D),
        (DOMAINS, D, 128), (DOMAINS, 128), (DOMAINS, 128), (1, 128),
    ]
    out_specs = [
        pl.BlockSpec((1, D, 256), lambda i, ids: (i, 0, 0)),
        pl.BlockSpec((1, 256, D), lambda i, ids: (i, 0, 0)),
    ] + [whole(s) for s in shapes[2:]]
    if back is not None:
        blocks, cols, cap = back.shape
        last = lambda i: jnp.minimum(i, blocks - 1)
        args.append(back)
        in_specs.append(pl.BlockSpec((1, cols, cap), lambda i, ids: (last(i), 0, 0)))
        shapes.insert(0, (1, blocks, cols, cap))
        out_specs.insert(0, pl.BlockSpec((1, 1, cols, cap), lambda i, ids: (0, last(i), 0, 0)))
    return pl.pallas_call(
        functools.partial(finish_kernel, 0 if back is None else back.shape[0]),
        grid_spec=pltpu.PrefetchScalarGridSpec(
            num_scalar_prefetch=1,
            grid=(14,),
            in_specs=in_specs,
            out_specs=out_specs,
            scratch_shapes=[pltpu.VMEM((4, REP_ROWS, LANES), F32)],
        ),
        out_shape=[jax.ShapeDtypeStruct(s, F32) for s in shapes],
        compiler_params=pltpu.CompilerParams(vmem_limit_bytes=VMEM),
        cost_estimate=pl.CostEstimate(flops=0, bytes_accessed=32 * 2**20, transcendentals=0),
        name="finish",
    )(ids, *args)


def shards(
    embed_table,
    requests,
    slot_index,
    event_mask,
    labels,
    dense_feats,
    proj_weight,
    dense_weight,
    proj_bias,
    up_weight,
    down_weight,
    norm_gain,
    norm_shift,
    gate_weight,
    tower_in,
    tower_bias,
    tower_out,
    tower_out_bias,
):
    narrow = lax.axis_size("narrow")
    me = lax.axis_index("narrow")
    chip, core = me // 2, me % 2
    ev_rows, fields = slot_index.shape
    rows = ev_rows // narrow
    owners, cap = requests.shape[1], requests.shape[2]
    hid_here = up_weight.shape[2]
    other_chip = [(i, i ^ 2) for i in range(narrow)]
    other_core = [(i, i ^ 1) for i in range(narrow)]
    full = 3 * chip + 2 * core
    half = 3 * chip + 1

    def swap(x, pairs):
        return lax.ppermute(x, "narrow", pairs)

    def chip_experts(w, which):
        return jnp.concatenate(
            [w[:SHARED], lax.dynamic_slice_in_dim(w, SHARED + 6 * which, 6, axis=0)], axis=0
        )

    def bring(w):
        far = swap(chip_experts(w, 1 - chip), other_chip)
        at = lambda x, start, size: lax.dynamic_slice_in_dim(x, start, size, axis=0)
        base = SHARED + 6 * chip
        away = 4 * (1 - core)
        theirs = jnp.stack(
            [
                jnp.concatenate([w[:SHARED], at(w, base + away, 2), at(w, base + 2, 2)], axis=0),
                jnp.concatenate([far[:SHARED], at(far, 2 + away, 2), far[4:6]], axis=0),
            ]
        )
        return w, far, swap(theirs, other_core)

    six = jnp.arange(6, dtype=jnp.int32)
    spot = jnp.where(six < 2, six, jnp.where(six < 4, six + 4 * core, six))
    offset = jnp.arange(narrow, dtype=jnp.int32)
    offset = jnp.where(chip == 1, (offset + 2) % 4, offset)
    offset = jnp.where(core == 1, offset + 1 - 2 * (offset % 2), offset)
    ids = jnp.concatenate(
        [
            jnp.where(six < 2, six, spot + 6 * chip),
            spot,
            jnp.stack([full, half, core]),
            (offset % 2) * 2 + offset // 2,
        ]
    ).astype(jnp.int32)
    mask_row, label_row = event_mask[None], labels[None]

    turn = lambda i: (i // 3) * 3 + (i % 3 + (i // 3) % 2) % 3
    table_rows = embed_table.shape[0]
    cols = fields * EMB
    blocks = ev_rows // HALF
    hi_n = 256
    lo_n = ev_rows // hi_n
    direct = cap % hi_n == 0
    asked = requests[0].transpose(0, 2, 1)
    if direct:
        embedded, far_up, far_down, their_up, their_down, proj_full, every = front(
            asked, embed_table.T, slot_index.T, dense_feats, mask_row, up_weight, down_weight, proj_weight
        )
        ups, downs = (up_weight, far_up, their_up), (down_weight, far_down, their_down)
    else:
        asked = lax.all_to_all(asked, "wide", 0, 0, tiled=True)
        ups, downs = bring(up_weight), bring(down_weight)
        proj_full = lax.all_gather(proj_weight, "narrow", axis=0)
        stats = local_stats(core[None], dense_feats, mask_row)
        stats = jnp.concatenate([stats, swap(stats, other_core)], axis=0)
        every = lax.all_to_all(
            jnp.broadcast_to(stats, (owners,) + stats.shape), "wide", 0, 0, tiled=True
        )
        tab = embed_table.reshape(32, table_rows // 32, cols).transpose(0, 2, 1)
        flat = asked.transpose(1, 0, 2).reshape(fields, DOMAINS, DSLOT).transpose(1, 0, 2)
        found = lookup(flat, tab, table_rows // 32, "lookup_rows", DOMAINS)
        found = found.transpose(1, 0, 2).reshape(cols, owners, cap).transpose(1, 0, 2)
        received = lax.all_to_all(found, "wide", 0, 0, tiled=True)
        received = received.transpose(1, 0, 2).reshape(cols, lo_n, hi_n).transpose(1, 0, 2)
        slots = slot_index.reshape(blocks, HALF, fields).transpose(0, 2, 1)
        embedded = lookup(slots, received, hi_n, "order_rows", narrow, turn)
        embedded = lax.all_to_all(embedded, "narrow", 0, 0, tiled=True)
    embedded = embedded.reshape(narrow * cols, rows)
    proj_full = proj_full.reshape(narrow * cols, D)

    tower = jnp.concatenate(
        [tower_bias, tower_out, jnp.pad(tower_out_bias[None], ((0, 3), (0, 128 - DOMAINS)))], axis=0
    )
    logits, own, embed_grad, extra = dense(
        ids, embedded, dense_feats, every, mask_row, label_row, proj_full, dense_weight, proj_bias[None],
        ups, downs, norm_gain, norm_shift, gate_weight.transpose(0, 2, 1), tower_in, tower,
    )
    extra = extra.reshape(narrow, ROWS_U, LANES)

    embed_grad = embed_grad.reshape(narrow, cols, rows)
    if not direct:
        embed_grad = lax.all_to_all(embed_grad, "narrow", 0, 0, tiled=True)
        returned = place(slot_index.T, embed_grad, (lo_n, cols, hi_n))
        returned = returned.transpose(1, 0, 2).reshape(cols, owners, cap).transpose(1, 0, 2)
        row_grads = lax.all_to_all(returned, "wide", 0, 0, tiled=True)

    if direct:
        sums, others, row_grads = reduce_all(own, extra, owners, REP_ROWS, (slot_index.T, embed_grad, cap))
    else:
        sums, others = reduce_all(own, extra, owners, REP_ROWS)
    expert = jnp.arange(14, dtype=jnp.int32)
    domain = (expert - SHARED) // DOM_EXP
    unit = jnp.where(domain % 3 == 0, 0, jnp.where(domain % 3 == 1, 4, 2)) + expert % 2
    away = jnp.where(domain // 3 == chip, 0, 16)
    unit = jnp.where(expert < SHARED, expert + 7, unit + away)
    marks = jnp.concatenate([unit, jnp.stack([me, me + 1 - 2 * core, me + 2 - 4 * chip, 3 - me])])
    outs = finish(marks.astype(jnp.int32), sums, others, cols, row_grads if direct else None)
    if not direct:
        outs = [row_grads.astype(F32)[None]] + list(outs)
    (row_grads, up_grad, down_grad, proj_grad, feat_grad, bias_grad, gain_grad, shift_grad, gate_grad, tower_grad,
     tower_bias_grad, tower_out_grad, out_bias_grad) = outs
    return (
        logits[0],
        row_grads.transpose(0, 1, 3, 2),
        proj_grad,
        feat_grad,
        bias_grad[0],
        up_grad,
        down_grad,
        gain_grad,
        shift_grad,
        gate_grad.transpose(0, 2, 1),
        tower_grad,
        tower_bias_grad,
        tower_out_grad,
        out_bias_grad[0, :DOMAINS],
    )


def solution(mesh):
    placed = (
        P("wide", "narrow"),
        P("wide", None, None, "narrow"),
        P("wide", "narrow"),
        P(("wide", "narrow")),
        P(("wide", "narrow")),
        P(("wide", "narrow"), None),
        P("narrow", None),
        P(),
        P(),
        P(None, None, "narrow"),
        P(None, "narrow", None),
        P(),
        P(),
        P(),
        P(),
        P(),
        P(),
        P(),
    )
    return jax.shard_map(
        shards,
        mesh=mesh,
        in_specs=placed,
        out_specs=(
            P(("wide", "narrow")),
            P("wide", None, None, "narrow"),
            P("narrow", None),
            P(),
            P(),
            P(None, None, "narrow"),
            P(None, "narrow", None),
            P(),
            P(),
            P(),
            P(),
            P(),
            P(),
            P(),
        ),
        check_vma=False,
    )
```

```python
import functools

import jax
import jax.numpy as jnp
from jax import lax
from jax.experimental import pallas as pl
from jax.experimental.pallas import tpu as pltpu
from jax.sharding import PartitionSpec as P

D = 512
HID = 1024
EMB = 16
DENSE = 128
DOMAINS = 6
SHARED = 2
DOM_EXP = 2
DSLOT = 1024
HALF = DSLOT // 2
VMEM = 56 * 2**20
BF = jnp.bfloat16
F32 = jnp.float32
MESH = pl.DeviceIdType.MESH
UNITS = 9
TURNED = 0
TOGETHER = 2
ROW_AT = 5
ROW_STEP = 1
ROWS_U = 1024
LANES = 256


def dot(a, b, ca, cb):
    return lax.dot_general(a, b, (((ca,), (cb,)), ((), ())), preferred_element_type=F32)


def lookup_kernel(lo_n, hi_n, fields, idx_ref, tab_ref, out_ref):
    length = idx_ref.shape[-1]
    shift = hi_n.bit_length() - 1
    for f in range(fields):
        idx = idx_ref[0, f : f + 1, :]
        hi = jnp.where(idx >= 0, idx & (hi_n - 1), -1)
        lo = lax.shift_right_logical(jnp.maximum(idx, 0), shift)
        hot = (lax.broadcasted_iota(jnp.int32, (hi_n, length), 0) == hi).astype(BF)
        cols = slice(f * EMB, (f + 1) * EMB)
        parts = [
            tab_ref[:, cols, j * hi_n : (j + 1) * hi_n].reshape(-1, hi_n) for j in range(tab_ref.shape[2] // hi_n)
        ]
        res = jnp.dot(jnp.concatenate(parts, axis=0), hot, preferred_element_type=F32)
        acc = res[0:EMB]
        for step in range(1, lo_n):
            acc = jnp.where(lo == step, res[step * EMB : (step + 1) * EMB], acc)
        out_ref[0, cols, :] = acc.astype(BF)


def lookup(idx, tab, hi_n, name, out_groups, order=lambda i: i):
    groups, fields, length = idx.shape
    outer, cols, inner = tab.shape
    lo_n = outer * inner // hi_n
    each = groups // out_groups
    return pl.pallas_call(
        functools.partial(lookup_kernel, lo_n, hi_n, fields),
        grid=(groups,),
        in_specs=[
            pl.BlockSpec((1, fields, length), lambda i: (order(i), 0, 0)),
            pl.BlockSpec(tab.shape, lambda i: (0, 0, 0)),
        ],
        out_specs=pl.BlockSpec((1, cols, length), lambda i: (i // each, 0, i % each)),
        out_shape=jax.ShapeDtypeStruct((out_groups, cols, length * each), BF),
        compiler_params=pltpu.CompilerParams(vmem_limit_bytes=VMEM),
        cost_estimate=pl.CostEstimate(
            flops=2 * groups * length * cols * lo_n * hi_n, bytes_accessed=8 * 2**20, transcendentals=0
        ),
        name=name,
    )(idx, tab)


def quarter_slots(slot_ref, q, field):
    half = slot_ref.shape[1] // 12
    parts = []
    for c in range(3):
        at = q * 3 * half + ((c + q % 2) % 3) * half
        at = at if isinstance(at, int) else pl.multiple_of(at, half)
        parts.append(slot_ref[pl.ds(field, 1), pl.ds(at, half)])
    return jnp.concatenate(parts, axis=1)


def place_one(idx_ref, grad_ref, out_ref, field):
    outer, _, inner = out_ref.shape
    length = grad_ref.shape[2]
    hi_n = 256
    lo_n = outer * inner // hi_n
    cols = pl.ds(pl.multiple_of(field * EMB, EMB), EMB)
    total = None
    for s in range(grad_ref.shape[0]):
        idx = quarter_slots(idx_ref, s, field)
        hi = idx & (hi_n - 1)
        lo = lax.shift_right_logical(idx, hi_n.bit_length() - 1)
        grad = grad_ref[s, cols, :]
        hot = (lax.broadcasted_iota(jnp.int32, (hi_n, length), 0) == hi).astype(BF)
        lhs = jnp.concatenate(
            [jnp.where(lo == step, grad, jnp.zeros_like(grad)) for step in range(lo_n)], axis=0
        )
        part = dot(lhs, hot, 1, 1)
        total = part if total is None else total + part
    total = total.astype(BF)
    each = inner // hi_n
    for i in range(outer * each):
        out_ref[i // each, cols, (i % each) * hi_n : (i % each + 1) * hi_n] = total[i * EMB : (i + 1) * EMB]


def place_kernel(idx_ref, grad_ref, out_ref):
    def one(field, _):
        place_one(idx_ref, grad_ref, out_ref, field)
        return 0

    lax.fori_loop(0, idx_ref.shape[0], one, 0)


def place(idx, grad, out_shape):
    return pl.pallas_call(
        place_kernel,
        out_shape=jax.ShapeDtypeStruct(out_shape, BF),
        compiler_params=pltpu.CompilerParams(vmem_limit_bytes=VMEM),
        name="place_rows",
    )(idx, grad)


def own_stats(feats_ref, mask_ref, out_ref, core):
    highest = lax.Precision.HIGHEST

    def block(c):
        at = pl.ds(pl.multiple_of(((c + core) % 3) * HALF, HALF), HALF)
        weight = jnp.broadcast_to(mask_ref[:, at].astype(F32), (8, HALF))
        return feats_ref[at, :], weight

    def total(weight, x):
        return jnp.dot(weight, x, preferred_element_type=F32, precision=highest)[0:1]

    for row, chunks in ((0, (0, 1)), (3, (2,))):
        count = sum(jnp.sum(block(c)[1][0:1], axis=1, keepdims=True) for c in chunks)
        mean = sum(total(block(c)[1], block(c)[0]) for c in chunks) / jnp.maximum(count, 1.0)
        off = lambda c: block(c)[0] - mean
        out_ref[row : row + 1, :] = mean
        out_ref[row + 1 : row + 2, :] = sum(total(block(c)[1], off(c) * off(c)) for c in chunks)
        out_ref[row + 2 : row + 3, :] = jnp.broadcast_to(count, mean.shape)


def stats_kernel(core_ref, feats_ref, mask_ref, out_ref):
    out_ref[...] = jnp.zeros_like(out_ref)
    own_stats(feats_ref, mask_ref, out_ref, core_ref[0])


def local_stats(core, feats, mask):
    return pl.pallas_call(
        stats_kernel,
        in_specs=[pl.BlockSpec(memory_space=pltpu.SMEM)] + [pl.BlockSpec(memory_space=pltpu.VMEM)] * 2,
        out_shape=jax.ShapeDtypeStruct((8, DENSE), F32),
        compiler_params=pltpu.CompilerParams(vmem_limit_bytes=VMEM),
        name="local_stats",
    )(core, feats, mask)


def front_kernel(
    groups, req_ref, table_ref, slot_ref, feats_ref, mask_ref, up_ref, down_ref, proj_ref,
    emb_ref, far_up, far_down, their_up, their_down, proj_out, every_ref,
    asked, found, received, ordered, both,
    req_send, req_recv, row_send, row_recv, near_send, near_recv, keep_sem,
    far_send, far_recv, side_send, above_send, own_send, own_recv, their_send, their_recv, proj_send, proj_recv,
    stat_send, stat_recv,
):
    wide, me = lax.axis_index("wide"), lax.axis_index("narrow")
    chip, core = me // 2, me % 2
    owners, fields, cap = req_ref.shape
    share = fields // groups
    parity, upper = wide % 2, (wide // 2) % 2
    near = [{"narrow": me + 1 - 2 * core}, {"narrow": me + 2 - 4 * chip}, {"narrow": 3 - me}]
    near_at = [me + 1 - 2 * core, me + 2 - 4 * chip, 3 - me]
    peers = [None] + [{"wide": (wide + d) % owners} for d in range(1, owners)]
    side, above = {"wide": wide + 1 - 2 * parity}, {"wide": wide + 2 - 4 * upper}
    barrier = pltpu.get_barrier_semaphore()
    for mate in near + peers[1:]:
        pl.semaphore_signal(barrier, inc=1, device_id=mate, device_id_type=MESH)
    pl.semaphore_wait(barrier, len(near) + len(peers) - 1)

    def remote(src, dst, send, recv, mate):
        return pltpu.make_async_remote_copy(
            src_ref=src, dst_ref=dst, send_sem=send, recv_sem=recv, device_id=mate, device_id_type=MESH
        )

    def req_copy(d):
        return remote(req_ref.at[(wide + d) % owners], asked.at[wide], req_send.at[d], req_recv.at[d], peers[d])

    for d in range(1, owners):
        req_copy(d).start()
    mine = pltpu.make_async_copy(req_ref.at[wide], asked.at[wide], keep_sem.at[0])
    mine.start()

    weights = ((up_ref, far_up, their_up), (down_ref, far_down, their_down))

    def far_at(j, side_of):
        return jnp.where(j == 0, 4 + side_of + 2 * upper, 2 * (j - 1) + side_of)

    def far_copy(j, a):
        p = far_at(j, parity)
        expert = jnp.where(p < 2, p, 6 * (1 - chip) + p)
        return remote(weights[a][0].at[expert], weights[a][1].at[p], far_send.at[a, j], far_recv.at[a, p], near[1])

    def side_copy(j, a, side_of):
        p = far_at(j, side_of)
        view = weights[a][1].at[p]
        return remote(view, view, side_send.at[a, j], far_recv.at[a, p], side)

    def above_copy(i, a, half):
        p = 4 + i + 2 * half
        view = weights[a][1].at[p]
        return remote(view, view, above_send.at[a, i], far_recv.at[a, p], above)

    def own_copy(i, a):
        expert = jnp.where(i < 2, i, 6 * chip + jnp.where(i < 4, i + 4 * (1 - core), i))
        return remote(weights[a][0].at[expert], weights[a][2].at[0, i], own_send.at[a, i], own_recv.at[a, i], near[0])

    def their_copy(p, a):
        i = jnp.where(p < 6, p, p - 4)
        return remote(weights[a][1].at[p], weights[a][2].at[1, i], their_send.at[a, i], their_recv.at[a, i], near[0])

    def wanted(p):
        ends = jnp.logical_or(jnp.logical_and(p < 4, core == 1), jnp.logical_and(p >= 6, core == 0))
        return jnp.logical_or(jnp.logical_or(p < 2, jnp.logical_and(p >= 4, p < 6)), ends)

    def for_all(n, f):
        def body(i, _):
            for a in range(2):
                f(i, a)
            return 0

        lax.fori_loop(0, n, body, 0)


    for_all(3, lambda j, a: far_copy(j, a).start())

    def stat_core():
        return remote(both.at[pl.ds(0, 8)], both.at[pl.ds(8, 8)], stat_send.at[0], stat_recv.at[0], near[0])

    def stat_copy(d):
        return remote(both, every_ref.at[wide], stat_send.at[d], stat_recv.at[d], peers[d])

    both[0:8, :] = jnp.zeros((8, DENSE), F32)
    own_stats(feats_ref, mask_ref, both, core)
    stat_core().start()

    def proj_copy(i):
        return remote(proj_ref, proj_out.at[me], proj_send.at[i], proj_recv.at[i], near[i])

    def proj_pass():
        view = proj_out.at[near_at[1]]
        return remote(view, view, proj_send.at[2], proj_recv.at[2], near[0])

    def other_proj():
        proj_copy(1).wait_recv()
        proj_pass().start()

    keep_proj = pltpu.make_async_copy(proj_ref, proj_out.at[me], keep_sem.at[1])
    keep_proj.start()
    for i in range(2):
        proj_copy(i).start()
    for_all(6, lambda i, a: own_copy(i, a).start())
    stat_core().wait_recv()
    for d in range(1, owners):
        stat_copy(d).start()
    keep_stat = pltpu.make_async_copy(both, every_ref.at[wide], keep_sem.at[2])
    keep_stat.start()

    def pass_on(p):
        @pl.when(wanted(p))
        def _():
            for a in range(2):
                their_copy(p, a).start()

    def lift(j, side_of):
        @pl.when(j == 0)
        def _():
            for a in range(2):
                above_copy(side_of, a, upper).start()

    def far_step(j):
        for a in range(2):
            far_copy(j, a).wait_recv()
            side_copy(j, a, parity).start()
        lift(j, parity)
        pass_on(far_at(j, parity))

    def side_step(j):
        for a in range(2):
            side_copy(j, a, 1 - parity).wait_recv()
        lift(j, 1 - parity)
        pass_on(far_at(j, 1 - parity))

    def above_step(i):
        for a in range(2):
            above_copy(i, a, 1 - upper).wait_recv()
        pass_on(4 + i + 2 * (1 - upper))

    hi_n = 512
    lo_n = table_ref.shape[1] // hi_n

    def find(f, owner_idx):
        idx = asked[owner_idx, pl.ds(f, 1), :]
        hi = jnp.where(idx >= 0, idx & (hi_n - 1), -1)
        lo = lax.shift_right_logical(jnp.maximum(idx, 0), hi_n.bit_length() - 1)
        hot = (lax.broadcasted_iota(jnp.int32, (hi_n, cap), 0) == hi).astype(BF)
        cols = pl.ds(pl.multiple_of(f * EMB, EMB), EMB)
        part = jnp.concatenate([table_ref[cols, l * hi_n : (l + 1) * hi_n] for l in range(lo_n)], axis=0)
        res = jnp.dot(part, hot, preferred_element_type=F32)
        acc = res[0:EMB]
        for step in range(1, lo_n):
            acc = jnp.where(lo == step, res[step * EMB : (step + 1) * EMB], acc)
        return cols, acc.astype(BF)

    def group_rows(g):
        return pl.ds(pl.multiple_of(g * share * EMB, share * EMB), share * EMB)

    def row_copy(g, d, mate):
        rows = group_rows(g)
        return remote(
            found.at[(wide + d) % owners, rows], received.at[wide, rows], row_send.at[g, d], row_recv.at[g, d], mate
        )

    def look(g):
        @pl.when(g == 0)
        def _():
            for d in range(1, owners):
                req_copy(d).wait_recv()

        def some(i, _):
            ahead = [i * TOGETHER + e for e in range(TOGETHER)]
            for d in ahead:
                for k in range(share):
                    cols, block = find(g * share + k, (wide + d) % owners)
                    found[(wide + d) % owners, cols, :] = block
            for d in ahead:
                @pl.when(d > 0)
                def _():
                    row_copy(g, d, {"wide": (wide + d) % owners}).start()

            return 0

        lax.fori_loop(0, owners // TOGETHER, some, 0)
        received[wide, group_rows(g), :] = found[wide, group_rows(g), :]

    hi_e = 256
    outer = owners * cap // hi_e

    def near_copy(g, i):
        rows = group_rows(g)
        return remote(
            ordered.at[near_at[i], rows], emb_ref.at[me, rows], near_send.at[g, i], near_recv.at[g, i], near[i]
        )

    def keep_copy(g):
        rows = group_rows(g)
        return pltpu.make_async_copy(ordered.at[me, rows], emb_ref.at[me, rows], keep_sem.at[3 + g])

    def order(g):
        def arrive(d, _):
            row_copy(g, d, {"wide": (wide + d) % owners}).wait_recv()
            return 0

        lax.fori_loop(1, owners, arrive, 0)
        tables = []
        for k in range(share):
            cols = pl.ds(pl.multiple_of((g * share + k) * EMB, EMB), EMB)
            parts = [
                received[o, cols, j * hi_e : (j + 1) * hi_e] for o in range(owners) for j in range(cap // hi_e)
            ]
            tables.append((cols, jnp.concatenate(parts, axis=0)))

        def quarter(q):
            for k, (cols, table) in enumerate(tables):
                idx = quarter_slots(slot_ref, q, g * share + k)
                hi = idx & (hi_e - 1)
                lo = lax.shift_right_logical(idx, hi_e.bit_length() - 1)
                hot = (lax.broadcasted_iota(jnp.int32, (hi_e, idx.shape[1]), 0) == hi).astype(BF)
                res = jnp.dot(table, hot, preferred_element_type=F32)
                acc = res[0:EMB]
                for step in range(1, outer):
                    acc = jnp.where(lo == step, res[step * EMB : (step + 1) * EMB], acc)
                ordered[q, cols, :] = acc.astype(BF)

        for i in (2, 1, 0):
            quarter(near_at[i])
            near_copy(g, i).start()
        quarter(me)
        keep_copy(g).start()

    mine.wait()

    def tick(t, _):
        @pl.when(t < groups)
        def _():
            look(t)

        @pl.when(jnp.logical_and(t >= 1, t < 4))
        def _():
            far_step(t - 1)

        @pl.when(t >= 2)
        def _():
            order(t - 2)

        @pl.when(t == 3)
        def _():
            other_proj()

        @pl.when(jnp.logical_and(t >= 3, t < 6))
        def _():
            side_step(t - 3)

        @pl.when(t >= 5)
        def _():
            above_step(jnp.where(t == 5, parity, 1 - parity))

        return 0

    lax.fori_loop(0, groups + 2, tick, 0)

    for d in range(1, owners):
        req_copy(d).wait_send()
        stat_copy(d).wait()
    stat_core().wait_send()
    keep_stat.wait()
    keep_proj.wait()
    proj_copy(0).wait()
    proj_copy(1).wait_send()
    proj_pass().wait()

    def rows_left(g, _):
        def one(d, _):
            row_copy(g, d, {"wide": (wide + d) % owners}).wait_send()
            return 0

        lax.fori_loop(1, owners, one, 0)
        for i in range(3):
            near_copy(g, i).wait()
        keep_copy(g).wait()
        return 0

    lax.fori_loop(0, groups, rows_left, 0)

    def weights_left(j, a):
        far_copy(j, a).wait_send()
        side_copy(j, a, parity).wait_send()

    for_all(3, weights_left)
    for_all(2, lambda i, a: above_copy(i, a, upper).wait_send())
    for_all(6, lambda i, a: own_copy(i, a).wait())

    def passed(p, a):
        @pl.when(wanted(p))
        def _():
            their_copy(p, a).wait_send()

    for_all(8, passed)
    for_all(6, lambda i, a: their_copy(i, a).wait_recv())


def front(req, table, slots, feats, mask, up, down, proj, groups=5):
    owners, fields, cap = req.shape
    cols = fields * EMB
    quarters = 4
    rows = slots.shape[1] // quarters
    any_space, vmem = pl.BlockSpec(memory_space=pl.ANY), pl.BlockSpec(memory_space=pltpu.VMEM)
    dma = pltpu.SemaphoreType.DMA
    return pl.pallas_call(
        functools.partial(front_kernel, groups),
        in_specs=[vmem] * 5 + [any_space] * 3,
        out_specs=[any_space] * 7,
        out_shape=[
            jax.ShapeDtypeStruct((quarters, cols, rows), BF),
            jax.ShapeDtypeStruct((8,) + up.shape[1:], BF),
            jax.ShapeDtypeStruct((8,) + down.shape[1:], BF),
            jax.ShapeDtypeStruct((2, 6) + up.shape[1:], BF),
            jax.ShapeDtypeStruct((2, 6) + down.shape[1:], BF),
            jax.ShapeDtypeStruct((quarters,) + proj.shape, BF),
            jax.ShapeDtypeStruct((owners, 16, DENSE), F32),
        ],
        scratch_shapes=[
            pltpu.VMEM((owners, fields, cap), jnp.int32),
            pltpu.VMEM((owners, cols, cap), BF),
            pltpu.VMEM((owners, cols, cap), BF),
            pltpu.VMEM((quarters, cols, rows), BF),
            pltpu.VMEM((16, DENSE), F32),
            dma((owners,)),
            dma((owners,)),
            dma((groups, owners)),
            dma((groups, owners)),
            dma((groups, 3)),
            dma((groups, 3)),
            dma((3 + groups,)),
            dma((2, 3)),
            dma((2, 8)),
            dma((2, 3)),
            dma((2, 2)),
            dma((2, 6)),
            dma((2, 6)),
            dma((2, 6)),
            dma((2, 6)),
            dma((3,)),
            dma((3,)),
            dma((owners,)),
            dma((owners,)),
        ],
        compiler_params=pltpu.CompilerParams(collective_id=1, has_side_effects=True, vmem_limit_bytes=VMEM),
        cost_estimate=pl.CostEstimate(flops=45 * 10**9, bytes_accessed=40 * 2**20, transcendentals=0),
        name="front",
    )(req, table, slots, feats, mask, up, down, proj)


def reduce_kernel(bits, with_rows, own_ref, extra_ref, *refs):
    if with_rows:
        slot_ref, grad_ref, out_ref, rep_ref, back_ref = refs[:5]
        grads, placed, near_send, near_recv, far_send, far_recv, keep_sem = refs[-7:]
        refs = refs[5:-7]
    else:
        out_ref, rep_ref = refs[:2]
        refs = refs[2:]
    acc, stage_buf, halves, got, local_sem, send, recv, rep_send, rep_recv, out_sem = refs
    wide=lax.axis_index("wide"); me=lax.axis_index("narrow")
    chip=me//2; core=me%2
    block=ROWS_U>>bits
    mates=[{"narrow": me+1-2*core},{"narrow": me+2-4*chip}]
    pairs=[{"wide": wide+(1<<k)*(1-2*((wide//(1<<k))%2))} for k in range(bits)]
    far={"narrow": 3-me}
    barrier=pltpu.get_barrier_semaphore()
    owners=1<<bits
    others=[{"wide": (wide+d)%owners} for d in range(1,owners)] if with_rows else pairs
    for mate in mates+[far]+others:
        pl.semaphore_signal(barrier, inc=1, device_id=mate, device_id_type=MESH)
    pl.semaphore_wait(barrier, len(others)+3)
    def power(k):
        return 1 << k, 1 << ((k + 1) % bits)

    def bit(u, k):
        here, there = power(k)
        return jnp.where(u == TURNED, (wide // there) % 2, (wide // here) % 2)

    def pair(u, k):
        here, there = power(k)
        step = jnp.where(u == TURNED, there, here)
        return {"wide": wide + step * (1 - 2 * bit(u, k))}

    def start_of(u, k):
        at = 0
        for j in range(k):
            at = at + bit(u, j) * (ROWS_U >> (j + 1))
        return pl.multiple_of(at, 16) if k else 0

    def copy(src, dst, s, u, mate):
        return pltpu.make_async_remote_copy(
            src_ref=src, dst_ref=dst, send_sem=send.at[s, u], recv_sem=recv.at[s, u], device_id=mate, device_id_type=MESH
        )

    def mine(u):
        return jnp.logical_or(u >= 4, jnp.where(u < 2, core == 0, core == 1))

    def theirs(u):
        return jnp.logical_or(u >= 4, jnp.where(u < 2, core == 1, core == 0))

    def domain_unit(u):
        return u < 6

    def local_at(u):
        return jnp.where(u < 2, u + 2, jnp.where(u < 6, u, u - 7))

    def core_copy(u, src):
        return copy(src, acc.at[u], 0, u, mates[0])

    def near_copy(u, src):
        return pltpu.make_async_copy(src, stage_buf.at[u % 2], local_sem.at[u % 2])

    def begin(u):
        @pl.when(u == 6)
        def _():
            core_copy(u, extra_ref.at[pl.ds(2, 2)]).start()
            near_copy(u, extra_ref.at[pl.ds(0, 2)]).start()

        @pl.when(jnp.logical_and(u != 6, mine(u)))
        def _():
            core_copy(u, own_ref.at[local_at(u), pl.ds(2, 2)]).start()
            near_copy(u, own_ref.at[local_at(u), pl.ds(0, 2)]).start()

    def add_region(u, sl, at, rows, src):
        tile = min(rows, 64)

        def body(i, _):
            r = pl.multiple_of(at + i * tile, 16)
            q = pl.multiple_of(i * tile, 16)
            for h in range(sl):
                a = acc[u, h, pl.ds(r, tile), :].astype(F32) + src[h, pl.ds(q, tile), :].astype(F32)
                acc[u, h, pl.ds(r, tile), :] = a.astype(BF)
            return 0

        lax.fori_loop(0, rows // tile, body, 0)

    half_at = [0]
    for k in range(bits):
        half_at.append(half_at[-1] + (ROWS_U >> (k + 1)))

    def half_view(u, k, parts):
        return halves.at[u, pl.ds(0, parts), pl.ds(half_at[k], ROWS_U >> (k + 1)), :]

    def send_half(u, k, parts):
        size = ROWS_U >> (k + 1)
        at = pl.multiple_of(start_of(u, k) + (1 - bit(u, k)) * size, 16)
        return copy(acc.at[u, pl.ds(0, parts), pl.ds(at, size), :], half_view(u, k, parts), 1 + k, u, pair(u, k))

    def take_half(u, k, parts):
        size = ROWS_U >> k
        copy(acc.at[u, pl.ds(0, parts), pl.ds(0, size), :], half_view(u, k - 1, parts), k, u, pair(u, k - 1)).wait_recv()
        add_region(u, parts, start_of(u, k), size, halves.at[u, :, pl.ds(half_at[k - 1], size), :])

    def y_whole(u):
        return copy(acc.at[u, 1], got.at[u, 1], bits + 1, u, mates[1])

    def y_block(u):
        at = start_of(u, bits)
        return copy(
            acc.at[u, 1, pl.ds(at, block), :], got.at[u, 1, pl.ds(at, block), :], bits + 1, u, mates[1]
        )

    def combine(u):
        @pl.when(theirs(u))
        def _():
            core_copy(u, acc.at[u]).wait_recv()

        @pl.when(mine(u))
        def _():
            near_copy(u, acc.at[u]).wait()
            sb = stage_buf.at[u % 2]

            @pl.when(theirs(u))
            def _():
                add_region(u, 2, 0, ROWS_U, sb)

            @pl.when(jnp.logical_not(theirs(u)))
            def _():
                def body(i, _):
                    r = pl.multiple_of(i * 64, 16)
                    for h in (0, 1):
                        acc[u, h, pl.ds(r, 64), :] = sb[h, pl.ds(r, 64), :]
                    return 0

                lax.fori_loop(0, ROWS_U // 64, body, 0)

    def grow_copy(u, j, parts):
        size = ROWS_U >> (j + 1)
        view = got.at[u, pl.ds(0, parts), pl.ds(start_of(u, j + 1), size), :]
        return copy(view, view, bits + 2 + (bits - 1 - j), u, pair(u, j))

    def out_copy(u, parts):
        return pltpu.make_async_copy(got.at[u, pl.ds(0, parts)], out_ref.at[u, pl.ds(0, parts)], out_sem.at[u])

    rep_mates = [mates[0], mates[1], far]
    rep_rows = rep_ref.shape[1]

    def rep_copy(i):
        return pltpu.make_async_remote_copy(
            src_ref=got.at[6, 0, pl.ds(0, rep_rows), :], dst_ref=rep_ref.at[i], send_sem=rep_send.at[i],
            recv_sem=rep_recv.at[i], device_id=rep_mates[i], device_id_type=MESH,
        )

    def by_kind(u, domain, shared):
        pl.when(domain_unit(u))(domain)
        pl.when(jnp.logical_not(domain_unit(u)))(shared)

    def start_grow(u):
        by_kind(u, lambda: grow_copy(u, bits - 1, 2).start(), lambda: grow_copy(u, bits - 1, 1).start())

    def stage_one(u):
        combine(u)
        by_kind(u, lambda: send_half(u, 0, 2).start(), lambda: y_whole(u).start())

    def halving(k, u):
        def domain():
            take_half(u, k, 2)
            if k < bits:
                send_half(u, k, 2).start()
            else:
                y_block(u).start()

        def shared():
            if k == 1:
                y_whole(u).wait_recv()
                add_region(u, 1, 0, ROWS_U, got.at[u, pl.ds(1, 1)])
            else:
                take_half(u, k - 1, 1)
            send_half(u, k - 1, 1).start()

        by_kind(u, domain, shared)

    def cross(u):
        at = start_of(u, bits)

        def domain():
            y_block(u).wait_recv()

        def shared():
            take_half(u, bits, 1)

        by_kind(u, domain, shared)
        got[u, 0, pl.ds(at, block), :] = acc[u, 0, pl.ds(at, block), :]
        start_grow(u)

    def grow(u, j):
        by_kind(u, lambda: grow_copy(u, j, 2).wait_recv(), lambda: grow_copy(u, j, 1).wait_recv())
        if j > 0:
            by_kind(u, lambda: grow_copy(u, j - 1, 2).start(), lambda: grow_copy(u, j - 1, 1).start())
        else:
            by_kind(u, lambda: out_copy(u, 2).start(), lambda: out_copy(u, 1).start())

            @pl.when(u == 6)
            def _():
                for i in range(3):
                    rep_copy(i).start()

    quarters=mates+[far]
    def quarter_at(i):
        return [me+1-2*core, me+2-4*chip, 3-me][i]
    def near_row_copy(i):
        return pltpu.make_async_remote_copy(src_ref=grad_ref.at[quarter_at(i)],dst_ref=grads.at[me],send_sem=near_send.at[i],recv_sem=near_recv.at[i],device_id=quarters[i],device_id_type=MESH)
    def keep_copy():
        return pltpu.make_async_copy(grad_ref.at[me],grads.at[me],keep_sem.at[0])
    def back_copy(d):
        return pltpu.make_async_remote_copy(src_ref=placed.at[(wide+d)%owners],dst_ref=back_ref.at[wide],send_sem=far_send.at[d],recv_sem=far_recv.at[d],device_id=others[d-1],device_id_type=MESH)
    def keep_back():
        return pltpu.make_async_copy(placed.at[wide],back_ref.at[wide],keep_sem.at[1])
    def place_field(f, _):
        place_one(slot_ref, grads, placed, f)
        return 0
    def row_step(t):
        fields=slot_ref.shape[0]
        @pl.when(t==ROW_AT)
        def _():
            keep_copy().wait()
            for i in range(3): near_row_copy(i).wait_recv()
        @pl.when(jnp.logical_and(t>=ROW_AT,t<ROW_AT+5))
        def _():
            lax.fori_loop((t-ROW_AT)*(fields//5),(t-ROW_AT+1)*(fields//5),place_field,0)
        for d in range(owners):
            @pl.when(t==ROW_AT+4+int(d*ROW_STEP))
            def _():
                if d==0: keep_back().start()
                else: back_copy(d).start()
    todo = [begin, stage_one]
    todo += [functools.partial(halving, k) for k in range(1, bits + 1)] + [cross]
    todo += [functools.partial(lambda j, u: grow(u, j), j) for j in reversed(range(bits))]
    plain_gaps = [0, 1, 2] + [1] * (len(todo) - 4) + [2]
    turned_gaps = [0, 1, 3, 4] + [1] * (len(todo) - 6) + [3, 3]
    plain_lag = [sum(plain_gaps[: i + 1]) for i in range(len(todo))]
    turned_lag = [sum(turned_gaps[: i + 1]) for i in range(len(todo))]

    def tick(t,_):
        for s in reversed(range(len(todo))):
            def stage(c, _):
                plain = t - plain_lag[s]
                u = jnp.where(c == 0, plain, TURNED)
                fits = jnp.logical_and(jnp.logical_and(plain >= 0, plain < UNITS), plain != TURNED)
                due = jnp.where(c == 0, fits, t == TURNED + turned_lag[s])

                @pl.when(due)
                def _():
                    todo[s](u)

                return 0

            lax.fori_loop(0, 2, stage, 0)
        if with_rows:
            row_step(t)
        return 0
    if with_rows:
        keep_copy().start()
        for i in range(3): near_row_copy(i).start()
    lax.fori_loop(0, max(UNITS + plain_lag[-1], TURNED + turned_lag[-1] + 1), tick, 0)
    if with_rows:
        keep_back().wait()
        for i in range(3): near_row_copy(i).wait_send()
        for d in range(1,owners): back_copy(d).wait()
    def finish(u,_):
        @pl.when(mine(u))
        def _():
            core_copy(u, acc.at[u]).wait_send()

        def left(parts):
            for k in range(bits):
                send_half(u, k, parts).wait_send()
            (y_block if parts == 2 else y_whole)(u).wait_send()
            for j in range(bits):
                grow_copy(u, j, parts).wait_send()
            out_copy(u, parts).wait()

        by_kind(u, lambda: left(2), lambda: left(1))
        return 0
    lax.fori_loop(0,UNITS,finish,0)
    for i in range(3):
        rep_copy(i).wait()

def reduce_all(own, extra, wide, rep_rows, rows=None):
    bits = wide.bit_length() - 1
    args = [own, extra]
    any_space = pl.BlockSpec(memory_space=pl.ANY)
    in_specs = [any_space] * 2
    out_shape = [
        jax.ShapeDtypeStruct((UNITS, 2, ROWS_U, LANES), BF),
        jax.ShapeDtypeStruct((3, rep_rows, LANES), BF),
    ]
    scratch = [
        pltpu.VMEM((UNITS, 2, ROWS_U, LANES), BF),
        pltpu.VMEM((2, 2, ROWS_U, LANES), BF),
        pltpu.VMEM((UNITS, 2, ROWS_U, LANES), BF),
        pltpu.VMEM((UNITS, 2, ROWS_U, LANES), BF),
        pltpu.SemaphoreType.DMA((2,)),
        pltpu.SemaphoreType.DMA((2 * bits + 2, UNITS)),
        pltpu.SemaphoreType.DMA((2 * bits + 2, UNITS)),
        pltpu.SemaphoreType.DMA((3,)),
        pltpu.SemaphoreType.DMA((3,)),
        pltpu.SemaphoreType.DMA((UNITS,)),
    ]
    if rows is not None:
        slots, grads, cap = rows
        args += [slots, grads]
        in_specs += [pl.BlockSpec(memory_space=pltpu.VMEM), any_space]
        back = (wide, grads.shape[1], cap)
        out_shape.append(jax.ShapeDtypeStruct(back, BF))
        scratch += [
            pltpu.VMEM(grads.shape, BF),
            pltpu.VMEM(back, BF),
            pltpu.SemaphoreType.DMA((3,)),
            pltpu.SemaphoreType.DMA((3,)),
            pltpu.SemaphoreType.DMA((wide,)),
            pltpu.SemaphoreType.DMA((wide,)),
            pltpu.SemaphoreType.DMA((2,)),
        ]
    return pl.pallas_call(
        functools.partial(reduce_kernel, bits, rows is not None),
        in_specs=in_specs,
        out_specs=[any_space] * len(out_shape),
        out_shape=out_shape,
        scratch_shapes=scratch,
        compiler_params=pltpu.CompilerParams(collective_id=0, has_side_effects=True, vmem_limit_bytes=VMEM),
        cost_estimate=pl.CostEstimate(flops=0, bytes_accessed=60 * 2**20, transcendentals=0),
        name="reduce_all",
    )(*args)


C0 = 0.7978845608028654
C1 = 0.044715
REP_ROWS = 512
GATE_AT = 256
GAIN_AT = 352
SHIFT_AT = 384
MISC_AT = 416


def gelu_both(x):
    square = x * x
    up = 0.5 * jnp.tanh(x * (square * (C0 * C1) + C0)) + 0.5
    act = x * up
    return act, up + (act - act * up) * (square * (6.0 * C0 * C1) + 2.0 * C0)


def soft_pair(a, b):
    top = jnp.maximum(a, b)
    ea, eb = jnp.exp(a - top), jnp.exp(b - top)
    total = ea + eb
    return ea / total, eb / total


def soft_pair_back(pa, pb, ga, gb):
    mean = pa * ga + pb * gb
    return pa * (ga - mean), pb * (gb - mean)


def fold(x):
    return sum(x[:, i * 128 : (i + 1) * 128] for i in range(x.shape[1] // 128))


def wide_lanes(x, n):
    return jnp.concatenate([x] * n, axis=1)


def split_low(x):
    high = x.astype(BF)
    return high, (x - high.astype(F32)).astype(BF)


def iota(shape, axis):
    return lax.broadcasted_iota(jnp.int32, shape, axis)


def row_of(rows, at):
    return (iota((rows, 128), 0) == at).astype(BF)


def dense_kernel(
    ids_ref, emb_ref, feats_ref, every_ref, mask_ref, label_ref, projw_ref, featw_ref, bias_ref,
    up_a, up_b, up_c, down_a, down_b, down_c, gain_ref, shift_ref, gate_f, gate_h, tin_f, tin_h,
    tower_ref,
    logit_ref, own_ref, emb_grad_ref, extra_ref,
    xt, act, slope, outs, og, ing, hid, hg, stat, inner, emb, feat, featw, gains, mixed, shifts, gates, tin,
    tbias, tout, tob, gain_acc, shift_acc, gate_acc, tin_acc, tbias_acc, tout_acc, tob_acc, emb_sem, extra_sem,
):
    ups = [up_a.at[0], up_b.at[0], up_c.at[0, 0], up_c.at[1, 0]]
    downs = [down_a.at[0], down_b.at[0], down_c.at[0, 0], down_c.at[1, 0]]
    step = pl.program_id(0)
    chunk, slot = step // 4, step % 4
    rows = xt.shape[1]
    core = ids_ref[14]
    owners = every_ref.shape[0]

    def expert_of(dom, k):
        return k if k < 2 else ids_ref[2 * dom + k]

    def raw_lanes(c):
        return pl.ds(pl.multiple_of(((c + core) % 3) * HALF, HALF), HALF)

    def pooled(sets):
        def sums(w, carry):
            total, mean = carry
            for at in sets:
                count = every_ref[w, at + 2 : at + 3, :]
                total, mean = total + count, mean + count * every_ref[w, at : at + 1, :]
            return total, mean

        zero = jnp.zeros((1, 128), F32)
        total, mean = lax.fori_loop(0, owners, sums, (zero, zero))
        mean = mean / total

        def squares(w, acc):
            for at in sets:
                off = every_ref[w, at : at + 1, :] - mean
                acc = acc + every_ref[w, at + 1 : at + 2, :] + every_ref[w, at + 2 : at + 3, :] * off * off
            return acc

        return mean, lax.rsqrt(lax.fori_loop(0, owners, squares, zero) / total + 1e-05)

    @pl.when(step == 0)
    def _():
        fetch = pltpu.make_async_copy(emb_ref, emb, emb_sem)
        fetch.start()
        for e in range(6):
            gains[e] = dot(gain_ref[...], row_of(14, ids_ref[e]), 0, 0).astype(BF)
        for dom, (gate, tower) in enumerate(((gate_f, tin_f), (gate_h, tin_h))):
            tin[dom] = tower[0]
            pick = (iota((16, 6), 0) % 8 == iota((16, 6), 1)).astype(BF)
            gates[dom] = dot(pick, gate[0], 1, 0).astype(BF)
            place = iota((16, 14), 0)
            ident = place % 4
            for k in range(4):
                ident = jnp.where(place % 4 == k, expert_of(dom, k), ident)
            same = ident == iota((16, 14), 1)
            first, second = jnp.logical_and(same, place < 4), jnp.logical_and(same, place < 8)
            third = jnp.logical_and(second, place >= 4)
            mixed[dom] = (
                dot(first.astype(BF), gain_ref[...], 1, 0) + dot(third.astype(BF), shift_ref[...], 1, 0)
            ).astype(BF)
            shifts[dom] = dot(second.astype(BF), shift_ref[...], 1, 0).astype(BF)
            d = ids_ref[12 + dom]
            tbias[dom] = dot(tower_ref[...], row_of(16, d), 0, 0)
            tout[dom] = dot(tower_ref[...], row_of(16, 6 + d), 0, 0)
            tob[dom] = dot(tower_ref[...], row_of(128, d), 1, 0)
        featw[0:128, :] = featw_ref[...]
        featw[128:144, :] = jnp.where(iota((16, D), 0) == 0, bias_ref[...].astype(F32), 0.0).astype(BF)
        feat[128:144, :] = (iota((16, rows), 0) == 0).astype(BF)
        moments = [pooled((0,)), pooled((3, 11))]
        for c in range(rows // HALF):
            mean, scale = moments[c // 2]
            x = (feats_ref[raw_lanes(c), :] - mean) * scale
            feat[0:128, c * HALF : (c + 1) * HALF] = x.T.astype(BF)
        for ref in (gain_acc, shift_acc, gate_acc, tin_acc, tbias_acc, tout_acc, tob_acc):
            ref[...] = jnp.zeros_like(ref)
        fetch.wait()
        for c in range(rows // HALF):
            cols = slice(c * HALF, (c + 1) * HALF)
            x = dot(projw_ref[...], emb[:, cols], 0, 0) + dot(featw[...], feat[:, cols], 0, 0)
            xt[:, cols] = x.astype(BF)

    @pl.when(step < 12)
    def _():
        lanes = pl.ds(pl.multiple_of(chunk * HALF, HALF), HALF)

        for s in range(4):
            pre = dot(ups[s][...], xt[:, lanes], 0, 0)
            a, g = gelu_both(pre)
            a = a.astype(BF)
            act[slot, s, :, lanes] = a
            slope[slot, s, :, lanes] = g.astype(BF)

        total = dot(downs[0][...], act[slot, 0, :, lanes], 0, 0)
        for s in range(1, 4):
            total += dot(downs[s][...], act[slot, s, :, lanes], 0, 0)
        outs[slot] = total

    def middle():
        lanes = pl.ds(pl.multiple_of(chunk * HALF, HALF), HALF)
        dom = chunk // 2
        x = xt[:, lanes]
        logit_gates = dot(gates[dom], x, 1, 0)
        s0, s1 = soft_pair(logit_gates[0:1], logit_gates[1:2])
        d0, d1 = soft_pair(logit_gates[2:3], logit_gates[3:4])
        t0, t1 = soft_pair(logit_gates[4:5], logit_gates[5:6])
        coef = jnp.concatenate([t0 * s0, t0 * s1, t1 * d0, t1 * d1], axis=0)
        high = coef.astype(BF).astype(F32)
        spare = jnp.zeros((8, HALF), F32)
        coef_low = jnp.concatenate([high, coef - high, spare], axis=0).astype(BF)
        hg[...] = dot(shifts[dom], coef_low, 0, 0)
        stat[8:12, :] = coef
        expert = [0, 1, 2 + 2 * dom, 3 + 2 * dom]

        def normalize(t, _):
            cols = pl.ds(pl.multiple_of(t * 128, 128), 128)
            for k in range(4):
                v = outs[k, :, cols]
                mean = jnp.sum(v, axis=0, keepdims=True) * (1.0 / D)
                v = v - mean
                var = jnp.sum(v * v, axis=0, keepdims=True) * (1.0 / D)
                stat[k : k + 1, cols] = mean
                stat[4 + k : 5 + k, cols] = lax.rsqrt(var + 1e-05)
            scale = [stat[4 + k : 5 + k, cols] * stat[8 + k : 9 + k, cols] for k in range(4)]
            for r in range(8):
                band = slice(r * 64, (r + 1) * 64)
                acc = hg[band, cols]
                for k in range(4):
                    n = (outs[k, band, cols] - stat[k : k + 1, cols]) * scale[k]
                    acc = acc + n * gains[expert[k], band, :].astype(F32)
                hid[band, cols] = acc.astype(BF)
            return 0

        lax.fori_loop(0, 4, normalize, 0)
        h = hid[...]
        pre = dot(tin[dom], h, 0, 0) + wide_lanes(tbias[dom], 4)
        tact, tslope = gelu_both(pre)
        weight = wide_lanes(tout[dom], 4)
        logit = jnp.sum(tact * weight, axis=0, keepdims=True) + wide_lanes(tob[dom, 12:13, :], 4)
        logit_ref[:, raw_lanes(chunk)] = logit
        live, label = mask_ref[:, raw_lanes(chunk)].astype(F32), label_ref[:, raw_lanes(chunk)].astype(F32)
        grad = (jax.nn.sigmoid(logit) - label) * live
        tob_acc[dom, 0:1, :] += fold(grad)
        tout_acc[dom] += fold(grad * tact)
        low = (grad * weight * tslope).astype(BF)
        tbias_acc[dom] += fold(low.astype(F32))
        tin_acc[dom] += dot(h, low, 1, 1)
        back = dot(tin[dom], low, 1, 0)
        hg[...] = back
        back_high, back_low = split_low(back)
        shift_acc[dom] += dot(back_high, coef_low, 1, 1) + dot(back_low, coef_low, 1, 1)
        inner[...] = dot(mixed[dom], back_high, 1, 0) + dot(mixed[dom], back_low, 1, 0)

        def denormalize(t, _):
            cols = pl.ds(pl.multiple_of(t * 128, 128), 128)
            place = pl.ds(pl.multiple_of(chunk * HALF + t * 128, 128), 128)
            for k in range(4):
                mean, rstd = stat[k : k + 1, cols], stat[4 + k : 5 + k, cols]
                c = stat[8 + k : 9 + k, cols]
                m2 = 0.0
                for r in range(8):
                    band = slice(r * 64, (r + 1) * 64)
                    w = (outs[k, band, cols] - mean) * rstd * hg[band, cols]
                    m2 = m2 + jnp.sum(w * gains[expert[k], band, :].astype(F32), axis=0, keepdims=True)
                    gain_acc[expert[k], band, :] += w * c
                m1 = inner[k : k + 1, cols]
                inner[4 + k : 5 + k, cols] += m2
                cr = c * rstd
                slant = cr * rstd * m2 * (1.0 / D)
                level = mean * slant - cr * m1 * (1.0 / D)
                for r in range(8):
                    band = slice(r * 64, (r + 1) * 64)
                    scaled = hg[band, cols] * gains[expert[k], band, :].astype(F32)
                    og[k, band, place] = (scaled * cr - outs[k, band, cols] * slant + level).astype(BF)
            return 0

        lax.fori_loop(0, 4, denormalize, 0)
        a = [inner[4 + k : 5 + k, :] for k in range(4)]
        g0, g1 = soft_pair_back(s0, s1, t0 * a[0], t0 * a[1])
        g2, g3 = soft_pair_back(d0, d1, t1 * a[2], t1 * a[3])
        g4, g5 = soft_pair_back(t0, t1, s0 * a[0] + s1 * a[1], d0 * a[2] + d1 * a[3])
        zero = jnp.zeros_like(g0)
        g = jnp.concatenate([g0, g1, g2, g3, g4, g5, zero, zero], axis=0)
        high = g.astype(BF).astype(F32)
        g = jnp.concatenate([high, g - high], axis=0).astype(BF)
        gate_acc[dom] += dot(g, x, 1, 1)
        ing[:, lanes] = dot(gates[dom], g, 0, 0)

    @pl.when(jnp.logical_and(step < 12, slot == 3))
    def _():
        middle()

    def back(k, at, n):
        lanes = slice(at, at + n)
        for s in range(4):
            p = dot(downs[s][...], og[k, :, lanes], 1, 0) * slope[k, s, :, lanes].astype(F32)
            slope[k, s, :, lanes] = p.astype(BF)

        for s in range(4):
            grad, p = og[k, :, lanes], slope[k, s, :, lanes]
            own_ref[0, s, 0:D, :] = dot(xt[:, lanes], p, 1, 1).astype(BF)
            d = dot(act[k, s, :, lanes], grad, 1, 1).astype(BF)
            own_ref[0, s, D : D + 256, :] = d[:, 0:256]
            own_ref[0, s, D + 256 : D + 512, :] = d[:, 256:512]

        for t in range(n // HALF):
            cols = slice(at + t * HALF, at + (t + 1) * HALF)
            total = dot(ups[0][...], slope[k, 0, :, cols], 1, 0)
            for s in range(1, 4):
                total += dot(ups[s][...], slope[k, s, :, cols], 1, 0)
            ing[:, cols] += total

    expert = step - 12

    @pl.when(jnp.logical_and(expert >= 0, expert < 2))
    def _():
        back(expert, 0, rows)

    @pl.when(jnp.logical_and(expert >= 2, expert < 4))
    def _():
        back(expert, 0, DSLOT)

    @pl.when(expert >= 4)
    def _():
        back(expert - 2, DSLOT, rows - DSLOT)

    def exact(select, x):
        high, low = split_low(x)
        return dot(select, high, 1, 1) + dot(select, low, 1, 1)

    @pl.when(expert == 5)
    def _():
        low = ing[...].astype(BF)
        proj = dot(emb[...], low, 1, 1).astype(BF)
        feat_grad = dot(feat[...], low, 1, 1)
        for c in range(rows // HALF):
            cols = slice(c * HALF, (c + 1) * HALF)
            emb[:, cols] = dot(projw_ref[...], low[:, cols], 1, 0).astype(BF)
        put = pltpu.make_async_copy(emb, emb_grad_ref, emb_sem)
        put.start()
        unit = act.at[:, :, :, 0:256]
        act[:, :, :, 0:256] = jnp.zeros((4, 4, 256, 256), BF)
        spots = [ids_ref[15 + q] for q in range(4)]
        for q in range(4):
            part = proj[q * 160 : (q + 1) * 160]
            act[spots[q], 2, 0:160, 0:256] = part[:, 0:256]
            act[spots[q], 2, 160:256, 0:256] = part[0:96, 256:512]
            act[spots[q], 3, 0:64, 0:256] = part[96:160, 256:512]
        for dom in range(2):
            d = ids_ref[12 + dom]
            tower = tin_acc[dom].astype(BF)
            act[ids_ref[15 + d // 2], d % 2, :, 0:128] = tower[0:256]
            act[ids_ref[15 + d // 2], d % 2, :, 128:256] = tower[256:512]
            g = gate_acc[dom]
            g = g[0:8] + g[8:16]
            place = pl.ds(pl.multiple_of(d * 16, 16), 16)
            act[spots[3], 1, place, 0:256] = jnp.concatenate([g[:, 0:256], g[:, 256:512]], axis=0).astype(BF)
        act[spots[3], 0, 0:128, 0:256] = feat_grad[0:128, 0:256].astype(BF)
        act[spots[3], 0, 128:256, 0:256] = feat_grad[0:128, 256:512].astype(BF)
        total = 0.0
        for e in range(6):
            total = total + exact(row_of(16, ids_ref[e]), gain_acc[e])
        offset = 0.0
        misc_a = misc_b = 0.0
        line = iota((16, 128), 0)
        lane = iota((16, 128), 1)
        for dom in range(2):
            col = iota((16, 16), 1)
            ident = col % 4
            for k in range(4):
                ident = jnp.where(col % 4 == k, expert_of(dom, k), ident)
            choose = jnp.logical_and(ident == iota((16, 16), 0), col < 8).astype(BF)
            offset = offset + exact(choose, shift_acc[dom])
            d = ids_ref[12 + dom]
            misc_a = misc_a + exact(row_of(16, d), tbias_acc[dom])
            misc_b = misc_b + exact(row_of(16, d), tout_acc[dom])
            bias = jnp.sum(tob_acc[dom, 0:1, :], axis=1, keepdims=True)
            misc_a = misc_a + jnp.where(jnp.logical_and(line == 8, lane == d), bias, 0.0)
        misc = jnp.concatenate([misc_a, misc_b], axis=1)
        line = iota((16, 256), 0)
        misc = misc + jnp.where(line == 6, feat_grad[128:129, 0:256], 0.0)
        misc = misc + jnp.where(line == 7, feat_grad[128:129, 256:512], 0.0)
        for at, x in ((GAIN_AT, total), (SHIFT_AT, offset)):
            act[spots[3], 1, at - 256 : at - 240, 0:256] = x[:, 0:256].astype(BF)
            act[spots[3], 1, at - 240 : at - 224, 0:256] = x[:, 256:512].astype(BF)
        act[spots[3], 1, MISC_AT - 256 : MISC_AT - 240, 0:256] = misc.astype(BF)
        out = pltpu.make_async_copy(unit, extra_ref, extra_sem)
        out.start()
        out.wait()
        put.wait()


def dense(ids, emb, feats, every, mask, label, projw, featw, bias, ups, downs, gains, shifts, gate, tin, tower):
    rows = emb.shape[1]

    def ahead(i):
        c, j = i // 4, i % 4
        front = jnp.where(j < 2, j, jnp.where(c < 2, j, j + 2))
        return jnp.where(i < 12, front, i - 12)

    def whole(x):
        return pl.BlockSpec(x.shape, lambda i, ids: (0,) * len(x.shape), pipeline_mode=pl.Buffered(1))

    any_space = pl.BlockSpec(memory_space=pl.ANY)
    in_specs = [any_space] + [whole(x) for x in (feats, every, mask, label, projw, featw, bias)]
    for group in (ups, downs):
        block = group[0].shape[1:]
        in_specs += [
            pl.BlockSpec((1,) + block, lambda i, ids: (ids[ahead(i)], 0, 0)),
            pl.BlockSpec((1,) + block, lambda i, ids: (ids[6 + ahead(i)], 0, 0)),
            pl.BlockSpec((2, 1) + block, lambda i, ids: (0, ahead(i), 0, 0)),
        ]
    in_specs += [whole(gains), whole(shifts)]
    for x in (gate, tin):
        for dom in range(2):
            in_specs.append(
                pl.BlockSpec(
                    (1,) + x.shape[1:], lambda i, ids, at=12 + dom: (ids[at], 0, 0), pipeline_mode=pl.Buffered(1)
                )
            )
    in_specs.append(whole(tower))
    return pl.pallas_call(
        dense_kernel,
        grid_spec=pltpu.PrefetchScalarGridSpec(
            num_scalar_prefetch=1,
            grid=(18,),
            in_specs=in_specs,
            out_specs=[
                pl.BlockSpec((1, rows), lambda i, ids: (0, 0)),
                pl.BlockSpec((1, 4, 2 * D, 256), lambda i, ids: (jnp.maximum(i - 12, 0), 0, 0, 0)),
                any_space,
                any_space,
            ],
            scratch_shapes=[
                pltpu.VMEM((D, rows), BF),
                pltpu.VMEM((4, 4, 256, rows), BF),
                pltpu.VMEM((4, 4, 256, rows), BF),
                pltpu.VMEM((4, D, HALF), F32),
                pltpu.VMEM((4, D, rows), BF),
                pltpu.VMEM((D, rows), F32),
                pltpu.VMEM((D, HALF), BF),
                pltpu.VMEM((D, HALF), F32),
                pltpu.VMEM((16, HALF), F32),
                pltpu.VMEM((16, HALF), F32),
                pltpu.VMEM(emb.shape, BF),
                pltpu.VMEM((144, rows), BF),
                pltpu.VMEM((144, D), BF),
                pltpu.VMEM((6, D, 128), BF),
                pltpu.VMEM((2, 16, D), BF),
                pltpu.VMEM((2, 16, D), BF),
                pltpu.VMEM((2, 16, D), BF),
                pltpu.VMEM((2, D, 128), BF),
                pltpu.VMEM((2, 128, 128), F32),
                pltpu.VMEM((2, 128, 128), F32),
                pltpu.VMEM((2, 16, 128), F32),
                pltpu.VMEM((6, D, 128), F32),
                pltpu.VMEM((2, D, 16), F32),
                pltpu.VMEM((2, 16, D), F32),
                pltpu.VMEM((2, D, 128), F32),
                pltpu.VMEM((2, 128, 128), F32),
                pltpu.VMEM((2, 128, 128), F32),
                pltpu.VMEM((2, 8, 128), F32),
                pltpu.SemaphoreType.DMA,
                pltpu.SemaphoreType.DMA,
            ],
        ),
        out_shape=[
            jax.ShapeDtypeStruct((1, rows), F32),
            jax.ShapeDtypeStruct((6, 4, 2 * D, 256), BF),
            jax.ShapeDtypeStruct(emb.shape, BF),
            jax.ShapeDtypeStruct((4, 4, 256, 256), BF),
        ],
        compiler_params=pltpu.CompilerParams(vmem_limit_bytes=62 * 2**20),
        cost_estimate=pl.CostEstimate(flops=39 * 10**9, bytes_accessed=60 * 2**20, transcendentals=0),
        name="dense_all",
    )(ids, emb, feats, every, mask, label, projw, featw, bias, *ups, *downs, gains, shifts, gate, gate, tin, tin, tower)


def finish_kernel(with_rows, ids_ref, sums_ref, unit_ref, others_ref, *refs):
    if with_rows:
        back_ref, row_ref = refs[0], refs[1]
        refs = refs[2:]
    (up_ref, down_ref, proj_ref, feat_ref, bias_ref, gain_ref, shift_ref, gate_ref, tin_ref, tbias_ref,
     tout_ref, tob_ref, quarters) = refs
    step = pl.program_id(0)
    up_ref[0] = sums_ref[0, 0, 0:D, :].astype(F32)
    down_ref[0, :, 0:256] = sums_ref[0, 0, D : D + 256, :].astype(F32)
    down_ref[0, :, 256:512] = sums_ref[0, 0, D + 256 : D + 512, :].astype(F32)
    if with_rows:
        @pl.when(step < with_rows)
        def _():
            row_ref[0, 0] = back_ref[0].astype(F32)

    @pl.when(step == 0)
    def _():
        me = ids_ref[14]
        quarters[me] = unit_ref[0, 0, 0:REP_ROWS, :].astype(F32)
        for i in range(3):
            quarters[ids_ref[15 + i]] = others_ref[i].astype(F32)
        cols = proj_ref.shape[0]
        proj_ref[:, 0:256] = unit_ref[0, 0, REP_ROWS : REP_ROWS + cols, :].astype(F32)
        proj_ref[:, 256:512] = unit_ref[0, 0, REP_ROWS + cols : REP_ROWS + 2 * cols, :].astype(F32)
        for d in range(DOMAINS):
            band = slice((d % 2) * 256, (d % 2) * 256 + 256)
            tin_ref[d, 0:256, :] = quarters[d // 2, band, 0:128]
            tin_ref[d, 256:512, :] = quarters[d // 2, band, 128:256]
            g = quarters[3, GATE_AT + 16 * d : GATE_AT + 16 * d + 16, :]
            g = jnp.concatenate([g[0:8], g[8:16]], axis=1)
            gate_ref[d] = g[0:6]
        feat_ref[:, 0:256] = quarters[3, 0:128, :]
        feat_ref[:, 256:512] = quarters[3, 128:256, :]
        for at, ref in ((GAIN_AT, gain_ref), (SHIFT_AT, shift_ref)):
            ref[:, 0:256] = quarters[3, at : at + 14, :]
            ref[:, 256:512] = quarters[3, at + 16 : at + 30, :]
        tbias_ref[...] = quarters[3, MISC_AT : MISC_AT + 6, 0:128]
        tout_ref[...] = quarters[3, MISC_AT : MISC_AT + 6, 128:256]
        bias_ref[:, 0:256] = quarters[3, MISC_AT + 6 : MISC_AT + 7, :]
        bias_ref[:, 256:512] = quarters[3, MISC_AT + 7 : MISC_AT + 8, :]
        tob_ref[...] = quarters[3, MISC_AT + 8 : MISC_AT + 9, 0:128]


def finish(ids, sums, others, proj_cols, back=None):
    def whole(s):
        return pl.BlockSpec(s, lambda i, ids: (0,) * len(s))

    def unit(i, ids):
        return (ids[i] % 16, ids[i] // 16, 0, 0)

    in_specs = [
        pl.BlockSpec((1, 1, ROWS_U, LANES), unit),
        pl.BlockSpec((1, 1, ROWS_U, LANES), lambda i, ids: (6, 0, 0, 0)),
        whole(others.shape),
    ]
    args = [sums, sums, others]
    shapes = [
        (14, D, 256), (14, 256, D), (proj_cols, D), (DENSE, D), (1, D), (14, D), (14, D), (DOMAINS, 6, D),
        (DOMAINS, D, 128), (DOMAINS, 128), (DOMAINS, 128), (1, 128),
    ]
    out_specs = [
        pl.BlockSpec((1, D, 256), lambda i, ids: (i, 0, 0)),
        pl.BlockSpec((1, 256, D), lambda i, ids: (i, 0, 0)),
    ] + [whole(s) for s in shapes[2:]]
    if back is not None:
        blocks, cols, cap = back.shape
        last = lambda i: jnp.minimum(i, blocks - 1)
        args.append(back)
        in_specs.append(pl.BlockSpec((1, cols, cap), lambda i, ids: (last(i), 0, 0)))
        shapes.insert(0, (1, blocks, cols, cap))
        out_specs.insert(0, pl.BlockSpec((1, 1, cols, cap), lambda i, ids: (0, last(i), 0, 0)))
    return pl.pallas_call(
        functools.partial(finish_kernel, 0 if back is None else back.shape[0]),
        grid_spec=pltpu.PrefetchScalarGridSpec(
            num_scalar_prefetch=1,
            grid=(14,),
            in_specs=in_specs,
            out_specs=out_specs,
            scratch_shapes=[pltpu.VMEM((4, REP_ROWS, LANES), F32)],
        ),
        out_shape=[jax.ShapeDtypeStruct(s, F32) for s in shapes],
        compiler_params=pltpu.CompilerParams(vmem_limit_bytes=VMEM),
        cost_estimate=pl.CostEstimate(flops=0, bytes_accessed=32 * 2**20, transcendentals=0),
        name="finish",
    )(ids, *args)


def shards(
    embed_table,
    requests,
    slot_index,
    event_mask,
    labels,
    dense_feats,
    proj_weight,
    dense_weight,
    proj_bias,
    up_weight,
    down_weight,
    norm_gain,
    norm_shift,
    gate_weight,
    tower_in,
    tower_bias,
    tower_out,
    tower_out_bias,
):
    narrow = lax.axis_size("narrow")
    me = lax.axis_index("narrow")
    chip, core = me // 2, me % 2
    ev_rows, fields = slot_index.shape
    rows = ev_rows // narrow
    owners, cap = requests.shape[1], requests.shape[2]
    hid_here = up_weight.shape[2]
    other_chip = [(i, i ^ 2) for i in range(narrow)]
    other_core = [(i, i ^ 1) for i in range(narrow)]
    full = 3 * chip + 2 * core
    half = 3 * chip + 1

    def swap(x, pairs):
        return lax.ppermute(x, "narrow", pairs)

    def chip_experts(w, which):
        return jnp.concatenate(
            [w[:SHARED], lax.dynamic_slice_in_dim(w, SHARED + 6 * which, 6, axis=0)], axis=0
        )

    def bring(w):
        far = swap(chip_experts(w, 1 - chip), other_chip)
        at = lambda x, start, size: lax.dynamic_slice_in_dim(x, start, size, axis=0)
        base = SHARED + 6 * chip
        away = 4 * (1 - core)
        theirs = jnp.stack(
            [
                jnp.concatenate([w[:SHARED], at(w, base + away, 2), at(w, base + 2, 2)], axis=0),
                jnp.concatenate([far[:SHARED], at(far, 2 + away, 2), far[4:6]], axis=0),
            ]
        )
        return w, far, swap(theirs, other_core)

    six = jnp.arange(6, dtype=jnp.int32)
    spot = jnp.where(six < 2, six, jnp.where(six < 4, six + 4 * core, six))
    offset = jnp.arange(narrow, dtype=jnp.int32)
    offset = jnp.where(chip == 1, (offset + 2) % 4, offset)
    offset = jnp.where(core == 1, offset + 1 - 2 * (offset % 2), offset)
    ids = jnp.concatenate(
        [
            jnp.where(six < 2, six, spot + 6 * chip),
            spot,
            jnp.stack([full, half, core]),
            (offset % 2) * 2 + offset // 2,
        ]
    ).astype(jnp.int32)
    mask_row, label_row = event_mask[None], labels[None]

    turn = lambda i: (i // 3) * 3 + (i % 3 + (i // 3) % 2) % 3
    table_rows = embed_table.shape[0]
    cols = fields * EMB
    blocks = ev_rows // HALF
    hi_n = 256
    lo_n = ev_rows // hi_n
    direct = cap % hi_n == 0
    asked = requests[0].transpose(0, 2, 1)
    if direct:
        embedded, far_up, far_down, their_up, their_down, proj_full, every = front(
            asked, embed_table.T, slot_index.T, dense_feats, mask_row, up_weight, down_weight, proj_weight
        )
        ups, downs = (up_weight, far_up, their_up), (down_weight, far_down, their_down)
    else:
        asked = lax.all_to_all(asked, "wide", 0, 0, tiled=True)
        ups, downs = bring(up_weight), bring(down_weight)
        proj_full = lax.all_gather(proj_weight, "narrow", axis=0)
        stats = local_stats(core[None], dense_feats, mask_row)
        stats = jnp.concatenate([stats, swap(stats, other_core)], axis=0)
        every = lax.all_to_all(
            jnp.broadcast_to(stats, (owners,) + stats.shape), "wide", 0, 0, tiled=True
        )
        tab = embed_table.reshape(32, table_rows // 32, cols).transpose(0, 2, 1)
        flat = asked.transpose(1, 0, 2).reshape(fields, DOMAINS, DSLOT).transpose(1, 0, 2)
        found = lookup(flat, tab, table_rows // 32, "lookup_rows", DOMAINS)
        found = found.transpose(1, 0, 2).reshape(cols, owners, cap).transpose(1, 0, 2)
        received = lax.all_to_all(found, "wide", 0, 0, tiled=True)
        received = received.transpose(1, 0, 2).reshape(cols, lo_n, hi_n).transpose(1, 0, 2)
        slots = slot_index.reshape(blocks, HALF, fields).transpose(0, 2, 1)
        embedded = lookup(slots, received, hi_n, "order_rows", narrow, turn)
        embedded = lax.all_to_all(embedded, "narrow", 0, 0, tiled=True)
    embedded = embedded.reshape(narrow * cols, rows)
    proj_full = proj_full.reshape(narrow * cols, D)

    tower = jnp.concatenate(
        [tower_bias, tower_out, jnp.pad(tower_out_bias[None], ((0, 3), (0, 128 - DOMAINS)))], axis=0
    )
    logits, own, embed_grad, extra = dense(
        ids, embedded, dense_feats, every, mask_row, label_row, proj_full, dense_weight, proj_bias[None],
        ups, downs, norm_gain, norm_shift, gate_weight.transpose(0, 2, 1), tower_in, tower,
    )
    extra = extra.reshape(narrow, ROWS_U, LANES)

    embed_grad = embed_grad.reshape(narrow, cols, rows)
    if not direct:
        embed_grad = lax.all_to_all(embed_grad, "narrow", 0, 0, tiled=True)
        returned = place(slot_index.T, embed_grad, (lo_n, cols, hi_n))
        returned = returned.transpose(1, 0, 2).reshape(cols, owners, cap).transpose(1, 0, 2)
        row_grads = lax.all_to_all(returned, "wide", 0, 0, tiled=True)

    if direct:
        sums, others, row_grads = reduce_all(own, extra, owners, REP_ROWS, (slot_index.T, embed_grad, cap))
    else:
        sums, others = reduce_all(own, extra, owners, REP_ROWS)
    expert = jnp.arange(14, dtype=jnp.int32)
    domain = (expert - SHARED) // DOM_EXP
    unit = jnp.where(domain % 3 == 0, 0, jnp.where(domain % 3 == 1, 4, 2)) + expert % 2
    away = jnp.where(domain // 3 == chip, 0, 16)
    unit = jnp.where(expert < SHARED, expert + 7, unit + away)
    marks = jnp.concatenate([unit, jnp.stack([me, me + 1 - 2 * core, me + 2 - 4 * chip, 3 - me])])
    outs = finish(marks.astype(jnp.int32), sums, others, cols, row_grads if direct else None)
    if not direct:
        outs = [row_grads.astype(F32)[None]] + list(outs)
    (row_grads, up_grad, down_grad, proj_grad, feat_grad, bias_grad, gain_grad, shift_grad, gate_grad, tower_grad,
     tower_bias_grad, tower_out_grad, out_bias_grad) = outs
    return (
        logits[0],
        row_grads.transpose(0, 1, 3, 2),
        proj_grad,
        feat_grad,
        bias_grad[0],
        up_grad,
        down_grad,
        gain_grad,
        shift_grad,
        gate_grad.transpose(0, 2, 1),
        tower_grad,
        tower_bias_grad,
        tower_out_grad,
        out_bias_grad[0, :DOMAINS],
    )


def solution(mesh):
    placed = (
        P("wide", "narrow"),
        P("wide", None, None, "narrow"),
        P("wide", "narrow"),
        P(("wide", "narrow")),
        P(("wide", "narrow")),
        P(("wide", "narrow"), None),
        P("narrow", None),
        P(),
        P(),
        P(None, None, "narrow"),
        P(None, "narrow", None),
        P(),
        P(),
        P(),
        P(),
        P(),
        P(),
        P(),
    )
    return jax.shard_map(
        shards,
        mesh=mesh,
        in_specs=placed,
        out_specs=(
            P(("wide", "narrow")),
            P("wide", None, None, "narrow"),
            P("narrow", None),
            P(),
            P(),
            P(None, None, "narrow"),
            P(None, "narrow", None),
            P(),
            P(),
            P(),
            P(),
            P(),
            P(),
            P(),
        ),
        check_vma=False,
    )
```

```python
import functools

import jax
import jax.numpy as jnp
from jax import lax
from jax.experimental import pallas as pl
from jax.experimental.pallas import tpu as pltpu
from jax.sharding import PartitionSpec as P

D = 512
HID = 1024
EMB = 16
DENSE = 128
DOMAINS = 6
SHARED = 2
DOM_EXP = 2
DSLOT = 1024
HALF = DSLOT // 2
VMEM = 56 * 2**20
BF = jnp.bfloat16
F32 = jnp.float32
MESH = pl.DeviceIdType.MESH
UNITS = 9
TURNED = 4
TOGETHER = 2
ROW_AT = 5
ROW_STEP = 1
ROWS_U = 1024
LANES = 256


def dot(a, b, ca, cb):
    return lax.dot_general(a, b, (((ca,), (cb,)), ((), ())), preferred_element_type=F32)


def lookup_kernel(lo_n, hi_n, fields, idx_ref, tab_ref, out_ref):
    length = idx_ref.shape[-1]
    shift = hi_n.bit_length() - 1
    for f in range(fields):
        idx = idx_ref[0, f : f + 1, :]
        hi = jnp.where(idx >= 0, idx & (hi_n - 1), -1)
        lo = lax.shift_right_logical(jnp.maximum(idx, 0), shift)
        hot = (lax.broadcasted_iota(jnp.int32, (hi_n, length), 0) == hi).astype(BF)
        cols = slice(f * EMB, (f + 1) * EMB)
        parts = [
            tab_ref[:, cols, j * hi_n : (j + 1) * hi_n].reshape(-1, hi_n) for j in range(tab_ref.shape[2] // hi_n)
        ]
        res = jnp.dot(jnp.concatenate(parts, axis=0), hot, preferred_element_type=F32)
        acc = res[0:EMB]
        for step in range(1, lo_n):
            acc = jnp.where(lo == step, res[step * EMB : (step + 1) * EMB], acc)
        out_ref[0, cols, :] = acc.astype(BF)


def lookup(idx, tab, hi_n, name, out_groups, order=lambda i: i):
    groups, fields, length = idx.shape
    outer, cols, inner = tab.shape
    lo_n = outer * inner // hi_n
    each = groups // out_groups
    return pl.pallas_call(
        functools.partial(lookup_kernel, lo_n, hi_n, fields),
        grid=(groups,),
        in_specs=[
            pl.BlockSpec((1, fields, length), lambda i: (order(i), 0, 0)),
            pl.BlockSpec(tab.shape, lambda i: (0, 0, 0)),
        ],
        out_specs=pl.BlockSpec((1, cols, length), lambda i: (i // each, 0, i % each)),
        out_shape=jax.ShapeDtypeStruct((out_groups, cols, length * each), BF),
        compiler_params=pltpu.CompilerParams(vmem_limit_bytes=VMEM),
        cost_estimate=pl.CostEstimate(
            flops=2 * groups * length * cols * lo_n * hi_n, bytes_accessed=8 * 2**20, transcendentals=0
        ),
        name=name,
    )(idx, tab)


def quarter_slots(slot_ref, q, field):
    half = slot_ref.shape[1] // 12
    parts = []
    for c in range(3):
        at = q * 3 * half + ((c + q % 2) % 3) * half
        at = at if isinstance(at, int) else pl.multiple_of(at, half)
        parts.append(slot_ref[pl.ds(field, 1), pl.ds(at, half)])
    return jnp.concatenate(parts, axis=1)


def place_one(idx_ref, grad_ref, out_ref, field):
    outer, _, inner = out_ref.shape
    length = grad_ref.shape[2]
    hi_n = 256
    lo_n = outer * inner // hi_n
    cols = pl.ds(pl.multiple_of(field * EMB, EMB), EMB)
    total = None
    for s in range(grad_ref.shape[0]):
        idx = quarter_slots(idx_ref, s, field)
        hi = idx & (hi_n - 1)
        lo = lax.shift_right_logical(idx, hi_n.bit_length() - 1)
        grad = grad_ref[s, cols, :]
        hot = (lax.broadcasted_iota(jnp.int32, (hi_n, length), 0) == hi).astype(BF)
        lhs = jnp.concatenate(
            [jnp.where(lo == step, grad, jnp.zeros_like(grad)) for step in range(lo_n)], axis=0
        )
        part = dot(lhs, hot, 1, 1)
        total = part if total is None else total + part
    total = total.astype(BF)
    each = inner // hi_n
    for i in range(outer * each):
        out_ref[i // each, cols, (i % each) * hi_n : (i % each + 1) * hi_n] = total[i * EMB : (i + 1) * EMB]


def place_kernel(idx_ref, grad_ref, out_ref):
    def one(field, _):
        place_one(idx_ref, grad_ref, out_ref, field)
        return 0

    lax.fori_loop(0, idx_ref.shape[0], one, 0)


def place(idx, grad, out_shape):
    return pl.pallas_call(
        place_kernel,
        out_shape=jax.ShapeDtypeStruct(out_shape, BF),
        compiler_params=pltpu.CompilerParams(vmem_limit_bytes=VMEM),
        name="place_rows",
    )(idx, grad)


def own_stats(feats_ref, mask_ref, out_ref, core):
    highest = lax.Precision.HIGHEST

    def block(c):
        at = pl.ds(pl.multiple_of(((c + core) % 3) * HALF, HALF), HALF)
        weight = jnp.broadcast_to(mask_ref[:, at].astype(F32), (8, HALF))
        return feats_ref[at, :], weight

    def total(weight, x):
        return jnp.dot(weight, x, preferred_element_type=F32, precision=highest)[0:1]

    for row, chunks in ((0, (0, 1)), (3, (2,))):
        count = sum(jnp.sum(block(c)[1][0:1], axis=1, keepdims=True) for c in chunks)
        mean = sum(total(block(c)[1], block(c)[0]) for c in chunks) / jnp.maximum(count, 1.0)
        off = lambda c: block(c)[0] - mean
        out_ref[row : row + 1, :] = mean
        out_ref[row + 1 : row + 2, :] = sum(total(block(c)[1], off(c) * off(c)) for c in chunks)
        out_ref[row + 2 : row + 3, :] = jnp.broadcast_to(count, mean.shape)


def stats_kernel(core_ref, feats_ref, mask_ref, out_ref):
    out_ref[...] = jnp.zeros_like(out_ref)
    own_stats(feats_ref, mask_ref, out_ref, core_ref[0])


def local_stats(core, feats, mask):
    return pl.pallas_call(
        stats_kernel,
        in_specs=[pl.BlockSpec(memory_space=pltpu.SMEM)] + [pl.BlockSpec(memory_space=pltpu.VMEM)] * 2,
        out_shape=jax.ShapeDtypeStruct((8, DENSE), F32),
        compiler_params=pltpu.CompilerParams(vmem_limit_bytes=VMEM),
        name="local_stats",
    )(core, feats, mask)


def front_kernel(
    groups, req_ref, table_ref, slot_ref, feats_ref, mask_ref, up_ref, down_ref, proj_ref,
    emb_ref, far_up, far_down, their_up, their_down, proj_out, every_ref,
    asked, found, received, ordered, both,
    req_send, req_recv, row_send, row_recv, near_send, near_recv, keep_sem,
    far_send, far_recv, side_send, above_send, own_send, own_recv, their_send, their_recv, proj_send, proj_recv,
    stat_send, stat_recv,
):
    wide, me = lax.axis_index("wide"), lax.axis_index("narrow")
    chip, core = me // 2, me % 2
    owners, fields, cap = req_ref.shape
    share = fields // groups
    parity, upper = wide % 2, (wide // 2) % 2
    near = [{"narrow": me + 1 - 2 * core}, {"narrow": me + 2 - 4 * chip}, {"narrow": 3 - me}]
    near_at = [me + 1 - 2 * core, me + 2 - 4 * chip, 3 - me]
    peers = [None] + [{"wide": (wide + d) % owners} for d in range(1, owners)]
    side, above = {"wide": wide + 1 - 2 * parity}, {"wide": wide + 2 - 4 * upper}
    barrier = pltpu.get_barrier_semaphore()
    for mate in near + peers[1:]:
        pl.semaphore_signal(barrier, inc=1, device_id=mate, device_id_type=MESH)
    pl.semaphore_wait(barrier, len(near) + len(peers) - 1)

    def remote(src, dst, send, recv, mate):
        return pltpu.make_async_remote_copy(
            src_ref=src, dst_ref=dst, send_sem=send, recv_sem=recv, device_id=mate, device_id_type=MESH
        )

    def req_copy(d):
        return remote(req_ref.at[(wide + d) % owners], asked.at[wide], req_send.at[d], req_recv.at[d], peers[d])

    for d in range(1, owners):
        req_copy(d).start()
    mine = pltpu.make_async_copy(req_ref.at[wide], asked.at[wide], keep_sem.at[0])
    mine.start()

    weights = ((up_ref, far_up, their_up), (down_ref, far_down, their_down))

    def far_at(j, side_of):
        return jnp.where(j == 0, 4 + side_of + 2 * upper, 2 * (j - 1) + side_of)

    def far_copy(j, a):
        p = far_at(j, parity)
        expert = jnp.where(p < 2, p, 6 * (1 - chip) + p)
        return remote(weights[a][0].at[expert], weights[a][1].at[p], far_send.at[a, j], far_recv.at[a, p], near[1])

    def side_copy(j, a, side_of):
        p = far_at(j, side_of)
        view = weights[a][1].at[p]
        return remote(view, view, side_send.at[a, j], far_recv.at[a, p], side)

    def above_copy(i, a, half):
        p = 4 + i + 2 * half
        view = weights[a][1].at[p]
        return remote(view, view, above_send.at[a, i], far_recv.at[a, p], above)

    def own_copy(i, a):
        expert = jnp.where(i < 2, i, 6 * chip + jnp.where(i < 4, i + 4 * (1 - core), i))
        return remote(weights[a][0].at[expert], weights[a][2].at[0, i], own_send.at[a, i], own_recv.at[a, i], near[0])

    def their_copy(p, a):
        i = jnp.where(p < 6, p, p - 4)
        return remote(weights[a][1].at[p], weights[a][2].at[1, i], their_send.at[a, i], their_recv.at[a, i], near[0])

    def wanted(p):
        ends = jnp.logical_or(jnp.logical_and(p < 4, core == 1), jnp.logical_and(p >= 6, core == 0))
        return jnp.logical_or(jnp.logical_or(p < 2, jnp.logical_and(p >= 4, p < 6)), ends)

    def for_all(n, f):
        def body(i, _):
            for a in range(2):
                f(i, a)
            return 0

        lax.fori_loop(0, n, body, 0)


    for_all(3, lambda j, a: far_copy(j, a).start())

    def stat_core():
        return remote(both.at[pl.ds(0, 8)], both.at[pl.ds(8, 8)], stat_send.at[0], stat_recv.at[0], near[0])

    def stat_copy(d):
        return remote(both, every_ref.at[wide], stat_send.at[d], stat_recv.at[d], peers[d])

    both[0:8, :] = jnp.zeros((8, DENSE), F32)
    own_stats(feats_ref, mask_ref, both, core)
    stat_core().start()

    def proj_copy(i):
        return remote(proj_ref, proj_out.at[me], proj_send.at[i], proj_recv.at[i], near[i])

    def proj_pass():
        view = proj_out.at[near_at[1]]
        return remote(view, view, proj_send.at[2], proj_recv.at[2], near[0])

    def other_proj():
        proj_copy(1).wait_recv()
        proj_pass().start()

    keep_proj = pltpu.make_async_copy(proj_ref, proj_out.at[me], keep_sem.at[1])
    keep_proj.start()
    for i in range(2):
        proj_copy(i).start()
    for_all(6, lambda i, a: own_copy(i, a).start())
    stat_core().wait_recv()
    for d in range(1, owners):
        stat_copy(d).start()
    keep_stat = pltpu.make_async_copy(both, every_ref.at[wide], keep_sem.at[2])
    keep_stat.start()

    def pass_on(p):
        @pl.when(wanted(p))
        def _():
            for a in range(2):
                their_copy(p, a).start()

    def lift(j, side_of):
        @pl.when(j == 0)
        def _():
            for a in range(2):
                above_copy(side_of, a, upper).start()

    def far_step(j):
        for a in range(2):
            far_copy(j, a).wait_recv()
            side_copy(j, a, parity).start()
        lift(j, parity)
        pass_on(far_at(j, parity))

    def side_step(j):
        for a in range(2):
            side_copy(j, a, 1 - parity).wait_recv()
        lift(j, 1 - parity)
        pass_on(far_at(j, 1 - parity))

    def above_step(i):
        for a in range(2):
            above_copy(i, a, 1 - upper).wait_recv()
        pass_on(4 + i + 2 * (1 - upper))

    hi_n = 512
    lo_n = table_ref.shape[1] // hi_n

    def find(f, owner_idx):
        idx = asked[owner_idx, pl.ds(f, 1), :]
        hi = jnp.where(idx >= 0, idx & (hi_n - 1), -1)
        lo = lax.shift_right_logical(jnp.maximum(idx, 0), hi_n.bit_length() - 1)
        hot = (lax.broadcasted_iota(jnp.int32, (hi_n, cap), 0) == hi).astype(BF)
        cols = pl.ds(pl.multiple_of(f * EMB, EMB), EMB)
        part = jnp.concatenate([table_ref[cols, l * hi_n : (l + 1) * hi_n] for l in range(lo_n)], axis=0)
        res = jnp.dot(part, hot, preferred_element_type=F32)
        acc = res[0:EMB]
        for step in range(1, lo_n):
            acc = jnp.where(lo == step, res[step * EMB : (step + 1) * EMB], acc)
        return cols, acc.astype(BF)

    def group_rows(g):
        return pl.ds(pl.multiple_of(g * share * EMB, share * EMB), share * EMB)

    def row_copy(g, d, mate):
        rows = group_rows(g)
        return remote(
            found.at[(wide + d) % owners, rows], received.at[wide, rows], row_send.at[g, d], row_recv.at[g, d], mate
        )

    def look(g):
        @pl.when(g == 0)
        def _():
            for d in range(1, owners):
                req_copy(d).wait_recv()

        def some(i, _):
            ahead = [i * TOGETHER + e for e in range(TOGETHER)]
            for d in ahead:
                for k in range(share):
                    cols, block = find(g * share + k, (wide + d) % owners)
                    found[(wide + d) % owners, cols, :] = block
            for d in ahead:
                @pl.when(d > 0)
                def _():
                    row_copy(g, d, {"wide": (wide + d) % owners}).start()

            return 0

        lax.fori_loop(0, owners // TOGETHER, some, 0)
        received[wide, group_rows(g), :] = found[wide, group_rows(g), :]

    hi_e = 256
    outer = owners * cap // hi_e

    def near_copy(g, i):
        rows = group_rows(g)
        return remote(
            ordered.at[near_at[i], rows], emb_ref.at[me, rows], near_send.at[g, i], near_recv.at[g, i], near[i]
        )

    def keep_copy(g):
        rows = group_rows(g)
        return pltpu.make_async_copy(ordered.at[me, rows], emb_ref.at[me, rows], keep_sem.at[3 + g])

    def order(g):
        def arrive(d, _):
            row_copy(g, d, {"wide": (wide + d) % owners}).wait_recv()
            return 0

        lax.fori_loop(1, owners, arrive, 0)
        tables = []
        for k in range(share):
            cols = pl.ds(pl.multiple_of((g * share + k) * EMB, EMB), EMB)
            parts = [
                received[o, cols, j * hi_e : (j + 1) * hi_e] for o in range(owners) for j in range(cap // hi_e)
            ]
            tables.append((cols, jnp.concatenate(parts, axis=0)))

        def quarter(q):
            for k, (cols, table) in enumerate(tables):
                idx = quarter_slots(slot_ref, q, g * share + k)
                hi = idx & (hi_e - 1)
                lo = lax.shift_right_logical(idx, hi_e.bit_length() - 1)
                hot = (lax.broadcasted_iota(jnp.int32, (hi_e, idx.shape[1]), 0) == hi).astype(BF)
                res = jnp.dot(table, hot, preferred_element_type=F32)
                acc = res[0:EMB]
                for step in range(1, outer):
                    acc = jnp.where(lo == step, res[step * EMB : (step + 1) * EMB], acc)
                ordered[q, cols, :] = acc.astype(BF)

        for i in (2, 1, 0):
            quarter(near_at[i])
            near_copy(g, i).start()
        quarter(me)
        keep_copy(g).start()

    mine.wait()

    def tick(t, _):
        @pl.when(t < groups)
        def _():
            look(t)

        @pl.when(jnp.logical_and(t >= 1, t < 4))
        def _():
            far_step(t - 1)

        @pl.when(t >= 2)
        def _():
            order(t - 2)

        @pl.when(t == 3)
        def _():
            other_proj()

        @pl.when(jnp.logical_and(t >= 3, t < 6))
        def _():
            side_step(t - 3)

        @pl.when(t >= 5)
        def _():
            above_step(jnp.where(t == 5, parity, 1 - parity))

        return 0

    lax.fori_loop(0, groups + 2, tick, 0)

    for d in range(1, owners):
        req_copy(d).wait_send()
        stat_copy(d).wait()
    stat_core().wait_send()
    keep_stat.wait()
    keep_proj.wait()
    proj_copy(0).wait()
    proj_copy(1).wait_send()
    proj_pass().wait()

    def rows_left(g, _):
        def one(d, _):
            row_copy(g, d, {"wide": (wide + d) % owners}).wait_send()
            return 0

        lax.fori_loop(1, owners, one, 0)
        for i in range(3):
            near_copy(g, i).wait()
        keep_copy(g).wait()
        return 0

    lax.fori_loop(0, groups, rows_left, 0)

    def weights_left(j, a):
        far_copy(j, a).wait_send()
        side_copy(j, a, parity).wait_send()

    for_all(3, weights_left)
    for_all(2, lambda i, a: above_copy(i, a, upper).wait_send())
    for_all(6, lambda i, a: own_copy(i, a).wait())

    def passed(p, a):
        @pl.when(wanted(p))
        def _():
            their_copy(p, a).wait_send()

    for_all(8, passed)
    for_all(6, lambda i, a: their_copy(i, a).wait_recv())


def front(req, table, slots, feats, mask, up, down, proj, groups=5):
    owners, fields, cap = req.shape
    cols = fields * EMB
    quarters = 4
    rows = slots.shape[1] // quarters
    any_space, vmem = pl.BlockSpec(memory_space=pl.ANY), pl.BlockSpec(memory_space=pltpu.VMEM)
    dma = pltpu.SemaphoreType.DMA
    return pl.pallas_call(
        functools.partial(front_kernel, groups),
        in_specs=[vmem] * 5 + [any_space] * 3,
        out_specs=[any_space] * 7,
        out_shape=[
            jax.ShapeDtypeStruct((quarters, cols, rows), BF),
            jax.ShapeDtypeStruct((8,) + up.shape[1:], BF),
            jax.ShapeDtypeStruct((8,) + down.shape[1:], BF),
            jax.ShapeDtypeStruct((2, 6) + up.shape[1:], BF),
            jax.ShapeDtypeStruct((2, 6) + down.shape[1:], BF),
            jax.ShapeDtypeStruct((quarters,) + proj.shape, BF),
            jax.ShapeDtypeStruct((owners, 16, DENSE), F32),
        ],
        scratch_shapes=[
            pltpu.VMEM((owners, fields, cap), jnp.int32),
            pltpu.VMEM((owners, cols, cap), BF),
            pltpu.VMEM((owners, cols, cap), BF),
            pltpu.VMEM((quarters, cols, rows), BF),
            pltpu.VMEM((16, DENSE), F32),
            dma((owners,)),
            dma((owners,)),
            dma((groups, owners)),
            dma((groups, owners)),
            dma((groups, 3)),
            dma((groups, 3)),
            dma((3 + groups,)),
            dma((2, 3)),
            dma((2, 8)),
            dma((2, 3)),
            dma((2, 2)),
            dma((2, 6)),
            dma((2, 6)),
            dma((2, 6)),
            dma((2, 6)),
            dma((3,)),
            dma((3,)),
            dma((owners,)),
            dma((owners,)),
        ],
        compiler_params=pltpu.CompilerParams(collective_id=1, has_side_effects=True, vmem_limit_bytes=VMEM),
        cost_estimate=pl.CostEstimate(flops=45 * 10**9, bytes_accessed=40 * 2**20, transcendentals=0),
        name="front",
    )(req, table, slots, feats, mask, up, down, proj)


def reduce_kernel(bits, with_rows, own_ref, extra_ref, *refs):
    if with_rows:
        slot_ref, grad_ref, out_ref, rep_ref, back_ref = refs[:5]
        grads, placed, near_send, near_recv, far_send, far_recv, keep_sem = refs[-7:]
        refs = refs[5:-7]
    else:
        out_ref, rep_ref = refs[:2]
        refs = refs[2:]
    acc, stage_buf, halves, got, local_sem, send, recv, rep_send, rep_recv, out_sem = refs
    wide=lax.axis_index("wide"); me=lax.axis_index("narrow")
    chip=me//2; core=me%2
    block=ROWS_U>>bits
    mates=[{"narrow": me+1-2*core},{"narrow": me+2-4*chip}]
    pairs=[{"wide": wide+(1<<k)*(1-2*((wide//(1<<k))%2))} for k in range(bits)]
    far={"narrow": 3-me}
    barrier=pltpu.get_barrier_semaphore()
    owners=1<<bits
    others=[{"wide": (wide+d)%owners} for d in range(1,owners)] if with_rows else pairs
    for mate in mates+[far]+others:
        pl.semaphore_signal(barrier, inc=1, device_id=mate, device_id_type=MESH)
    pl.semaphore_wait(barrier, len(others)+3)
    def power(k):
        return 1 << k, 1 << ((k + 1) % bits)

    def bit(u, k):
        here, there = power(k)
        return jnp.where(u == TURNED, (wide // there) % 2, (wide // here) % 2)

    def pair(u, k):
        here, there = power(k)
        step = jnp.where(u == TURNED, there, here)
        return {"wide": wide + step * (1 - 2 * bit(u, k))}

    def start_of(u, k):
        at = 0
        for j in range(k):
            at = at + bit(u, j) * (ROWS_U >> (j + 1))
        return pl.multiple_of(at, 16) if k else 0

    def copy(src, dst, s, u, mate):
        return pltpu.make_async_remote_copy(
            src_ref=src, dst_ref=dst, send_sem=send.at[s, u], recv_sem=recv.at[s, u], device_id=mate, device_id_type=MESH
        )

    def mine(u):
        return jnp.logical_or(u >= 4, jnp.where(u < 2, core == 0, core == 1))

    def theirs(u):
        return jnp.logical_or(u >= 4, jnp.where(u < 2, core == 1, core == 0))

    def domain_unit(u):
        return u < 6

    def local_at(u):
        return jnp.where(u < 2, u + 2, jnp.where(u < 6, u, u - 7))

    def core_copy(u, src):
        return copy(src, acc.at[u], 0, u, mates[0])

    def near_copy(u, src):
        return pltpu.make_async_copy(src, stage_buf.at[u % 2], local_sem.at[u % 2])

    def begin(u):
        @pl.when(u == 6)
        def _():
            core_copy(u, extra_ref.at[pl.ds(2, 2)]).start()
            near_copy(u, extra_ref.at[pl.ds(0, 2)]).start()

        @pl.when(jnp.logical_and(u != 6, mine(u)))
        def _():
            core_copy(u, own_ref.at[local_at(u), pl.ds(2, 2)]).start()
            near_copy(u, own_ref.at[local_at(u), pl.ds(0, 2)]).start()

    def add_region(u, sl, at, rows, src):
        tile = min(rows, 64)

        def body(i, _):
            r = pl.multiple_of(at + i * tile, 16)
            q = pl.multiple_of(i * tile, 16)
            for h in range(sl):
                a = acc[u, h, pl.ds(r, tile), :].astype(F32) + src[h, pl.ds(q, tile), :].astype(F32)
                acc[u, h, pl.ds(r, tile), :] = a.astype(BF)
            return 0

        lax.fori_loop(0, rows // tile, body, 0)

    half_at = [0]
    for k in range(bits):
        half_at.append(half_at[-1] + (ROWS_U >> (k + 1)))

    def half_view(u, k, parts):
        return halves.at[u, pl.ds(0, parts), pl.ds(half_at[k], ROWS_U >> (k + 1)), :]

    def send_half(u, k, parts):
        size = ROWS_U >> (k + 1)
        at = pl.multiple_of(start_of(u, k) + (1 - bit(u, k)) * size, 16)
        return copy(acc.at[u, pl.ds(0, parts), pl.ds(at, size), :], half_view(u, k, parts), 1 + k, u, pair(u, k))

    def take_half(u, k, parts):
        size = ROWS_U >> k
        copy(acc.at[u, pl.ds(0, parts), pl.ds(0, size), :], half_view(u, k - 1, parts), k, u, pair(u, k - 1)).wait_recv()
        add_region(u, parts, start_of(u, k), size, halves.at[u, :, pl.ds(half_at[k - 1], size), :])

    def y_whole(u):
        return copy(acc.at[u, 1], got.at[u, 1], bits + 1, u, mates[1])

    def y_block(u):
        at = start_of(u, bits)
        return copy(
            acc.at[u, 1, pl.ds(at, block), :], got.at[u, 1, pl.ds(at, block), :], bits + 1, u, mates[1]
        )

    def combine(u):
        @pl.when(theirs(u))
        def _():
            core_copy(u, acc.at[u]).wait_recv()

        @pl.when(mine(u))
        def _():
            near_copy(u, acc.at[u]).wait()
            sb = stage_buf.at[u % 2]

            @pl.when(theirs(u))
            def _():
                add_region(u, 2, 0, ROWS_U, sb)

            @pl.when(jnp.logical_not(theirs(u)))
            def _():
                def body(i, _):
                    r = pl.multiple_of(i * 64, 16)
                    for h in (0, 1):
                        acc[u, h, pl.ds(r, 64), :] = sb[h, pl.ds(r, 64), :]
                    return 0

                lax.fori_loop(0, ROWS_U // 64, body, 0)

    def grow_copy(u, j, parts):
        size = ROWS_U >> (j + 1)
        view = got.at[u, pl.ds(0, parts), pl.ds(start_of(u, j + 1), size), :]
        return copy(view, view, bits + 2 + (bits - 1 - j), u, pair(u, j))

    def out_copy(u, parts):
        return pltpu.make_async_copy(got.at[u, pl.ds(0, parts)], out_ref.at[u, pl.ds(0, parts)], out_sem.at[u])

    rep_mates = [mates[0], mates[1], far]
    rep_rows = rep_ref.shape[1]

    def rep_copy(i):
        return pltpu.make_async_remote_copy(
            src_ref=got.at[6, 0, pl.ds(0, rep_rows), :], dst_ref=rep_ref.at[i], send_sem=rep_send.at[i],
            recv_sem=rep_recv.at[i], device_id=rep_mates[i], device_id_type=MESH,
        )

    def by_kind(u, domain, shared):
        pl.when(domain_unit(u))(domain)
        pl.when(jnp.logical_not(domain_unit(u)))(shared)

    def start_grow(u):
        by_kind(u, lambda: grow_copy(u, bits - 1, 2).start(), lambda: grow_copy(u, bits - 1, 1).start())

    def stage_one(u):
        combine(u)
        by_kind(u, lambda: send_half(u, 0, 2).start(), lambda: y_whole(u).start())

    def halving(k, u):
        def domain():
            take_half(u, k, 2)
            if k < bits:
                send_half(u, k, 2).start()
            else:
                y_block(u).start()

        def shared():
            if k == 1:
                y_whole(u).wait_recv()
                add_region(u, 1, 0, ROWS_U, got.at[u, pl.ds(1, 1)])
            else:
                take_half(u, k - 1, 1)
            send_half(u, k - 1, 1).start()

        by_kind(u, domain, shared)

    def cross(u):
        at = start_of(u, bits)

        def domain():
            y_block(u).wait_recv()

        def shared():
            take_half(u, bits, 1)

        by_kind(u, domain, shared)
        got[u, 0, pl.ds(at, block), :] = acc[u, 0, pl.ds(at, block), :]
        start_grow(u)

    def grow(u, j):
        by_kind(u, lambda: grow_copy(u, j, 2).wait_recv(), lambda: grow_copy(u, j, 1).wait_recv())
        if j > 0:
            by_kind(u, lambda: grow_copy(u, j - 1, 2).start(), lambda: grow_copy(u, j - 1, 1).start())
        else:
            by_kind(u, lambda: out_copy(u, 2).start(), lambda: out_copy(u, 1).start())

            @pl.when(u == 6)
            def _():
                for i in range(3):
                    rep_copy(i).start()

    quarters=mates+[far]
    def quarter_at(i):
        return [me+1-2*core, me+2-4*chip, 3-me][i]
    def near_row_copy(i):
        return pltpu.make_async_remote_copy(src_ref=grad_ref.at[quarter_at(i)],dst_ref=grads.at[me],send_sem=near_send.at[i],recv_sem=near_recv.at[i],device_id=quarters[i],device_id_type=MESH)
    def keep_copy():
        return pltpu.make_async_copy(grad_ref.at[me],grads.at[me],keep_sem.at[0])
    def back_copy(d):
        return pltpu.make_async_remote_copy(src_ref=placed.at[(wide+d)%owners],dst_ref=back_ref.at[wide],send_sem=far_send.at[d],recv_sem=far_recv.at[d],device_id=others[d-1],device_id_type=MESH)
    def keep_back():
        return pltpu.make_async_copy(placed.at[wide],back_ref.at[wide],keep_sem.at[1])
    def place_field(f, _):
        place_one(slot_ref, grads, placed, f)
        return 0
    def row_step(t):
        fields=slot_ref.shape[0]
        @pl.when(t==ROW_AT)
        def _():
            keep_copy().wait()
            for i in range(3): near_row_copy(i).wait_recv()
        @pl.when(jnp.logical_and(t>=ROW_AT,t<ROW_AT+5))
        def _():
            lax.fori_loop((t-ROW_AT)*(fields//5),(t-ROW_AT+1)*(fields//5),place_field,0)
        for d in range(owners):
            @pl.when(t==ROW_AT+4+int(d*ROW_STEP))
            def _():
                if d==0: keep_back().start()
                else: back_copy(d).start()
    todo = [begin, stage_one]
    todo += [functools.partial(halving, k) for k in range(1, bits + 1)] + [cross]
    todo += [functools.partial(lambda j, u: grow(u, j), j) for j in reversed(range(bits))]
    plain_gaps = [0, 1, 2] + [1] * (len(todo) - 4) + [2]
    turned_gaps = [0, 1, 3, 4] + [1] * (len(todo) - 6) + [4, 3]
    plain_lag = [sum(plain_gaps[: i + 1]) for i in range(len(todo))]
    turned_lag = [sum(turned_gaps[: i + 1]) for i in range(len(todo))]

    def tick(t,_):
        for s in reversed(range(len(todo))):
            def stage(c, _):
                at = t - plain_lag[s]
                plain = jnp.where(at < 2, at + 4, jnp.where(at < 6, at - 2, at))
                u = jnp.where(c == 0, plain, TURNED)
                fits = jnp.logical_and(jnp.logical_and(at >= 0, at < UNITS), plain != TURNED)
                due = jnp.where(c == 0, fits, t == turned_lag[s])

                @pl.when(due)
                def _():
                    todo[s](u)

                return 0

            lax.fori_loop(0, 2, stage, 0)
        if with_rows:
            row_step(t)
        return 0
    if with_rows:
        keep_copy().start()
        for i in range(3): near_row_copy(i).start()
    lax.fori_loop(0, max(UNITS + plain_lag[-1], turned_lag[-1] + 1), tick, 0)
    if with_rows:
        keep_back().wait()
        for i in range(3): near_row_copy(i).wait_send()
        for d in range(1,owners): back_copy(d).wait()
    def finish(u,_):
        @pl.when(mine(u))
        def _():
            core_copy(u, acc.at[u]).wait_send()

        def left(parts):
            for k in range(bits):
                send_half(u, k, parts).wait_send()
            (y_block if parts == 2 else y_whole)(u).wait_send()
            for j in range(bits):
                grow_copy(u, j, parts).wait_send()
            out_copy(u, parts).wait()

        by_kind(u, lambda: left(2), lambda: left(1))
        return 0
    lax.fori_loop(0,UNITS,finish,0)
    for i in range(3):
        rep_copy(i).wait()

def reduce_all(own, extra, wide, rep_rows, rows=None):
    bits = wide.bit_length() - 1
    args = [own, extra]
    any_space = pl.BlockSpec(memory_space=pl.ANY)
    in_specs = [any_space] * 2
    out_shape = [
        jax.ShapeDtypeStruct((UNITS, 2, ROWS_U, LANES), BF),
        jax.ShapeDtypeStruct((3, rep_rows, LANES), BF),
    ]
    scratch = [
        pltpu.VMEM((UNITS, 2, ROWS_U, LANES), BF),
        pltpu.VMEM((2, 2, ROWS_U, LANES), BF),
        pltpu.VMEM((UNITS, 2, ROWS_U, LANES), BF),
        pltpu.VMEM((UNITS, 2, ROWS_U, LANES), BF),
        pltpu.SemaphoreType.DMA((2,)),
        pltpu.SemaphoreType.DMA((2 * bits + 2, UNITS)),
        pltpu.SemaphoreType.DMA((2 * bits + 2, UNITS)),
        pltpu.SemaphoreType.DMA((3,)),
        pltpu.SemaphoreType.DMA((3,)),
        pltpu.SemaphoreType.DMA((UNITS,)),
    ]
    if rows is not None:
        slots, grads, cap = rows
        args += [slots, grads]
        in_specs += [pl.BlockSpec(memory_space=pltpu.VMEM), any_space]
        back = (wide, grads.shape[1], cap)
        out_shape.append(jax.ShapeDtypeStruct(back, BF))
        scratch += [
            pltpu.VMEM(grads.shape, BF),
            pltpu.VMEM(back, BF),
            pltpu.SemaphoreType.DMA((3,)),
            pltpu.SemaphoreType.DMA((3,)),
            pltpu.SemaphoreType.DMA((wide,)),
            pltpu.SemaphoreType.DMA((wide,)),
            pltpu.SemaphoreType.DMA((2,)),
        ]
    return pl.pallas_call(
        functools.partial(reduce_kernel, bits, rows is not None),
        in_specs=in_specs,
        out_specs=[any_space] * len(out_shape),
        out_shape=out_shape,
        scratch_shapes=scratch,
        compiler_params=pltpu.CompilerParams(collective_id=0, has_side_effects=True, vmem_limit_bytes=VMEM),
        cost_estimate=pl.CostEstimate(flops=0, bytes_accessed=60 * 2**20, transcendentals=0),
        name="reduce_all",
    )(*args)


C0 = 0.7978845608028654
C1 = 0.044715
REP_ROWS = 512
GATE_AT = 256
GAIN_AT = 352
SHIFT_AT = 384
MISC_AT = 416


def gelu_both(x):
    square = x * x
    up = 0.5 * jnp.tanh(x * (square * (C0 * C1) + C0)) + 0.5
    act = x * up
    return act, up + (act - act * up) * (square * (6.0 * C0 * C1) + 2.0 * C0)


def soft_pair(a, b):
    top = jnp.maximum(a, b)
    ea, eb = jnp.exp(a - top), jnp.exp(b - top)
    total = ea + eb
    return ea / total, eb / total


def soft_pair_back(pa, pb, ga, gb):
    mean = pa * ga + pb * gb
    return pa * (ga - mean), pb * (gb - mean)


def fold(x):
    return sum(x[:, i * 128 : (i + 1) * 128] for i in range(x.shape[1] // 128))


def wide_lanes(x, n):
    return jnp.concatenate([x] * n, axis=1)


def split_low(x):
    high = x.astype(BF)
    return high, (x - high.astype(F32)).astype(BF)


def iota(shape, axis):
    return lax.broadcasted_iota(jnp.int32, shape, axis)


def row_of(rows, at):
    return (iota((rows, 128), 0) == at).astype(BF)


def dense_kernel(
    ids_ref, emb_ref, feats_ref, every_ref, mask_ref, label_ref, projw_ref, featw_ref, bias_ref,
    up_a, up_b, up_c, down_a, down_b, down_c, gain_ref, shift_ref, gate_f, gate_h, tin_f, tin_h,
    tower_ref,
    logit_ref, own_ref, emb_grad_ref, extra_ref,
    xt, act, slope, outs, og, ing, hid, hg, stat, inner, emb, feat, featw, gains, mixed, shifts, gates, tin,
    tbias, tout, tob, gain_acc, shift_acc, gate_acc, tin_acc, tbias_acc, tout_acc, tob_acc, emb_sem, extra_sem,
):
    ups = [up_a.at[0], up_b.at[0], up_c.at[0, 0], up_c.at[1, 0]]
    downs = [down_a.at[0], down_b.at[0], down_c.at[0, 0], down_c.at[1, 0]]
    step = pl.program_id(0)
    chunk, slot = step // 4, step % 4
    rows = xt.shape[1]
    core = ids_ref[14]
    owners = every_ref.shape[0]

    def expert_of(dom, k):
        return k if k < 2 else ids_ref[2 * dom + k]

    def raw_lanes(c):
        return pl.ds(pl.multiple_of(((c + core) % 3) * HALF, HALF), HALF)

    def pooled(sets):
        def sums(w, carry):
            total, mean = carry
            for at in sets:
                count = every_ref[w, at + 2 : at + 3, :]
                total, mean = total + count, mean + count * every_ref[w, at : at + 1, :]
            return total, mean

        zero = jnp.zeros((1, 128), F32)
        total, mean = lax.fori_loop(0, owners, sums, (zero, zero))
        mean = mean / total

        def squares(w, acc):
            for at in sets:
                off = every_ref[w, at : at + 1, :] - mean
                acc = acc + every_ref[w, at + 1 : at + 2, :] + every_ref[w, at + 2 : at + 3, :] * off * off
            return acc

        return mean, lax.rsqrt(lax.fori_loop(0, owners, squares, zero) / total + 1e-05)

    @pl.when(step == 0)
    def _():
        fetch = pltpu.make_async_copy(emb_ref, emb, emb_sem)
        fetch.start()
        for e in range(6):
            gains[e] = dot(gain_ref[...], row_of(14, ids_ref[e]), 0, 0).astype(BF)
        for dom, (gate, tower) in enumerate(((gate_f, tin_f), (gate_h, tin_h))):
            tin[dom] = tower[0]
            pick = (iota((16, 6), 0) % 8 == iota((16, 6), 1)).astype(BF)
            gates[dom] = dot(pick, gate[0], 1, 0).astype(BF)
            place = iota((16, 14), 0)
            ident = place % 4
            for k in range(4):
                ident = jnp.where(place % 4 == k, expert_of(dom, k), ident)
            same = ident == iota((16, 14), 1)
            first, second = jnp.logical_and(same, place < 4), jnp.logical_and(same, place < 8)
            third = jnp.logical_and(second, place >= 4)
            mixed[dom] = (
                dot(first.astype(BF), gain_ref[...], 1, 0) + dot(third.astype(BF), shift_ref[...], 1, 0)
            ).astype(BF)
            shifts[dom] = dot(second.astype(BF), shift_ref[...], 1, 0).astype(BF)
            d = ids_ref[12 + dom]
            tbias[dom] = dot(tower_ref[...], row_of(16, d), 0, 0)
            tout[dom] = dot(tower_ref[...], row_of(16, 6 + d), 0, 0)
            tob[dom] = dot(tower_ref[...], row_of(128, d), 1, 0)
        featw[0:128, :] = featw_ref[...]
        featw[128:144, :] = jnp.where(iota((16, D), 0) == 0, bias_ref[...].astype(F32), 0.0).astype(BF)
        feat[128:144, :] = (iota((16, rows), 0) == 0).astype(BF)
        moments = [pooled((0,)), pooled((3, 11))]
        for c in range(rows // HALF):
            mean, scale = moments[c // 2]
            x = (feats_ref[raw_lanes(c), :] - mean) * scale
            feat[0:128, c * HALF : (c + 1) * HALF] = x.T.astype(BF)
        for ref in (gain_acc, shift_acc, gate_acc, tin_acc, tbias_acc, tout_acc, tob_acc):
            ref[...] = jnp.zeros_like(ref)
        fetch.wait()
        for c in range(rows // HALF):
            cols = slice(c * HALF, (c + 1) * HALF)
            x = dot(projw_ref[...], emb[:, cols], 0, 0) + dot(featw[...], feat[:, cols], 0, 0)
            xt[:, cols] = x.astype(BF)

    @pl.when(step < 12)
    def _():
        lanes = pl.ds(pl.multiple_of(chunk * HALF, HALF), HALF)

        for s in range(4):
            pre = dot(ups[s][...], xt[:, lanes], 0, 0)
            a, g = gelu_both(pre)
            a = a.astype(BF)
            act[slot, s, :, lanes] = a
            slope[slot, s, :, lanes] = g.astype(BF)

        total = dot(downs[0][...], act[slot, 0, :, lanes], 0, 0)
        for s in range(1, 4):
            total += dot(downs[s][...], act[slot, s, :, lanes], 0, 0)
        outs[slot] = total

    def middle():
        lanes = pl.ds(pl.multiple_of(chunk * HALF, HALF), HALF)
        dom = chunk // 2
        x = xt[:, lanes]
        logit_gates = dot(gates[dom], x, 1, 0)
        s0, s1 = soft_pair(logit_gates[0:1], logit_gates[1:2])
        d0, d1 = soft_pair(logit_gates[2:3], logit_gates[3:4])
        t0, t1 = soft_pair(logit_gates[4:5], logit_gates[5:6])
        coef = jnp.concatenate([t0 * s0, t0 * s1, t1 * d0, t1 * d1], axis=0)
        high = coef.astype(BF).astype(F32)
        spare = jnp.zeros((8, HALF), F32)
        coef_low = jnp.concatenate([high, coef - high, spare], axis=0).astype(BF)
        hg[...] = dot(shifts[dom], coef_low, 0, 0)
        stat[8:12, :] = coef
        expert = [0, 1, 2 + 2 * dom, 3 + 2 * dom]

        def normalize(t, _):
            cols = pl.ds(pl.multiple_of(t * 128, 128), 128)
            for k in range(4):
                v = outs[k, :, cols]
                mean = jnp.sum(v, axis=0, keepdims=True) * (1.0 / D)
                v = v - mean
                var = jnp.sum(v * v, axis=0, keepdims=True) * (1.0 / D)
                stat[k : k + 1, cols] = mean
                stat[4 + k : 5 + k, cols] = lax.rsqrt(var + 1e-05)
            scale = [stat[4 + k : 5 + k, cols] * stat[8 + k : 9 + k, cols] for k in range(4)]
            for r in range(8):
                band = slice(r * 64, (r + 1) * 64)
                acc = hg[band, cols]
                for k in range(4):
                    n = (outs[k, band, cols] - stat[k : k + 1, cols]) * scale[k]
                    acc = acc + n * gains[expert[k], band, :].astype(F32)
                hid[band, cols] = acc.astype(BF)
            return 0

        lax.fori_loop(0, 4, normalize, 0)
        h = hid[...]
        pre = dot(tin[dom], h, 0, 0) + wide_lanes(tbias[dom], 4)
        tact, tslope = gelu_both(pre)
        weight = wide_lanes(tout[dom], 4)
        logit = jnp.sum(tact * weight, axis=0, keepdims=True) + wide_lanes(tob[dom, 12:13, :], 4)
        logit_ref[:, raw_lanes(chunk)] = logit
        live, label = mask_ref[:, raw_lanes(chunk)].astype(F32), label_ref[:, raw_lanes(chunk)].astype(F32)
        grad = (jax.nn.sigmoid(logit) - label) * live
        tob_acc[dom, 0:1, :] += fold(grad)
        tout_acc[dom] += fold(grad * tact)
        low = (grad * weight * tslope).astype(BF)
        tbias_acc[dom] += fold(low.astype(F32))
        tin_acc[dom] += dot(h, low, 1, 1)
        back = dot(tin[dom], low, 1, 0)
        hg[...] = back
        back_high, back_low = split_low(back)
        shift_acc[dom] += dot(back_high, coef_low, 1, 1) + dot(back_low, coef_low, 1, 1)
        inner[...] = dot(mixed[dom], back_high, 1, 0) + dot(mixed[dom], back_low, 1, 0)

        def denormalize(t, _):
            cols = pl.ds(pl.multiple_of(t * 128, 128), 128)
            place = pl.ds(pl.multiple_of(chunk * HALF + t * 128, 128), 128)
            for k in range(4):
                mean, rstd = stat[k : k + 1, cols], stat[4 + k : 5 + k, cols]
                c = stat[8 + k : 9 + k, cols]
                m2 = 0.0
                for r in range(8):
                    band = slice(r * 64, (r + 1) * 64)
                    w = (outs[k, band, cols] - mean) * rstd * hg[band, cols]
                    m2 = m2 + jnp.sum(w * gains[expert[k], band, :].astype(F32), axis=0, keepdims=True)
                    gain_acc[expert[k], band, :] += w * c
                m1 = inner[k : k + 1, cols]
                inner[4 + k : 5 + k, cols] += m2
                cr = c * rstd
                slant = cr * rstd * m2 * (1.0 / D)
                level = mean * slant - cr * m1 * (1.0 / D)
                for r in range(8):
                    band = slice(r * 64, (r + 1) * 64)
                    scaled = hg[band, cols] * gains[expert[k], band, :].astype(F32)
                    og[k, band, place] = (scaled * cr - outs[k, band, cols] * slant + level).astype(BF)
            return 0

        lax.fori_loop(0, 4, denormalize, 0)
        a = [inner[4 + k : 5 + k, :] for k in range(4)]
        g0, g1 = soft_pair_back(s0, s1, t0 * a[0], t0 * a[1])
        g2, g3 = soft_pair_back(d0, d1, t1 * a[2], t1 * a[3])
        g4, g5 = soft_pair_back(t0, t1, s0 * a[0] + s1 * a[1], d0 * a[2] + d1 * a[3])
        zero = jnp.zeros_like(g0)
        g = jnp.concatenate([g0, g1, g2, g3, g4, g5, zero, zero], axis=0)
        high = g.astype(BF).astype(F32)
        g = jnp.concatenate([high, g - high], axis=0).astype(BF)
        gate_acc[dom] += dot(g, x, 1, 1)
        ing[:, lanes] = dot(gates[dom], g, 0, 0)

    @pl.when(jnp.logical_and(step < 12, slot == 3))
    def _():
        middle()

    def back(k, at, n):
        lanes = slice(at, at + n)
        for s in range(4):
            p = dot(downs[s][...], og[k, :, lanes], 1, 0) * slope[k, s, :, lanes].astype(F32)
            slope[k, s, :, lanes] = p.astype(BF)

        for s in range(4):
            grad, p = og[k, :, lanes], slope[k, s, :, lanes]
            own_ref[0, s, 0:D, :] = dot(xt[:, lanes], p, 1, 1).astype(BF)
            d = dot(act[k, s, :, lanes], grad, 1, 1).astype(BF)
            own_ref[0, s, D : D + 256, :] = d[:, 0:256]
            own_ref[0, s, D + 256 : D + 512, :] = d[:, 256:512]

        for t in range(n // HALF):
            cols = slice(at + t * HALF, at + (t + 1) * HALF)
            total = dot(ups[0][...], slope[k, 0, :, cols], 1, 0)
            for s in range(1, 4):
                total += dot(ups[s][...], slope[k, s, :, cols], 1, 0)
            ing[:, cols] += total

    expert = step - 12

    @pl.when(jnp.logical_and(expert >= 0, expert < 2))
    def _():
        back(expert, 0, rows)

    @pl.when(jnp.logical_and(expert >= 2, expert < 4))
    def _():
        back(expert, 0, DSLOT)

    @pl.when(expert >= 4)
    def _():
        back(expert - 2, DSLOT, rows - DSLOT)

    def exact(select, x):
        high, low = split_low(x)
        return dot(select, high, 1, 1) + dot(select, low, 1, 1)

    @pl.when(expert == 5)
    def _():
        low = ing[...].astype(BF)
        proj = dot(emb[...], low, 1, 1).astype(BF)
        feat_grad = dot(feat[...], low, 1, 1)
        for c in range(rows // HALF):
            cols = slice(c * HALF, (c + 1) * HALF)
            emb[:, cols] = dot(projw_ref[...], low[:, cols], 1, 0).astype(BF)
        put = pltpu.make_async_copy(emb, emb_grad_ref, emb_sem)
        put.start()
        unit = act.at[:, :, :, 0:256]
        act[:, :, :, 0:256] = jnp.zeros((4, 4, 256, 256), BF)
        spots = [ids_ref[15 + q] for q in range(4)]
        for q in range(4):
            part = proj[q * 160 : (q + 1) * 160]
            act[spots[q], 2, 0:160, 0:256] = part[:, 0:256]
            act[spots[q], 2, 160:256, 0:256] = part[0:96, 256:512]
            act[spots[q], 3, 0:64, 0:256] = part[96:160, 256:512]
        for dom in range(2):
            d = ids_ref[12 + dom]
            tower = tin_acc[dom].astype(BF)
            act[ids_ref[15 + d // 2], d % 2, :, 0:128] = tower[0:256]
            act[ids_ref[15 + d // 2], d % 2, :, 128:256] = tower[256:512]
            g = gate_acc[dom]
            g = g[0:8] + g[8:16]
            place = pl.ds(pl.multiple_of(d * 16, 16), 16)
            act[spots[3], 1, place, 0:256] = jnp.concatenate([g[:, 0:256], g[:, 256:512]], axis=0).astype(BF)
        act[spots[3], 0, 0:128, 0:256] = feat_grad[0:128, 0:256].astype(BF)
        act[spots[3], 0, 128:256, 0:256] = feat_grad[0:128, 256:512].astype(BF)
        total = 0.0
        for e in range(6):
            total = total + exact(row_of(16, ids_ref[e]), gain_acc[e])
        offset = 0.0
        misc_a = misc_b = 0.0
        line = iota((16, 128), 0)
        lane = iota((16, 128), 1)
        for dom in range(2):
            col = iota((16, 16), 1)
            ident = col % 4
            for k in range(4):
                ident = jnp.where(col % 4 == k, expert_of(dom, k), ident)
            choose = jnp.logical_and(ident == iota((16, 16), 0), col < 8).astype(BF)
            offset = offset + exact(choose, shift_acc[dom])
            d = ids_ref[12 + dom]
            misc_a = misc_a + exact(row_of(16, d), tbias_acc[dom])
            misc_b = misc_b + exact(row_of(16, d), tout_acc[dom])
            bias = jnp.sum(tob_acc[dom, 0:1, :], axis=1, keepdims=True)
            misc_a = misc_a + jnp.where(jnp.logical_and(line == 8, lane == d), bias, 0.0)
        misc = jnp.concatenate([misc_a, misc_b], axis=1)
        line = iota((16, 256), 0)
        misc = misc + jnp.where(line == 6, feat_grad[128:129, 0:256], 0.0)
        misc = misc + jnp.where(line == 7, feat_grad[128:129, 256:512], 0.0)
        for at, x in ((GAIN_AT, total), (SHIFT_AT, offset)):
            act[spots[3], 1, at - 256 : at - 240, 0:256] = x[:, 0:256].astype(BF)
            act[spots[3], 1, at - 240 : at - 224, 0:256] = x[:, 256:512].astype(BF)
        act[spots[3], 1, MISC_AT - 256 : MISC_AT - 240, 0:256] = misc.astype(BF)
        out = pltpu.make_async_copy(unit, extra_ref, extra_sem)
        out.start()
        out.wait()
        put.wait()


def dense(ids, emb, feats, every, mask, label, projw, featw, bias, ups, downs, gains, shifts, gate, tin, tower):
    rows = emb.shape[1]

    def ahead(i):
        c, j = i // 4, i % 4
        front = jnp.where(j < 2, j, jnp.where(c < 2, j, j + 2))
        return jnp.where(i < 12, front, i - 12)

    def whole(x):
        return pl.BlockSpec(x.shape, lambda i, ids: (0,) * len(x.shape), pipeline_mode=pl.Buffered(1))

    any_space = pl.BlockSpec(memory_space=pl.ANY)
    in_specs = [any_space] + [whole(x) for x in (feats, every, mask, label, projw, featw, bias)]
    for group in (ups, downs):
        block = group[0].shape[1:]
        in_specs += [
            pl.BlockSpec((1,) + block, lambda i, ids: (ids[ahead(i)], 0, 0)),
            pl.BlockSpec((1,) + block, lambda i, ids: (ids[6 + ahead(i)], 0, 0)),
            pl.BlockSpec((2, 1) + block, lambda i, ids: (0, ahead(i), 0, 0)),
        ]
    in_specs += [whole(gains), whole(shifts)]
    for x in (gate, tin):
        for dom in range(2):
            in_specs.append(
                pl.BlockSpec(
                    (1,) + x.shape[1:], lambda i, ids, at=12 + dom: (ids[at], 0, 0), pipeline_mode=pl.Buffered(1)
                )
            )
    in_specs.append(whole(tower))
    return pl.pallas_call(
        dense_kernel,
        grid_spec=pltpu.PrefetchScalarGridSpec(
            num_scalar_prefetch=1,
            grid=(18,),
            in_specs=in_specs,
            out_specs=[
                pl.BlockSpec((1, rows), lambda i, ids: (0, 0)),
                pl.BlockSpec((1, 4, 2 * D, 256), lambda i, ids: (jnp.maximum(i - 12, 0), 0, 0, 0)),
                any_space,
                any_space,
            ],
            scratch_shapes=[
                pltpu.VMEM((D, rows), BF),
                pltpu.VMEM((4, 4, 256, rows), BF),
                pltpu.VMEM((4, 4, 256, rows), BF),
                pltpu.VMEM((4, D, HALF), F32),
                pltpu.VMEM((4, D, rows), BF),
                pltpu.VMEM((D, rows), F32),
                pltpu.VMEM((D, HALF), BF),
                pltpu.VMEM((D, HALF), F32),
                pltpu.VMEM((16, HALF), F32),
                pltpu.VMEM((16, HALF), F32),
                pltpu.VMEM(emb.shape, BF),
                pltpu.VMEM((144, rows), BF),
                pltpu.VMEM((144, D), BF),
                pltpu.VMEM((6, D, 128), BF),
                pltpu.VMEM((2, 16, D), BF),
                pltpu.VMEM((2, 16, D), BF),
                pltpu.VMEM((2, 16, D), BF),
                pltpu.VMEM((2, D, 128), BF),
                pltpu.VMEM((2, 128, 128), F32),
                pltpu.VMEM((2, 128, 128), F32),
                pltpu.VMEM((2, 16, 128), F32),
                pltpu.VMEM((6, D, 128), F32),
                pltpu.VMEM((2, D, 16), F32),
                pltpu.VMEM((2, 16, D), F32),
                pltpu.VMEM((2, D, 128), F32),
                pltpu.VMEM((2, 128, 128), F32),
                pltpu.VMEM((2, 128, 128), F32),
                pltpu.VMEM((2, 8, 128), F32),
                pltpu.SemaphoreType.DMA,
                pltpu.SemaphoreType.DMA,
            ],
        ),
        out_shape=[
            jax.ShapeDtypeStruct((1, rows), F32),
            jax.ShapeDtypeStruct((6, 4, 2 * D, 256), BF),
            jax.ShapeDtypeStruct(emb.shape, BF),
            jax.ShapeDtypeStruct((4, 4, 256, 256), BF),
        ],
        compiler_params=pltpu.CompilerParams(vmem_limit_bytes=62 * 2**20),
        cost_estimate=pl.CostEstimate(flops=39 * 10**9, bytes_accessed=60 * 2**20, transcendentals=0),
        name="dense_all",
    )(ids, emb, feats, every, mask, label, projw, featw, bias, *ups, *downs, gains, shifts, gate, gate, tin, tin, tower)


def finish_kernel(with_rows, ids_ref, even_ref, odd_ref, unit_ref, others_ref, *refs):
    if with_rows:
        back_ref, row_ref = refs[0], refs[1]
        refs = refs[2:]
    (up_ref, down_ref, proj_ref, feat_ref, bias_ref, gain_ref, shift_ref, gate_ref, tin_ref, tbias_ref,
     tout_ref, tob_ref, quarters) = refs
    step = pl.program_id(0)
    for i, sums_ref in enumerate((even_ref, odd_ref)):
        up_ref[i] = sums_ref[0, 0, 0:D, :].astype(F32)
        down_ref[i, :, 0:256] = sums_ref[0, 0, D : D + 256, :].astype(F32)
        down_ref[i, :, 256:512] = sums_ref[0, 0, D + 256 : D + 512, :].astype(F32)
    if with_rows:
        @pl.when(step < with_rows)
        def _():
            row_ref[0] = back_ref[...].astype(F32)

    @pl.when(step == 0)
    def _():
        me = ids_ref[14]
        quarters[me] = unit_ref[0, 0, 0:REP_ROWS, :].astype(F32)
        for i in range(3):
            quarters[ids_ref[15 + i]] = others_ref[i].astype(F32)
        cols = proj_ref.shape[0]
        proj_ref[:, 0:256] = unit_ref[0, 0, REP_ROWS : REP_ROWS + cols, :].astype(F32)
        proj_ref[:, 256:512] = unit_ref[0, 0, REP_ROWS + cols : REP_ROWS + 2 * cols, :].astype(F32)
        for d in range(DOMAINS):
            band = slice((d % 2) * 256, (d % 2) * 256 + 256)
            tin_ref[d, 0:256, :] = quarters[d // 2, band, 0:128]
            tin_ref[d, 256:512, :] = quarters[d // 2, band, 128:256]
            g = quarters[3, GATE_AT + 16 * d : GATE_AT + 16 * d + 16, :]
            g = jnp.concatenate([g[0:8], g[8:16]], axis=1)
            gate_ref[d] = g[0:6]
        feat_ref[:, 0:256] = quarters[3, 0:128, :]
        feat_ref[:, 256:512] = quarters[3, 128:256, :]
        for at, ref in ((GAIN_AT, gain_ref), (SHIFT_AT, shift_ref)):
            ref[:, 0:256] = quarters[3, at : at + 14, :]
            ref[:, 256:512] = quarters[3, at + 16 : at + 30, :]
        tbias_ref[...] = quarters[3, MISC_AT : MISC_AT + 6, 0:128]
        tout_ref[...] = quarters[3, MISC_AT : MISC_AT + 6, 128:256]
        bias_ref[:, 0:256] = quarters[3, MISC_AT + 6 : MISC_AT + 7, :]
        bias_ref[:, 256:512] = quarters[3, MISC_AT + 7 : MISC_AT + 8, :]
        tob_ref[...] = quarters[3, MISC_AT + 8 : MISC_AT + 9, 0:128]


def finish(ids, sums, others, proj_cols, back=None):
    def whole(s):
        return pl.BlockSpec(s, lambda i, ids: (0,) * len(s))

    def unit(odd):
        return lambda i, ids: (ids[2 * i + odd] % 16, ids[2 * i + odd] // 16, 0, 0)

    in_specs = [
        pl.BlockSpec((1, 1, ROWS_U, LANES), unit(0)),
        pl.BlockSpec((1, 1, ROWS_U, LANES), unit(1)),
        pl.BlockSpec((1, 1, ROWS_U, LANES), lambda i, ids: (6, 0, 0, 0)),
        whole(others.shape),
    ]
    args = [sums, sums, sums, others]
    shapes = [
        (14, D, 256), (14, 256, D), (proj_cols, D), (DENSE, D), (1, D), (14, D), (14, D), (DOMAINS, 6, D),
        (DOMAINS, D, 128), (DOMAINS, 128), (DOMAINS, 128), (1, 128),
    ]
    out_specs = [
        pl.BlockSpec((2, D, 256), lambda i, ids: (i, 0, 0)),
        pl.BlockSpec((2, 256, D), lambda i, ids: (i, 0, 0)),
    ] + [whole(s) for s in shapes[2:]]
    if back is not None:
        blocks, cols, cap = back.shape
        each = -(-blocks // 7)
        last = lambda i: jnp.minimum(i, blocks // each - 1)
        args.append(back)
        in_specs.append(pl.BlockSpec((each, cols, cap), lambda i, ids: (last(i), 0, 0)))
        shapes.insert(0, (1, blocks, cols, cap))
        out_specs.insert(0, pl.BlockSpec((1, each, cols, cap), lambda i, ids: (0, last(i), 0, 0)))
    return pl.pallas_call(
        functools.partial(finish_kernel, 0 if back is None else blocks // each),
        grid_spec=pltpu.PrefetchScalarGridSpec(
            num_scalar_prefetch=1,
            grid=(7,),
            in_specs=in_specs,
            out_specs=out_specs,
            scratch_shapes=[pltpu.VMEM((4, REP_ROWS, LANES), F32)],
        ),
        out_shape=[jax.ShapeDtypeStruct(s, F32) for s in shapes],
        compiler_params=pltpu.CompilerParams(vmem_limit_bytes=VMEM),
        cost_estimate=pl.CostEstimate(flops=0, bytes_accessed=32 * 2**20, transcendentals=0),
        name="finish",
    )(ids, *args)


def shards(
    embed_table,
    requests,
    slot_index,
    event_mask,
    labels,
    dense_feats,
    proj_weight,
    dense_weight,
    proj_bias,
    up_weight,
    down_weight,
    norm_gain,
    norm_shift,
    gate_weight,
    tower_in,
    tower_bias,
    tower_out,
    tower_out_bias,
):
    narrow = lax.axis_size("narrow")
    me = lax.axis_index("narrow")
    chip, core = me // 2, me % 2
    ev_rows, fields = slot_index.shape
    rows = ev_rows // narrow
    owners, cap = requests.shape[1], requests.shape[2]
    hid_here = up_weight.shape[2]
    other_chip = [(i, i ^ 2) for i in range(narrow)]
    other_core = [(i, i ^ 1) for i in range(narrow)]
    full = 3 * chip + 2 * core
    half = 3 * chip + 1

    def swap(x, pairs):
        return lax.ppermute(x, "narrow", pairs)

    def chip_experts(w, which):
        return jnp.concatenate(
            [w[:SHARED], lax.dynamic_slice_in_dim(w, SHARED + 6 * which, 6, axis=0)], axis=0
        )

    def bring(w):
        far = swap(chip_experts(w, 1 - chip), other_chip)
        at = lambda x, start, size: lax.dynamic_slice_in_dim(x, start, size, axis=0)
        base = SHARED + 6 * chip
        away = 4 * (1 - core)
        theirs = jnp.stack(
            [
                jnp.concatenate([w[:SHARED], at(w, base + away, 2), at(w, base + 2, 2)], axis=0),
                jnp.concatenate([far[:SHARED], at(far, 2 + away, 2), far[4:6]], axis=0),
            ]
        )
        return w, far, swap(theirs, other_core)

    six = jnp.arange(6, dtype=jnp.int32)
    spot = jnp.where(six < 2, six, jnp.where(six < 4, six + 4 * core, six))
    offset = jnp.arange(narrow, dtype=jnp.int32)
    offset = jnp.where(chip == 1, (offset + 2) % 4, offset)
    offset = jnp.where(core == 1, offset + 1 - 2 * (offset % 2), offset)
    ids = jnp.concatenate(
        [
            jnp.where(six < 2, six, spot + 6 * chip),
            spot,
            jnp.stack([full, half, core]),
            (offset % 2) * 2 + offset // 2,
        ]
    ).astype(jnp.int32)
    mask_row, label_row = event_mask[None], labels[None]

    turn = lambda i: (i // 3) * 3 + (i % 3 + (i // 3) % 2) % 3
    table_rows = embed_table.shape[0]
    cols = fields * EMB
    blocks = ev_rows // HALF
    hi_n = 256
    lo_n = ev_rows // hi_n
    direct = cap % hi_n == 0
    asked = requests[0].transpose(0, 2, 1)
    if direct:
        embedded, far_up, far_down, their_up, their_down, proj_full, every = front(
            asked, embed_table.T, slot_index.T, dense_feats, mask_row, up_weight, down_weight, proj_weight
        )
        ups, downs = (up_weight, far_up, their_up), (down_weight, far_down, their_down)
    else:
        asked = lax.all_to_all(asked, "wide", 0, 0, tiled=True)
        ups, downs = bring(up_weight), bring(down_weight)
        proj_full = lax.all_gather(proj_weight, "narrow", axis=0)
        stats = local_stats(core[None], dense_feats, mask_row)
        stats = jnp.concatenate([stats, swap(stats, other_core)], axis=0)
        every = lax.all_to_all(
            jnp.broadcast_to(stats, (owners,) + stats.shape), "wide", 0, 0, tiled=True
        )
        tab = embed_table.reshape(32, table_rows // 32, cols).transpose(0, 2, 1)
        flat = asked.transpose(1, 0, 2).reshape(fields, DOMAINS, DSLOT).transpose(1, 0, 2)
        found = lookup(flat, tab, table_rows // 32, "lookup_rows", DOMAINS)
        found = found.transpose(1, 0, 2).reshape(cols, owners, cap).transpose(1, 0, 2)
        received = lax.all_to_all(found, "wide", 0, 0, tiled=True)
        received = received.transpose(1, 0, 2).reshape(cols, lo_n, hi_n).transpose(1, 0, 2)
        slots = slot_index.reshape(blocks, HALF, fields).transpose(0, 2, 1)
        embedded = lookup(slots, received, hi_n, "order_rows", narrow, turn)
        embedded = lax.all_to_all(embedded, "narrow", 0, 0, tiled=True)
    embedded = embedded.reshape(narrow * cols, rows)
    proj_full = proj_full.reshape(narrow * cols, D)

    tower = jnp.concatenate(
        [tower_bias, tower_out, jnp.pad(tower_out_bias[None], ((0, 3), (0, 128 - DOMAINS)))], axis=0
    )
    logits, own, embed_grad, extra = dense(
        ids, embedded, dense_feats, every, mask_row, label_row, proj_full, dense_weight, proj_bias[None],
        ups, downs, norm_gain, norm_shift, gate_weight.transpose(0, 2, 1), tower_in, tower,
    )
    extra = extra.reshape(narrow, ROWS_U, LANES)

    embed_grad = embed_grad.reshape(narrow, cols, rows)
    if not direct:
        embed_grad = lax.all_to_all(embed_grad, "narrow", 0, 0, tiled=True)
        returned = place(slot_index.T, embed_grad, (lo_n, cols, hi_n))
        returned = returned.transpose(1, 0, 2).reshape(cols, owners, cap).transpose(1, 0, 2)
        row_grads = lax.all_to_all(returned, "wide", 0, 0, tiled=True)

    if direct:
        sums, others, row_grads = reduce_all(own, extra, owners, REP_ROWS, (slot_index.T, embed_grad, cap))
    else:
        sums, others = reduce_all(own, extra, owners, REP_ROWS)
    expert = jnp.arange(14, dtype=jnp.int32)
    domain = (expert - SHARED) // DOM_EXP
    unit = jnp.where(domain % 3 == 0, 0, jnp.where(domain % 3 == 1, 4, 2)) + expert % 2
    away = jnp.where(domain // 3 == chip, 0, 16)
    unit = jnp.where(expert < SHARED, expert + 7, unit + away)
    marks = jnp.concatenate([unit, jnp.stack([me, me + 1 - 2 * core, me + 2 - 4 * chip, 3 - me])])
    outs = finish(marks.astype(jnp.int32), sums, others, cols, row_grads if direct else None)
    if not direct:
        outs = [row_grads.astype(F32)[None]] + list(outs)
    (row_grads, up_grad, down_grad, proj_grad, feat_grad, bias_grad, gain_grad, shift_grad, gate_grad, tower_grad,
     tower_bias_grad, tower_out_grad, out_bias_grad) = outs
    return (
        logits[0],
        row_grads.transpose(0, 1, 3, 2),
        proj_grad,
        feat_grad,
        bias_grad[0],
        up_grad,
        down_grad,
        gain_grad,
        shift_grad,
        gate_grad.transpose(0, 2, 1),
        tower_grad,
        tower_bias_grad,
        tower_out_grad,
        out_bias_grad[0, :DOMAINS],
    )


def solution(mesh):
    placed = (
        P("wide", "narrow"),
        P("wide", None, None, "narrow"),
        P("wide", "narrow"),
        P(("wide", "narrow")),
        P(("wide", "narrow")),
        P(("wide", "narrow"), None),
        P("narrow", None),
        P(),
        P(),
        P(None, None, "narrow"),
        P(None, "narrow", None),
        P(),
        P(),
        P(),
        P(),
        P(),
        P(),
        P(),
    )
    return jax.shard_map(
        shards,
        mesh=mesh,
        in_specs=placed,
        out_specs=(
            P(("wide", "narrow")),
            P("wide", None, None, "narrow"),
            P("narrow", None),
            P(),
            P(),
            P(None, None, "narrow"),
            P(None, "narrow", None),
            P(),
            P(),
            P(),
            P(),
            P(),
            P(),
            P(),
        ),
        check_vma=False,
    )
```

```python
import functools

import jax
import jax.numpy as jnp
from jax import lax
from jax.experimental import pallas as pl
from jax.experimental.pallas import tpu as pltpu
from jax.sharding import PartitionSpec as P

D = 512
HID = 1024
EMB = 16
DENSE = 128
DOMAINS = 6
SHARED = 2
DOM_EXP = 2
DSLOT = 1024
HALF = DSLOT // 2
VMEM = 56 * 2**20
BF = jnp.bfloat16
F32 = jnp.float32
MESH = pl.DeviceIdType.MESH
UNITS = 9
TURNED = 4
TOGETHER = 2
ROW_AT = 6
ROW_STEP = 1
ROWS_U = 1024
LANES = 256


def dot(a, b, ca, cb):
    return lax.dot_general(a, b, (((ca,), (cb,)), ((), ())), preferred_element_type=F32)


def lookup_kernel(lo_n, hi_n, fields, idx_ref, tab_ref, out_ref):
    length = idx_ref.shape[-1]
    shift = hi_n.bit_length() - 1
    for f in range(fields):
        idx = idx_ref[0, f : f + 1, :]
        hi = jnp.where(idx >= 0, idx & (hi_n - 1), -1)
        lo = lax.shift_right_logical(jnp.maximum(idx, 0), shift)
        hot = (lax.broadcasted_iota(jnp.int32, (hi_n, length), 0) == hi).astype(BF)
        cols = slice(f * EMB, (f + 1) * EMB)
        parts = [
            tab_ref[:, cols, j * hi_n : (j + 1) * hi_n].reshape(-1, hi_n) for j in range(tab_ref.shape[2] // hi_n)
        ]
        res = jnp.dot(jnp.concatenate(parts, axis=0), hot, preferred_element_type=F32)
        acc = res[0:EMB]
        for step in range(1, lo_n):
            acc = jnp.where(lo == step, res[step * EMB : (step + 1) * EMB], acc)
        out_ref[0, cols, :] = acc.astype(BF)


def lookup(idx, tab, hi_n, name, out_groups, order=lambda i: i):
    groups, fields, length = idx.shape
    outer, cols, inner = tab.shape
    lo_n = outer * inner // hi_n
    each = groups // out_groups
    return pl.pallas_call(
        functools.partial(lookup_kernel, lo_n, hi_n, fields),
        grid=(groups,),
        in_specs=[
            pl.BlockSpec((1, fields, length), lambda i: (order(i), 0, 0)),
            pl.BlockSpec(tab.shape, lambda i: (0, 0, 0)),
        ],
        out_specs=pl.BlockSpec((1, cols, length), lambda i: (i // each, 0, i % each)),
        out_shape=jax.ShapeDtypeStruct((out_groups, cols, length * each), BF),
        compiler_params=pltpu.CompilerParams(vmem_limit_bytes=VMEM),
        cost_estimate=pl.CostEstimate(
            flops=2 * groups * length * cols * lo_n * hi_n, bytes_accessed=8 * 2**20, transcendentals=0
        ),
        name=name,
    )(idx, tab)


def quarter_slots(slot_ref, q, field):
    half = slot_ref.shape[1] // 12
    parts = []
    for c in range(3):
        at = q * 3 * half + ((c + q % 2) % 3) * half
        at = at if isinstance(at, int) else pl.multiple_of(at, half)
        parts.append(slot_ref[pl.ds(field, 1), pl.ds(at, half)])
    return jnp.concatenate(parts, axis=1)


def place_one(idx_ref, grad_ref, out_ref, field):
    outer, _, inner = out_ref.shape
    length = grad_ref.shape[2]
    hi_n = 256
    lo_n = outer * inner // hi_n
    cols = pl.ds(pl.multiple_of(field * EMB, EMB), EMB)
    total = None
    for s in range(grad_ref.shape[0]):
        idx = quarter_slots(idx_ref, s, field)
        hi = idx & (hi_n - 1)
        lo = lax.shift_right_logical(idx, hi_n.bit_length() - 1)
        grad = grad_ref[s, cols, :]
        hot = (lax.broadcasted_iota(jnp.int32, (hi_n, length), 0) == hi).astype(BF)
        lhs = jnp.concatenate(
            [jnp.where(lo == step, grad, jnp.zeros_like(grad)) for step in range(lo_n)], axis=0
        )
        part = dot(lhs, hot, 1, 1)
        total = part if total is None else total + part
    total = total.astype(BF)
    each = inner // hi_n
    for i in range(outer * each):
        out_ref[i // each, cols, (i % each) * hi_n : (i % each + 1) * hi_n] = total[i * EMB : (i + 1) * EMB]


def place_kernel(idx_ref, grad_ref, out_ref):
    def one(field, _):
        place_one(idx_ref, grad_ref, out_ref, field)
        return 0

    lax.fori_loop(0, idx_ref.shape[0], one, 0)


def place(idx, grad, out_shape):
    return pl.pallas_call(
        place_kernel,
        out_shape=jax.ShapeDtypeStruct(out_shape, BF),
        compiler_params=pltpu.CompilerParams(vmem_limit_bytes=VMEM),
        name="place_rows",
    )(idx, grad)


def own_stats(feats_ref, mask_ref, out_ref, core):
    highest = lax.Precision.HIGHEST

    def block(c):
        at = pl.ds(pl.multiple_of(((c + core) % 3) * HALF, HALF), HALF)
        weight = jnp.broadcast_to(mask_ref[:, at].astype(F32), (8, HALF))
        return feats_ref[at, :], weight

    def total(weight, x):
        return jnp.dot(weight, x, preferred_element_type=F32, precision=highest)[0:1]

    for row, chunks in ((0, (0, 1)), (3, (2,))):
        count = sum(jnp.sum(block(c)[1][0:1], axis=1, keepdims=True) for c in chunks)
        mean = sum(total(block(c)[1], block(c)[0]) for c in chunks) / jnp.maximum(count, 1.0)
        off = lambda c: block(c)[0] - mean
        out_ref[row : row + 1, :] = mean
        out_ref[row + 1 : row + 2, :] = sum(total(block(c)[1], off(c) * off(c)) for c in chunks)
        out_ref[row + 2 : row + 3, :] = jnp.broadcast_to(count, mean.shape)


def stats_kernel(core_ref, feats_ref, mask_ref, out_ref):
    out_ref[...] = jnp.zeros_like(out_ref)
    own_stats(feats_ref, mask_ref, out_ref, core_ref[0])


def local_stats(core, feats, mask):
    return pl.pallas_call(
        stats_kernel,
        in_specs=[pl.BlockSpec(memory_space=pltpu.SMEM)] + [pl.BlockSpec(memory_space=pltpu.VMEM)] * 2,
        out_shape=jax.ShapeDtypeStruct((8, DENSE), F32),
        compiler_params=pltpu.CompilerParams(vmem_limit_bytes=VMEM),
        name="local_stats",
    )(core, feats, mask)


def front_kernel(
    groups, req_ref, table_ref, slot_ref, feats_ref, mask_ref, up_ref, down_ref, proj_ref,
    emb_ref, far_up, far_down, their_up, their_down, proj_out, every_ref,
    asked, found, received, ordered, both,
    req_send, req_recv, row_send, row_recv, near_send, near_recv, keep_sem,
    far_send, far_recv, side_send, above_send, own_send, own_recv, their_send, their_recv, proj_send, proj_recv,
    stat_send, stat_recv,
):
    wide, me = lax.axis_index("wide"), lax.axis_index("narrow")
    chip, core = me // 2, me % 2
    owners, fields, cap = req_ref.shape
    share = fields // groups
    parity, upper = wide % 2, (wide // 2) % 2
    near = [{"narrow": me + 1 - 2 * core}, {"narrow": me + 2 - 4 * chip}, {"narrow": 3 - me}]
    near_at = [me + 1 - 2 * core, me + 2 - 4 * chip, 3 - me]
    peers = [None] + [{"wide": (wide + d) % owners} for d in range(1, owners)]
    side, above = {"wide": wide + 1 - 2 * parity}, {"wide": wide + 2 - 4 * upper}
    barrier = pltpu.get_barrier_semaphore()
    for mate in near + peers[1:]:
        pl.semaphore_signal(barrier, inc=1, device_id=mate, device_id_type=MESH)
    pl.semaphore_wait(barrier, len(near) + len(peers) - 1)

    def remote(src, dst, send, recv, mate):
        return pltpu.make_async_remote_copy(
            src_ref=src, dst_ref=dst, send_sem=send, recv_sem=recv, device_id=mate, device_id_type=MESH
        )

    def req_copy(d):
        return remote(req_ref.at[(wide + d) % owners], asked.at[wide], req_send.at[d], req_recv.at[d], peers[d])

    for d in range(1, owners):
        req_copy(d).start()
    mine = pltpu.make_async_copy(req_ref.at[wide], asked.at[wide], keep_sem.at[0])
    mine.start()

    weights = ((up_ref, far_up, their_up), (down_ref, far_down, their_down))

    def far_at(j, side_of):
        return jnp.where(j == 0, 4 + side_of + 2 * upper, 2 * (j - 1) + side_of)

    def far_copy(j, a):
        p = far_at(j, parity)
        expert = jnp.where(p < 2, p, 6 * (1 - chip) + p)
        return remote(weights[a][0].at[expert], weights[a][1].at[p], far_send.at[a, j], far_recv.at[a, p], near[1])

    def side_copy(j, a, side_of):
        p = far_at(j, side_of)
        view = weights[a][1].at[p]
        return remote(view, view, side_send.at[a, j], far_recv.at[a, p], side)

    def above_copy(i, a, half):
        p = 4 + i + 2 * half
        view = weights[a][1].at[p]
        return remote(view, view, above_send.at[a, i], far_recv.at[a, p], above)

    def own_copy(i, a):
        expert = jnp.where(i < 2, i, 6 * chip + jnp.where(i < 4, i + 4 * (1 - core), i))
        return remote(weights[a][0].at[expert], weights[a][2].at[0, i], own_send.at[a, i], own_recv.at[a, i], near[0])

    def their_copy(p, a):
        i = jnp.where(p < 6, p, p - 4)
        return remote(weights[a][1].at[p], weights[a][2].at[1, i], their_send.at[a, i], their_recv.at[a, i], near[0])

    def wanted(p):
        ends = jnp.logical_or(jnp.logical_and(p < 4, core == 1), jnp.logical_and(p >= 6, core == 0))
        return jnp.logical_or(jnp.logical_or(p < 2, jnp.logical_and(p >= 4, p < 6)), ends)

    def for_all(n, f):
        def body(i, _):
            for a in range(2):
                f(i, a)
            return 0

        lax.fori_loop(0, n, body, 0)


    for_all(3, lambda j, a: far_copy(j, a).start())

    def stat_core():
        return remote(both.at[pl.ds(0, 8)], both.at[pl.ds(8, 8)], stat_send.at[0], stat_recv.at[0], near[0])

    def stat_copy(d):
        return remote(both, every_ref.at[wide], stat_send.at[d], stat_recv.at[d], peers[d])

    both[0:8, :] = jnp.zeros((8, DENSE), F32)
    own_stats(feats_ref, mask_ref, both, core)
    stat_core().start()

    def proj_copy(i):
        return remote(proj_ref, proj_out.at[me], proj_send.at[i], proj_recv.at[i], near[i])

    def proj_pass():
        view = proj_out.at[near_at[1]]
        return remote(view, view, proj_send.at[2], proj_recv.at[2], near[0])

    def other_proj():
        proj_copy(1).wait_recv()
        proj_pass().start()

    keep_proj = pltpu.make_async_copy(proj_ref, proj_out.at[me], keep_sem.at[1])
    keep_proj.start()
    for i in range(2):
        proj_copy(i).start()
    for_all(6, lambda i, a: own_copy(i, a).start())
    stat_core().wait_recv()
    for d in range(1, owners):
        stat_copy(d).start()
    keep_stat = pltpu.make_async_copy(both, every_ref.at[wide], keep_sem.at[2])
    keep_stat.start()

    def pass_on(p):
        @pl.when(wanted(p))
        def _():
            for a in range(2):
                their_copy(p, a).start()

    def lift(j, side_of):
        @pl.when(j == 0)
        def _():
            for a in range(2):
                above_copy(side_of, a, upper).start()

    def far_step(j):
        for a in range(2):
            far_copy(j, a).wait_recv()
            side_copy(j, a, parity).start()
        lift(j, parity)
        pass_on(far_at(j, parity))

    def side_step(j):
        for a in range(2):
            side_copy(j, a, 1 - parity).wait_recv()
        lift(j, 1 - parity)
        pass_on(far_at(j, 1 - parity))

    def above_step(i):
        for a in range(2):
            above_copy(i, a, 1 - upper).wait_recv()
        pass_on(4 + i + 2 * (1 - upper))

    hi_n = 512
    lo_n = table_ref.shape[1] // hi_n

    def find(f, owner_idx):
        idx = asked[owner_idx, pl.ds(f, 1), :]
        hi = jnp.where(idx >= 0, idx & (hi_n - 1), -1)
        lo = lax.shift_right_logical(jnp.maximum(idx, 0), hi_n.bit_length() - 1)
        hot = (lax.broadcasted_iota(jnp.int32, (hi_n, cap), 0) == hi).astype(BF)
        cols = pl.ds(pl.multiple_of(f * EMB, EMB), EMB)
        part = jnp.concatenate([table_ref[cols, l * hi_n : (l + 1) * hi_n] for l in range(lo_n)], axis=0)
        res = jnp.dot(part, hot, preferred_element_type=F32)
        acc = res[0:EMB]
        for step in range(1, lo_n):
            acc = jnp.where(lo == step, res[step * EMB : (step + 1) * EMB], acc)
        return cols, acc.astype(BF)

    def group_rows(g):
        return pl.ds(pl.multiple_of(g * share * EMB, share * EMB), share * EMB)

    def row_copy(g, d, mate):
        rows = group_rows(g)
        return remote(
            found.at[(wide + d) % owners, rows], received.at[wide, rows], row_send.at[g, d], row_recv.at[g, d], mate
        )

    def look(g):
        @pl.when(g == 0)
        def _():
            for d in range(1, owners):
                req_copy(d).wait_recv()

        def some(i, _):
            ahead = [i * TOGETHER + e for e in range(TOGETHER)]
            for d in ahead:
                for k in range(share):
                    cols, block = find(g * share + k, (wide + d) % owners)
                    found[(wide + d) % owners, cols, :] = block
            for d in ahead:
                @pl.when(d > 0)
                def _():
                    row_copy(g, d, {"wide": (wide + d) % owners}).start()

            return 0

        lax.fori_loop(0, owners // TOGETHER, some, 0)
        received[wide, group_rows(g), :] = found[wide, group_rows(g), :]

    hi_e = 256
    outer = owners * cap // hi_e

    def near_copy(g, i):
        rows = group_rows(g)
        return remote(
            ordered.at[near_at[i], rows], emb_ref.at[me, rows], near_send.at[g, i], near_recv.at[g, i], near[i]
        )

    def keep_copy(g):
        rows = group_rows(g)
        return pltpu.make_async_copy(ordered.at[me, rows], emb_ref.at[me, rows], keep_sem.at[3 + g])

    def order(g):
        def arrive(d, _):
            row_copy(g, d, {"wide": (wide + d) % owners}).wait_recv()
            return 0

        lax.fori_loop(1, owners, arrive, 0)
        tables = []
        for k in range(share):
            cols = pl.ds(pl.multiple_of((g * share + k) * EMB, EMB), EMB)
            parts = [
                received[o, cols, j * hi_e : (j + 1) * hi_e] for o in range(owners) for j in range(cap // hi_e)
            ]
            tables.append((cols, jnp.concatenate(parts, axis=0)))

        def quarter(q):
            for k, (cols, table) in enumerate(tables):
                idx = quarter_slots(slot_ref, q, g * share + k)
                hi = idx & (hi_e - 1)
                lo = lax.shift_right_logical(idx, hi_e.bit_length() - 1)
                hot = (lax.broadcasted_iota(jnp.int32, (hi_e, idx.shape[1]), 0) == hi).astype(BF)
                res = jnp.dot(table, hot, preferred_element_type=F32)
                acc = res[0:EMB]
                for step in range(1, outer):
                    acc = jnp.where(lo == step, res[step * EMB : (step + 1) * EMB], acc)
                ordered[q, cols, :] = acc.astype(BF)

        for i in (2, 1, 0):
            quarter(near_at[i])
            near_copy(g, i).start()
        quarter(me)
        keep_copy(g).start()

    mine.wait()

    def tick(t, _):
        @pl.when(t >= 2)
        def _():
            order(t - 2)

        @pl.when(t < groups)
        def _():
            look(t)

        @pl.when(t < 3)
        def _():
            far_step(t)

        @pl.when(t == 3)
        def _():
            other_proj()

        @pl.when(jnp.logical_and(t >= 2, t < 5))
        def _():
            side_step(t - 2)

        @pl.when(jnp.logical_and(t >= 4, t < 6))
        def _():
            above_step(jnp.where(t == 4, parity, 1 - parity))

        return 0

    lax.fori_loop(0, groups + 2, tick, 0)

    for d in range(1, owners):
        req_copy(d).wait_send()
        stat_copy(d).wait()
    stat_core().wait_send()
    keep_stat.wait()
    keep_proj.wait()
    proj_copy(0).wait()
    proj_copy(1).wait_send()
    proj_pass().wait()

    def rows_left(g, _):
        def one(d, _):
            row_copy(g, d, {"wide": (wide + d) % owners}).wait_send()
            return 0

        lax.fori_loop(1, owners, one, 0)
        for i in range(3):
            near_copy(g, i).wait()
        keep_copy(g).wait()
        return 0

    lax.fori_loop(0, groups, rows_left, 0)

    def weights_left(j, a):
        far_copy(j, a).wait_send()
        side_copy(j, a, parity).wait_send()

    for_all(3, weights_left)
    for_all(2, lambda i, a: above_copy(i, a, upper).wait_send())
    for_all(6, lambda i, a: own_copy(i, a).wait())

    def passed(p, a):
        @pl.when(wanted(p))
        def _():
            their_copy(p, a).wait_send()

    for_all(8, passed)
    for_all(6, lambda i, a: their_copy(i, a).wait_recv())


def front(req, table, slots, feats, mask, up, down, proj, groups=5):
    owners, fields, cap = req.shape
    cols = fields * EMB
    quarters = 4
    rows = slots.shape[1] // quarters
    any_space, vmem = pl.BlockSpec(memory_space=pl.ANY), pl.BlockSpec(memory_space=pltpu.VMEM)
    dma = pltpu.SemaphoreType.DMA
    return pl.pallas_call(
        functools.partial(front_kernel, groups),
        in_specs=[vmem] * 5 + [any_space] * 3,
        out_specs=[any_space] * 7,
        out_shape=[
            jax.ShapeDtypeStruct((quarters, cols, rows), BF),
            jax.ShapeDtypeStruct((8,) + up.shape[1:], BF),
            jax.ShapeDtypeStruct((8,) + down.shape[1:], BF),
            jax.ShapeDtypeStruct((2, 6) + up.shape[1:], BF),
            jax.ShapeDtypeStruct((2, 6) + down.shape[1:], BF),
            jax.ShapeDtypeStruct((quarters,) + proj.shape, BF),
            jax.ShapeDtypeStruct((owners, 16, DENSE), F32),
        ],
        scratch_shapes=[
            pltpu.VMEM((owners, fields, cap), jnp.int32),
            pltpu.VMEM((owners, cols, cap), BF),
            pltpu.VMEM((owners, cols, cap), BF),
            pltpu.VMEM((quarters, cols, rows), BF),
            pltpu.VMEM((16, DENSE), F32),
            dma((owners,)),
            dma((owners,)),
            dma((groups, owners)),
            dma((groups, owners)),
            dma((groups, 3)),
            dma((groups, 3)),
            dma((3 + groups,)),
            dma((2, 3)),
            dma((2, 8)),
            dma((2, 3)),
            dma((2, 2)),
            dma((2, 6)),
            dma((2, 6)),
            dma((2, 6)),
            dma((2, 6)),
            dma((3,)),
            dma((3,)),
            dma((owners,)),
            dma((owners,)),
        ],
        compiler_params=pltpu.CompilerParams(collective_id=1, has_side_effects=True, vmem_limit_bytes=VMEM),
        cost_estimate=pl.CostEstimate(flops=45 * 10**9, bytes_accessed=40 * 2**20, transcendentals=0),
        name="front",
    )(req, table, slots, feats, mask, up, down, proj)


def reduce_kernel(bits, with_rows, own_ref, extra_ref, *refs):
    if with_rows:
        slot_ref, grad_ref, out_ref, rep_ref, back_ref = refs[:5]
        grads, placed, near_send, near_recv, far_send, far_recv, keep_sem = refs[-7:]
        refs = refs[5:-7]
    else:
        out_ref, rep_ref = refs[:2]
        refs = refs[2:]
    acc, stage_buf, halves, got, local_sem, send, recv, rep_send, rep_recv, out_sem = refs
    wide=lax.axis_index("wide"); me=lax.axis_index("narrow")
    chip=me//2; core=me%2
    block=ROWS_U>>bits
    mates=[{"narrow": me+1-2*core},{"narrow": me+2-4*chip}]
    pairs=[{"wide": wide+(1<<k)*(1-2*((wide//(1<<k))%2))} for k in range(bits)]
    far={"narrow": 3-me}
    barrier=pltpu.get_barrier_semaphore()
    owners=1<<bits
    others=[{"wide": (wide+d)%owners} for d in range(1,owners)] if with_rows else pairs
    for mate in mates+[far]+others:
        pl.semaphore_signal(barrier, inc=1, device_id=mate, device_id_type=MESH)
    pl.semaphore_wait(barrier, len(others)+3)
    def power(k):
        return 1 << k, 1 << ((k + 1) % bits)

    def bit(u, k):
        here, there = power(k)
        return jnp.where(u == TURNED, (wide // there) % 2, (wide // here) % 2)

    def pair(u, k):
        here, there = power(k)
        step = jnp.where(u == TURNED, there, here)
        return {"wide": wide + step * (1 - 2 * bit(u, k))}

    def start_of(u, k):
        at = 0
        for j in range(k):
            at = at + bit(u, j) * (ROWS_U >> (j + 1))
        return pl.multiple_of(at, 16) if k else 0

    def copy(src, dst, s, u, mate):
        return pltpu.make_async_remote_copy(
            src_ref=src, dst_ref=dst, send_sem=send.at[s, u], recv_sem=recv.at[s, u], device_id=mate, device_id_type=MESH
        )

    def mine(u):
        return jnp.logical_or(u >= 4, jnp.where(u < 2, core == 0, core == 1))

    def theirs(u):
        return jnp.logical_or(u >= 4, jnp.where(u < 2, core == 1, core == 0))

    def domain_unit(u):
        return u < 6

    def local_at(u):
        return jnp.where(u < 2, u + 2, jnp.where(u < 6, u, u - 7))

    def core_copy(u, src):
        return copy(src, acc.at[u], 0, u, mates[0])

    def near_copy(u, src):
        return pltpu.make_async_copy(src, stage_buf.at[u % 2], local_sem.at[u % 2])

    def begin(u):
        @pl.when(u == 6)
        def _():
            core_copy(u, extra_ref.at[pl.ds(2, 2)]).start()
            near_copy(u, extra_ref.at[pl.ds(0, 2)]).start()

        @pl.when(jnp.logical_and(u != 6, mine(u)))
        def _():
            core_copy(u, own_ref.at[local_at(u), pl.ds(2, 2)]).start()
            near_copy(u, own_ref.at[local_at(u), pl.ds(0, 2)]).start()

    def add_region(u, sl, at, rows, src):
        tile = min(rows, 64)

        def body(i, _):
            r = pl.multiple_of(at + i * tile, 16)
            q = pl.multiple_of(i * tile, 16)
            for h in range(sl):
                a = acc[u, h, pl.ds(r, tile), :].astype(F32) + src[h, pl.ds(q, tile), :].astype(F32)
                acc[u, h, pl.ds(r, tile), :] = a.astype(BF)
            return 0

        lax.fori_loop(0, rows // tile, body, 0)

    half_at = [0]
    for k in range(bits):
        half_at.append(half_at[-1] + (ROWS_U >> (k + 1)))

    def half_view(u, k, parts):
        return halves.at[u, pl.ds(0, parts), pl.ds(half_at[k], ROWS_U >> (k + 1)), :]

    def send_half(u, k, parts):
        size = ROWS_U >> (k + 1)
        at = pl.multiple_of(start_of(u, k) + (1 - bit(u, k)) * size, 16)
        return copy(acc.at[u, pl.ds(0, parts), pl.ds(at, size), :], half_view(u, k, parts), 1 + k, u, pair(u, k))

    def take_half(u, k, parts):
        size = ROWS_U >> k
        copy(acc.at[u, pl.ds(0, parts), pl.ds(0, size), :], half_view(u, k - 1, parts), k, u, pair(u, k - 1)).wait_recv()
        add_region(u, parts, start_of(u, k), size, halves.at[u, :, pl.ds(half_at[k - 1], size), :])

    def y_whole(u):
        return copy(acc.at[u, 1], got.at[u, 1], bits + 1, u, mates[1])

    def y_block(u):
        at = start_of(u, bits)
        return copy(
            acc.at[u, 1, pl.ds(at, block), :], got.at[u, 1, pl.ds(at, block), :], bits + 1, u, mates[1]
        )

    def combine(u):
        @pl.when(theirs(u))
        def _():
            core_copy(u, acc.at[u]).wait_recv()

        @pl.when(mine(u))
        def _():
            near_copy(u, acc.at[u]).wait()
            sb = stage_buf.at[u % 2]

            @pl.when(theirs(u))
            def _():
                add_region(u, 2, 0, ROWS_U, sb)

            @pl.when(jnp.logical_not(theirs(u)))
            def _():
                def body(i, _):
                    r = pl.multiple_of(i * 64, 16)
                    for h in (0, 1):
                        acc[u, h, pl.ds(r, 64), :] = sb[h, pl.ds(r, 64), :]
                    return 0

                lax.fori_loop(0, ROWS_U // 64, body, 0)

    def grow_copy(u, j, parts):
        size = ROWS_U >> (j + 1)
        view = got.at[u, pl.ds(0, parts), pl.ds(start_of(u, j + 1), size), :]
        return copy(view, view, bits + 2 + (bits - 1 - j), u, pair(u, j))

    def out_copy(u, parts):
        return pltpu.make_async_copy(got.at[u, pl.ds(0, parts)], out_ref.at[u, pl.ds(0, parts)], out_sem.at[u])

    rep_mates = [mates[0], mates[1], far]
    rep_rows = rep_ref.shape[1]

    def rep_copy(i):
        return pltpu.make_async_remote_copy(
            src_ref=got.at[6, 0, pl.ds(0, rep_rows), :], dst_ref=rep_ref.at[i], send_sem=rep_send.at[i],
            recv_sem=rep_recv.at[i], device_id=rep_mates[i], device_id_type=MESH,
        )

    def by_kind(u, domain, shared):
        pl.when(domain_unit(u))(domain)
        pl.when(jnp.logical_not(domain_unit(u)))(shared)

    def start_grow(u):
        by_kind(u, lambda: grow_copy(u, bits - 1, 2).start(), lambda: grow_copy(u, bits - 1, 1).start())

    def stage_one(u):
        combine(u)
        by_kind(u, lambda: send_half(u, 0, 2).start(), lambda: y_whole(u).start())

    def halving(k, u):
        def domain():
            take_half(u, k, 2)
            if k < bits:
                send_half(u, k, 2).start()
            else:
                y_block(u).start()

        def shared():
            if k == 1:
                y_whole(u).wait_recv()
                add_region(u, 1, 0, ROWS_U, got.at[u, pl.ds(1, 1)])
            else:
                take_half(u, k - 1, 1)
            send_half(u, k - 1, 1).start()

        by_kind(u, domain, shared)

    def cross(u):
        at = start_of(u, bits)

        def domain():
            y_block(u).wait_recv()

        def shared():
            take_half(u, bits, 1)

        by_kind(u, domain, shared)
        got[u, 0, pl.ds(at, block), :] = acc[u, 0, pl.ds(at, block), :]
        start_grow(u)

    def grow(u, j):
        by_kind(u, lambda: grow_copy(u, j, 2).wait_recv(), lambda: grow_copy(u, j, 1).wait_recv())
        if j > 0:
            by_kind(u, lambda: grow_copy(u, j - 1, 2).start(), lambda: grow_copy(u, j - 1, 1).start())
        else:
            by_kind(u, lambda: out_copy(u, 2).start(), lambda: out_copy(u, 1).start())

            @pl.when(u == 6)
            def _():
                for i in range(3):
                    rep_copy(i).start()

    quarters=mates+[far]
    def quarter_at(i):
        return [me+1-2*core, me+2-4*chip, 3-me][i]
    def near_row_copy(i):
        return pltpu.make_async_remote_copy(src_ref=grad_ref.at[quarter_at(i)],dst_ref=grads.at[me],send_sem=near_send.at[i],recv_sem=near_recv.at[i],device_id=quarters[i],device_id_type=MESH)
    def keep_copy():
        return pltpu.make_async_copy(grad_ref.at[me],grads.at[me],keep_sem.at[0])
    def back_copy(d):
        return pltpu.make_async_remote_copy(src_ref=placed.at[(wide+d)%owners],dst_ref=back_ref.at[wide],send_sem=far_send.at[d],recv_sem=far_recv.at[d],device_id=others[d-1],device_id_type=MESH)
    def keep_back():
        return pltpu.make_async_copy(placed.at[wide],back_ref.at[wide],keep_sem.at[1])
    def place_field(f, _):
        place_one(slot_ref, grads, placed, f)
        return 0
    def row_step(t):
        fields=slot_ref.shape[0]
        @pl.when(t==ROW_AT)
        def _():
            keep_copy().wait()
            for i in range(3): near_row_copy(i).wait_recv()
        @pl.when(jnp.logical_and(t>=ROW_AT,t<ROW_AT+5))
        def _():
            lax.fori_loop((t-ROW_AT)*(fields//5),(t-ROW_AT+1)*(fields//5),place_field,0)
        for d in range(owners):
            @pl.when(t==ROW_AT+4+int(d*ROW_STEP))
            def _():
                if d==0: keep_back().start()
                else: back_copy(d).start()
    todo = [begin, stage_one]
    todo += [functools.partial(halving, k) for k in range(1, bits + 1)] + [cross]
    todo += [functools.partial(lambda j, u: grow(u, j), j) for j in reversed(range(bits))]
    plain_gaps = [0, 1, 2] + [1] * (len(todo) - 4) + [2]
    turned_gaps = [0, 1, 3, 4] + [1] * (len(todo) - 6) + [4, 3]
    plain_lag = [sum(plain_gaps[: i + 1]) for i in range(len(todo))]
    turned_lag = [sum(turned_gaps[: i + 1]) for i in range(len(todo))]

    def tick(t,_):
        for s in reversed(range(len(todo))):
            def stage(c, _):
                at = t - plain_lag[s]
                plain = jnp.where(at < 2, at + 4, jnp.where(at < 6, at - 2, at))
                u = jnp.where(c == 0, plain, TURNED)
                fits = jnp.logical_and(jnp.logical_and(at >= 0, at < UNITS), plain != TURNED)
                due = jnp.where(c == 0, fits, t == turned_lag[s])

                @pl.when(due)
                def _():
                    todo[s](u)

                return 0

            lax.fori_loop(0, 2, stage, 0)
        if with_rows:
            row_step(t)
        return 0
    if with_rows:
        keep_copy().start()
        for i in range(3): near_row_copy(i).start()
    lax.fori_loop(0, max(UNITS + plain_lag[-1], turned_lag[-1] + 1), tick, 0)
    if with_rows:
        keep_back().wait()
        for i in range(3): near_row_copy(i).wait_send()
        for d in range(1,owners): back_copy(d).wait()
    def finish(u,_):
        @pl.when(mine(u))
        def _():
            core_copy(u, acc.at[u]).wait_send()

        def left(parts):
            for k in range(bits):
                send_half(u, k, parts).wait_send()
            (y_block if parts == 2 else y_whole)(u).wait_send()
            for j in range(bits):
                grow_copy(u, j, parts).wait_send()
            out_copy(u, parts).wait()

        by_kind(u, lambda: left(2), lambda: left(1))
        return 0
    lax.fori_loop(0,UNITS,finish,0)
    for i in range(3):
        rep_copy(i).wait()

def reduce_all(own, extra, wide, rep_rows, rows=None):
    bits = wide.bit_length() - 1
    args = [own, extra]
    any_space = pl.BlockSpec(memory_space=pl.ANY)
    in_specs = [any_space] * 2
    out_shape = [
        jax.ShapeDtypeStruct((UNITS, 2, ROWS_U, LANES), BF),
        jax.ShapeDtypeStruct((3, rep_rows, LANES), BF),
    ]
    scratch = [
        pltpu.VMEM((UNITS, 2, ROWS_U, LANES), BF),
        pltpu.VMEM((2, 2, ROWS_U, LANES), BF),
        pltpu.VMEM((UNITS, 2, ROWS_U, LANES), BF),
        pltpu.VMEM((UNITS, 2, ROWS_U, LANES), BF),
        pltpu.SemaphoreType.DMA((2,)),
        pltpu.SemaphoreType.DMA((2 * bits + 2, UNITS)),
        pltpu.SemaphoreType.DMA((2 * bits + 2, UNITS)),
        pltpu.SemaphoreType.DMA((3,)),
        pltpu.SemaphoreType.DMA((3,)),
        pltpu.SemaphoreType.DMA((UNITS,)),
    ]
    if rows is not None:
        slots, grads, cap = rows
        args += [slots, grads]
        in_specs += [pl.BlockSpec(memory_space=pltpu.VMEM), any_space]
        back = (wide, grads.shape[1], cap)
        out_shape.append(jax.ShapeDtypeStruct(back, BF))
        scratch += [
            pltpu.VMEM(grads.shape, BF),
            pltpu.VMEM(back, BF),
            pltpu.SemaphoreType.DMA((3,)),
            pltpu.SemaphoreType.DMA((3,)),
            pltpu.SemaphoreType.DMA((wide,)),
            pltpu.SemaphoreType.DMA((wide,)),
            pltpu.SemaphoreType.DMA((2,)),
        ]
    return pl.pallas_call(
        functools.partial(reduce_kernel, bits, rows is not None),
        in_specs=in_specs,
        out_specs=[any_space] * len(out_shape),
        out_shape=out_shape,
        scratch_shapes=scratch,
        compiler_params=pltpu.CompilerParams(collective_id=0, has_side_effects=True, vmem_limit_bytes=VMEM),
        cost_estimate=pl.CostEstimate(flops=0, bytes_accessed=60 * 2**20, transcendentals=0),
        name="reduce_all",
    )(*args)


C0 = 0.7978845608028654
C1 = 0.044715
REP_ROWS = 512
GATE_AT = 256
GAIN_AT = 352
SHIFT_AT = 384
MISC_AT = 416


def gelu_both(x):
    square = x * x
    up = 0.5 * jnp.tanh(x * (square * (C0 * C1) + C0)) + 0.5
    act = x * up
    return act, up + (act - act * up) * (square * (6.0 * C0 * C1) + 2.0 * C0)


def soft_pair(a, b):
    top = jnp.maximum(a, b)
    ea, eb = jnp.exp(a - top), jnp.exp(b - top)
    total = ea + eb
    return ea / total, eb / total


def soft_pair_back(pa, pb, ga, gb):
    mean = pa * ga + pb * gb
    return pa * (ga - mean), pb * (gb - mean)


def fold(x):
    return sum(x[:, i * 128 : (i + 1) * 128] for i in range(x.shape[1] // 128))


def wide_lanes(x, n):
    return jnp.concatenate([x] * n, axis=1)


def split_low(x):
    high = x.astype(BF)
    return high, (x - high.astype(F32)).astype(BF)


def iota(shape, axis):
    return lax.broadcasted_iota(jnp.int32, shape, axis)


def row_of(rows, at):
    return (iota((rows, 128), 0) == at).astype(BF)


def dense_kernel(
    ids_ref, emb_ref, feats_ref, every_ref, mask_ref, label_ref, projw_ref, featw_ref, bias_ref,
    up_a, up_b, up_c, down_a, down_b, down_c, gain_ref, shift_ref, gate_f, gate_h, tin_f, tin_h,
    tower_ref,
    logit_ref, own_ref, emb_grad_ref, extra_ref,
    xt, act, slope, outs, og, ing, hid, hg, stat, inner, emb, feat, featw, gains, mixed, shifts, gates, tin,
    tbias, tout, tob, gain_acc, shift_acc, gate_acc, tin_acc, tbias_acc, tout_acc, tob_acc, emb_sem, extra_sem,
):
    ups = [up_a.at[0], up_b.at[0], up_c.at[0, 0], up_c.at[1, 0]]
    downs = [down_a.at[0], down_b.at[0], down_c.at[0, 0], down_c.at[1, 0]]
    step = pl.program_id(0)
    chunk, slot = step // 4, step % 4
    rows = xt.shape[1]
    core = ids_ref[14]
    owners = every_ref.shape[0]

    def expert_of(dom, k):
        return k if k < 2 else ids_ref[2 * dom + k]

    def raw_lanes(c):
        return pl.ds(pl.multiple_of(((c + core) % 3) * HALF, HALF), HALF)

    def pooled(sets):
        def sums(w, carry):
            total, mean = carry
            for at in sets:
                count = every_ref[w, at + 2 : at + 3, :]
                total, mean = total + count, mean + count * every_ref[w, at : at + 1, :]
            return total, mean

        zero = jnp.zeros((1, 128), F32)
        total, mean = lax.fori_loop(0, owners, sums, (zero, zero))
        mean = mean / total

        def squares(w, acc):
            for at in sets:
                off = every_ref[w, at : at + 1, :] - mean
                acc = acc + every_ref[w, at + 1 : at + 2, :] + every_ref[w, at + 2 : at + 3, :] * off * off
            return acc

        return mean, lax.rsqrt(lax.fori_loop(0, owners, squares, zero) / total + 1e-05)

    @pl.when(step == 0)
    def _():
        fetch = pltpu.make_async_copy(emb_ref, emb, emb_sem)
        fetch.start()
        for e in range(6):
            gains[e] = dot(gain_ref[...], row_of(14, ids_ref[e]), 0, 0).astype(BF)
        for dom, (gate, tower) in enumerate(((gate_f, tin_f), (gate_h, tin_h))):
            tin[dom] = tower[0]
            pick = (iota((16, 6), 0) % 8 == iota((16, 6), 1)).astype(BF)
            gates[dom] = dot(pick, gate[0], 1, 0).astype(BF)
            place = iota((16, 14), 0)
            ident = place % 4
            for k in range(4):
                ident = jnp.where(place % 4 == k, expert_of(dom, k), ident)
            same = ident == iota((16, 14), 1)
            first, second = jnp.logical_and(same, place < 4), jnp.logical_and(same, place < 8)
            third = jnp.logical_and(second, place >= 4)
            mixed[dom] = (
                dot(first.astype(BF), gain_ref[...], 1, 0) + dot(third.astype(BF), shift_ref[...], 1, 0)
            ).astype(BF)
            shifts[dom] = dot(second.astype(BF), shift_ref[...], 1, 0).astype(BF)
            d = ids_ref[12 + dom]
            tbias[dom] = dot(tower_ref[...], row_of(16, d), 0, 0)
            tout[dom] = dot(tower_ref[...], row_of(16, 6 + d), 0, 0)
            tob[dom] = dot(tower_ref[...], row_of(128, d), 1, 0)
        featw[0:128, :] = featw_ref[...]
        featw[128:144, :] = jnp.where(iota((16, D), 0) == 0, bias_ref[...].astype(F32), 0.0).astype(BF)
        feat[128:144, :] = (iota((16, rows), 0) == 0).astype(BF)
        moments = [pooled((0,)), pooled((3, 11))]
        for c in range(rows // HALF):
            mean, scale = moments[c // 2]
            x = (feats_ref[raw_lanes(c), :] - mean) * scale
            feat[0:128, c * HALF : (c + 1) * HALF] = x.T.astype(BF)
        for ref in (gain_acc, shift_acc, gate_acc, tin_acc, tbias_acc, tout_acc, tob_acc):
            ref[...] = jnp.zeros_like(ref)
        fetch.wait()
        for c in range(rows // HALF):
            cols = slice(c * HALF, (c + 1) * HALF)
            x = dot(projw_ref[...], emb[:, cols], 0, 0) + dot(featw[...], feat[:, cols], 0, 0)
            xt[:, cols] = x.astype(BF)

    @pl.when(step < 12)
    def _():
        lanes = pl.ds(pl.multiple_of(chunk * HALF, HALF), HALF)

        for s in range(4):
            pre = dot(ups[s][...], xt[:, lanes], 0, 0)
            a, g = gelu_both(pre)
            a = a.astype(BF)
            act[slot, s, :, lanes] = a
            slope[slot, s, :, lanes] = g.astype(BF)

        total = dot(downs[0][...], act[slot, 0, :, lanes], 0, 0)
        for s in range(1, 4):
            total += dot(downs[s][...], act[slot, s, :, lanes], 0, 0)
        outs[slot] = total

    def middle():
        lanes = pl.ds(pl.multiple_of(chunk * HALF, HALF), HALF)
        dom = chunk // 2
        x = xt[:, lanes]
        logit_gates = dot(gates[dom], x, 1, 0)
        s0, s1 = soft_pair(logit_gates[0:1], logit_gates[1:2])
        d0, d1 = soft_pair(logit_gates[2:3], logit_gates[3:4])
        t0, t1 = soft_pair(logit_gates[4:5], logit_gates[5:6])
        coef = jnp.concatenate([t0 * s0, t0 * s1, t1 * d0, t1 * d1], axis=0)
        high = coef.astype(BF).astype(F32)
        spare = jnp.zeros((8, HALF), F32)
        coef_low = jnp.concatenate([high, coef - high, spare], axis=0).astype(BF)
        hg[...] = dot(shifts[dom], coef_low, 0, 0)
        stat[8:12, :] = coef
        expert = [0, 1, 2 + 2 * dom, 3 + 2 * dom]

        def normalize(t, _):
            cols = pl.ds(pl.multiple_of(t * 128, 128), 128)
            for k in range(4):
                v = outs[k, :, cols]
                mean = jnp.sum(v, axis=0, keepdims=True) * (1.0 / D)
                v = v - mean
                var = jnp.sum(v * v, axis=0, keepdims=True) * (1.0 / D)
                stat[k : k + 1, cols] = mean
                stat[4 + k : 5 + k, cols] = lax.rsqrt(var + 1e-05)
            scale = [stat[4 + k : 5 + k, cols] * stat[8 + k : 9 + k, cols] for k in range(4)]
            for r in range(8):
                band = slice(r * 64, (r + 1) * 64)
                acc = hg[band, cols]
                for k in range(4):
                    n = (outs[k, band, cols] - stat[k : k + 1, cols]) * scale[k]
                    acc = acc + n * gains[expert[k], band, :].astype(F32)
                hid[band, cols] = acc.astype(BF)
            return 0

        lax.fori_loop(0, 4, normalize, 0)
        h = hid[...]
        pre = dot(tin[dom], h, 0, 0) + wide_lanes(tbias[dom], 4)
        tact, tslope = gelu_both(pre)
        weight = wide_lanes(tout[dom], 4)
        logit = jnp.sum(tact * weight, axis=0, keepdims=True) + wide_lanes(tob[dom, 12:13, :], 4)
        logit_ref[:, raw_lanes(chunk)] = logit
        live, label = mask_ref[:, raw_lanes(chunk)].astype(F32), label_ref[:, raw_lanes(chunk)].astype(F32)
        grad = (jax.nn.sigmoid(logit) - label) * live
        tob_acc[dom, 0:1, :] += fold(grad)
        tout_acc[dom] += fold(grad * tact)
        low = (grad * weight * tslope).astype(BF)
        tbias_acc[dom] += fold(low.astype(F32))
        tin_acc[dom] += dot(h, low, 1, 1)
        back = dot(tin[dom], low, 1, 0)
        hg[...] = back
        back_high, back_low = split_low(back)
        shift_acc[dom] += dot(back_high, coef_low, 1, 1) + dot(back_low, coef_low, 1, 1)
        inner[...] = dot(mixed[dom], back_high, 1, 0) + dot(mixed[dom], back_low, 1, 0)

        def denormalize(t, _):
            cols = pl.ds(pl.multiple_of(t * 128, 128), 128)
            place = pl.ds(pl.multiple_of(chunk * HALF + t * 128, 128), 128)
            for k in range(4):
                mean, rstd = stat[k : k + 1, cols], stat[4 + k : 5 + k, cols]
                c = stat[8 + k : 9 + k, cols]
                m2 = 0.0
                for r in range(8):
                    band = slice(r * 64, (r + 1) * 64)
                    w = (outs[k, band, cols] - mean) * rstd * hg[band, cols]
                    m2 = m2 + jnp.sum(w * gains[expert[k], band, :].astype(F32), axis=0, keepdims=True)
                    gain_acc[expert[k], band, :] += w * c
                m1 = inner[k : k + 1, cols]
                inner[4 + k : 5 + k, cols] += m2
                cr = c * rstd
                slant = cr * rstd * m2 * (1.0 / D)
                level = mean * slant - cr * m1 * (1.0 / D)
                for r in range(8):
                    band = slice(r * 64, (r + 1) * 64)
                    scaled = hg[band, cols] * gains[expert[k], band, :].astype(F32)
                    og[k, band, place] = (scaled * cr - outs[k, band, cols] * slant + level).astype(BF)
            return 0

        lax.fori_loop(0, 4, denormalize, 0)
        a = [inner[4 + k : 5 + k, :] for k in range(4)]
        g0, g1 = soft_pair_back(s0, s1, t0 * a[0], t0 * a[1])
        g2, g3 = soft_pair_back(d0, d1, t1 * a[2], t1 * a[3])
        g4, g5 = soft_pair_back(t0, t1, s0 * a[0] + s1 * a[1], d0 * a[2] + d1 * a[3])
        zero = jnp.zeros_like(g0)
        g = jnp.concatenate([g0, g1, g2, g3, g4, g5, zero, zero], axis=0)
        high = g.astype(BF).astype(F32)
        g = jnp.concatenate([high, g - high], axis=0).astype(BF)
        gate_acc[dom] += dot(g, x, 1, 1)
        ing[:, lanes] = dot(gates[dom], g, 0, 0)

    @pl.when(jnp.logical_and(step < 12, slot == 3))
    def _():
        middle()

    def back(k, at, n):
        lanes = slice(at, at + n)
        for s in range(4):
            p = dot(downs[s][...], og[k, :, lanes], 1, 0) * slope[k, s, :, lanes].astype(F32)
            slope[k, s, :, lanes] = p.astype(BF)

        for s in range(4):
            grad, p = og[k, :, lanes], slope[k, s, :, lanes]
            own_ref[0, s, 0:D, :] = dot(xt[:, lanes], p, 1, 1).astype(BF)
            d = dot(act[k, s, :, lanes], grad, 1, 1).astype(BF)
            own_ref[0, s, D : D + 256, :] = d[:, 0:256]
            own_ref[0, s, D + 256 : D + 512, :] = d[:, 256:512]

        for t in range(n // HALF):
            cols = slice(at + t * HALF, at + (t + 1) * HALF)
            total = dot(ups[0][...], slope[k, 0, :, cols], 1, 0)
            for s in range(1, 4):
                total += dot(ups[s][...], slope[k, s, :, cols], 1, 0)
            ing[:, cols] += total

    expert = step - 12

    @pl.when(jnp.logical_and(expert >= 0, expert < 2))
    def _():
        back(expert, 0, rows)

    @pl.when(jnp.logical_and(expert >= 2, expert < 4))
    def _():
        back(expert, 0, DSLOT)

    @pl.when(expert >= 4)
    def _():
        back(expert - 2, DSLOT, rows - DSLOT)

    def exact(select, x):
        high, low = split_low(x)
        return dot(select, high, 1, 1) + dot(select, low, 1, 1)

    @pl.when(expert == 5)
    def _():
        low = ing[...].astype(BF)
        proj = dot(emb[...], low, 1, 1).astype(BF)
        feat_grad = dot(feat[...], low, 1, 1)
        for c in range(rows // HALF):
            cols = slice(c * HALF, (c + 1) * HALF)
            emb[:, cols] = dot(projw_ref[...], low[:, cols], 1, 0).astype(BF)
        put = pltpu.make_async_copy(emb, emb_grad_ref, emb_sem)
        put.start()
        unit = act.at[:, :, :, 0:256]
        act[:, :, :, 0:256] = jnp.zeros((4, 4, 256, 256), BF)
        spots = [ids_ref[15 + q] for q in range(4)]
        for q in range(4):
            part = proj[q * 160 : (q + 1) * 160]
            act[spots[q], 2, 0:160, 0:256] = part[:, 0:256]
            act[spots[q], 2, 160:256, 0:256] = part[0:96, 256:512]
            act[spots[q], 3, 0:64, 0:256] = part[96:160, 256:512]
        for dom in range(2):
            d = ids_ref[12 + dom]
            tower = tin_acc[dom].astype(BF)
            act[ids_ref[15 + d // 2], d % 2, :, 0:128] = tower[0:256]
            act[ids_ref[15 + d // 2], d % 2, :, 128:256] = tower[256:512]
            g = gate_acc[dom]
            g = g[0:8] + g[8:16]
            place = pl.ds(pl.multiple_of(d * 16, 16), 16)
            act[spots[3], 1, place, 0:256] = jnp.concatenate([g[:, 0:256], g[:, 256:512]], axis=0).astype(BF)
        act[spots[3], 0, 0:128, 0:256] = feat_grad[0:128, 0:256].astype(BF)
        act[spots[3], 0, 128:256, 0:256] = feat_grad[0:128, 256:512].astype(BF)
        total = 0.0
        for e in range(6):
            total = total + exact(row_of(16, ids_ref[e]), gain_acc[e])
        offset = 0.0
        misc_a = misc_b = 0.0
        line = iota((16, 128), 0)
        lane = iota((16, 128), 1)
        for dom in range(2):
            col = iota((16, 16), 1)
            ident = col % 4
            for k in range(4):
                ident = jnp.where(col % 4 == k, expert_of(dom, k), ident)
            choose = jnp.logical_and(ident == iota((16, 16), 0), col < 8).astype(BF)
            offset = offset + exact(choose, shift_acc[dom])
            d = ids_ref[12 + dom]
            misc_a = misc_a + exact(row_of(16, d), tbias_acc[dom])
            misc_b = misc_b + exact(row_of(16, d), tout_acc[dom])
            bias = jnp.sum(tob_acc[dom, 0:1, :], axis=1, keepdims=True)
            misc_a = misc_a + jnp.where(jnp.logical_and(line == 8, lane == d), bias, 0.0)
        misc = jnp.concatenate([misc_a, misc_b], axis=1)
        line = iota((16, 256), 0)
        misc = misc + jnp.where(line == 6, feat_grad[128:129, 0:256], 0.0)
        misc = misc + jnp.where(line == 7, feat_grad[128:129, 256:512], 0.0)
        for at, x in ((GAIN_AT, total), (SHIFT_AT, offset)):
            act[spots[3], 1, at - 256 : at - 240, 0:256] = x[:, 0:256].astype(BF)
            act[spots[3], 1, at - 240 : at - 224, 0:256] = x[:, 256:512].astype(BF)
        act[spots[3], 1, MISC_AT - 256 : MISC_AT - 240, 0:256] = misc.astype(BF)
        out = pltpu.make_async_copy(unit, extra_ref, extra_sem)
        out.start()
        out.wait()
        put.wait()


def dense(ids, emb, feats, every, mask, label, projw, featw, bias, ups, downs, gains, shifts, gate, tin, tower):
    rows = emb.shape[1]

    def ahead(i):
        c, j = i // 4, i % 4
        front = jnp.where(j < 2, j, jnp.where(c < 2, j, j + 2))
        return jnp.where(i < 12, front, i - 12)

    def whole(x):
        return pl.BlockSpec(x.shape, lambda i, ids: (0,) * len(x.shape), pipeline_mode=pl.Buffered(1))

    any_space = pl.BlockSpec(memory_space=pl.ANY)
    in_specs = [any_space] + [whole(x) for x in (feats, every, mask, label, projw, featw, bias)]
    for group in (ups, downs):
        block = group[0].shape[1:]
        in_specs += [
            pl.BlockSpec((1,) + block, lambda i, ids: (ids[ahead(i)], 0, 0)),
            pl.BlockSpec((1,) + block, lambda i, ids: (ids[6 + ahead(i)], 0, 0)),
            pl.BlockSpec((2, 1) + block, lambda i, ids: (0, ahead(i), 0, 0)),
        ]
    in_specs += [whole(gains), whole(shifts)]
    for x in (gate, tin):
        for dom in range(2):
            in_specs.append(
                pl.BlockSpec(
                    (1,) + x.shape[1:], lambda i, ids, at=12 + dom: (ids[at], 0, 0), pipeline_mode=pl.Buffered(1)
                )
            )
    in_specs.append(whole(tower))
    return pl.pallas_call(
        dense_kernel,
        grid_spec=pltpu.PrefetchScalarGridSpec(
            num_scalar_prefetch=1,
            grid=(18,),
            in_specs=in_specs,
            out_specs=[
                pl.BlockSpec((1, rows), lambda i, ids: (0, 0)),
                pl.BlockSpec((1, 4, 2 * D, 256), lambda i, ids: (jnp.maximum(i - 12, 0), 0, 0, 0)),
                any_space,
                any_space,
            ],
            scratch_shapes=[
                pltpu.VMEM((D, rows), BF),
                pltpu.VMEM((4, 4, 256, rows), BF),
                pltpu.VMEM((4, 4, 256, rows), BF),
                pltpu.VMEM((4, D, HALF), F32),
                pltpu.VMEM((4, D, rows), BF),
                pltpu.VMEM((D, rows), F32),
                pltpu.VMEM((D, HALF), BF),
                pltpu.VMEM((D, HALF), F32),
                pltpu.VMEM((16, HALF), F32),
                pltpu.VMEM((16, HALF), F32),
                pltpu.VMEM(emb.shape, BF),
                pltpu.VMEM((144, rows), BF),
                pltpu.VMEM((144, D), BF),
                pltpu.VMEM((6, D, 128), BF),
                pltpu.VMEM((2, 16, D), BF),
                pltpu.VMEM((2, 16, D), BF),
                pltpu.VMEM((2, 16, D), BF),
                pltpu.VMEM((2, D, 128), BF),
                pltpu.VMEM((2, 128, 128), F32),
                pltpu.VMEM((2, 128, 128), F32),
                pltpu.VMEM((2, 16, 128), F32),
                pltpu.VMEM((6, D, 128), F32),
                pltpu.VMEM((2, D, 16), F32),
                pltpu.VMEM((2, 16, D), F32),
                pltpu.VMEM((2, D, 128), F32),
                pltpu.VMEM((2, 128, 128), F32),
                pltpu.VMEM((2, 128, 128), F32),
                pltpu.VMEM((2, 8, 128), F32),
                pltpu.SemaphoreType.DMA,
                pltpu.SemaphoreType.DMA,
            ],
        ),
        out_shape=[
            jax.ShapeDtypeStruct((1, rows), F32),
            jax.ShapeDtypeStruct((6, 4, 2 * D, 256), BF),
            jax.ShapeDtypeStruct(emb.shape, BF),
            jax.ShapeDtypeStruct((4, 4, 256, 256), BF),
        ],
        compiler_params=pltpu.CompilerParams(vmem_limit_bytes=62 * 2**20),
        cost_estimate=pl.CostEstimate(flops=39 * 10**9, bytes_accessed=60 * 2**20, transcendentals=0),
        name="dense_all",
    )(ids, emb, feats, every, mask, label, projw, featw, bias, *ups, *downs, gains, shifts, gate, gate, tin, tin, tower)


def finish_kernel(with_rows, ids_ref, even_ref, odd_ref, unit_ref, others_ref, *refs):
    if with_rows:
        back_ref, row_ref = refs[0], refs[1]
        refs = refs[2:]
    (up_ref, down_ref, proj_ref, feat_ref, bias_ref, gain_ref, shift_ref, gate_ref, tin_ref, tbias_ref,
     tout_ref, tob_ref, quarters) = refs
    step = pl.program_id(0)
    for i, sums_ref in enumerate((even_ref, odd_ref)):
        up_ref[i] = sums_ref[0, 0, 0:D, :].astype(F32)
        down_ref[i, :, 0:256] = sums_ref[0, 0, D : D + 256, :].astype(F32)
        down_ref[i, :, 256:512] = sums_ref[0, 0, D + 256 : D + 512, :].astype(F32)
    if with_rows:
        @pl.when(step < with_rows)
        def _():
            row_ref[0] = back_ref[...].astype(F32)

    @pl.when(step == 0)
    def _():
        me = ids_ref[14]
        quarters[me] = unit_ref[0, 0, 0:REP_ROWS, :].astype(F32)
        for i in range(3):
            quarters[ids_ref[15 + i]] = others_ref[i].astype(F32)
        cols = proj_ref.shape[0]
        proj_ref[:, 0:256] = unit_ref[0, 0, REP_ROWS : REP_ROWS + cols, :].astype(F32)
        proj_ref[:, 256:512] = unit_ref[0, 0, REP_ROWS + cols : REP_ROWS + 2 * cols, :].astype(F32)
        for d in range(DOMAINS):
            band = slice((d % 2) * 256, (d % 2) * 256 + 256)
            tin_ref[d, 0:256, :] = quarters[d // 2, band, 0:128]
            tin_ref[d, 256:512, :] = quarters[d // 2, band, 128:256]
            g = quarters[3, GATE_AT + 16 * d : GATE_AT + 16 * d + 16, :]
            g = jnp.concatenate([g[0:8], g[8:16]], axis=1)
            gate_ref[d] = g[0:6]
        feat_ref[:, 0:256] = quarters[3, 0:128, :]
        feat_ref[:, 256:512] = quarters[3, 128:256, :]
        for at, ref in ((GAIN_AT, gain_ref), (SHIFT_AT, shift_ref)):
            ref[:, 0:256] = quarters[3, at : at + 14, :]
            ref[:, 256:512] = quarters[3, at + 16 : at + 30, :]
        tbias_ref[...] = quarters[3, MISC_AT : MISC_AT + 6, 0:128]
        tout_ref[...] = quarters[3, MISC_AT : MISC_AT + 6, 128:256]
        bias_ref[:, 0:256] = quarters[3, MISC_AT + 6 : MISC_AT + 7, :]
        bias_ref[:, 256:512] = quarters[3, MISC_AT + 7 : MISC_AT + 8, :]
        tob_ref[...] = quarters[3, MISC_AT + 8 : MISC_AT + 9, 0:128]


def finish(ids, sums, others, proj_cols, back=None):
    def whole(s):
        return pl.BlockSpec(s, lambda i, ids: (0,) * len(s))

    def unit(odd):
        return lambda i, ids: (ids[2 * i + odd] % 16, ids[2 * i + odd] // 16, 0, 0)

    in_specs = [
        pl.BlockSpec((1, 1, ROWS_U, LANES), unit(0)),
        pl.BlockSpec((1, 1, ROWS_U, LANES), unit(1)),
        pl.BlockSpec((1, 1, ROWS_U, LANES), lambda i, ids: (6, 0, 0, 0)),
        whole(others.shape),
    ]
    args = [sums, sums, sums, others]
    shapes = [
        (14, D, 256), (14, 256, D), (proj_cols, D), (DENSE, D), (1, D), (14, D), (14, D), (DOMAINS, 6, D),
        (DOMAINS, D, 128), (DOMAINS, 128), (DOMAINS, 128), (1, 128),
    ]
    out_specs = [
        pl.BlockSpec((2, D, 256), lambda i, ids: (i, 0, 0)),
        pl.BlockSpec((2, 256, D), lambda i, ids: (i, 0, 0)),
    ] + [whole(s) for s in shapes[2:]]
    if back is not None:
        blocks, cols, cap = back.shape
        each = -(-blocks // 7)
        last = lambda i: jnp.minimum(i, blocks // each - 1)
        args.append(back)
        in_specs.append(pl.BlockSpec((each, cols, cap), lambda i, ids: (last(i), 0, 0)))
        shapes.insert(0, (1, blocks, cols, cap))
        out_specs.insert(0, pl.BlockSpec((1, each, cols, cap), lambda i, ids: (0, last(i), 0, 0)))
    return pl.pallas_call(
        functools.partial(finish_kernel, 0 if back is None else blocks // each),
        grid_spec=pltpu.PrefetchScalarGridSpec(
            num_scalar_prefetch=1,
            grid=(7,),
            in_specs=in_specs,
            out_specs=out_specs,
            scratch_shapes=[pltpu.VMEM((4, REP_ROWS, LANES), F32)],
        ),
        out_shape=[jax.ShapeDtypeStruct(s, F32) for s in shapes],
        compiler_params=pltpu.CompilerParams(vmem_limit_bytes=VMEM),
        cost_estimate=pl.CostEstimate(flops=0, bytes_accessed=32 * 2**20, transcendentals=0),
        name="finish",
    )(ids, *args)


def shards(
    embed_table,
    requests,
    slot_index,
    event_mask,
    labels,
    dense_feats,
    proj_weight,
    dense_weight,
    proj_bias,
    up_weight,
    down_weight,
    norm_gain,
    norm_shift,
    gate_weight,
    tower_in,
    tower_bias,
    tower_out,
    tower_out_bias,
):
    narrow = lax.axis_size("narrow")
    me = lax.axis_index("narrow")
    chip, core = me // 2, me % 2
    ev_rows, fields = slot_index.shape
    rows = ev_rows // narrow
    owners, cap = requests.shape[1], requests.shape[2]
    hid_here = up_weight.shape[2]
    other_chip = [(i, i ^ 2) for i in range(narrow)]
    other_core = [(i, i ^ 1) for i in range(narrow)]
    full = 3 * chip + 2 * core
    half = 3 * chip + 1

    def swap(x, pairs):
        return lax.ppermute(x, "narrow", pairs)

    def chip_experts(w, which):
        return jnp.concatenate(
            [w[:SHARED], lax.dynamic_slice_in_dim(w, SHARED + 6 * which, 6, axis=0)], axis=0
        )

    def bring(w):
        far = swap(chip_experts(w, 1 - chip), other_chip)
        at = lambda x, start, size: lax.dynamic_slice_in_dim(x, start, size, axis=0)
        base = SHARED + 6 * chip
        away = 4 * (1 - core)
        theirs = jnp.stack(
            [
                jnp.concatenate([w[:SHARED], at(w, base + away, 2), at(w, base + 2, 2)], axis=0),
                jnp.concatenate([far[:SHARED], at(far, 2 + away, 2), far[4:6]], axis=0),
            ]
        )
        return w, far, swap(theirs, other_core)

    six = jnp.arange(6, dtype=jnp.int32)
    spot = jnp.where(six < 2, six, jnp.where(six < 4, six + 4 * core, six))
    offset = jnp.arange(narrow, dtype=jnp.int32)
    offset = jnp.where(chip == 1, (offset + 2) % 4, offset)
    offset = jnp.where(core == 1, offset + 1 - 2 * (offset % 2), offset)
    ids = jnp.concatenate(
        [
            jnp.where(six < 2, six, spot + 6 * chip),
            spot,
            jnp.stack([full, half, core]),
            (offset % 2) * 2 + offset // 2,
        ]
    ).astype(jnp.int32)
    mask_row, label_row = event_mask[None], labels[None]

    turn = lambda i: (i // 3) * 3 + (i % 3 + (i // 3) % 2) % 3
    table_rows = embed_table.shape[0]
    cols = fields * EMB
    blocks = ev_rows // HALF
    hi_n = 256
    lo_n = ev_rows // hi_n
    direct = cap % hi_n == 0
    asked = requests[0].transpose(0, 2, 1)
    if direct:
        embedded, far_up, far_down, their_up, their_down, proj_full, every = front(
            asked, embed_table.T, slot_index.T, dense_feats, mask_row, up_weight, down_weight, proj_weight
        )
        ups, downs = (up_weight, far_up, their_up), (down_weight, far_down, their_down)
    else:
        asked = lax.all_to_all(asked, "wide", 0, 0, tiled=True)
        ups, downs = bring(up_weight), bring(down_weight)
        proj_full = lax.all_gather(proj_weight, "narrow", axis=0)
        stats = local_stats(core[None], dense_feats, mask_row)
        stats = jnp.concatenate([stats, swap(stats, other_core)], axis=0)
        every = lax.all_to_all(
            jnp.broadcast_to(stats, (owners,) + stats.shape), "wide", 0, 0, tiled=True
        )
        tab = embed_table.reshape(32, table_rows // 32, cols).transpose(0, 2, 1)
        flat = asked.transpose(1, 0, 2).reshape(fields, DOMAINS, DSLOT).transpose(1, 0, 2)
        found = lookup(flat, tab, table_rows // 32, "lookup_rows", DOMAINS)
        found = found.transpose(1, 0, 2).reshape(cols, owners, cap).transpose(1, 0, 2)
        received = lax.all_to_all(found, "wide", 0, 0, tiled=True)
        received = received.transpose(1, 0, 2).reshape(cols, lo_n, hi_n).transpose(1, 0, 2)
        slots = slot_index.reshape(blocks, HALF, fields).transpose(0, 2, 1)
        embedded = lookup(slots, received, hi_n, "order_rows", narrow, turn)
        embedded = lax.all_to_all(embedded, "narrow", 0, 0, tiled=True)
    embedded = embedded.reshape(narrow * cols, rows)
    proj_full = proj_full.reshape(narrow * cols, D)

    tower = jnp.concatenate(
        [tower_bias, tower_out, jnp.pad(tower_out_bias[None], ((0, 3), (0, 128 - DOMAINS)))], axis=0
    )
    logits, own, embed_grad, extra = dense(
        ids, embedded, dense_feats, every, mask_row, label_row, proj_full, dense_weight, proj_bias[None],
        ups, downs, norm_gain, norm_shift, gate_weight.transpose(0, 2, 1), tower_in, tower,
    )
    extra = extra.reshape(narrow, ROWS_U, LANES)

    embed_grad = embed_grad.reshape(narrow, cols, rows)
    if not direct:
        embed_grad = lax.all_to_all(embed_grad, "narrow", 0, 0, tiled=True)
        returned = place(slot_index.T, embed_grad, (lo_n, cols, hi_n))
        returned = returned.transpose(1, 0, 2).reshape(cols, owners, cap).transpose(1, 0, 2)
        row_grads = lax.all_to_all(returned, "wide", 0, 0, tiled=True)

    if direct:
        sums, others, row_grads = reduce_all(own, extra, owners, REP_ROWS, (slot_index.T, embed_grad, cap))
    else:
        sums, others = reduce_all(own, extra, owners, REP_ROWS)
    expert = jnp.arange(14, dtype=jnp.int32)
    domain = (expert - SHARED) // DOM_EXP
    unit = jnp.where(domain % 3 == 0, 0, jnp.where(domain % 3 == 1, 4, 2)) + expert % 2
    away = jnp.where(domain // 3 == chip, 0, 16)
    unit = jnp.where(expert < SHARED, expert + 7, unit + away)
    marks = jnp.concatenate([unit, jnp.stack([me, me + 1 - 2 * core, me + 2 - 4 * chip, 3 - me])])
    outs = finish(marks.astype(jnp.int32), sums, others, cols, row_grads if direct else None)
    if not direct:
        outs = [row_grads.astype(F32)[None]] + list(outs)
    (row_grads, up_grad, down_grad, proj_grad, feat_grad, bias_grad, gain_grad, shift_grad, gate_grad, tower_grad,
     tower_bias_grad, tower_out_grad, out_bias_grad) = outs
    return (
        logits[0],
        row_grads.transpose(0, 1, 3, 2),
        proj_grad,
        feat_grad,
        bias_grad[0],
        up_grad,
        down_grad,
        gain_grad,
        shift_grad,
        gate_grad.transpose(0, 2, 1),
        tower_grad,
        tower_bias_grad,
        tower_out_grad,
        out_bias_grad[0, :DOMAINS],
    )


def solution(mesh):
    placed = (
        P("wide", "narrow"),
        P("wide", None, None, "narrow"),
        P("wide", "narrow"),
        P(("wide", "narrow")),
        P(("wide", "narrow")),
        P(("wide", "narrow"), None),
        P("narrow", None),
        P(),
        P(),
        P(None, None, "narrow"),
        P(None, "narrow", None),
        P(),
        P(),
        P(),
        P(),
        P(),
        P(),
        P(),
    )
    return jax.shard_map(
        shards,
        mesh=mesh,
        in_specs=placed,
        out_specs=(
            P(("wide", "narrow")),
            P("wide", None, None, "narrow"),
            P("narrow", None),
            P(),
            P(),
            P(None, None, "narrow"),
            P(None, "narrow", None),
            P(),
            P(),
            P(),
            P(),
            P(),
            P(),
            P(),
        ),
        check_vma=False,
    )
```
